32 devices in a mesh: expert: 8 (over y, x, core), wshard: 4 (over z).
Axes of the slice: x: 2, y: 2, z: 4, core: 2. Of those that a mesh axis runs over, the one named last changes fastest.
Arguments:
- tokens: bfloat16 [4096, 2048], P(('expert', 'wshard')), may hold values from -6 to 6
- segment_ids: int32 [4096], P('expert'), may hold values from 0 to 15, never falling along the last dimension, each value on 1 to 512 neighbouring positions
- routes: int32 [4096, 8], P(('expert', 'wshard')), may hold values from 0 to 15, all different within a row; in each aligned block of 128 rows (0 to 127, 128 to 255, ...) at most 128 rows name the same one
- pair_order: int32 [32768], P(('expert', 'wshard')), may hold values from 0 to 32767, each once
- attn_gain: bfloat16 [2048], P(('expert', 'wshard')), may hold values from 0.5 to 1.5
- w_query: bfloat16 [2048, 2048], P(('expert', 'wshard')), may hold values from -0.125 to 0.125
- w_key: bfloat16 [2048, 2048], P(('expert', 'wshard')), may hold values from -0.125 to 0.125
- w_value: bfloat16 [2048, 2048], P(('expert', 'wshard')), may hold values from -0.125 to 0.125
- query_gain: bfloat16 [128], P(('expert', 'wshard')), may hold values from 0.5 to 1.5
- key_gain: bfloat16 [128], P(('expert', 'wshard')), may hold values from 0.5 to 1.5
- w_out: bfloat16 [2048, 2048], P(('expert', 'wshard')), may hold values from -1 to 1
- ffn_gain: bfloat16 [2048], P(('expert', 'wshard')), may hold values from 0.5 to 1.5
- w_router: bfloat16 [2048, 16], P(('expert', 'wshard')), may hold values from -0.0625 to 0.0625
- w_gate: bfloat16 [16, 2048, 1024], P('expert', 'wshard'), may hold values from -0.125 to 0.125
- w_up: bfloat16 [16, 2048, 1024], P('expert', 'wshard'), may hold values from -0.125 to 0.125
- w_down: bfloat16 [16, 1024, 2048], P('expert', None, 'wshard'), may hold values from -1.5 to 1.5
- out_grad: bfloat16 [4096, 2048], P(('expert', 'wshard')), may hold values from -6 to 6
Outputs:
- mixed_out: bfloat16 [4096, 2048], P(('expert', 'wshard'))
- tokens_grad: bfloat16 [4096, 2048], P(('expert', 'wshard'))
- attn_gain_grad: float32 [2048], P(('expert', 'wshard'))
- w_query_grad: float32 [2048, 2048], P(('expert', 'wshard'))
- w_key_grad: float32 [2048, 2048], P(('expert', 'wshard'))
- w_value_grad: float32 [2048, 2048], P(('expert', 'wshard'))
- query_gain_grad: float32 [128], P(('expert', 'wshard'))
- key_gain_grad: float32 [128], P(('expert', 'wshard'))
- w_out_grad: float32 [2048, 2048], P(('expert', 'wshard'))
- ffn_gain_grad: float32 [2048], P(('expert', 'wshard'))
- w_router_grad: float32 [2048, 16], P(('expert', 'wshard'))
- w_gate_grad: float32 [16, 2048, 1024], P('expert', 'wshard')
- w_up_grad: float32 [16, 2048, 1024], P('expert', 'wshard')
- w_down_grad: float32 [16, 1024, 2048], P('expert', None, 'wshard')
The draws below stay inside these ranges and needn't reach their ends.
Inputs may be any that keep to these rules, and one draw needn't show every extreme that they name: `routes`: each row names 8 different experts; in each aligned block of 128 rows (the rows of one device) no expert is named by more than 128 rows, and some expert reaches 128. `pair_order`: each number once. `segment_ids`: never falling; each document has 1 to 512 tokens, one has exactly 512.
All inputs are finite; a program needn't handle non-finite values.
Results may differ from the reference program's by a relative error of at most 0.019.
Values may be sent and summed in bfloat16 or wider, within the bound.
A program may use at most 384 MiB of HBM per device.

```python
import math
import jax
import jax.numpy as jnp
import numpy as np
from jax import lax

D = 2048
HEADS = 16
HD = 128
FF = 1024
TOPK = 8
TOK_DEV = 128
EXPERTS = 16
SEQLEN = 512
TOKENS = 4096
MOST = 128
CAP = 640
N_WSHARD = 4


def block_scale(stream_key, shape, cuts, smallest, largest):
    level = 1.0
    for dim, blocks in cuts:
        steps = jax.random.uniform(jax.random.fold_in(jax.random.fold_in(stream_key, 6), dim), (blocks,), jnp.float32, smallest / len(cuts), largest / len(cuts))
        level = level * jnp.repeat(jnp.exp(steps), shape[dim] // blocks).reshape((-1,) + (1,) * (len(shape) - 1 - dim))
    return level


def profile(amount, total, reach, lean):
    portions = [(1 << 20) // math.isqrt(rank ** lean) + 1 for rank in range(2, amount + 1)]
    spare, counts = total - reach - (amount - 1), [1] * (amount - 1)
    while spare > 0:
        candidates = [i for i in range(amount - 1) if counts[i] < reach]
        pool, budget = sum([portions[i] for i in candidates]), spare
        for i in candidates:
            extra = min(reach - counts[i], max(1, budget * portions[i] // pool), spare)
            counts[i] = counts[i] + extra
            spare = spare - extra
    return np.array([reach] + counts)


def ragged(stream_key, number_of, total, bound, lean):
    if number_of == 2:
        one = jax.random.randint(stream_key, (), max(1, total - bound), min(bound, total - 1) + 1)
        return jnp.stack([one, total - one])
    lengths = jnp.asarray(profile(number_of, total, bound, lean), jnp.int32)
    pairs = (number_of - 1) // 2
    giver, receiver = lengths[1:1 + 2 * pairs:2], lengths[2:2 + 2 * pairs:2]
    margin = jnp.minimum(giver - 1, bound - receiver)
    moved = jax.random.randint(jax.random.fold_in(stream_key, 1), (pairs,), 0, 1 << 20) % (margin + 1)
    lengths = lengths.at[1:1 + 2 * pairs:2].set(giver - moved).at[2:2 + 2 * pairs:2].set(receiver + moved)
    return lengths[jax.random.permutation(jax.random.fold_in(stream_key, 2), number_of)]


def assign_block(key, own, number, rows, count, top, most, skew):
    ranking = jax.random.permutation(key, count)
    packed, usual = portions_of(count, rows * top, most, skew, True), portions_of(count, rows * top, most, skew, False)
    places = jnp.arange(count)

    def named(lengths, offset_by):
        used = int((lengths > 0).sum())
        fixed = max(1, used // 4)
        passed = fixed + (places - fixed + offset_by * (used - fixed)) % max(1, count - fixed)
        return jnp.zeros((count,), jnp.int32).at[ranking[jnp.where(places < fixed, places, passed)]].set(jnp.asarray(lengths, jnp.int32))

    lengths = jnp.where(number % 4 == 0, named(packed, number // 4), named(usual, number - number // 4 - 1))
    mixed = jax.random.permutation(jax.random.fold_in(own, 3), count)
    donor, taker = mixed[0:count // 2 * 2:2], mixed[1:count // 2 * 2:2]
    margin = jnp.minimum(lengths[donor] - 1, most - lengths[taker]) // 2
    margin = jnp.where((donor == ranking[0]) | (taker == ranking[0]) | (lengths[taker] == 0), 0, jnp.maximum(margin, 0))
    passed = jax.random.randint(jax.random.fold_in(own, 4), (count // 2,), 0, 1 << 20) % (margin + 1)
    lengths = lengths.at[donor].add(-passed).at[taker].add(passed)
    labels = jnp.searchsorted(jnp.cumsum(lengths), jnp.arange(rows * top), side="right").astype(jnp.int32)
    listing = labels.reshape(top, rows).T
    listing = listing[jax.random.permutation(jax.random.fold_in(own, 1), rows)]
    offset_by = jax.random.randint(jax.random.fold_in(own, 2), (rows, 1), 0, top)
    return jnp.take_along_axis(listing, (jnp.arange(top)[None, :] + offset_by) % top, axis=1)


def portions_of(count, total, reach, skew, full):
    weights = [(1 << 20) // math.isqrt(standing ** skew) + 1 for standing in range(1, count + 1)]
    largest = reach if full else min(reach, max(-(-total // count), total * weights[0] // sum(weights)))
    least = 1 if total - largest >= count - 1 else 0
    given, spare = [largest] + [least] * (count - 1), total - largest - least * (count - 1)
    while spare > 0:
        free = [i for i in range(1, count) if given[i] < largest] or [i for i in range(1, count) if given[i] < reach]
        pool, remaining = sum([weights[i] for i in free]), spare
        for i in free:
            addition = min(reach - given[i], max(1, remaining * weights[i] // pool), spare)
            given[i] = given[i] + addition
            spare = spare - addition
    return np.array(given)


def noise(stream_key, shape, spread, limit, split=(), held_as=jnp.bfloat16):
    values = spread * jax.random.normal(stream_key, shape, jnp.float32)
    if split:
        values = values * block_scale(stream_key, shape, split, -0.22, 0.18)
    return jnp.clip(values, -limit, limit).astype(held_as)


def setup_inputs(seed: int = 0) -> dict:
    seeds = jax.random.split(jax.random.key(seed), 18)
    tokens = noise(seeds[0], (TOKENS, D), 1.0, 6.0, ((0, 32),))
    segment_ids = jnp.searchsorted(jnp.cumsum(ragged(seeds[1], TOKENS // (2 * TOK_DEV), TOKENS, SEQLEN, 2)), jnp.arange(TOKENS), side="right").astype(jnp.int32)
    routes_keys = jax.random.split(jax.random.fold_in(seeds[2], 1), TOKENS // TOK_DEV)
    routes_turns = jax.random.permutation(jax.random.fold_in(seeds[2], 3), TOKENS // TOK_DEV)
    routes = jax.vmap(lambda own, number: assign_block(jax.random.fold_in(seeds[2], 2), own, number, TOK_DEV, EXPERTS, TOPK, MOST, 2))(routes_keys, routes_turns).reshape((TOKENS, TOPK))
    pair_order = jax.random.permutation(seeds[3], TOKENS * TOPK).astype(jnp.int32)
    attn_gain = jnp.clip(1.0 + 0.1 * jax.random.normal(seeds[4], (D,), jnp.float32), 0.5, 1.5).astype(jnp.bfloat16)
    w_query = noise(seeds[5], (D, D), D ** -0.5, 0.125, ((0, 32),))
    w_key = noise(seeds[6], (D, D), D ** -0.5, 0.125, ((0, 32),))
    w_value = noise(seeds[7], (D, D), D ** -0.5, 0.125, ((0, 32),))
    query_gain = jnp.clip(1.0 + 0.1 * jax.random.normal(seeds[8], (HD,), jnp.float32), 0.5, 1.5).astype(jnp.bfloat16)
    key_gain = jnp.clip(1.0 + 0.1 * jax.random.normal(seeds[9], (HD,), jnp.float32), 0.5, 1.5).astype(jnp.bfloat16)
    w_out = noise(seeds[10], (D, D), (D // 64) ** -0.5, 1.0, ((0, 32),))
    ffn_gain = jnp.clip(1.0 + 0.1 * jax.random.normal(seeds[11], (D,), jnp.float32), 0.5, 1.5).astype(jnp.bfloat16)
    w_router = noise(seeds[12], (D, EXPERTS), (4 * D) ** -0.5, 0.0625, ((0, 32),))
    w_gate = noise(seeds[13], (EXPERTS, D, FF), D ** -0.5, 0.125, ((0, 8), (1, 4)))
    w_up = noise(seeds[14], (EXPERTS, D, FF), D ** -0.5, 0.125, ((0, 8), (1, 4)))
    w_down = noise(seeds[15], (EXPERTS, FF, D), (max(TOPK * FF // (2 * EXPERTS * EXPERTS), 1)) ** -0.5, 1.5, ((0, 8), (2, 4)))
    out_grad = noise(seeds[16], (TOKENS, D), 1.0, 6.0, ((0, 32),))
    return dict(tokens=tokens, segment_ids=segment_ids, routes=routes, pair_order=pair_order, attn_gain=attn_gain, w_query=w_query, w_key=w_key, w_value=w_value, query_gain=query_gain, key_gain=key_gain, w_out=w_out, ffn_gain=ffn_gain, w_router=w_router, w_gate=w_gate, w_up=w_up, w_down=w_down, out_grad=out_grad)


HIGHEST = lax.Precision.HIGHEST
EPSILON = 1e-06
THETA = 10000.0

@jax.custom_vjp
def low(v):
    return lax.optimization_barrier(v.astype(jnp.bfloat16)).astype(jnp.float32)

@jax.custom_vjp
def low_back(v):
    return v

def low_keep(v):
    return (low(v), None)

def low_pass(kept, grad):
    return (grad,)

def back_keep(v):
    return (v, None)

def back_low(kept, grad):
    return (low(grad),)
low.defvjp(low_keep, low_pass)
low_back.defvjp(back_keep, back_low)

def matmul(left, right):
    return jnp.dot(left, right, precision=HIGHEST, preferred_element_type=jnp.float32)

def rms_scale(values, scale_gain):
    factor = lax.rsqrt(lax.optimization_barrier(jnp.mean(values * values, axis=-1, keepdims=True)) + EPSILON)
    return values * factor * scale_gain

def rope_tables(positions):
    exponent = jnp.arange(HD // 2, dtype=jnp.float32) * (2.0 / HD)
    frequency = jnp.power(jnp.float32(THETA), -exponent)
    angles = positions.astype(jnp.float32)[:, None] * frequency[None, :]
    return (jnp.cos(angles), jnp.sin(angles))

def rotate(values, cosine, sine):
    first_half = values[..., :HD // 2]
    second_half = values[..., HD // 2:]
    cos_part = cosine[:, None, :]
    sin_part = sine[:, None, :]
    return jnp.concatenate([first_half * cos_part - second_half * sin_part, second_half * cos_part + first_half * sin_part], axis=-1)

def attend(query_raw, key_raw, value_raw, segment, query_scale, key_scale):
    length = query_raw.shape[0]
    cosine, sine = rope_tables(jnp.arange(length, dtype=jnp.int32))
    query_heads = rms_scale(query_raw.reshape(length, HEADS, HD), query_scale)
    key_heads = rms_scale(key_raw.reshape(length, HEADS, HD), key_scale)
    query_rot = low(rotate(query_heads, cosine, sine) * HD ** (-0.5))
    key_rot = low(rotate(key_heads, cosine, sine))
    value_heads = low(value_raw.reshape(length, HEADS, HD))
    scores = low_back(jnp.einsum('qhd,khd->hqk', query_rot, key_rot, precision=HIGHEST))
    allowed = segment[:, None] == segment[None, :]
    scores = jnp.where(allowed[None], scores, -1e+30)
    weights = low(jax.nn.softmax(scores, axis=-1))
    mixed = jnp.einsum('hqk,khd->qhd', weights, value_heads, precision=HIGHEST)
    return low(low_back(mixed.reshape(length, D)))

def expert_block(padded, slot_token, gate_w, up_w, down_w):
    inputs = low_back(padded[slot_token])
    gate_act = low_back(matmul(inputs, gate_w))
    up_act = low_back(matmul(inputs, up_w))
    swiglu = low(jax.nn.silu(gate_act) * up_act)
    return low(low_back(matmul(swiglu, down_w)))

def slot_tables(routes, pair_order):
    total_pairs = TOKENS * TOPK
    pair_index = jnp.arange(total_pairs, dtype=jnp.int32)
    token_index = pair_index // TOPK
    group_index = token_index // TOK_DEV % N_WSHARD
    expert_index = routes.reshape(-1).astype(jnp.int32)
    cell_index = group_index * EXPERTS + expert_index
    sort_keys = cell_index * total_pairs + pair_order.astype(jnp.int32)
    sorted_pairs = jnp.argsort(sort_keys).astype(jnp.int32)
    placement = jnp.zeros((total_pairs,), jnp.int32).at[sorted_pairs].set(pair_index)
    cell_counts = jnp.zeros((N_WSHARD * EXPERTS,), jnp.int32).at[cell_index].add(1)
    cell_start = (jnp.cumsum(cell_counts) - cell_counts).astype(jnp.int32)
    slot_rank = placement - cell_start[cell_index]
    retained = slot_rank < CAP
    slot_flat = (expert_index * N_WSHARD + group_index) * CAP + slot_rank
    room = EXPERTS * N_WSHARD * CAP
    target = jnp.where(retained, slot_flat, room).astype(jnp.int32)
    slot_token = jnp.full((room,), TOKENS, jnp.int32).at[target].set(token_index, mode='drop')
    return (slot_token.reshape(EXPERTS, N_WSHARD * CAP), target.reshape(TOKENS, TOPK))

def reference(tokens, segment_ids, routes, pair_order, attn_gain, w_query, w_key, w_value, query_gain, key_gain, w_out, ffn_gain, w_router, w_gate, w_up, w_down, out_grad):
    slot_token, pair_slot = slot_tables(routes, pair_order)
    seq_count = TOKENS // SEQLEN
    segment_rows = segment_ids.reshape(seq_count, SEQLEN)
    attend_saved = jax.checkpoint(attend)
    expert_saved = jax.checkpoint(expert_block)

    def forward(inputs, attn_scale, query_w, key_w, value_w, query_scale, key_scale, out_w, ffn_scale, router_w, gate_w, up_w, down_w):
        normed = low(rms_scale(inputs, attn_scale))
        query_raw = low_back(matmul(normed, query_w))
        key_raw = low_back(matmul(normed, key_w))
        value_raw = low_back(matmul(normed, value_w))

        def per_sequence(pieces):
            return attend_saved(pieces[0], pieces[1], pieces[2], pieces[3], query_scale, key_scale)
        mixed = lax.map(per_sequence, (query_raw.reshape(seq_count, SEQLEN, D), key_raw.reshape(seq_count, SEQLEN, D), value_raw.reshape(seq_count, SEQLEN, D), segment_rows))
        mixed = mixed.reshape(TOKENS, D)
        hidden = inputs + low_back(matmul(mixed, out_w))
        normed_two = low(rms_scale(hidden, ffn_scale))
        logits = low_back(matmul(normed_two, router_w))
        route_weight = jnp.take_along_axis(jax.nn.softmax(logits, axis=-1), routes, axis=1)
        padded = jnp.concatenate([normed_two, jnp.zeros((1, D), jnp.float32)], axis=0)

        def per_expert(pieces):
            return expert_saved(padded, pieces[0], pieces[1], pieces[2], pieces[3])
        expert_rows = lax.map(per_expert, (slot_token, gate_w, up_w, down_w))
        flat_rows = jnp.concatenate([expert_rows.reshape(-1, D), jnp.zeros((1, D), jnp.float32)], axis=0)
        combined = jnp.zeros((TOKENS, D), jnp.float32)
        for choice_slot in range(TOPK):
            combined = combined + route_weight[:, choice_slot:choice_slot + 1] * flat_rows[pair_slot[:, choice_slot]]
        return hidden + combined
    float_inputs = tuple((argument.astype(jnp.float32) for argument in (tokens, attn_gain, w_query, w_key, w_value, query_gain, key_gain, w_out, ffn_gain, w_router, w_gate, w_up, w_down)))
    result, pullback = jax.vjp(forward, *float_inputs)
    grads = pullback(out_grad.astype(jnp.float32))
    return (result.astype(jnp.bfloat16), grads[0].astype(jnp.bfloat16), grads[1], grads[2], grads[3], grads[4], grads[5], grads[6], grads[7], grads[8], grads[9], grads[10], grads[11], grads[12])
```

```python
import functools

import jax
import jax.numpy as jnp
import numpy as np
from jax import lax
from jax.experimental import pallas as pl
from jax.experimental.pallas import tpu as pltpu
from jax.sharding import PartitionSpec as P

HEADS = 16
HD = 128


EXPERT = "expert"
SHARD = "wshard"
BOTH = (EXPERT, SHARD)

SUM_QHD_KHD_HQK = "qhd,khd->hqk"
SUM_HQK_KHD_QHD = "hqk,khd->qhd"
SUM_ECD_EDF_ECF = "ecd,edf->ecf"
SUM_ECF_EFD_ECD = "ecf,efd->ecd"
SUM_TK_TKD_TD = "tk,tkd->td"
SUM_TD_TKD_TK = "td,tkd->tk"
SUM_ECD_EFD_ECF = "ecd,efd->ecf"
SUM_ECF_ECD_EFD = "ecf,ecd->efd"
SUM_ECD_ECF_EDF = "ecd,ecf->edf"
SUM_ECF_EDF_ECD = "ecf,edf->ecd"
SUM_HQK_QHD_KHD = "hqk,qhd->khd"
EPSILON = 1e-06
THETA = 10000.0


def matmul(left, right):
    return jnp.dot(left, right, preferred_element_type=jnp.float32)


def matmul_tn(left, right):
    return lax.dot_general(
        left, right, (((0,), (0,)), ((), ())), preferred_element_type=jnp.float32
    )


def matmul_nt(left, right):
    return lax.dot_general(
        left, right, (((1,), (1,)), ((), ())), preferred_element_type=jnp.float32
    )


def rms_scale(values, scale_gain):
    factor = lax.rsqrt(jnp.mean(values * values, axis=-1, keepdims=True) + EPSILON)
    return values * factor * scale_gain


def rope_tables(positions):
    exponent = jnp.arange(HD // 2, dtype=jnp.float32) * (2.0 / HD)
    frequency = jnp.power(jnp.float32(THETA), -exponent)
    angles = positions.astype(jnp.float32)[:, None] * frequency[None, :]
    return (jnp.cos(angles), jnp.sin(angles))


def rotate(values, cosine, sine):
    first_half = values[..., : HD // 2]
    second_half = values[..., HD // 2 :]
    cos_part = cosine[:, None, :]
    sin_part = sine[:, None, :]
    return jnp.concatenate(
        [
            first_half * cos_part - second_half * sin_part,
            second_half * cos_part + first_half * sin_part,
        ],
        axis=-1,
    )


def padded_rows(rows):
    return jnp.concatenate([jnp.zeros((1,) + rows.shape[1:], rows.dtype), rows], axis=0)


def masked_scores(query_rot, key_rot, query_segment, key_segment):
    scores = jnp.einsum(SUM_QHD_KHD_HQK, query_rot, key_rot, preferred_element_type=jnp.float32)
    allowed = query_segment[:, None] == key_segment[None, :]
    return jnp.where(allowed[None], scores, -1e30)


def swiglu_fn(gate_in, up_in):
    return jax.nn.silu(gate_in) * up_in


def general_local(
    tokens,
    segment_ids,
    routes,
    pair_order,
    attn_gain,
    w_query,
    w_key,
    w_value,
    query_gain,
    key_gain,
    w_out,
    ffn_gain,
    w_router,
    w_gate,
    w_up,
    w_down,
    out_grad,
):
    tok_rows, width = tokens.shape
    top_count = routes.shape[1]
    expert_devs = lax.axis_size(EXPERT)
    shard_devs = lax.axis_size(SHARD)
    local_experts = w_gate.shape[0]
    expert_count = local_experts * expert_devs
    most_rows = 2 * tok_rows * top_count // expert_count
    capacity = 5 * tok_rows * top_count // (4 * local_experts)
    seq_length = segment_ids.shape[0]
    device_expert = lax.axis_index(EXPERT)
    device_shard = lax.axis_index(SHARD)
    low_type = jnp.bfloat16
    wide_type = jnp.float32
    gathered = (
        lax.all_gather(attn_gain, BOTH, axis=0, tiled=True),
        lax.all_gather(w_query, BOTH, axis=0, tiled=True),
        lax.all_gather(w_key, BOTH, axis=0, tiled=True),
        lax.all_gather(w_value, BOTH, axis=0, tiled=True),
        lax.all_gather(query_gain, BOTH, axis=0, tiled=True),
        lax.all_gather(key_gain, BOTH, axis=0, tiled=True),
        lax.all_gather(w_out, BOTH, axis=0, tiled=True),
        lax.all_gather(ffn_gain, BOTH, axis=0, tiled=True),
        lax.all_gather(w_router, BOTH, axis=0, tiled=True),
    )
    attn_scale = gathered[0].astype(wide_type)
    query_w, key_w, value_w = (gathered[1], gathered[2], gathered[3])
    query_scale = gathered[4].astype(wide_type)
    key_scale = gathered[5].astype(wide_type)
    out_w = gathered[6]
    ffn_scale = gathered[7].astype(wide_type)
    router_w = gathered[8]
    inputs = tokens.astype(wide_type)
    normed, norm_one_pull = jax.vjp(rms_scale, inputs, attn_scale)
    normed_low = normed.astype(low_type)
    query_raw = matmul(normed_low, query_w)
    key_raw = matmul(normed_low, key_w)
    value_low = matmul(normed_low, value_w).astype(low_type)
    positions = device_shard * tok_rows + jnp.arange(tok_rows, dtype=jnp.int32)
    cosine, sine = rope_tables(positions)

    def prepare(query_in, key_in, query_g, key_g):
        query_heads = rms_scale(query_in.reshape(tok_rows, HEADS, HD), query_g)
        key_heads = rms_scale(key_in.reshape(tok_rows, HEADS, HD), key_g)
        return (rotate(query_heads, cosine, sine) * HD ** (-0.5), rotate(key_heads, cosine, sine))

    rotated, prepare_pull = jax.vjp(prepare, query_raw, key_raw, query_scale, key_scale)
    query_low = rotated[0].astype(low_type)
    key_low = rotated[1].astype(low_type).reshape(tok_rows, width)
    seq_keys, seq_values = (
        lax.all_gather(key_low, SHARD, axis=0, tiled=True),
        lax.all_gather(value_low, SHARD, axis=0, tiled=True),
    )
    query_segment = lax.dynamic_slice_in_dim(segment_ids, device_shard * tok_rows, tok_rows)
    scores = masked_scores(
        query_low, seq_keys.reshape(seq_length, HEADS, HD), query_segment, segment_ids
    )
    row_max = jnp.max(scores, axis=-1, keepdims=True)
    shifted = jnp.exp(scores - row_max)
    totals = jnp.sum(shifted, axis=-1, keepdims=True)
    log_total = row_max + jnp.log(totals)
    probs_low = (shifted / totals).astype(low_type)
    mixed = jnp.einsum(
        SUM_HQK_KHD_QHD,
        probs_low,
        seq_values.reshape(seq_length, HEADS, HD),
        preferred_element_type=wide_type,
    )
    mixed_low = mixed.reshape(tok_rows, width).astype(low_type)
    hidden = inputs + matmul(mixed_low, out_w)
    normed_two, norm_two_pull = jax.vjp(rms_scale, hidden, ffn_scale)
    normed_two_low = normed_two.astype(low_type)
    logits = matmul(normed_two_low, router_w)

    def router_weights(logit_values):
        return jnp.take_along_axis(jax.nn.softmax(logit_values, axis=-1), routes, axis=1)

    route_weight, route_pull = jax.vjp(router_weights, logits)
    group_routes, group_order = (
        lax.all_gather(routes, EXPERT, axis=0, tiled=True),
        lax.all_gather(pair_order, EXPERT, axis=0, tiled=True),
    )
    per_source = tok_rows * top_count
    group_pairs = per_source * expert_devs
    expert_of = group_routes.reshape(-1)
    pair_index = jnp.arange(group_pairs, dtype=jnp.int32)
    source_of = pair_index // per_source
    expert_ids = jnp.arange(expert_count, dtype=jnp.int32)
    onehot = (expert_of.reshape(expert_devs, per_source, 1) == expert_ids).astype(jnp.int32)
    position_of = (jnp.sum(jnp.cumsum(onehot, axis=1) * onehot, axis=-1) - 1).reshape(-1)
    order_span = group_pairs * shard_devs
    sort_keys = expert_of * order_span + group_order
    sorted_pairs = jnp.argsort(sort_keys)
    placement = jnp.zeros((group_pairs,), jnp.int32).at[sorted_pairs].set(pair_index)
    expert_counts = jnp.sum(onehot, axis=(0, 1))
    expert_start = jnp.cumsum(expert_counts) - expert_counts
    start_of = jnp.sum(onehot.reshape(group_pairs, expert_count) * expert_start[None, :], axis=-1)
    slot_rank = placement - start_of
    retained = slot_rank < capacity
    own_expert = routes.reshape(-1)
    own_position = lax.dynamic_slice_in_dim(position_of, device_expert * per_source, per_source)
    send_slot = own_expert * most_rows + own_position
    send_pair = (
        jnp.zeros((expert_count * most_rows,), jnp.int32)
        .at[send_slot]
        .set(jnp.arange(per_source, dtype=jnp.int32) + 1)
    )
    send_token = jnp.where(send_pair > 0, (send_pair - 1) // top_count + 1, 0)
    owner_local = expert_of % local_experts
    is_mine = expert_of // local_experts == device_expert
    recv_row = source_of * (local_experts * most_rows) + owner_local * most_rows + position_of
    slot_target = jnp.where(
        is_mine & retained, owner_local * capacity + slot_rank, local_experts * capacity
    )
    slot_source = (
        jnp.zeros((local_experts * capacity,), jnp.int32)
        .at[slot_target]
        .set(recv_row + 1, mode="drop")
    )
    back_room = expert_devs * local_experts * most_rows
    back_target = jnp.where(is_mine, recv_row, back_room)
    back_source = (
        jnp.zeros((back_room,), jnp.int32)
        .at[back_target]
        .set(jnp.where(retained, owner_local * capacity + slot_rank + 1, 0), mode="drop")
    )
    send_rows = padded_rows(normed_two_low)[send_token].reshape(
        expert_devs, local_experts * most_rows, width
    )
    recv_rows = lax.all_to_all(
        send_rows, EXPERT, split_axis=0, concat_axis=0, tiled=True
    ).reshape(-1, width)
    slot_rows = padded_rows(recv_rows)[slot_source].reshape(local_experts, capacity, width)
    full_gate, full_up, full_down = (
        lax.all_gather(w_gate, SHARD, axis=1, tiled=True),
        lax.all_gather(w_up, SHARD, axis=1, tiled=True),
        lax.all_gather(w_down, SHARD, axis=2, tiled=True),
    )
    gate_act = jnp.einsum(SUM_ECD_EDF_ECF, slot_rows, full_gate, preferred_element_type=wide_type)
    up_act = jnp.einsum(SUM_ECD_EDF_ECF, slot_rows, full_up, preferred_element_type=wide_type)
    swiglu_out, swiglu_pull = jax.vjp(swiglu_fn, gate_act, up_act)
    swiglu_low = swiglu_out.astype(low_type)
    expert_out = jnp.einsum(
        SUM_ECF_EFD_ECD, swiglu_low, full_down, preferred_element_type=wide_type
    ).astype(low_type)
    back_rows = padded_rows(expert_out.reshape(-1, width))[back_source].reshape(
        expert_devs, local_experts * most_rows, width
    )
    returned = lax.all_to_all(back_rows, EXPERT, split_axis=0, concat_axis=0, tiled=True).reshape(
        -1, width
    )
    pair_rows = returned[send_slot].reshape(tok_rows, top_count, width)
    combined = jnp.einsum(SUM_TK_TKD_TD, route_weight, pair_rows, preferred_element_type=wide_type)
    mixed_out = (hidden + combined).astype(low_type)
    result_grad = out_grad.astype(wide_type)
    weight_grad = jnp.einsum(SUM_TD_TKD_TK, result_grad, pair_rows, preferred_element_type=wide_type)
    pair_grad = (
        (route_weight[:, :, None] * result_grad[:, None, :])
        .astype(low_type)
        .reshape(per_source, width)
    )
    send_grad = padded_rows(pair_grad)[send_pair].reshape(
        expert_devs, local_experts * most_rows, width
    )
    recv_grad = lax.all_to_all(
        send_grad, EXPERT, split_axis=0, concat_axis=0, tiled=True
    ).reshape(-1, width)
    slot_grad = padded_rows(recv_grad)[slot_source].reshape(local_experts, capacity, width)
    act_grad = jnp.einsum(SUM_ECD_EFD_ECF, slot_grad, full_down, preferred_element_type=wide_type)
    down_grad = jnp.einsum(SUM_ECF_ECD_EFD, swiglu_low, slot_grad, preferred_element_type=wide_type)
    gate_grad, up_grad = swiglu_pull(act_grad)
    gate_low = gate_grad.astype(low_type)
    up_low = up_grad.astype(low_type)
    gate_w_grad = jnp.einsum(SUM_ECD_ECF_EDF, slot_rows, gate_low, preferred_element_type=wide_type)
    up_w_grad = jnp.einsum(SUM_ECD_ECF_EDF, slot_rows, up_low, preferred_element_type=wide_type)
    slot_in_grad = jnp.einsum(SUM_ECF_EDF_ECD, gate_low, full_gate, preferred_element_type=wide_type)
    slot_in_grad = (
        slot_in_grad + jnp.einsum(SUM_ECF_EDF_ECD, up_low, full_up, preferred_element_type=wide_type)
    ).astype(low_type)
    gate_shard, up_shard, down_shard = (
        lax.psum_scatter(
            gate_w_grad.astype(jnp.bfloat16), SHARD, scatter_dimension=1, tiled=True
        ).astype(jnp.float32),
        lax.psum_scatter(
            up_w_grad.astype(jnp.bfloat16), SHARD, scatter_dimension=1, tiled=True
        ).astype(jnp.float32),
        lax.psum_scatter(
            down_grad.astype(jnp.bfloat16), SHARD, scatter_dimension=2, tiled=True
        ).astype(jnp.float32),
    )
    back_grad = padded_rows(slot_in_grad.reshape(-1, width))[back_source].reshape(
        expert_devs, local_experts * most_rows, width
    )
    returned_grad = lax.all_to_all(
        back_grad, EXPERT, split_axis=0, concat_axis=0, tiled=True
    ).reshape(-1, width)
    expert_in_grad = jnp.sum(
        returned_grad[send_slot].reshape(tok_rows, top_count, width).astype(wide_type), axis=1
    )
    logit_grad = route_pull(weight_grad)[0]
    logit_low = logit_grad.astype(low_type)
    router_grad = matmul_tn(normed_two_low, logit_low)
    normed_two_grad = expert_in_grad + matmul_nt(logit_low, router_w)
    hidden_norm_grad, ffn_scale_grad = norm_two_pull(normed_two_grad)
    hidden_grad = result_grad + hidden_norm_grad
    attn_low = hidden_grad.astype(low_type)
    out_w_grad = matmul_tn(mixed_low, attn_low)
    mixed_grad = matmul_nt(attn_low, out_w).astype(low_type).reshape(tok_rows, HEADS, HD)
    back_keys, back_values = (seq_keys, seq_values)
    key_heads = back_keys.reshape(seq_length, HEADS, HD)
    value_heads = back_values.reshape(seq_length, HEADS, HD)
    scores_again = masked_scores(query_low, key_heads, query_segment, segment_ids)
    probs_again = jnp.exp(scores_again - log_total)
    probs_again_low = probs_again.astype(low_type)
    prob_grad = jnp.einsum(
        SUM_QHD_KHD_HQK, mixed_grad, value_heads, preferred_element_type=wide_type
    )
    value_part = jnp.einsum(
        SUM_HQK_QHD_KHD, probs_again_low, mixed_grad, preferred_element_type=wide_type
    )
    row_inner = jnp.sum(probs_again * prob_grad, axis=-1, keepdims=True)
    score_low = (probs_again * (prob_grad - row_inner)).astype(low_type)
    query_rot_grad = jnp.einsum(
        SUM_HQK_KHD_QHD, score_low, key_heads, preferred_element_type=wide_type
    )
    key_part = jnp.einsum(SUM_HQK_QHD_KHD, score_low, query_low, preferred_element_type=wide_type)
    key_rot_grad, value_grad = (
        lax.psum_scatter(
            key_part.reshape(seq_length, width).astype(jnp.bfloat16),
            SHARD,
            scatter_dimension=0,
            tiled=True,
        ).astype(jnp.float32),
        lax.psum_scatter(
            value_part.reshape(seq_length, width).astype(jnp.bfloat16),
            SHARD,
            scatter_dimension=0,
            tiled=True,
        ).astype(jnp.float32),
    )
    query_raw_grad, key_raw_grad, query_scale_grad, key_scale_grad = prepare_pull(
        (query_rot_grad, key_rot_grad.reshape(tok_rows, HEADS, HD))
    )
    query_grad_low = query_raw_grad.astype(low_type)
    key_grad_low = key_raw_grad.astype(low_type)
    value_grad_low = value_grad.astype(low_type)
    query_w_grad = matmul_tn(normed_low, query_grad_low)
    key_w_grad = matmul_tn(normed_low, key_grad_low)
    value_w_grad = matmul_tn(normed_low, value_grad_low)
    normed_grad = (
        matmul_nt(query_grad_low, query_w)
        + matmul_nt(key_grad_low, key_w)
        + matmul_nt(value_grad_low, value_w)
    )
    input_norm_grad, attn_scale_grad = norm_one_pull(normed_grad)
    input_grad = (hidden_grad + input_norm_grad).astype(low_type)
    summed = (
        lax.psum_scatter(attn_scale_grad, BOTH, scatter_dimension=0, tiled=True),
        lax.psum_scatter(query_w_grad, BOTH, scatter_dimension=0, tiled=True),
        lax.psum_scatter(key_w_grad, BOTH, scatter_dimension=0, tiled=True),
        lax.psum_scatter(value_w_grad, BOTH, scatter_dimension=0, tiled=True),
        lax.psum_scatter(query_scale_grad, BOTH, scatter_dimension=0, tiled=True),
        lax.psum_scatter(key_scale_grad, BOTH, scatter_dimension=0, tiled=True),
        lax.psum_scatter(out_w_grad, BOTH, scatter_dimension=0, tiled=True),
        lax.psum_scatter(ffn_scale_grad, BOTH, scatter_dimension=0, tiled=True),
        lax.psum_scatter(router_grad, BOTH, scatter_dimension=0, tiled=True),
    )
    return (
        mixed_out,
        input_grad,
        summed[0],
        summed[1],
        summed[2],
        summed[3],
        summed[4],
        summed[5],
        summed[6],
        summed[7],
        summed[8],
        gate_shard,
        up_shard,
        down_shard,
    )


MIB = 1 << 20


def nt_dot(left, right):
    return lax.dot_general(
        left, right, (((1,), (1,)), ((), ())), preferred_element_type=jnp.float32
    )


def tn_dot(left, right):
    return lax.dot_general(
        left, right, (((0,), (0,)), ((), ())), preferred_element_type=jnp.float32
    )


def vmem_params(mib):
    return pltpu.CompilerParams(vmem_limit_bytes=mib * MIB)


def turn_tables(length):
    exponent = np.arange(HD // 2, dtype=np.float32) * np.float32(2.0 / HD)
    frequency = np.power(np.float32(THETA), -exponent).astype(np.float32)
    angles = np.arange(length, dtype=np.float32)[:, None] * frequency[None, :]
    cosine, sine = np.cos(angles), np.sin(angles)
    return (
        jnp.asarray(np.concatenate([cosine, cosine], axis=1), jnp.float32),
        jnp.asarray(np.concatenate([-sine, sine], axis=1), jnp.float32),
    )


def norm_factor(values):
    return lax.rsqrt(jnp.mean(values * values, axis=-1, keepdims=True) + EPSILON)


def attend_kernel(
    tokens, gain, weight, query_gain, key_gain, cosine, sine, seg_row, seg_col,
    normed_out, raw_out, low_out, mixed_out, total_out, qkv,
):
    part = mixed_out.shape[1]
    values = tokens[...].astype(jnp.float32)
    normed = (values * norm_factor(values) * gain[...]).astype(jnp.bfloat16)
    normed_out[...] = normed
    qkv[...] = jnp.dot(normed, weight[...], preferred_element_type=jnp.float32)
    raw_out[...] = qkv[:, : 2 * part]
    low_out[:, 2 * part :] = qkv[:, 2 * part :].astype(jnp.bfloat16)
    allowed = seg_col[...] == seg_row[...]
    for head in range(part // HD):
        span = pl.ds(head * HD, HD)
        for offset, scale_gain, scale in ((0, query_gain, HD ** (-0.5)), (part, key_gain, 1.0)):
            raw = qkv[:, pl.ds(offset + head * HD, HD)]
            unit = raw * norm_factor(raw) * scale_gain[...]
            turned = unit * cosine[...] + pltpu.roll(unit, HD // 2, 1) * sine[...]
            low_out[:, pl.ds(offset + head * HD, HD)] = (turned * scale).astype(jnp.bfloat16)
        query, key = low_out[:, span], low_out[:, pl.ds(part + head * HD, HD)]
        scores = jnp.where(allowed, nt_dot(query, key), -1e30)
        top = jnp.max(scores, axis=-1, keepdims=True)
        shifted = jnp.exp(scores - top)
        total = jnp.sum(shifted, axis=-1, keepdims=True)
        probs = (shifted / total).astype(jnp.bfloat16)
        mixed = jnp.dot(
            probs, low_out[:, pl.ds(2 * part + head * HD, HD)], preferred_element_type=jnp.float32
        )
        mixed_out[:, span] = mixed.astype(jnp.bfloat16)
        total_out[:, head : head + 1] = top + jnp.log(total)


def attend_call(tokens, gain, weight, query_gain, key_gain, tables, seg_row, seg_col):
    seq, width = tokens.shape
    part = weight.shape[1] // 3
    return pl.pallas_call(
        attend_kernel,
        out_shape=(
            jax.ShapeDtypeStruct((seq, width), jnp.bfloat16),
            jax.ShapeDtypeStruct((seq, 2 * part), jnp.float32),
            jax.ShapeDtypeStruct((seq, 3 * part), jnp.bfloat16),
            jax.ShapeDtypeStruct((seq, part), jnp.bfloat16),
            jax.ShapeDtypeStruct((seq, 128), jnp.float32),
        ),
        scratch_shapes=[pltpu.VMEM((seq, 3 * part), jnp.float32)],
        compiler_params=vmem_params(52),
        cost_estimate=pl.CostEstimate(
            flops=2 * seq * width * 3 * part, bytes_accessed=16 * MIB, transcendentals=seq * seq * 4
        ),
    )(tokens, gain, weight, query_gain, key_gain, *tables, seg_row, seg_col)


def join_kernel(mixed, weight, tokens, gain, hidden_out, normed_out):
    shards, _, part = mixed.shape
    total = tokens[...].astype(jnp.float32)
    for shard in range(shards):
        total = total + jnp.dot(
            mixed[shard], weight[pl.ds(shard * part, part), :], preferred_element_type=jnp.float32
        )
    hidden_out[...] = total
    normed_out[...] = (total * norm_factor(total) * gain[...]).astype(jnp.bfloat16)


def join_call(mixed, weight, tokens, gain):
    shards, seq, part = mixed.shape
    width = weight.shape[1]
    tile = seq // 2
    return pl.pallas_call(
        join_kernel,
        grid=(2,),
        in_specs=[
            pl.BlockSpec((shards, tile, part), lambda i: (0, i, 0)),
            pl.BlockSpec(weight.shape, lambda i: (0, 0), pipeline_mode=pl.Buffered(1)),
            pl.BlockSpec((tile, width), lambda i: (i, 0)),
            pl.BlockSpec((1, width), lambda i: (0, 0)),
        ],
        out_specs=[
            pl.BlockSpec((tile, width), lambda i: (i, 0)),
            pl.BlockSpec((tile, width), lambda i: (i, 0)),
        ],
        out_shape=(
            jax.ShapeDtypeStruct((seq, width), jnp.float32),
            jax.ShapeDtypeStruct((seq, width), jnp.bfloat16),
        ),
        compiler_params=vmem_params(40),
        cost_estimate=pl.CostEstimate(
            flops=2 * seq * width * width, bytes_accessed=18 * MIB, transcendentals=0
        ),
    )(mixed, weight, tokens, gain)


def expert_kernel(
    first, experts, blocks, x, g, keep, wide_w, router_w, down_w, hot, *refs
):
    del blocks
    if first:
        out, grad, wide_sum, router_sum, down_sum, acc, racc, dacc, sems = refs
    else:
        wide_in, router_in, down_in, out, grad, wide_sum, router_sum, down_sum = refs[:8]
        acc, racc, dacc, sems = refs[8:]
    step, steps = pl.program_id(0), pl.num_programs(0)

    @pl.when(step == 0)
    def _():
        if first:
            acc[...] = jnp.zeros_like(acc)
            racc[...] = jnp.zeros_like(racc)
            dacc[...] = jnp.zeros_like(dacc)
        else:
            pltpu.make_async_copy(wide_in, acc, sems.at[0]).start()
            pltpu.make_async_copy(router_in, racc, sems.at[1]).start()
            pltpu.make_async_copy(down_in, dacc, sems.at[2]).start()

    shards, units, part = down_w.shape
    own = keep.shape[1]
    each = units // own
    wide = jnp.dot(x[...], wide_w[...], preferred_element_type=jnp.float32)
    logits = jnp.dot(x[...], router_w[...], preferred_element_type=jnp.float32)
    back = nt_dot(g[:, :part], down_w[0])
    for shard in range(1, shards):
        back = back + nt_dot(g[:, shard * part : (shard + 1) * part], down_w[shard])
    lane = lax.broadcasted_iota(jnp.int32, logits.shape, 1)
    logits = jnp.where(lane < experts, logits, -1e30)
    shifted = jnp.exp(logits - jnp.max(logits, axis=-1, keepdims=True))
    probs = shifted / jnp.sum(shifted, axis=-1, keepdims=True)
    dense = jnp.zeros_like(probs)
    acts, gates, ups = [], [], []
    for index in range(own):
        mark = hot[index : index + 1, :]
        kept = keep[:, index : index + 1]
        route = jnp.sum(probs * mark, axis=-1, keepdims=True) * kept
        gate = wide[:, index * each : (index + 1) * each]
        up = wide[:, units + index * each : units + (index + 1) * each]
        behind = back[:, index * each : (index + 1) * each]
        sigma = 1.0 / (1.0 + jnp.exp(-gate))
        silu = gate * sigma
        act = silu * up
        dense = dense + jnp.sum(act * behind, axis=-1, keepdims=True) * kept * mark
        acts.append((act * route).astype(jnp.bfloat16))
        act_grad = behind * route
        gates.append((act_grad * up * sigma * (1.0 + gate * (1.0 - sigma))).astype(jnp.bfloat16))
        ups.append((act_grad * silu).astype(jnp.bfloat16))
    logit_grad = probs * (dense - jnp.sum(probs * dense, axis=-1, keepdims=True))
    logit_low = logit_grad.astype(jnp.bfloat16)
    act_low = jnp.concatenate(acts, axis=1)
    wide_low = jnp.concatenate(gates + ups, axis=1)
    for shard in range(shards):
        out[:, shard * part : (shard + 1) * part] = jnp.dot(
            act_low, down_w[shard], preferred_element_type=jnp.float32
        ).astype(jnp.bfloat16)
    grad[...] = (nt_dot(wide_low, wide_w[...]) + nt_dot(logit_low, router_w[...])).astype(
        jnp.bfloat16
    )
    if not first:

        @pl.when(step == 0)
        def _():
            pltpu.make_async_copy(wide_in, acc, sems.at[0]).wait()
            pltpu.make_async_copy(router_in, racc, sems.at[1]).wait()
            pltpu.make_async_copy(down_in, dacc, sems.at[2]).wait()

    acc[...] += tn_dot(x[...], wide_low)
    racc[...] += tn_dot(x[...], logit_low)
    for shard in range(shards):
        dacc[shard] += tn_dot(act_low, g[:, shard * part : (shard + 1) * part])

    @pl.when(step == steps - 1)
    def _():
        copies = [
            pltpu.make_async_copy(acc, wide_sum, sems.at[0]),
            pltpu.make_async_copy(racc, router_sum, sems.at[1]),
            pltpu.make_async_copy(dacc, down_sum, sems.at[2]),
        ]
        for copy in copies:
            copy.start()
        for copy in copies:
            copy.wait()


def expert_call(blocks, x_all, g_all, keep, wide_w, router_w, down_w, hot, experts, sums):
    _, rows, width = x_all.shape
    count = blocks.shape[0]
    tile = 256
    per = rows // tile
    hbm = pl.BlockSpec(memory_space=pl.ANY)

    def whole(value):
        zeros = (0,) * value.ndim
        return pl.BlockSpec(value.shape, lambda i, b: zeros, pipeline_mode=pl.Buffered(1))

    def chosen(lanes):
        return pl.BlockSpec((None, tile, lanes), lambda i, b: (b[i // per], i % per, 0))

    rowwise = pl.BlockSpec((None, tile, width), lambda i, b: (i // per, i % per, 0))
    shapes = (
        jax.ShapeDtypeStruct(wide_w.shape, jnp.float32),
        jax.ShapeDtypeStruct(router_w.shape, jnp.float32),
        jax.ShapeDtypeStruct(down_w.shape, jnp.float32),
    )
    first = sums is None
    result = pl.pallas_call(
        functools.partial(expert_kernel, first, experts),
        grid_spec=pltpu.PrefetchScalarGridSpec(
            num_scalar_prefetch=1,
            grid=(count * per,),
            in_specs=[
                chosen(width),
                chosen(width),
                chosen(keep.shape[2]),
                whole(wide_w),
                whole(router_w),
                whole(down_w),
                whole(hot),
            ]
            + ([] if first else [hbm] * 3),
            out_specs=[rowwise, rowwise, hbm, hbm, hbm],
            scratch_shapes=[
                pltpu.VMEM(wide_w.shape, jnp.float32),
                pltpu.VMEM(router_w.shape, jnp.float32),
                pltpu.VMEM(down_w.shape, jnp.float32),
                pltpu.SemaphoreType.DMA((3,)),
            ],
        ),
        out_shape=(
            jax.ShapeDtypeStruct((count, rows, width), jnp.bfloat16),
            jax.ShapeDtypeStruct((count, rows, width), jnp.bfloat16),
        )
        + shapes,
        input_output_aliases={} if first else {8: 2, 9: 3, 10: 4},
        compiler_params=vmem_params(56),
        cost_estimate=pl.CostEstimate(
            flops=2 * count * rows * width * (3 * wide_w.shape[1] + 3 * down_w.shape[1]),
            bytes_accessed=40 * MIB,
            transcendentals=count * rows * down_w.shape[1],
        ),
    )(blocks, x_all, g_all, keep, wide_w, router_w, down_w, hot, *(() if first else sums))
    return result[0], result[1], result[2:]


def turn_back_kernel(
    hidden, grad, out_grad, gain, weight, hidden_grad_out, low_out, message_out, gain_grad_out
):
    shards, _, part = message_out.shape
    factor = norm_factor(hidden[...])
    gain_grad_out[...] = jnp.sum(grad[...] * hidden[...] * factor, axis=0, keepdims=True)
    scaled = grad[...] * gain[...]
    inner = jnp.mean(scaled * hidden[...], axis=-1, keepdims=True)
    total = out_grad[...].astype(jnp.float32) + factor * scaled
    total = total - hidden[...] * (factor * factor * factor) * inner
    hidden_grad_out[...] = total
    low = total.astype(jnp.bfloat16)
    low_out[...] = low
    for shard in range(shards):
        message_out[shard] = nt_dot(low, weight[pl.ds(shard * part, part), :]).astype(jnp.bfloat16)


def turn_back_call(hidden, grad, out_grad, gain, weight, shards):
    rows, width = hidden.shape
    return pl.pallas_call(
        turn_back_kernel,
        out_shape=(
            jax.ShapeDtypeStruct((rows, width), jnp.float32),
            jax.ShapeDtypeStruct((rows, width), jnp.bfloat16),
            jax.ShapeDtypeStruct((shards, rows, width // shards), jnp.bfloat16),
            jax.ShapeDtypeStruct((1, width), jnp.float32),
        ),
        compiler_params=vmem_params(40),
        cost_estimate=pl.CostEstimate(
            flops=2 * rows * width * width, bytes_accessed=12 * MIB, transcendentals=0
        ),
    )(hidden, grad, out_grad, gain, weight)


def attend_back_kernel(
    mixed_grad, raw, low, total, weight, query_gain, key_gain, cosine, sine, seg_row, seg_col,
    qkv_grad_out, normed_grad_out, query_gain_out, key_gain_out,
):
    part = mixed_grad.shape[1]
    allowed = seg_col[...] == seg_row[...]
    gain_sums = [None, None]
    for head in range(part // HD):
        span = pl.ds(head * HD, HD)
        query, key = low[:, span], low[:, pl.ds(part + head * HD, HD)]
        value = low[:, pl.ds(2 * part + head * HD, HD)]
        out_grad = mixed_grad[:, span]
        scores = jnp.where(allowed, nt_dot(query, key), -1e30)
        probs = jnp.exp(scores - total[:, head : head + 1])
        prob_grad = nt_dot(out_grad, value)
        value_grad = tn_dot(probs.astype(jnp.bfloat16), out_grad)
        qkv_grad_out[:, pl.ds(2 * part + head * HD, HD)] = value_grad.astype(jnp.bfloat16)
        inner = jnp.sum(probs * prob_grad, axis=-1, keepdims=True)
        score_grad = (probs * (prob_grad - inner)).astype(jnp.bfloat16)
        rotated = (
            jnp.dot(score_grad, key, preferred_element_type=jnp.float32) * HD ** (-0.5),
            tn_dot(score_grad, query),
        )
        for which, (offset, scale_gain) in enumerate(((0, query_gain), (part, key_gain))):
            grad = rotated[which]
            grad = grad * cosine[...] - pltpu.roll(grad, HD // 2, 1) * sine[...]
            source = raw[:, pl.ds(offset + head * HD, HD)]
            factor = norm_factor(source)
            gain_sum = jnp.sum(grad * source * factor, axis=0, keepdims=True)
            gain_sums[which] = gain_sum if head == 0 else gain_sums[which] + gain_sum
            scaled = grad * scale_gain[...]
            inner = jnp.mean(scaled * source, axis=-1, keepdims=True)
            result = factor * scaled - source * (factor * factor * factor) * inner
            qkv_grad_out[:, pl.ds(offset + head * HD, HD)] = result.astype(jnp.bfloat16)
    query_gain_out[...] = gain_sums[0]
    key_gain_out[...] = gain_sums[1]
    normed_grad_out[...] = nt_dot(qkv_grad_out[...], weight[...]).astype(jnp.bfloat16)


def attend_back_call(
    mixed_grad, raw, low, total, weight, query_gain, key_gain, tables, seg_row, seg_col
):
    seq = mixed_grad.shape[0]
    width = weight.shape[0]
    return pl.pallas_call(
        attend_back_kernel,
        out_shape=(
            jax.ShapeDtypeStruct(low.shape, jnp.bfloat16),
            jax.ShapeDtypeStruct((seq, width), jnp.bfloat16),
            jax.ShapeDtypeStruct((1, HD), jnp.float32),
            jax.ShapeDtypeStruct((1, HD), jnp.float32),
        ),
        compiler_params=vmem_params(52),
        cost_estimate=pl.CostEstimate(
            flops=2 * seq * width * low.shape[1], bytes_accessed=16 * MIB, transcendentals=seq * seq * 4
        ),
    )(mixed_grad, raw, low, total, weight, query_gain, key_gain, *tables, seg_row, seg_col)


def finish_kernel(pieces, tokens, hidden_grad, gain, grad_out, gain_grad_out):
    grad = pieces[0].astype(jnp.float32)
    for shard in range(1, pieces.shape[0]):
        grad = grad + pieces[shard].astype(jnp.float32)
    values = tokens[...].astype(jnp.float32)
    factor = norm_factor(values)
    gain_grad_out[...] = jnp.sum(grad * values * factor, axis=0, keepdims=True)
    scaled = grad * gain[...]
    inner = jnp.mean(scaled * values, axis=-1, keepdims=True)
    total = hidden_grad[...] + factor * scaled - values * (factor * factor * factor) * inner
    grad_out[...] = total.astype(jnp.bfloat16)


def finish_call(pieces, tokens, hidden_grad, gain):
    rows, width = tokens.shape
    return pl.pallas_call(
        finish_kernel,
        out_shape=(
            jax.ShapeDtypeStruct((rows, width), jnp.bfloat16),
            jax.ShapeDtypeStruct((1, width), jnp.float32),
        ),
        compiler_params=vmem_params(24),
    )(pieces, tokens, hidden_grad, gain)


def copy_kernel(*refs):
    half = len(refs) // 2
    for source, result in zip(refs[:half], refs[half:], strict=True):
        result[...] = source[...].reshape(result.shape).astype(result.dtype)


def unpack_units(wide, narrow, own):
    shards, part, count = wide.shape
    each = count // (2 * own)
    gate = pl.BlockSpec((1, part, each), lambda e, s: (s, 0, e))
    up = pl.BlockSpec((1, part, each), lambda e, s: (s, 0, own + e))
    result = pl.BlockSpec((1, part, each), lambda e, s: (e, 0, s))
    shape = jax.ShapeDtypeStruct((own, part, shards * each), jnp.float32)
    gate_grad, up_grad = pl.pallas_call(
        copy_kernel,
        grid=(own, shards),
        in_specs=[gate, up],
        out_specs=[result, result],
        out_shape=[shape, shape],
        compiler_params=vmem_params(16),
    )(wide, wide)
    down_grad = pl.pallas_call(
        copy_kernel,
        grid=(own, shards),
        in_specs=[pl.BlockSpec((1, each, part), lambda e, s: (s, e, 0))],
        out_specs=[pl.BlockSpec((1, each, part), lambda e, s: (e, s, 0))],
        out_shape=[jax.ShapeDtypeStruct((own, shards * each, part), jnp.float32)],
        compiler_params=vmem_params(16),
    )(narrow)[0]
    return gate_grad, up_grad, down_grad


CORE, XBIT, YBIT = 1, 2, 4


MESH = pl.DeviceIdType.MESH


class Wires:
    def __init__(self, send, recv):
        self.send, self.recv, self.used = send, recv, 0
        self.device, self.shard = lax.axis_index(EXPERT), lax.axis_index(SHARD)

    def slot(self):
        self.used += 1
        return self.used - 1

    def peer(self, bits=0, step=0, shards=1):
        shard = lax.rem(self.shard + step, shards) if step else self.shard
        return (self.device ^ bits, shard)

    def copy(self, source, target, slot, peer):
        return pltpu.make_async_remote_copy(
            src_ref=source,
            dst_ref=target,
            send_sem=self.send.at[slot],
            recv_sem=self.recv.at[slot],
            device_id=peer,
            device_id_type=MESH,
        )


def greet(peers):
    barrier = pltpu.get_barrier_semaphore()
    for peer in peers:
        pl.semaphore_signal(barrier, inc=1, device_id=peer, device_id_type=MESH)
    pl.semaphore_wait(barrier, len(peers))


class Relay:
    def __init__(self, wires, shards, views):
        self.wires, self.shards, self.views = wires, shards, views
        self.slots = [[[wires.slot() for _ in views] for _ in range(shards - 1)] for _ in range(2)]

    def copies(self, way, step, block):
        wires = self.wires
        peer = (wires.device, wires.shard + (1 if way == 0 else -1))
        return [
            wires.copy(view(block), view(block), slot, peer)
            for view, slot in zip(self.views, self.slots[way][step], strict=True)
        ]

    def has(self, way, step):
        shard = self.wires.shard
        return shard - step >= 0 if way == 0 else shard + step < self.shards

    def sends(self, way, step):
        shard = self.wires.shard
        edge = shard < self.shards - 1 if way == 0 else shard > 0
        return jnp.logical_and(edge, self.has(way, step))

    def block(self, way, step):
        return self.wires.shard + (-step if way == 0 else step)

    def run(self, step, first=None):
        for way in range(2):
            if step > 0:

                @pl.when(self.has(way, step))
                def _(way=way):
                    for copy in self.copies(way, step - 1, self.block(way, step)):
                        copy.wait_recv()

            if step < self.shards - 1:

                @pl.when(self.sends(way, step))
                def _(way=way):
                    if first is None:
                        copies = self.copies(way, step, self.block(way, step))
                    else:
                        wires = self.wires
                        peer = (wires.device, wires.shard + (1 if way == 0 else -1))
                        block = self.block(way, step)
                        copies = [
                            wires.copy(source, view(block), slot, peer)
                            for source, view, slot in zip(
                                first, self.views, self.slots[way][step], strict=True
                            )
                        ]
                    for copy in copies:
                        copy.start()

    def drain(self):
        for way in range(2):
            for step in range(self.shards - 1):

                @pl.when(self.sends(way, step))
                def _(way=way, step=step):
                    for copy in self.copies(way, step, self.block(way, step)):
                        copy.wait_send()


class Plane:
    def __init__(self, wires, views, whole):
        self.wires, self.views, self.whole = wires, views, whole
        count = len(views)
        self.first = [[wires.slot() for _ in range(count)] for _ in range(2)]
        self.second = [[[wires.slot() for _ in range(count)] for _ in range(2)] for _ in range(2)]
        self.last = [[wires.slot() for _ in range(count)] for _ in range(4)]
        self.sent = []

    def start(self, copies):
        for copy in copies:
            copy.start()
        self.sent += copies

    def one(self, owner, half, bits, slots):
        wires = self.wires
        return [
            wires.copy(view(owner, half), view(owner, half), slot, wires.peer(bits))
            for view, slot in zip(self.views, slots, strict=True)
        ]

    def step_one(self):
        me = self.wires.device
        for half, bits in enumerate((XBIT, YBIT)):
            self.start(self.one(me, half, bits, self.first[half]))

    def step_two(self):
        me = self.wires.device
        for half, bits in enumerate((XBIT, YBIT)):
            for copy in self.one(me ^ bits, half, bits, self.first[half]):
                copy.wait_recv()
        for half, bits in enumerate((XBIT, YBIT)):
            other = (XBIT | YBIT) ^ bits
            self.start(self.one(me, half, other, self.second[half][0]))
            self.start(self.one(me ^ bits, half, other, self.second[half][1]))

    def cores(self, index):
        wires = self.wires
        owner = wires.device ^ (0, XBIT, YBIT, XBIT | YBIT)[index]
        return [
            wires.copy(place(owner), place(owner), slot, wires.peer(CORE))
            for place, slot in zip(self.whole, self.last[index], strict=True)
        ]

    def step_three(self):
        me = self.wires.device
        for half, bits in enumerate((XBIT, YBIT)):
            other = (XBIT | YBIT) ^ bits
            for owner, slots in ((me ^ other, 0), (me ^ other ^ bits, 1)):
                for copy in self.one(owner, half, other, self.second[half][slots]):
                    copy.wait_recv()
        for index in range(1, 4):
            self.start(self.cores(index))

    def finish(self):
        for index, bits in enumerate((0, XBIT, YBIT, XBIT | YBIT)):
            owner = self.wires.device ^ CORE ^ bits
            for place, slot in zip(self.whole, self.last[index], strict=True):
                self.wires.copy(
                    place(owner), place(owner), slot, self.wires.peer(CORE)
                ).wait_recv()
        for copy in self.sent:
            copy.wait_send()


def opening_kernel(
    shards, small, w_query, w_key, w_value, tokens, w_out, out_grad,
    small_all, qkv_w, tokens_all, out_block, grad_seq, send, recv, local,
):
    wires = Wires(send, recv)
    device, shard = wires.device, wires.shard
    weights = (w_query, w_key, w_value)
    block, width = w_query.shape
    rows = tokens.shape[0]
    part = width // shards
    greet(
        [wires.peer(step=step, shards=shards) for step in range(1, shards)]
        + [wires.peer(XBIT), wires.peer(YBIT), wires.peer(CORE)]
    )

    def place(source_shard, which):
        start = pl.multiple_of((device * shards + source_shard) * block, block)
        return qkv_w.at[pl.ds(start, block), pl.ds(which * part, part)]

    def cut(which, target):
        return weights[which].at[:, pl.ds(pl.multiple_of(target * part, part), part)]

    exchange = [[wires.slot() for _ in range(4)] for _ in range(1, shards)]
    sent = []
    for step in range(1, shards):
        peer = wires.peer(step=step, shards=shards)
        copies = [
            wires.copy(small, small_all.at[device * shards + shard], exchange[step - 1][3], peer)
        ] + [
            wires.copy(cut(which, peer[1]), place(shard, which), exchange[step - 1][which], peer)
            for which in range(3)
        ]
        for copy in copies:
            copy.start()
        sent += copies
    own = [
        pltpu.make_async_copy(cut(which, shard), place(shard, which), local.at[which])
        for which in range(3)
    ]
    own += [
        pltpu.make_async_copy(small, small_all.at[device * shards + shard], local.at[3]),
        pltpu.make_async_copy(
            tokens, tokens_all.at[pl.ds(pl.multiple_of(shard * rows, rows), rows)], local.at[4]
        ),
        pltpu.make_async_copy(
            w_out, out_block.at[pl.ds(pl.multiple_of(shard * block, block), block)], local.at[5]
        ),
        pltpu.make_async_copy(
            out_grad, grad_seq.at[pl.ds(pl.multiple_of(shard * rows, rows), rows)], local.at[6]
        ),
    ]
    for copy in own:
        copy.start()
    line = Relay(
        wires,
        shards,
        [
            lambda b: tokens_all.at[pl.ds(pl.multiple_of(b * rows, rows), rows)],
            lambda b: out_block.at[pl.ds(pl.multiple_of(b * block, block), block)],
            lambda b: grad_seq.at[pl.ds(pl.multiple_of(b * rows, rows), rows)],
        ],
    )
    line.run(0, (tokens, w_out, out_grad))
    for copy in own:
        copy.wait()
    for step in range(1, shards):
        peer = wires.peer(step=shards - step, shards=shards)
        source = peer[1]
        slots = exchange[step - 1]
        wires.copy(small, small_all.at[device * shards + source], slots[3], peer).wait_recv()
        for which in range(3):
            wires.copy(place(source, which), place(source, which), slots[which], peer).wait_recv()

    each = shards * block // 2

    def rows_of(owner, half):
        return qkv_w.at[pl.ds(pl.multiple_of((owner * 2 + half) * each, each), each)]

    def small_of(owner, half):
        return small_all.at[pl.ds((owner * 2 + half) * (shards // 2), shards // 2)]

    plane = Plane(
        wires,
        [rows_of, small_of],
        [
            lambda owner: qkv_w.at[pl.ds(pl.multiple_of(owner * 2 * each, 2 * each), 2 * each)],
            lambda owner: small_all.at[pl.ds(owner * shards, shards)],
        ],
    )
    plane.step_one()
    plane.start(plane.cores(0))
    plane.step_two()
    line.run(1)
    line.run(2)
    plane.step_three()
    for step in range(3, shards):
        line.run(step)
    plane.finish()
    for copy in sent:
        copy.wait_send()
    line.drain()


def opening_call(small, w_query, w_key, w_value, tokens, w_out, out_grad, planes, shards):
    block, width = w_query.shape
    rows = tokens.shape[0]
    hbm = pl.BlockSpec(memory_space=pl.ANY)
    slots = 64
    return pl.pallas_call(
        functools.partial(opening_kernel, shards),
        in_specs=[hbm] * 7,
        out_specs=[hbm] * 5,
        out_shape=(
            jax.ShapeDtypeStruct((planes * shards,) + small.shape, small.dtype),
            jax.ShapeDtypeStruct((planes * shards * block, 3 * width // shards), w_query.dtype),
            jax.ShapeDtypeStruct((shards * rows, width), tokens.dtype),
            jax.ShapeDtypeStruct((shards * block, width), w_out.dtype),
            jax.ShapeDtypeStruct((shards * rows, width), out_grad.dtype),
        ),
        scratch_shapes=[
            pltpu.SemaphoreType.DMA((slots,)),
            pltpu.SemaphoreType.DMA((slots,)),
            pltpu.SemaphoreType.DMA((7,)),
        ],
        compiler_params=pltpu.CompilerParams(
            collective_id=1, has_side_effects=True, vmem_limit_bytes=4 * MIB
        ),
        cost_estimate=pl.CostEstimate(flops=0, bytes_accessed=200 * MIB, transcendentals=0),
    )(small, w_query, w_key, w_value, tokens, w_out, out_grad)


def middle_kernel(shards, mixed, out_block, mixed_all, out_w, send, recv, local):
    wires = Wires(send, recv)
    device, shard = wires.device, wires.shard
    greet(
        [wires.peer(step=step, shards=shards) for step in range(1, shards)]
        + [wires.peer(XBIT), wires.peer(YBIT), wires.peer(CORE)]
    )
    each = out_block.shape[0] // 2
    line = Relay(wires, shards, [lambda b: mixed_all.at[b]])
    line.run(0, (mixed,))
    own = [
        pltpu.make_async_copy(
            out_block,
            out_w.at[pl.ds(pl.multiple_of(device * 2 * each, 2 * each), 2 * each)],
            local.at[0],
        ),
        pltpu.make_async_copy(mixed, mixed_all.at[shard], local.at[1]),
    ]
    for copy in own:
        copy.start()
    for copy in own:
        copy.wait()
    plane = Plane(
        wires,
        [lambda owner, half: out_w.at[pl.ds(pl.multiple_of((owner * 2 + half) * each, each), each)]],
        [lambda owner: out_w.at[pl.ds(pl.multiple_of(owner * 2 * each, 2 * each), 2 * each)]],
    )
    plane.step_one()
    plane.start(plane.cores(0))
    line.run(1)
    plane.step_two()
    line.run(2)
    for step in range(3, shards):
        line.run(step)
    plane.step_three()
    plane.finish()
    line.drain()


def middle_call(mixed, out_block, planes, shards):
    hbm = pl.BlockSpec(memory_space=pl.ANY)
    slots = 32
    return pl.pallas_call(
        functools.partial(middle_kernel, shards),
        in_specs=[hbm] * 2,
        out_specs=[hbm] * 2,
        out_shape=(
            jax.ShapeDtypeStruct((shards,) + mixed.shape, mixed.dtype),
            jax.ShapeDtypeStruct((planes * out_block.shape[0], out_block.shape[1]), mixed.dtype),
        ),
        scratch_shapes=[
            pltpu.SemaphoreType.DMA((slots,)),
            pltpu.SemaphoreType.DMA((slots,)),
            pltpu.SemaphoreType.DMA((2,)),
        ],
        compiler_params=pltpu.CompilerParams(
            collective_id=2, has_side_effects=True, vmem_limit_bytes=4 * MIB
        ),
        cost_estimate=pl.CostEstimate(flops=0, bytes_accessed=150 * MIB, transcendentals=0),
    )(mixed, out_block)


def meeting_kernel(
    shards, normed, grad_seq, gate, up, down,
    normed_all, grad_all, wide_w, down_w, send, recv, local,
):
    wires = Wires(send, recv)
    device, shard = wires.device, wires.shard
    own, part, hidden_units = gate.shape
    each = hidden_units // shards
    half = normed.shape[0] // 2
    greet(
        [wires.peer(step=step, shards=shards) for step in range(1, shards)]
        + [wires.peer(XBIT), wires.peer(YBIT), wires.peer(CORE)]
    )

    def wide_pair(source, target):
        lanes = pl.ds(pl.multiple_of(target * each, each), each)
        pairs = []
        for which, weight in enumerate((gate, up)):
            for index in range(own):
                place = wide_w.at[source, :, pl.ds((which * own + index) * each, each)]
                pairs.append((weight.at[index, :, lanes], place))
        return pairs

    def down_pair(source, target):
        lines = pl.ds(pl.multiple_of(target * each, each), each)
        return [
            (down.at[index, lines, :], down_w.at[source, pl.ds(index * each, each), :])
            for index in range(own)
        ]

    sent, pending = [], []
    token_plane = Plane(
        wires, [lambda owner, part_of: normed_all.at[owner, pl.ds(part_of * half, half)]],
        [lambda owner: normed_all.at[owner]],
    )
    grad_plane = Plane(
        wires, [lambda owner, part_of: grad_all.at[owner, pl.ds(part_of * half, half)]],
        [lambda owner: grad_all.at[owner]],
    )
    own_copies = [
        pltpu.make_async_copy(normed, normed_all.at[device], local.at[0]),
        pltpu.make_async_copy(grad_seq, grad_all.at[device], local.at[1]),
    ]
    for index, (source, place) in enumerate(wide_pair(shard, shard) + down_pair(shard, shard)):
        own_copies.append(pltpu.make_async_copy(source, place, local.at[2 + index]))
    for copy in own_copies:
        copy.start()
    for pair in (wide_pair, down_pair):
        for step in range(1, shards):
            peer = wires.peer(step=step, shards=shards)
            back = wires.peer(step=shards - step, shards=shards)
            for (source, place), (_, mine) in zip(
                pair(shard, peer[1]), pair(back[1], shard), strict=True
            ):
                slot = wires.slot()
                copy = wires.copy(source, place, slot, peer)
                copy.start()
                sent.append(copy)
                pending.append((mine, slot, back))
    for copy in own_copies:
        copy.wait()
    token_plane.step_one()
    token_plane.start(token_plane.cores(0))
    grad_plane.start(grad_plane.cores(0))
    token_plane.step_two()
    grad_plane.step_one()
    token_plane.step_three()
    grad_plane.step_two()
    grad_plane.step_three()
    token_plane.finish()
    grad_plane.finish()
    for mine, slot, back in pending:
        wires.copy(mine, mine, slot, back).wait_recv()
    for copy in sent:
        copy.wait_send()


def meeting_call(normed, grad_seq, gate, up, down, planes, shards):
    hbm = pl.BlockSpec(memory_space=pl.ANY)
    own, part, hidden_units = gate.shape
    count = own * hidden_units // shards
    slots = 48
    return pl.pallas_call(
        functools.partial(meeting_kernel, shards),
        in_specs=[hbm] * 5,
        out_specs=[hbm] * 4,
        out_shape=(
            jax.ShapeDtypeStruct((planes,) + normed.shape, normed.dtype),
            jax.ShapeDtypeStruct((planes,) + grad_seq.shape, grad_seq.dtype),
            jax.ShapeDtypeStruct((shards, part, 2 * count), gate.dtype),
            jax.ShapeDtypeStruct((shards, count, part), down.dtype),
        ),
        scratch_shapes=[
            pltpu.SemaphoreType.DMA((slots,)),
            pltpu.SemaphoreType.DMA((slots,)),
            pltpu.SemaphoreType.DMA((2 + 3 * own,)),
        ],
        compiler_params=pltpu.CompilerParams(
            collective_id=3, has_side_effects=True, vmem_limit_bytes=4 * MIB
        ),
        cost_estimate=pl.CostEstimate(flops=0, bytes_accessed=300 * MIB, transcendentals=0),
    )(normed, grad_seq, gate, up, down)


LOW = jnp.bfloat16
WIDE = jnp.float32


def swap(value, bits):
    count = lax.axis_size(EXPERT)
    return lax.ppermute(value, EXPERT, [(i, i ^ bits) for i in range(count)])


def shard_exchange(pieces, shard):
    size = lax.axis_size(SHARD)
    result = pieces
    for step in range(1, size):
        target = (shard + step) % size
        sent = lax.dynamic_index_in_dim(pieces, target, 0, keepdims=True)
        got = lax.ppermute(sent, SHARD, [(i, (i + step) % size) for i in range(size)])
        result = lax.dynamic_update_slice_in_dim(result, got, (shard - step) % size, 0)
    return result


def plane_scatter(parts, device):
    shape = parts.shape[1:]
    core, xbit, ybit = device & 1, (device >> 1) & 1, (device >> 2) & 1
    cube = parts.reshape((2, 2, 2) + shape)
    keep = lax.dynamic_index_in_dim(cube, core, 2, keepdims=False)
    give = lax.dynamic_index_in_dim(cube, 1 - core, 2, keepdims=False)
    cube = keep.astype(WIDE) + swap(give.astype(LOW), CORE).astype(WIDE)
    half = shape[0] // 2

    def halves(value, first, second, first_bit, second_bit, axis):
        keep = lax.dynamic_index_in_dim(value, first, axis, keepdims=False)
        give = lax.dynamic_index_in_dim(value, 1 - first, axis, keepdims=False)
        value = keep + swap(give.astype(LOW), first_bit).astype(WIDE)
        keep = lax.dynamic_index_in_dim(value, second, 0, keepdims=False)
        give = lax.dynamic_index_in_dim(value, 1 - second, 0, keepdims=False)
        return keep + swap(give.astype(LOW), second_bit).astype(WIDE)

    low_half = halves(cube[:, :, :half], xbit, ybit, XBIT, YBIT, 1)
    high_half = halves(cube[:, :, half:], ybit, xbit, YBIT, XBIT, 0)
    return jnp.concatenate([low_half, high_half], axis=0)


def tiny_scatter(table, device, shard):
    planes, shards = lax.axis_size(EXPERT), lax.axis_size(SHARD)
    cube = table.reshape(2, 2, 2, shards, -1)
    for axis, bits in ((2, CORE), (1, XBIT), (0, YBIT)):
        mine = (device // bits) & 1
        keep = lax.dynamic_index_in_dim(cube, mine, axis, keepdims=True)
        give = lax.dynamic_index_in_dim(cube, 1 - mine, axis, keepdims=True)
        cube = keep + swap(give, bits)
    return jnp.sum(shard_exchange(cube.reshape(shards, -1), shard), axis=0)


def fast_local(
    tokens,
    segment_ids,
    routes,
    pair_order,
    attn_gain,
    w_query,
    w_key,
    w_value,
    query_gain,
    key_gain,
    w_out,
    ffn_gain,
    w_router,
    w_gate,
    w_up,
    w_down,
    out_grad,
):
    rows, width = tokens.shape
    top_count = routes.shape[1]
    planes = lax.axis_size(EXPERT)
    shards = lax.axis_size(SHARD)
    own_experts = w_gate.shape[0]
    experts = own_experts * planes
    capacity = 5 * rows * top_count // (4 * own_experts)
    seq = segment_ids.shape[0]
    device = lax.axis_index(EXPERT)
    shard = lax.axis_index(SHARD)
    part = width // shards
    both = BOTH

    order = pair_order.reshape(rows, top_count)
    expert_ids = jnp.arange(experts, dtype=jnp.int32)
    chosen = routes[:, :, None] == expert_ids[None, None, :]
    dense_order = jnp.sum(jnp.where(chosen, order[:, :, None] + 1, 0), axis=1)
    small = jnp.concatenate(
        [
            (dense_order // 256).astype(LOW).reshape(-1),
            (dense_order % 256).astype(LOW).reshape(-1),
            w_router.reshape(-1),
            attn_gain,
            ffn_gain,
            query_gain,
            key_gain,
        ]
    )
    used = small.shape[0]
    lines = -(-used // (128 * 16)) * 16
    small = jnp.pad(small, (0, lines * 128 - used)).reshape(lines, 128)
    small, qkv_w, tokens_seq, out_block, grad_seq = opening_call(
        small, w_query, w_key, w_value, tokens, w_out, out_grad, planes, shards
    )
    small = small.reshape(planes, shards, -1)[:, :, :used]
    cuts = [rows * experts, rows * experts, w_router.size, attn_gain.size, ffn_gain.size]
    cuts += [query_gain.size, key_gain.size]
    fields, at = [], 0
    for size in cuts:
        fields.append(small[:, :, at : at + size])
        at += size
    all_order = fields[0].astype(jnp.int32) * 256 + fields[1].astype(jnp.int32)
    all_order = all_order.reshape(planes, shards, rows, experts)
    router_w = fields[2].reshape(width, experts)
    attn_scale = fields[3].reshape(width).astype(WIDE)
    ffn_scale = fields[4].reshape(width).astype(WIDE)
    query_scale = fields[5].reshape(HD).astype(WIDE)
    key_scale = fields[6].reshape(HD).astype(WIDE)

    attn_row, ffn_row = attn_scale.reshape(1, width), ffn_scale.reshape(1, width)
    query_row, key_row = query_scale.reshape(1, HD), key_scale.reshape(1, HD)
    tables = turn_tables(seq)
    seg_row, seg_col = segment_ids.reshape(1, seq), segment_ids.reshape(seq, 1)
    normed_low, raw, low, mixed_own, total = attend_call(
        tokens_seq, attn_row, qkv_w, query_row, key_row, tables, seg_row, seg_col
    )
    mixed, out_w = middle_call(mixed_own, out_block, planes, shards)
    hidden_seq, normed_seq = join_call(mixed, out_w, tokens_seq, ffn_row)

    token_all, grad_all, wide_w, down_w = meeting_call(
        normed_seq, grad_seq, w_gate, w_up, w_down, planes, shards
    )
    wide_w = wide_w.reshape(width, -1)
    extra = 128
    router_pad = jnp.pad(router_w, ((0, 0), (0, extra - experts)))
    own_ids = device * own_experts + jnp.arange(own_experts, dtype=jnp.int32)
    own_hot = (own_ids[:, None] == jnp.arange(extra, dtype=jnp.int32)[None, :]).astype(WIDE)
    mine = jnp.stack(
        [lax.dynamic_index_in_dim(all_order, own_ids[i], 3, keepdims=False) for i in range(own_experts)]
    )
    mine = mine.transpose(0, 2, 1, 3).reshape(own_experts, shards, planes * rows)
    smaller = (mine[:, :, None, :] < mine[:, :, :, None]) & (mine[:, :, None, :] > 0)
    rank = jnp.sum(smaller.astype(jnp.int32), axis=-1)
    kept = ((mine > 0) & (rank < capacity)).astype(WIDE)
    kept = kept.reshape(own_experts, shards, planes, rows).transpose(2, 1, 3, 0)
    kept = kept.reshape(planes, seq, own_experts)

    sums = None
    out_parts, in_parts = [None] * 4, [None] * 4
    for chip in (3, 1, 2, 0):
        blocks = jnp.stack([device ^ (2 * chip), device ^ (2 * chip + 1)])
        out_parts[chip], in_parts[chip], sums = expert_call(
            blocks, token_all, grad_all, kept, wide_w, router_pad, down_w, own_hot, experts, sums
        )
    wide_grad, router_grad, down_grad = sums

    def combine(parts):
        total = None
        for chip, bits in enumerate((0, XBIT, YBIT, XBIT | YBIT)):
            value = parts[chip]
            value = value[0].astype(WIDE) + swap(value[1], CORE).astype(WIDE)
            if bits:
                value = swap(value.astype(LOW), bits).astype(WIDE)
            total = value if total is None else total + value
        pieces = shard_exchange(total.astype(LOW).reshape(shards, rows, width), shard)
        return jnp.sum(pieces.astype(WIDE), axis=0)

    normed_two_grad = combine(in_parts)
    out_parts, _ = lax.optimization_barrier((out_parts, normed_two_grad))
    expert_sum = combine(out_parts)
    hidden = lax.dynamic_slice_in_dim(hidden_seq, shard * rows, rows)
    mixed_out = (hidden + expert_sum).astype(LOW)

    hidden_grad, attn_low, message, ffn_scale_grad = turn_back_call(
        hidden, normed_two_grad, out_grad, ffn_row, out_w, shards
    )
    mixed_grad = shard_exchange(message, shard).reshape(seq, part)
    qkv_grad, normed_grad, query_scale_grad, key_scale_grad = attend_back_call(
        mixed_grad, raw, low, total, qkv_w, query_row, key_row, tables, seg_row, seg_col
    )
    pieces = shard_exchange(normed_grad.reshape(shards, rows, width), shard)
    input_grad, attn_scale_grad = finish_call(pieces, tokens, hidden_grad, attn_row)

    qkv_w_grad = matmul_tn(normed_low, qkv_grad).reshape(planes, -1, 3 * part)
    qkv_w_grad = plane_scatter(qkv_w_grad, device).astype(LOW)
    qkv_w_grad = shard_exchange(qkv_w_grad.reshape(shards, -1, 3 * part), shard).astype(WIDE)
    qkv_w_grad = qkv_w_grad.reshape(shards, -1, 3, part).transpose(2, 1, 0, 3)
    qkv_w_grad = qkv_w_grad.reshape(3, -1, width)

    own_mixed = lax.dynamic_slice_in_dim(mixed, shard * rows, rows, 1)
    own_mixed = own_mixed.transpose(1, 0, 2).reshape(rows, width)
    out_w_grad = matmul_tn(own_mixed, attn_low).reshape(planes, -1, width)
    out_w_grad = plane_scatter(out_w_grad, device).astype(LOW)
    out_w_grad = shard_exchange(out_w_grad.reshape(shards, -1, width), shard)
    out_w_grad = jnp.sum(out_w_grad.astype(WIDE), axis=0)

    wide_pieces = shard_exchange(wide_grad.astype(LOW).reshape(shards, part, -1), shard)
    down_pieces = shard_exchange(down_grad.astype(LOW), shard)
    gate_grad, up_grad, down_grad = unpack_units(wide_pieces, down_pieces, own_experts)

    devices = planes * shards
    tiny = [router_grad[:, :experts], ffn_scale_grad, attn_scale_grad, query_scale_grad, key_scale_grad]
    tiny = [value.reshape(devices, -1) for value in tiny]
    sizes = [value.shape[1] for value in tiny]
    summed = tiny_scatter(jnp.concatenate(tiny, axis=1), device, shard)
    fields, at = [], 0
    for size in sizes:
        fields.append(summed[at : at + size])
        at += size
    return (
        mixed_out,
        input_grad,
        fields[2],
        qkv_w_grad[0],
        qkv_w_grad[1],
        qkv_w_grad[2],
        fields[3],
        fields[4],
        out_w_grad,
        fields[1],
        fields[0].reshape(-1, experts),
        gate_grad,
        up_grad,
        down_grad,
    )


def solution(mesh):
    local = fast_local if mesh.shape[EXPERT] == 8 else general_local
    return jax.shard_map(
        local,
        mesh=mesh,
        in_specs=(
            P(BOTH, None),
            P(EXPERT),
            P(BOTH, None),
            P(BOTH),
            P(BOTH),
            P(BOTH, None),
            P(BOTH, None),
            P(BOTH, None),
            P(BOTH),
            P(BOTH),
            P(BOTH, None),
            P(BOTH),
            P(BOTH, None),
            P(EXPERT, SHARD, None),
            P(EXPERT, SHARD, None),
            P(EXPERT, None, SHARD),
            P(BOTH, None),
        ),
        out_specs=(
            P(BOTH, None),
            P(BOTH, None),
            P(BOTH),
            P(BOTH, None),
            P(BOTH, None),
            P(BOTH, None),
            P(BOTH),
            P(BOTH),
            P(BOTH, None),
            P(BOTH),
            P(BOTH, None),
            P(EXPERT, SHARD, None),
            P(EXPERT, SHARD, None),
            P(EXPERT, None, SHARD),
        ),
        check_vma=False,
    )
```

```python
import functools

import jax
import jax.numpy as jnp
import numpy as np
from jax import lax
from jax.experimental import pallas as pl
from jax.experimental.pallas import tpu as pltpu
from jax.sharding import PartitionSpec as P

HEADS = 16
HD = 128


EXPERT = "expert"
SHARD = "wshard"
BOTH = (EXPERT, SHARD)

SUM_QHD_KHD_HQK = "qhd,khd->hqk"
SUM_HQK_KHD_QHD = "hqk,khd->qhd"
SUM_ECD_EDF_ECF = "ecd,edf->ecf"
SUM_ECF_EFD_ECD = "ecf,efd->ecd"
SUM_TK_TKD_TD = "tk,tkd->td"
SUM_TD_TKD_TK = "td,tkd->tk"
SUM_ECD_EFD_ECF = "ecd,efd->ecf"
SUM_ECF_ECD_EFD = "ecf,ecd->efd"
SUM_ECD_ECF_EDF = "ecd,ecf->edf"
SUM_ECF_EDF_ECD = "ecf,edf->ecd"
SUM_HQK_QHD_KHD = "hqk,qhd->khd"
EPSILON = 1e-06
THETA = 10000.0


def matmul(left, right):
    return jnp.dot(left, right, preferred_element_type=jnp.float32)


def matmul_tn(left, right):
    return lax.dot_general(
        left, right, (((0,), (0,)), ((), ())), preferred_element_type=jnp.float32
    )


def matmul_nt(left, right):
    return lax.dot_general(
        left, right, (((1,), (1,)), ((), ())), preferred_element_type=jnp.float32
    )


def rms_scale(values, scale_gain):
    factor = lax.rsqrt(jnp.mean(values * values, axis=-1, keepdims=True) + EPSILON)
    return values * factor * scale_gain


def rope_tables(positions):
    exponent = jnp.arange(HD // 2, dtype=jnp.float32) * (2.0 / HD)
    frequency = jnp.power(jnp.float32(THETA), -exponent)
    angles = positions.astype(jnp.float32)[:, None] * frequency[None, :]
    return (jnp.cos(angles), jnp.sin(angles))


def rotate(values, cosine, sine):
    first_half = values[..., : HD // 2]
    second_half = values[..., HD // 2 :]
    cos_part = cosine[:, None, :]
    sin_part = sine[:, None, :]
    return jnp.concatenate(
        [
            first_half * cos_part - second_half * sin_part,
            second_half * cos_part + first_half * sin_part,
        ],
        axis=-1,
    )


def padded_rows(rows):
    return jnp.concatenate([jnp.zeros((1,) + rows.shape[1:], rows.dtype), rows], axis=0)


def masked_scores(query_rot, key_rot, query_segment, key_segment):
    scores = jnp.einsum(SUM_QHD_KHD_HQK, query_rot, key_rot, preferred_element_type=jnp.float32)
    allowed = query_segment[:, None] == key_segment[None, :]
    return jnp.where(allowed[None], scores, -1e30)


def swiglu_fn(gate_in, up_in):
    return jax.nn.silu(gate_in) * up_in


def general_local(
    tokens,
    segment_ids,
    routes,
    pair_order,
    attn_gain,
    w_query,
    w_key,
    w_value,
    query_gain,
    key_gain,
    w_out,
    ffn_gain,
    w_router,
    w_gate,
    w_up,
    w_down,
    out_grad,
):
    tok_rows, width = tokens.shape
    top_count = routes.shape[1]
    expert_devs = lax.axis_size(EXPERT)
    shard_devs = lax.axis_size(SHARD)
    local_experts = w_gate.shape[0]
    expert_count = local_experts * expert_devs
    most_rows = 2 * tok_rows * top_count // expert_count
    capacity = 5 * tok_rows * top_count // (4 * local_experts)
    seq_length = segment_ids.shape[0]
    device_expert = lax.axis_index(EXPERT)
    device_shard = lax.axis_index(SHARD)
    low_type = jnp.bfloat16
    wide_type = jnp.float32
    gathered = (
        lax.all_gather(attn_gain, BOTH, axis=0, tiled=True),
        lax.all_gather(w_query, BOTH, axis=0, tiled=True),
        lax.all_gather(w_key, BOTH, axis=0, tiled=True),
        lax.all_gather(w_value, BOTH, axis=0, tiled=True),
        lax.all_gather(query_gain, BOTH, axis=0, tiled=True),
        lax.all_gather(key_gain, BOTH, axis=0, tiled=True),
        lax.all_gather(w_out, BOTH, axis=0, tiled=True),
        lax.all_gather(ffn_gain, BOTH, axis=0, tiled=True),
        lax.all_gather(w_router, BOTH, axis=0, tiled=True),
    )
    attn_scale = gathered[0].astype(wide_type)
    query_w, key_w, value_w = (gathered[1], gathered[2], gathered[3])
    query_scale = gathered[4].astype(wide_type)
    key_scale = gathered[5].astype(wide_type)
    out_w = gathered[6]
    ffn_scale = gathered[7].astype(wide_type)
    router_w = gathered[8]
    inputs = tokens.astype(wide_type)
    normed, norm_one_pull = jax.vjp(rms_scale, inputs, attn_scale)
    normed_low = normed.astype(low_type)
    query_raw = matmul(normed_low, query_w)
    key_raw = matmul(normed_low, key_w)
    value_low = matmul(normed_low, value_w).astype(low_type)
    positions = device_shard * tok_rows + jnp.arange(tok_rows, dtype=jnp.int32)
    cosine, sine = rope_tables(positions)

    def prepare(query_in, key_in, query_g, key_g):
        query_heads = rms_scale(query_in.reshape(tok_rows, HEADS, HD), query_g)
        key_heads = rms_scale(key_in.reshape(tok_rows, HEADS, HD), key_g)
        return (rotate(query_heads, cosine, sine) * HD ** (-0.5), rotate(key_heads, cosine, sine))

    rotated, prepare_pull = jax.vjp(prepare, query_raw, key_raw, query_scale, key_scale)
    query_low = rotated[0].astype(low_type)
    key_low = rotated[1].astype(low_type).reshape(tok_rows, width)
    seq_keys, seq_values = (
        lax.all_gather(key_low, SHARD, axis=0, tiled=True),
        lax.all_gather(value_low, SHARD, axis=0, tiled=True),
    )
    query_segment = lax.dynamic_slice_in_dim(segment_ids, device_shard * tok_rows, tok_rows)
    scores = masked_scores(
        query_low, seq_keys.reshape(seq_length, HEADS, HD), query_segment, segment_ids
    )
    row_max = jnp.max(scores, axis=-1, keepdims=True)
    shifted = jnp.exp(scores - row_max)
    totals = jnp.sum(shifted, axis=-1, keepdims=True)
    log_total = row_max + jnp.log(totals)
    probs_low = (shifted / totals).astype(low_type)
    mixed = jnp.einsum(
        SUM_HQK_KHD_QHD,
        probs_low,
        seq_values.reshape(seq_length, HEADS, HD),
        preferred_element_type=wide_type,
    )
    mixed_low = mixed.reshape(tok_rows, width).astype(low_type)
    hidden = inputs + matmul(mixed_low, out_w)
    normed_two, norm_two_pull = jax.vjp(rms_scale, hidden, ffn_scale)
    normed_two_low = normed_two.astype(low_type)
    logits = matmul(normed_two_low, router_w)

    def router_weights(logit_values):
        return jnp.take_along_axis(jax.nn.softmax(logit_values, axis=-1), routes, axis=1)

    route_weight, route_pull = jax.vjp(router_weights, logits)
    group_routes, group_order = (
        lax.all_gather(routes, EXPERT, axis=0, tiled=True),
        lax.all_gather(pair_order, EXPERT, axis=0, tiled=True),
    )
    per_source = tok_rows * top_count
    group_pairs = per_source * expert_devs
    expert_of = group_routes.reshape(-1)
    pair_index = jnp.arange(group_pairs, dtype=jnp.int32)
    source_of = pair_index // per_source
    expert_ids = jnp.arange(expert_count, dtype=jnp.int32)
    onehot = (expert_of.reshape(expert_devs, per_source, 1) == expert_ids).astype(jnp.int32)
    position_of = (jnp.sum(jnp.cumsum(onehot, axis=1) * onehot, axis=-1) - 1).reshape(-1)
    order_span = group_pairs * shard_devs
    sort_keys = expert_of * order_span + group_order
    sorted_pairs = jnp.argsort(sort_keys)
    placement = jnp.zeros((group_pairs,), jnp.int32).at[sorted_pairs].set(pair_index)
    expert_counts = jnp.sum(onehot, axis=(0, 1))
    expert_start = jnp.cumsum(expert_counts) - expert_counts
    start_of = jnp.sum(onehot.reshape(group_pairs, expert_count) * expert_start[None, :], axis=-1)
    slot_rank = placement - start_of
    retained = slot_rank < capacity
    own_expert = routes.reshape(-1)
    own_position = lax.dynamic_slice_in_dim(position_of, device_expert * per_source, per_source)
    send_slot = own_expert * most_rows + own_position
    send_pair = (
        jnp.zeros((expert_count * most_rows,), jnp.int32)
        .at[send_slot]
        .set(jnp.arange(per_source, dtype=jnp.int32) + 1)
    )
    send_token = jnp.where(send_pair > 0, (send_pair - 1) // top_count + 1, 0)
    owner_local = expert_of % local_experts
    is_mine = expert_of // local_experts == device_expert
    recv_row = source_of * (local_experts * most_rows) + owner_local * most_rows + position_of
    slot_target = jnp.where(
        is_mine & retained, owner_local * capacity + slot_rank, local_experts * capacity
    )
    slot_source = (
        jnp.zeros((local_experts * capacity,), jnp.int32)
        .at[slot_target]
        .set(recv_row + 1, mode="drop")
    )
    back_room = expert_devs * local_experts * most_rows
    back_target = jnp.where(is_mine, recv_row, back_room)
    back_source = (
        jnp.zeros((back_room,), jnp.int32)
        .at[back_target]
        .set(jnp.where(retained, owner_local * capacity + slot_rank + 1, 0), mode="drop")
    )
    send_rows = padded_rows(normed_two_low)[send_token].reshape(
        expert_devs, local_experts * most_rows, width
    )
    recv_rows = lax.all_to_all(
        send_rows, EXPERT, split_axis=0, concat_axis=0, tiled=True
    ).reshape(-1, width)
    slot_rows = padded_rows(recv_rows)[slot_source].reshape(local_experts, capacity, width)
    full_gate, full_up, full_down = (
        lax.all_gather(w_gate, SHARD, axis=1, tiled=True),
        lax.all_gather(w_up, SHARD, axis=1, tiled=True),
        lax.all_gather(w_down, SHARD, axis=2, tiled=True),
    )
    gate_act = jnp.einsum(SUM_ECD_EDF_ECF, slot_rows, full_gate, preferred_element_type=wide_type)
    up_act = jnp.einsum(SUM_ECD_EDF_ECF, slot_rows, full_up, preferred_element_type=wide_type)
    swiglu_out, swiglu_pull = jax.vjp(swiglu_fn, gate_act, up_act)
    swiglu_low = swiglu_out.astype(low_type)
    expert_out = jnp.einsum(
        SUM_ECF_EFD_ECD, swiglu_low, full_down, preferred_element_type=wide_type
    ).astype(low_type)
    back_rows = padded_rows(expert_out.reshape(-1, width))[back_source].reshape(
        expert_devs, local_experts * most_rows, width
    )
    returned = lax.all_to_all(back_rows, EXPERT, split_axis=0, concat_axis=0, tiled=True).reshape(
        -1, width
    )
    pair_rows = returned[send_slot].reshape(tok_rows, top_count, width)
    combined = jnp.einsum(SUM_TK_TKD_TD, route_weight, pair_rows, preferred_element_type=wide_type)
    mixed_out = (hidden + combined).astype(low_type)
    result_grad = out_grad.astype(wide_type)
    weight_grad = jnp.einsum(SUM_TD_TKD_TK, result_grad, pair_rows, preferred_element_type=wide_type)
    pair_grad = (
        (route_weight[:, :, None] * result_grad[:, None, :])
        .astype(low_type)
        .reshape(per_source, width)
    )
    send_grad = padded_rows(pair_grad)[send_pair].reshape(
        expert_devs, local_experts * most_rows, width
    )
    recv_grad = lax.all_to_all(
        send_grad, EXPERT, split_axis=0, concat_axis=0, tiled=True
    ).reshape(-1, width)
    slot_grad = padded_rows(recv_grad)[slot_source].reshape(local_experts, capacity, width)
    act_grad = jnp.einsum(SUM_ECD_EFD_ECF, slot_grad, full_down, preferred_element_type=wide_type)
    down_grad = jnp.einsum(SUM_ECF_ECD_EFD, swiglu_low, slot_grad, preferred_element_type=wide_type)
    gate_grad, up_grad = swiglu_pull(act_grad)
    gate_low = gate_grad.astype(low_type)
    up_low = up_grad.astype(low_type)
    gate_w_grad = jnp.einsum(SUM_ECD_ECF_EDF, slot_rows, gate_low, preferred_element_type=wide_type)
    up_w_grad = jnp.einsum(SUM_ECD_ECF_EDF, slot_rows, up_low, preferred_element_type=wide_type)
    slot_in_grad = jnp.einsum(SUM_ECF_EDF_ECD, gate_low, full_gate, preferred_element_type=wide_type)
    slot_in_grad = (
        slot_in_grad + jnp.einsum(SUM_ECF_EDF_ECD, up_low, full_up, preferred_element_type=wide_type)
    ).astype(low_type)
    gate_shard, up_shard, down_shard = (
        lax.psum_scatter(
            gate_w_grad.astype(jnp.bfloat16), SHARD, scatter_dimension=1, tiled=True
        ).astype(jnp.float32),
        lax.psum_scatter(
            up_w_grad.astype(jnp.bfloat16), SHARD, scatter_dimension=1, tiled=True
        ).astype(jnp.float32),
        lax.psum_scatter(
            down_grad.astype(jnp.bfloat16), SHARD, scatter_dimension=2, tiled=True
        ).astype(jnp.float32),
    )
    back_grad = padded_rows(slot_in_grad.reshape(-1, width))[back_source].reshape(
        expert_devs, local_experts * most_rows, width
    )
    returned_grad = lax.all_to_all(
        back_grad, EXPERT, split_axis=0, concat_axis=0, tiled=True
    ).reshape(-1, width)
    expert_in_grad = jnp.sum(
        returned_grad[send_slot].reshape(tok_rows, top_count, width).astype(wide_type), axis=1
    )
    logit_grad = route_pull(weight_grad)[0]
    logit_low = logit_grad.astype(low_type)
    router_grad = matmul_tn(normed_two_low, logit_low)
    normed_two_grad = expert_in_grad + matmul_nt(logit_low, router_w)
    hidden_norm_grad, ffn_scale_grad = norm_two_pull(normed_two_grad)
    hidden_grad = result_grad + hidden_norm_grad
    attn_low = hidden_grad.astype(low_type)
    out_w_grad = matmul_tn(mixed_low, attn_low)
    mixed_grad = matmul_nt(attn_low, out_w).astype(low_type).reshape(tok_rows, HEADS, HD)
    back_keys, back_values = (seq_keys, seq_values)
    key_heads = back_keys.reshape(seq_length, HEADS, HD)
    value_heads = back_values.reshape(seq_length, HEADS, HD)
    scores_again = masked_scores(query_low, key_heads, query_segment, segment_ids)
    probs_again = jnp.exp(scores_again - log_total)
    probs_again_low = probs_again.astype(low_type)
    prob_grad = jnp.einsum(
        SUM_QHD_KHD_HQK, mixed_grad, value_heads, preferred_element_type=wide_type
    )
    value_part = jnp.einsum(
        SUM_HQK_QHD_KHD, probs_again_low, mixed_grad, preferred_element_type=wide_type
    )
    row_inner = jnp.sum(probs_again * prob_grad, axis=-1, keepdims=True)
    score_low = (probs_again * (prob_grad - row_inner)).astype(low_type)
    query_rot_grad = jnp.einsum(
        SUM_HQK_KHD_QHD, score_low, key_heads, preferred_element_type=wide_type
    )
    key_part = jnp.einsum(SUM_HQK_QHD_KHD, score_low, query_low, preferred_element_type=wide_type)
    key_rot_grad, value_grad = (
        lax.psum_scatter(
            key_part.reshape(seq_length, width).astype(jnp.bfloat16),
            SHARD,
            scatter_dimension=0,
            tiled=True,
        ).astype(jnp.float32),
        lax.psum_scatter(
            value_part.reshape(seq_length, width).astype(jnp.bfloat16),
            SHARD,
            scatter_dimension=0,
            tiled=True,
        ).astype(jnp.float32),
    )
    query_raw_grad, key_raw_grad, query_scale_grad, key_scale_grad = prepare_pull(
        (query_rot_grad, key_rot_grad.reshape(tok_rows, HEADS, HD))
    )
    query_grad_low = query_raw_grad.astype(low_type)
    key_grad_low = key_raw_grad.astype(low_type)
    value_grad_low = value_grad.astype(low_type)
    query_w_grad = matmul_tn(normed_low, query_grad_low)
    key_w_grad = matmul_tn(normed_low, key_grad_low)
    value_w_grad = matmul_tn(normed_low, value_grad_low)
    normed_grad = (
        matmul_nt(query_grad_low, query_w)
        + matmul_nt(key_grad_low, key_w)
        + matmul_nt(value_grad_low, value_w)
    )
    input_norm_grad, attn_scale_grad = norm_one_pull(normed_grad)
    input_grad = (hidden_grad + input_norm_grad).astype(low_type)
    summed = (
        lax.psum_scatter(attn_scale_grad, BOTH, scatter_dimension=0, tiled=True),
        lax.psum_scatter(query_w_grad, BOTH, scatter_dimension=0, tiled=True),
        lax.psum_scatter(key_w_grad, BOTH, scatter_dimension=0, tiled=True),
        lax.psum_scatter(value_w_grad, BOTH, scatter_dimension=0, tiled=True),
        lax.psum_scatter(query_scale_grad, BOTH, scatter_dimension=0, tiled=True),
        lax.psum_scatter(key_scale_grad, BOTH, scatter_dimension=0, tiled=True),
        lax.psum_scatter(out_w_grad, BOTH, scatter_dimension=0, tiled=True),
        lax.psum_scatter(ffn_scale_grad, BOTH, scatter_dimension=0, tiled=True),
        lax.psum_scatter(router_grad, BOTH, scatter_dimension=0, tiled=True),
    )
    return (
        mixed_out,
        input_grad,
        summed[0],
        summed[1],
        summed[2],
        summed[3],
        summed[4],
        summed[5],
        summed[6],
        summed[7],
        summed[8],
        gate_shard,
        up_shard,
        down_shard,
    )


MIB = 1 << 20


def nt_dot(left, right):
    return lax.dot_general(
        left, right, (((1,), (1,)), ((), ())), preferred_element_type=jnp.float32
    )


def tn_dot(left, right):
    return lax.dot_general(
        left, right, (((0,), (0,)), ((), ())), preferred_element_type=jnp.float32
    )


def vmem_params(mib):
    return pltpu.CompilerParams(vmem_limit_bytes=mib * MIB)


def turn_tables(length):
    exponent = np.arange(HD // 2, dtype=np.float32) * np.float32(2.0 / HD)
    frequency = np.power(np.float32(THETA), -exponent).astype(np.float32)
    angles = np.arange(length, dtype=np.float32)[:, None] * frequency[None, :]
    cosine, sine = np.cos(angles), np.sin(angles)
    return (
        jnp.asarray(np.concatenate([cosine, cosine], axis=1), jnp.float32),
        jnp.asarray(np.concatenate([-sine, sine], axis=1), jnp.float32),
    )


def norm_factor(values):
    return lax.rsqrt(jnp.mean(values * values, axis=-1, keepdims=True) + EPSILON)


def attend_kernel(
    tokens, gain, weight, query_gain, key_gain, cosine, sine, seg_row, seg_col,
    normed_out, raw_out, low_out, mixed_out, total_out, qkv,
):
    part = mixed_out.shape[1]
    values = tokens[...].astype(jnp.float32)
    normed = (values * norm_factor(values) * gain[...]).astype(jnp.bfloat16)
    normed_out[...] = normed
    qkv[...] = jnp.dot(normed, weight[...], preferred_element_type=jnp.float32)
    raw_out[...] = qkv[:, : 2 * part]
    low_out[:, 2 * part :] = qkv[:, 2 * part :].astype(jnp.bfloat16)
    allowed = seg_col[...] == seg_row[...]
    for head in range(part // HD):
        span = pl.ds(head * HD, HD)
        for offset, scale_gain, scale in ((0, query_gain, HD ** (-0.5)), (part, key_gain, 1.0)):
            raw = qkv[:, pl.ds(offset + head * HD, HD)]
            unit = raw * norm_factor(raw) * scale_gain[...]
            turned = unit * cosine[...] + pltpu.roll(unit, HD // 2, 1) * sine[...]
            low_out[:, pl.ds(offset + head * HD, HD)] = (turned * scale).astype(jnp.bfloat16)
        query, key = low_out[:, span], low_out[:, pl.ds(part + head * HD, HD)]
        scores = jnp.where(allowed, nt_dot(query, key), -1e30)
        top = jnp.max(scores, axis=-1, keepdims=True)
        shifted = jnp.exp(scores - top)
        total = jnp.sum(shifted, axis=-1, keepdims=True)
        probs = (shifted / total).astype(jnp.bfloat16)
        mixed = jnp.dot(
            probs, low_out[:, pl.ds(2 * part + head * HD, HD)], preferred_element_type=jnp.float32
        )
        mixed_out[:, span] = mixed.astype(jnp.bfloat16)
        total_out[:, head : head + 1] = top + jnp.log(total)


def attend_call(tokens, gain, weight, query_gain, key_gain, tables, seg_row, seg_col):
    seq, width = tokens.shape
    part = weight.shape[1] // 3
    return pl.pallas_call(
        attend_kernel,
        out_shape=(
            jax.ShapeDtypeStruct((seq, width), jnp.bfloat16),
            jax.ShapeDtypeStruct((seq, 2 * part), jnp.float32),
            jax.ShapeDtypeStruct((seq, 3 * part), jnp.bfloat16),
            jax.ShapeDtypeStruct((seq, part), jnp.bfloat16),
            jax.ShapeDtypeStruct((seq, 128), jnp.float32),
        ),
        scratch_shapes=[pltpu.VMEM((seq, 3 * part), jnp.float32)],
        compiler_params=vmem_params(52),
        cost_estimate=pl.CostEstimate(
            flops=2 * seq * width * 3 * part, bytes_accessed=16 * MIB, transcendentals=seq * seq * 4
        ),
    )(tokens, gain, weight, query_gain, key_gain, *tables, seg_row, seg_col)


def join_kernel(mixed, weight, tokens, gain, hidden_out, normed_out):
    shards, _, part = mixed.shape
    total = tokens[...].astype(jnp.float32)
    for shard in range(shards):
        total = total + jnp.dot(
            mixed[shard], weight[pl.ds(shard * part, part), :], preferred_element_type=jnp.float32
        )
    hidden_out[...] = total
    normed_out[...] = (total * norm_factor(total) * gain[...]).astype(jnp.bfloat16)


def join_call(mixed, weight, tokens, gain):
    shards, seq, part = mixed.shape
    width = weight.shape[1]
    tile = seq // 2
    return pl.pallas_call(
        join_kernel,
        grid=(2,),
        in_specs=[
            pl.BlockSpec((shards, tile, part), lambda i: (0, i, 0)),
            pl.BlockSpec(weight.shape, lambda i: (0, 0), pipeline_mode=pl.Buffered(1)),
            pl.BlockSpec((tile, width), lambda i: (i, 0)),
            pl.BlockSpec((1, width), lambda i: (0, 0)),
        ],
        out_specs=[
            pl.BlockSpec((tile, width), lambda i: (i, 0)),
            pl.BlockSpec((tile, width), lambda i: (i, 0)),
        ],
        out_shape=(
            jax.ShapeDtypeStruct((seq, width), jnp.float32),
            jax.ShapeDtypeStruct((seq, width), jnp.bfloat16),
        ),
        compiler_params=vmem_params(40),
        cost_estimate=pl.CostEstimate(
            flops=2 * seq * width * width, bytes_accessed=18 * MIB, transcendentals=0
        ),
    )(mixed, weight, tokens, gain)


def expert_kernel(
    experts, x, g, keep, wide_w, router_w, down_w, hot,
    out, grad, wide_sum, router_sum, down_sum, acc, racc, dacc, wide_out, down_out, sems,
):
    step, steps = pl.program_id(0), pl.num_programs(0)

    @pl.when(step == 0)
    def _():
        acc[...] = jnp.zeros_like(acc)
        racc[...] = jnp.zeros_like(racc)
        dacc[...] = jnp.zeros_like(dacc)

    shards, units, part = down_w.shape
    own = keep.shape[1]
    each = units // own
    wide = jnp.dot(x[...], wide_w[...], preferred_element_type=jnp.float32)
    logits = jnp.dot(x[...], router_w[...], preferred_element_type=jnp.float32)
    back = nt_dot(g[:, :part], down_w[0])
    for shard in range(1, shards):
        back = back + nt_dot(g[:, shard * part : (shard + 1) * part], down_w[shard])
    lane = lax.broadcasted_iota(jnp.int32, logits.shape, 1)
    logits = jnp.where(lane < experts, logits, -1e30)
    shifted = jnp.exp(logits - jnp.max(logits, axis=-1, keepdims=True))
    probs = shifted / jnp.sum(shifted, axis=-1, keepdims=True)
    dense = jnp.zeros_like(probs)
    acts, gates, ups = [], [], []
    for index in range(own):
        mark = hot[index : index + 1, :]
        kept = keep[:, index : index + 1]
        route = jnp.sum(probs * mark, axis=-1, keepdims=True) * kept
        gate = wide[:, index * each : (index + 1) * each]
        up = wide[:, units + index * each : units + (index + 1) * each]
        behind = back[:, index * each : (index + 1) * each]
        sigma = 1.0 / (1.0 + jnp.exp(-gate))
        silu = gate * sigma
        act = silu * up
        dense = dense + jnp.sum(act * behind, axis=-1, keepdims=True) * kept * mark
        acts.append((act * route).astype(jnp.bfloat16))
        act_grad = behind * route
        gates.append((act_grad * up * sigma * (1.0 + gate * (1.0 - sigma))).astype(jnp.bfloat16))
        ups.append((act_grad * silu).astype(jnp.bfloat16))
    logit_grad = probs * (dense - jnp.sum(probs * dense, axis=-1, keepdims=True))
    logit_low = logit_grad.astype(jnp.bfloat16)
    act_low = jnp.concatenate(acts, axis=1)
    wide_low = jnp.concatenate(gates + ups, axis=1)
    for shard in range(shards):
        out[:, shard * part : (shard + 1) * part] = jnp.dot(
            act_low, down_w[shard], preferred_element_type=jnp.float32
        ).astype(jnp.bfloat16)
    grad[...] = (nt_dot(wide_low, wide_w[...]) + nt_dot(logit_low, router_w[...])).astype(
        jnp.bfloat16
    )
    acc[...] += tn_dot(x[...], wide_low)
    racc[...] += tn_dot(x[...], logit_low)
    for shard in range(shards):
        dacc[shard] += tn_dot(act_low, g[:, shard * part : (shard + 1) * part])

    @pl.when(step == steps - 1)
    def _():
        router_copy = pltpu.make_async_copy(racc, router_sum, sems.at[1])
        router_copy.start()
        wide_out[...] = acc[...].astype(jnp.bfloat16)
        wide_copy = pltpu.make_async_copy(wide_out, wide_sum, sems.at[0])
        wide_copy.start()
        down_out[...] = dacc[...].astype(jnp.bfloat16)
        down_copy = pltpu.make_async_copy(down_out, down_sum, sems.at[2])
        down_copy.start()
        router_copy.wait()
        wide_copy.wait()
        down_copy.wait()


def expert_call(x_all, g_all, keep, wide_w, router_w, down_w, hot, experts):
    planes, rows, width = x_all.shape
    tile = 256
    per = rows // tile
    hbm = pl.BlockSpec(memory_space=pltpu.HBM)

    def whole(value):
        zeros = (0,) * value.ndim
        return pl.BlockSpec(value.shape, lambda i: zeros, pipeline_mode=pl.Buffered(1))

    def rowwise(lanes):
        return pl.BlockSpec((None, tile, lanes), lambda i: (i // per, i % per, 0))

    return pl.pallas_call(
        functools.partial(expert_kernel, experts),
        grid=(planes * per,),
        in_specs=[
            rowwise(width),
            rowwise(width),
            rowwise(keep.shape[2]),
            whole(wide_w),
            whole(router_w),
            whole(down_w),
            whole(hot),
        ],
        out_specs=[rowwise(width), rowwise(width), hbm, hbm, hbm],
        scratch_shapes=[
            pltpu.VMEM(wide_w.shape, jnp.float32),
            pltpu.VMEM(router_w.shape, jnp.float32),
            pltpu.VMEM(down_w.shape, jnp.float32),
            pltpu.VMEM(wide_w.shape, jnp.bfloat16),
            pltpu.VMEM(down_w.shape, jnp.bfloat16),
            pltpu.SemaphoreType.DMA((3,)),
        ],
        out_shape=(
            jax.ShapeDtypeStruct((planes, rows, width), jnp.bfloat16),
            jax.ShapeDtypeStruct((planes, rows, width), jnp.bfloat16),
            jax.ShapeDtypeStruct(wide_w.shape, jnp.bfloat16),
            jax.ShapeDtypeStruct(router_w.shape, jnp.float32),
            jax.ShapeDtypeStruct(down_w.shape, jnp.bfloat16),
        ),
        compiler_params=vmem_params(56),
        cost_estimate=pl.CostEstimate(
            flops=2 * planes * rows * width * (3 * wide_w.shape[1] + 3 * down_w.shape[1]),
            bytes_accessed=100 * MIB,
            transcendentals=planes * rows * down_w.shape[1],
        ),
    )(x_all, g_all, keep, wide_w, router_w, down_w, hot)


def attend_back_kernel(
    mixed_grad, raw, low, total, weight, query_gain, key_gain, cosine, sine, seg_row, seg_col,
    qkv_grad_out, normed_grad_out, query_gain_out, key_gain_out,
):
    part = mixed_grad.shape[1]
    allowed = seg_col[...] == seg_row[...]
    gain_sums = [None, None]
    for head in range(part // HD):
        span = pl.ds(head * HD, HD)
        query, key = low[:, span], low[:, pl.ds(part + head * HD, HD)]
        value = low[:, pl.ds(2 * part + head * HD, HD)]
        out_grad = mixed_grad[:, span]
        scores = jnp.where(allowed, nt_dot(query, key), -1e30)
        probs = jnp.exp(scores - total[:, head : head + 1])
        prob_grad = nt_dot(out_grad, value)
        value_grad = tn_dot(probs.astype(jnp.bfloat16), out_grad)
        qkv_grad_out[:, pl.ds(2 * part + head * HD, HD)] = value_grad.astype(jnp.bfloat16)
        inner = jnp.sum(probs * prob_grad, axis=-1, keepdims=True)
        score_grad = (probs * (prob_grad - inner)).astype(jnp.bfloat16)
        rotated = (
            jnp.dot(score_grad, key, preferred_element_type=jnp.float32) * HD ** (-0.5),
            tn_dot(score_grad, query),
        )
        for which, (offset, scale_gain) in enumerate(((0, query_gain), (part, key_gain))):
            grad = rotated[which]
            grad = grad * cosine[...] - pltpu.roll(grad, HD // 2, 1) * sine[...]
            source = raw[:, pl.ds(offset + head * HD, HD)]
            factor = norm_factor(source)
            gain_sum = jnp.sum(grad * source * factor, axis=0, keepdims=True)
            gain_sums[which] = gain_sum if head == 0 else gain_sums[which] + gain_sum
            scaled = grad * scale_gain[...]
            inner = jnp.mean(scaled * source, axis=-1, keepdims=True)
            result = factor * scaled - source * (factor * factor * factor) * inner
            qkv_grad_out[:, pl.ds(offset + head * HD, HD)] = result.astype(jnp.bfloat16)
    query_gain_out[...] = gain_sums[0]
    key_gain_out[...] = gain_sums[1]
    normed_grad_out[...] = nt_dot(qkv_grad_out[...], weight[...]).astype(jnp.bfloat16)


def attend_back_call(
    mixed_grad, raw, low, total, weight, query_gain, key_gain, tables, seg_row, seg_col
):
    seq = mixed_grad.shape[0]
    width = weight.shape[0]
    return pl.pallas_call(
        attend_back_kernel,
        out_shape=(
            jax.ShapeDtypeStruct(low.shape, jnp.bfloat16),
            jax.ShapeDtypeStruct((seq, width), jnp.bfloat16),
            jax.ShapeDtypeStruct((1, HD), jnp.float32),
            jax.ShapeDtypeStruct((1, HD), jnp.float32),
        ),
        compiler_params=vmem_params(52),
        cost_estimate=pl.CostEstimate(
            flops=2 * seq * width * low.shape[1], bytes_accessed=16 * MIB, transcendentals=seq * seq * 4
        ),
    )(mixed_grad, raw, low, total, weight, query_gain, key_gain, *tables, seg_row, seg_col)


def copy_kernel(*refs):
    half = len(refs) // 2
    for source, result in zip(refs[:half], refs[half:], strict=True):
        result[...] = source[...].reshape(result.shape).astype(result.dtype)


def unpack_units(wide, narrow, own):
    shards, part, count = wide.shape
    each = count // (2 * own)
    gate = pl.BlockSpec((1, part, each), lambda e, s: (s, 0, e))
    up = pl.BlockSpec((1, part, each), lambda e, s: (s, 0, own + e))
    result = pl.BlockSpec((1, part, each), lambda e, s: (e, 0, s))
    shape = jax.ShapeDtypeStruct((own, part, shards * each), jnp.float32)
    gate_grad, up_grad = pl.pallas_call(
        copy_kernel,
        grid=(own, shards),
        in_specs=[gate, up],
        out_specs=[result, result],
        out_shape=[shape, shape],
        compiler_params=vmem_params(16),
    )(wide, wide)
    down_grad = pl.pallas_call(
        copy_kernel,
        grid=(own, shards),
        in_specs=[pl.BlockSpec((1, each, part), lambda e, s: (s, e, 0))],
        out_specs=[pl.BlockSpec((1, each, part), lambda e, s: (e, s, 0))],
        out_shape=[jax.ShapeDtypeStruct((own, shards * each, part), jnp.float32)],
        compiler_params=vmem_params(16),
    )(narrow)[0]
    return gate_grad, up_grad, down_grad


def keep_kernel(capacity, bits, shards, high, low, keep_out):
    own, _, rows = high.shape
    for index in range(own):
        order = high[index].astype(jnp.float32) * 256.0 + low[index].astype(jnp.float32)
        there = order > 0.0
        row = lax.broadcasted_iota(jnp.int32, order.shape, 0)
        group = lax.rem(row, shards)
        bound = jnp.zeros_like(order)
        for bit in reversed(range(bits)):
            trial = bound + float(1 << bit)
            within = jnp.where(there & (order <= trial), 1.0, 0.0)
            for shard in range(shards):
                here = group == shard
                count = jnp.sum(jnp.where(here, within, 0.0), keepdims=True)
                bound = jnp.where(here & (count <= float(capacity)), trial, bound)
        kept = jnp.where(there & (order <= bound), 1.0, 0.0).T
        for block in range(order.shape[0]):
            place = keep_out.at[block // shards, pl.ds(block % shards * rows, rows)]
            place[:, index : index + 1] = kept[:, block : block + 1]


def keep_call(high, low, capacity, most, planes, shards):
    own, _, rows = high.shape
    return pl.pallas_call(
        functools.partial(keep_kernel, capacity, most.bit_length(), shards),
        out_shape=jax.ShapeDtypeStruct((planes, shards * rows, own), jnp.float32),
        compiler_params=vmem_params(24),
    )(high, low)


CORE, XBIT, YBIT = 1, 2, 4


MESH = pl.DeviceIdType.MESH


class Wires:
    def __init__(self, send, recv):
        self.send, self.recv, self.used = send, recv, 0
        self.device, self.shard = lax.axis_index(EXPERT), lax.axis_index(SHARD)

    def slot(self):
        self.used += 1
        return self.used - 1

    def peer(self, bits=0, step=0, shards=1):
        shard = lax.rem(self.shard + step, shards) if step else self.shard
        return (self.device ^ bits, shard)

    def copy(self, source, target, slot, peer):
        return pltpu.make_async_remote_copy(
            src_ref=source,
            dst_ref=target,
            send_sem=self.send.at[slot],
            recv_sem=self.recv.at[slot],
            device_id=peer,
            device_id_type=MESH,
        )


def greet(peers):
    barrier = pltpu.get_barrier_semaphore()
    for peer in peers:
        pl.semaphore_signal(barrier, inc=1, device_id=peer, device_id_type=MESH)
    pl.semaphore_wait(barrier, len(peers))


class Relay:
    def __init__(self, wires, shards, views):
        self.wires, self.shards, self.views = wires, shards, views
        self.slots = [[[wires.slot() for _ in views] for _ in range(shards - 1)] for _ in range(2)]

    def copies(self, way, step, block):
        wires = self.wires
        peer = (wires.device, wires.shard + (1 if way == 0 else -1))
        return [
            wires.copy(view(block), view(block), slot, peer)
            for view, slot in zip(self.views, self.slots[way][step], strict=True)
        ]

    def has(self, way, step):
        shard = self.wires.shard
        return shard - step >= 0 if way == 0 else shard + step < self.shards

    def sends(self, way, step):
        shard = self.wires.shard
        edge = shard < self.shards - 1 if way == 0 else shard > 0
        return jnp.logical_and(edge, self.has(way, step))

    def block(self, way, step):
        return self.wires.shard + (-step if way == 0 else step)

    def run(self, step, first=None):
        for way in range(2):
            if step > 0:

                @pl.when(self.has(way, step))
                def _(way=way):
                    for copy in self.copies(way, step - 1, self.block(way, step)):
                        copy.wait_recv()

            if step < self.shards - 1:

                @pl.when(self.sends(way, step))
                def _(way=way):
                    if first is None:
                        copies = self.copies(way, step, self.block(way, step))
                    else:
                        wires = self.wires
                        peer = (wires.device, wires.shard + (1 if way == 0 else -1))
                        block = self.block(way, step)
                        copies = [
                            wires.copy(source, view(block), slot, peer)
                            for source, view, slot in zip(
                                first, self.views, self.slots[way][step], strict=True
                            )
                        ]
                    for copy in copies:
                        copy.start()

    def drain(self):
        for way in range(2):
            for step in range(self.shards - 1):

                @pl.when(self.sends(way, step))
                def _(way=way, step=step):
                    for copy in self.copies(way, step, self.block(way, step)):
                        copy.wait_send()


class Plane:
    def __init__(self, wires, views, whole):
        self.wires, self.views, self.whole = wires, views, whole
        count = len(views)
        self.first = [[wires.slot() for _ in range(count)] for _ in range(2)]
        self.second = [[[wires.slot() for _ in range(count)] for _ in range(2)] for _ in range(2)]
        self.last = [[wires.slot() for _ in range(count)] for _ in range(4)]
        self.sent = []

    def start(self, copies):
        for copy in copies:
            copy.start()
        self.sent += copies

    def one(self, owner, half, bits, slots):
        wires = self.wires
        return [
            wires.copy(view(owner, half), view(owner, half), slot, wires.peer(bits))
            for view, slot in zip(self.views, slots, strict=True)
        ]

    def step_one(self):
        me = self.wires.device
        for half, bits in enumerate((XBIT, YBIT)):
            self.start(self.one(me, half, bits, self.first[half]))

    def step_two(self):
        me = self.wires.device
        for half, bits in enumerate((XBIT, YBIT)):
            for copy in self.one(me ^ bits, half, bits, self.first[half]):
                copy.wait_recv()
        for half, bits in enumerate((XBIT, YBIT)):
            other = (XBIT | YBIT) ^ bits
            self.start(self.one(me, half, other, self.second[half][0]))
            self.start(self.one(me ^ bits, half, other, self.second[half][1]))

    def cores(self, index):
        wires = self.wires
        owner = wires.device ^ (0, XBIT, YBIT, XBIT | YBIT)[index]
        return [
            wires.copy(place(owner), place(owner), slot, wires.peer(CORE))
            for place, slot in zip(self.whole, self.last[index], strict=True)
        ]

    def step_three(self):
        me = self.wires.device
        for half, bits in enumerate((XBIT, YBIT)):
            other = (XBIT | YBIT) ^ bits
            for owner, slots in ((me ^ other, 0), (me ^ other ^ bits, 1)):
                for copy in self.one(owner, half, other, self.second[half][slots]):
                    copy.wait_recv()
        for index in range(1, 4):
            self.start(self.cores(index))

    def finish(self):
        for index, bits in enumerate((0, XBIT, YBIT, XBIT | YBIT)):
            owner = self.wires.device ^ CORE ^ bits
            for place, slot in zip(self.whole, self.last[index], strict=True):
                self.wires.copy(
                    place(owner), place(owner), slot, self.wires.peer(CORE)
                ).wait_recv()
        for copy in self.sent:
            copy.wait_send()


def opening_kernel(
    shards, experts, routes, order, gains, router, w_query, w_key, w_value, tokens, w_out, out_grad,
    small_all, router_all, qkv_w, tokens_all, out_block, grad_seq, small, send, recv, local,
):
    wires = Wires(send, recv)
    device, shard = wires.device, wires.shard
    weights = (w_query, w_key, w_value)
    block, width = w_query.shape
    rows = tokens.shape[0]
    part = width // shards
    greet(
        [wires.peer(step=step, shards=shards) for step in range(1, shards)]
        + [wires.peer(XBIT), wires.peer(YBIT), wires.peer(CORE)]
    )

    def place(source_shard, which):
        start = pl.multiple_of((device * shards + source_shard) * block, block)
        return qkv_w.at[pl.ds(start, block), pl.ds(which * part, part)]

    def cut(which, target):
        return weights[which].at[:, pl.ds(pl.multiple_of(target * part, part), part)]

    mine = device * shards + shard
    exchange = [[wires.slot() for _ in range(5)] for _ in range(1, shards)]
    sent = []
    for step in range(1, shards):
        peer = wires.peer(step=step, shards=shards)
        slots = exchange[step - 1]
        copies = [wires.copy(router, router_all.at[mine], slots[4], peer)] + [
            wires.copy(cut(which, peer[1]), place(shard, which), slots[which], peer)
            for which in range(3)
        ]
        for copy in copies:
            copy.start()
        sent += copies
    own = [
        pltpu.make_async_copy(cut(which, shard), place(shard, which), local.at[which])
        for which in range(3)
    ]
    own += [
        pltpu.make_async_copy(router, router_all.at[mine], local.at[3]),
        pltpu.make_async_copy(
            tokens, tokens_all.at[pl.ds(pl.multiple_of(shard * rows, rows), rows)], local.at[4]
        ),
        pltpu.make_async_copy(
            w_out, out_block.at[pl.ds(pl.multiple_of(shard * block, block), block)], local.at[5]
        ),
        pltpu.make_async_copy(
            out_grad, grad_seq.at[pl.ds(pl.multiple_of(shard * rows, rows), rows)], local.at[6]
        ),
    ]
    for copy in own:
        copy.start()
    line = Relay(
        wires,
        shards,
        [
            lambda b: tokens_all.at[pl.ds(pl.multiple_of(b * rows, rows), rows)],
            lambda b: out_block.at[pl.ds(pl.multiple_of(b * block, block), block)],
            lambda b: grad_seq.at[pl.ds(pl.multiple_of(b * rows, rows), rows)],
        ],
    )
    line.run(0, (tokens, w_out, out_grad))
    column = lax.broadcasted_iota(jnp.int32, (rows, 128), 1)
    dense = jnp.zeros((rows, 128), jnp.int32)
    for choice in range(routes.shape[1]):
        named = routes[:, choice : choice + 1] == column
        dense = dense + jnp.where(named, order[:, choice : choice + 1] + 1, 0)
    high = lax.shift_right_logical(dense, 8)
    for start, digits in ((0, high), (experts, dense - high * 256)):
        turned = digits.astype(jnp.float32).T
        small[pl.ds(start, experts), :] = turned[:experts, :].astype(small.dtype)
    small[pl.ds(2 * experts, gains.shape[0]), :] = gains[...]
    for step in range(1, shards):
        peer = wires.peer(step=step, shards=shards)
        copy = wires.copy(small, small_all.at[mine], exchange[step - 1][3], peer)
        copy.start()
        sent.append(copy)
    own.append(pltpu.make_async_copy(small, small_all.at[mine], local.at[7]))
    own[-1].start()
    for copy in own:
        copy.wait()
    for step in range(1, shards):
        peer = wires.peer(step=shards - step, shards=shards)
        source = peer[1]
        slots = exchange[step - 1]
        wires.copy(small, small_all.at[device * shards + source], slots[3], peer).wait_recv()
        wires.copy(router, router_all.at[device * shards + source], slots[4], peer).wait_recv()
        for which in range(3):
            wires.copy(place(source, which), place(source, which), slots[which], peer).wait_recv()

    each = shards * block // 2

    def rows_of(owner, half):
        return qkv_w.at[pl.ds(pl.multiple_of((owner * 2 + half) * each, each), each)]

    def small_of(owner, half):
        return small_all.at[pl.ds((owner * 2 + half) * (shards // 2), shards // 2)]

    def router_of(owner, half):
        return router_all.at[pl.ds((owner * 2 + half) * (shards // 2), shards // 2)]

    plane = Plane(
        wires,
        [rows_of, small_of, router_of],
        [
            lambda owner: qkv_w.at[pl.ds(pl.multiple_of(owner * 2 * each, 2 * each), 2 * each)],
            lambda owner: small_all.at[pl.ds(owner * shards, shards)],
            lambda owner: router_all.at[pl.ds(owner * shards, shards)],
        ],
    )
    plane.step_one()
    plane.start(plane.cores(0))
    plane.step_two()
    line.run(1)
    line.run(2)
    plane.step_three()
    for step in range(3, shards):
        line.run(step)
    plane.finish()
    for copy in sent:
        copy.wait_send()
    line.drain()


def opening_call(
    routes, order, gains, router, w_query, w_key, w_value, tokens, w_out, out_grad, experts, planes, shards
):
    block, width = w_query.shape
    rows = tokens.shape[0]
    hbm = pl.BlockSpec(memory_space=pltpu.HBM)
    vmem = pl.BlockSpec(memory_space=pltpu.VMEM)
    slots = 72
    small = (2 * experts + gains.shape[0], 128)
    return pl.pallas_call(
        functools.partial(opening_kernel, shards, experts),
        in_specs=[vmem] * 3 + [hbm] * 7,
        out_specs=[hbm] * 6,
        out_shape=(
            jax.ShapeDtypeStruct((planes * shards,) + small, gains.dtype),
            jax.ShapeDtypeStruct((planes * shards,) + router.shape, router.dtype),
            jax.ShapeDtypeStruct((planes * shards * block, 3 * width // shards), w_query.dtype),
            jax.ShapeDtypeStruct((shards * rows, width), tokens.dtype),
            jax.ShapeDtypeStruct((shards * block, width), w_out.dtype),
            jax.ShapeDtypeStruct((shards * rows, width), out_grad.dtype),
        ),
        scratch_shapes=[
            pltpu.VMEM(small, gains.dtype),
            pltpu.SemaphoreType.DMA((slots,)),
            pltpu.SemaphoreType.DMA((slots,)),
            pltpu.SemaphoreType.DMA((8,)),
        ],
        compiler_params=pltpu.CompilerParams(
            collective_id=1, has_side_effects=True, vmem_limit_bytes=4 * MIB
        ),
        cost_estimate=pl.CostEstimate(flops=0, bytes_accessed=200 * MIB, transcendentals=0),
    )(routes, order, gains, router, w_query, w_key, w_value, tokens, w_out, out_grad)


def middle_kernel(shards, mixed, out_block, mixed_all, out_w, send, recv, local):
    wires = Wires(send, recv)
    device, shard = wires.device, wires.shard
    greet(
        [wires.peer(step=step, shards=shards) for step in range(1, shards)]
        + [wires.peer(XBIT), wires.peer(YBIT), wires.peer(CORE)]
    )
    each = out_block.shape[0] // 2
    line = Relay(wires, shards, [lambda b: mixed_all.at[b]])
    line.run(0, (mixed,))
    own = [
        pltpu.make_async_copy(
            out_block,
            out_w.at[pl.ds(pl.multiple_of(device * 2 * each, 2 * each), 2 * each)],
            local.at[0],
        ),
        pltpu.make_async_copy(mixed, mixed_all.at[shard], local.at[1]),
    ]
    for copy in own:
        copy.start()
    for copy in own:
        copy.wait()
    plane = Plane(
        wires,
        [lambda owner, half: out_w.at[pl.ds(pl.multiple_of((owner * 2 + half) * each, each), each)]],
        [lambda owner: out_w.at[pl.ds(pl.multiple_of(owner * 2 * each, 2 * each), 2 * each)]],
    )
    plane.step_one()
    plane.start(plane.cores(0))
    line.run(1)
    plane.step_two()
    line.run(2)
    for step in range(3, shards):
        line.run(step)
    plane.step_three()
    plane.finish()
    line.drain()


def middle_call(mixed, out_block, planes, shards):
    hbm = pl.BlockSpec(memory_space=pltpu.HBM)
    slots = 32
    return pl.pallas_call(
        functools.partial(middle_kernel, shards),
        in_specs=[hbm] * 2,
        out_specs=[hbm] * 2,
        out_shape=(
            jax.ShapeDtypeStruct((shards,) + mixed.shape, mixed.dtype),
            jax.ShapeDtypeStruct((planes * out_block.shape[0], out_block.shape[1]), mixed.dtype),
        ),
        scratch_shapes=[
            pltpu.SemaphoreType.DMA((slots,)),
            pltpu.SemaphoreType.DMA((slots,)),
            pltpu.SemaphoreType.DMA((2,)),
        ],
        compiler_params=pltpu.CompilerParams(
            collective_id=2, has_side_effects=True, vmem_limit_bytes=4 * MIB
        ),
        cost_estimate=pl.CostEstimate(flops=0, bytes_accessed=150 * MIB, transcendentals=0),
    )(mixed, out_block)


def meeting_kernel(
    shards, normed, grad_seq, gate, up, down,
    normed_all, grad_all, wide_w, down_w, send, recv, local,
):
    wires = Wires(send, recv)
    device, shard = wires.device, wires.shard
    own, part, hidden_units = gate.shape
    each = hidden_units // shards
    half = normed.shape[0] // 2
    greet(
        [wires.peer(step=step, shards=shards) for step in range(1, shards)]
        + [wires.peer(XBIT), wires.peer(YBIT), wires.peer(CORE)]
    )

    def wide_pair(source, target):
        lanes = pl.ds(pl.multiple_of(target * each, each), each)
        pairs = []
        for which, weight in enumerate((gate, up)):
            for index in range(own):
                place = wide_w.at[source, :, pl.ds((which * own + index) * each, each)]
                pairs.append((weight.at[index, :, lanes], place))
        return pairs

    def down_pair(source, target):
        lines = pl.ds(pl.multiple_of(target * each, each), each)
        return [
            (down.at[index, lines, :], down_w.at[source, pl.ds(index * each, each), :])
            for index in range(own)
        ]

    sent, pending = [], []
    token_plane = Plane(
        wires, [lambda owner, part_of: normed_all.at[owner, pl.ds(part_of * half, half)]],
        [lambda owner: normed_all.at[owner]],
    )
    grad_plane = Plane(
        wires, [lambda owner, part_of: grad_all.at[owner, pl.ds(part_of * half, half)]],
        [lambda owner: grad_all.at[owner]],
    )
    own_copies = [
        pltpu.make_async_copy(normed, normed_all.at[device], local.at[0]),
        pltpu.make_async_copy(grad_seq, grad_all.at[device], local.at[1]),
    ]
    for index, (source, place) in enumerate(wide_pair(shard, shard) + down_pair(shard, shard)):
        own_copies.append(pltpu.make_async_copy(source, place, local.at[2 + index]))
    for copy in own_copies:
        copy.start()
    for pair in (wide_pair, down_pair):
        for step in range(1, shards):
            peer = wires.peer(step=step, shards=shards)
            back = wires.peer(step=shards - step, shards=shards)
            for (source, place), (_, mine) in zip(
                pair(shard, peer[1]), pair(back[1], shard), strict=True
            ):
                slot = wires.slot()
                copy = wires.copy(source, place, slot, peer)
                copy.start()
                sent.append(copy)
                pending.append((mine, slot, back))
    for copy in own_copies:
        copy.wait()
    token_plane.step_one()
    token_plane.start(token_plane.cores(0))
    grad_plane.start(grad_plane.cores(0))
    token_plane.step_two()
    grad_plane.step_one()
    token_plane.step_three()
    grad_plane.step_two()
    grad_plane.step_three()
    token_plane.finish()
    grad_plane.finish()
    for mine, slot, back in pending:
        wires.copy(mine, mine, slot, back).wait_recv()
    for copy in sent:
        copy.wait_send()


def meeting_call(normed, grad_seq, gate, up, down, planes, shards):
    hbm = pl.BlockSpec(memory_space=pltpu.HBM)
    own, part, hidden_units = gate.shape
    count = own * hidden_units // shards
    slots = 48
    return pl.pallas_call(
        functools.partial(meeting_kernel, shards),
        in_specs=[hbm] * 5,
        out_specs=[hbm] * 4,
        out_shape=(
            jax.ShapeDtypeStruct((planes,) + normed.shape, normed.dtype),
            jax.ShapeDtypeStruct((planes,) + grad_seq.shape, grad_seq.dtype),
            jax.ShapeDtypeStruct((shards, part, 2 * count), gate.dtype),
            jax.ShapeDtypeStruct((shards, count, part), down.dtype),
        ),
        scratch_shapes=[
            pltpu.SemaphoreType.DMA((slots,)),
            pltpu.SemaphoreType.DMA((slots,)),
            pltpu.SemaphoreType.DMA((2 + 3 * own,)),
        ],
        compiler_params=pltpu.CompilerParams(
            collective_id=3, has_side_effects=True, vmem_limit_bytes=4 * MIB
        ),
        cost_estimate=pl.CostEstimate(flops=0, bytes_accessed=300 * MIB, transcendentals=0),
    )(normed, grad_seq, gate, up, down)


def add_rows(target, sources, lines):
    rows = target.shape[0]

    def body(index, carry):
        span = pl.ds(pl.multiple_of(index * lines, lines), lines)
        total = target[span, :].astype(jnp.float32)
        for source in sources:
            total = total + source[span, :].astype(jnp.float32)
        target[span, :] = total.astype(target.dtype)
        return carry

    lax.fori_loop(0, rows // lines, body, 0)


class PlaneSum:
    def __init__(self, wires, part, held, came, diag, side, local, base):
        self.wires, self.part, self.local, self.base = wires, part, local, base
        self.held, self.came, self.diag, self.side = held, came, diag, side
        self.half = held.shape[1] // 2
        self.core = [wires.slot() for _ in range(4)]
        self.corner = [wires.slot() for _ in range(2)]
        self.edge = [wires.slot() for _ in range(2)]
        self.sent = []

    def start(self, copy):
        copy.start()
        self.sent.append(copy)

    def load(self, chip):
        return pltpu.make_async_copy(
            self.part(chip, 0), self.held.at[chip], self.local.at[self.base + chip]
        )

    def begin(self):
        for chip in (3, 1, 2, 0):
            self.load(chip).start()
            self.start(
                self.wires.copy(
                    self.part(chip, 1), self.came.at[chip], self.core[chip], self.wires.peer(CORE)
                )
            )

    def add_core(self, chip):
        self.load(chip).wait()
        place = self.came.at[chip]
        self.wires.copy(place, place, self.core[chip], self.wires.peer(CORE)).wait_recv()
        add_rows(self.held.at[chip], [place], 64)

    def part_of_corner(self, which):
        return self.held.at[3, pl.ds(which * self.half, self.half)]

    def send_corner(self):
        self.add_core(3)
        for which, bits in enumerate((XBIT, YBIT)):
            self.start(
                self.wires.copy(
                    self.part_of_corner(which),
                    self.diag.at[which],
                    self.corner[which],
                    self.wires.peer(bits),
                )
            )

    def add_cores(self):
        for chip in (1, 2, 0):
            self.add_core(chip)

    def send_sides(self):
        for which, (bits, chip) in enumerate(((XBIT, 2), (YBIT, 1))):
            place = self.diag.at[which]
            self.wires.copy(place, place, self.corner[which], self.wires.peer(bits)).wait_recv()
            add_rows(self.held.at[chip, pl.ds(which * self.half, self.half)], [place], 64)
            self.start(
                self.wires.copy(
                    self.held.at[chip],
                    self.side.at[1 - which],
                    self.edge[1 - which],
                    self.wires.peer((XBIT | YBIT) ^ bits),
                )
            )

    def end(self):
        for which, bits in enumerate((XBIT, YBIT)):
            place = self.side.at[which]
            self.wires.copy(place, place, self.edge[which], self.wires.peer(bits)).wait_recv()
        add_rows(self.held.at[0], [self.side.at[0], self.side.at[1]], 64)

    def drain(self):
        for copy in self.sent:
            copy.wait_send()


class LineSum:
    def __init__(self, wires, shards, source, landing):
        self.wires, self.shards, self.source, self.landing = wires, shards, source, landing
        self.slots = [wires.slot() for _ in range(shards - 1)]
        self.sent = []

    def begin(self):
        wires = self.wires
        for step in range(1, self.shards):
            peer = wires.peer(step=step, shards=self.shards)
            copy = wires.copy(
                self.source(peer[1]), self.landing(wires.shard), self.slots[step - 1], peer
            )
            copy.start()
            self.sent.append(copy)

    def arrive(self):
        wires = self.wires
        for step in range(1, self.shards):
            peer = wires.peer(step=self.shards - step, shards=self.shards)
            place = self.landing(peer[1])
            wires.copy(place, place, self.slots[step - 1], peer).wait_recv()

    def drain(self):
        for copy in self.sent:
            copy.wait_send()


def line_total(landing, shards):
    total = landing[0].astype(jnp.float32)
    for shard in range(1, shards):
        total = total + landing[shard].astype(jnp.float32)
    return total


def aligned(index, size):
    return pl.ds(pl.multiple_of(index * size, size), size)


def returning_kernel(
    shards, ins, outs, wide,
    in_total, out_total, wide_all,
    held, came, diag, side, held2, came2, diag2, side2, landing, send, recv, local,
):
    wires = Wires(send, recv)
    device, shard = wires.device, wires.shard
    rows = in_total.shape[0]
    greet(
        [wires.peer(step=step, shards=shards) for step in range(1, shards)]
        + [wires.peer(XBIT), wires.peer(YBIT), wires.peer(CORE)]
    )

    def rel(source):
        return lambda chip, core: source.at[device ^ (2 * chip + core)]

    grads = PlaneSum(wires, rel(ins), held, came, diag, side, local, 0)
    values = PlaneSum(wires, rel(outs), held2, came2, diag2, side2, local, 4)
    weights = LineSum(wires, shards, lambda t: wide.at[t], lambda s: wide_all.at[s])
    line = LineSum(
        wires, shards, lambda t: held.at[0, aligned(t, rows)], lambda s: landing.at[s]
    )
    grads.begin()
    weights.begin()
    own = pltpu.make_async_copy(wide.at[shard], wide_all.at[shard], local.at[8])
    own.start()
    grads.send_corner()
    values.begin()
    grads.add_cores()
    grads.send_sides()
    values.send_corner()
    values.add_cores()
    grads.end()
    line.begin()
    values.send_sides()
    landing[shard] = held[0, aligned(shard, rows), :]
    line.arrive()
    in_total[...] = line_total(landing, shards)
    values.end()
    back = pltpu.make_async_copy(held2.at[0], out_total, local.at[9])
    back.start()
    weights.arrive()
    own.wait()
    back.wait()
    for group in (grads, values, weights, line):
        group.drain()


def returning_call(ins, outs, wide, shards):
    _, seq, width = ins.shape
    rows = seq // shards
    hbm = pl.BlockSpec(memory_space=pltpu.HBM)
    vmem = pl.BlockSpec(memory_space=pltpu.VMEM)
    low = jnp.bfloat16
    work = [
        pltpu.VMEM((4, seq, width), low),
        pltpu.VMEM((4, seq, width), low),
        pltpu.VMEM((2, seq // 2, width), low),
        pltpu.VMEM((2, seq, width), low),
    ]
    return pl.pallas_call(
        functools.partial(returning_kernel, shards),
        in_specs=[hbm] * 3,
        out_specs=[vmem, hbm, hbm],
        out_shape=(
            jax.ShapeDtypeStruct((rows, width), jnp.float32),
            jax.ShapeDtypeStruct((seq, width), low),
            jax.ShapeDtypeStruct(wide.shape, wide.dtype),
        ),
        scratch_shapes=work
        + work
        + [
            pltpu.VMEM((shards, rows, width), low),
            pltpu.SemaphoreType.DMA((32,)),
            pltpu.SemaphoreType.DMA((32,)),
            pltpu.SemaphoreType.DMA((10,)),
        ],
        compiler_params=pltpu.CompilerParams(
            collective_id=4, has_side_effects=True, vmem_limit_bytes=58 * MIB
        ),
        cost_estimate=pl.CostEstimate(flops=0, bytes_accessed=300 * MIB, transcendentals=0),
    )(ins, outs, wide)


def turn_back_kernel(
    shards, hidden, grad, out_grad, gain, weight,
    hidden_grad_out, low_out, gain_grad_out, message_all, message, send, recv, local,
):
    wires = Wires(send, recv)
    part = message.shape[2]
    greet([wires.peer(step=step, shards=shards) for step in range(1, shards)])
    factor = norm_factor(hidden[...])
    gain_grad_out[...] = jnp.sum(grad[...] * hidden[...] * factor, axis=0, keepdims=True)
    scaled = grad[...] * gain[...]
    inner = jnp.mean(scaled * hidden[...], axis=-1, keepdims=True)
    total = out_grad[...].astype(jnp.float32) + factor * scaled
    total = total - hidden[...] * (factor * factor * factor) * inner
    hidden_grad_out[...] = total
    low = total.astype(jnp.bfloat16)
    low_out[...] = low
    for shard in range(shards):
        message[shard] = nt_dot(low, weight[pl.ds(shard * part, part), :]).astype(jnp.bfloat16)
    line = LineSum(wires, shards, lambda t: message.at[t], lambda s: message_all.at[s])
    line.begin()
    own = pltpu.make_async_copy(message.at[wires.shard], message_all.at[wires.shard], local.at[0])
    own.start()
    own.wait()
    line.arrive()
    line.drain()


def turn_back_call(hidden, grad, out_grad, gain, weight, shards):
    rows, width = hidden.shape
    part = width // shards
    vmem = pl.BlockSpec(memory_space=pltpu.VMEM)
    return pl.pallas_call(
        functools.partial(turn_back_kernel, shards),
        in_specs=[vmem] * 5,
        out_specs=[vmem] * 3 + [pl.BlockSpec(memory_space=pltpu.HBM)],
        out_shape=(
            jax.ShapeDtypeStruct((rows, width), jnp.float32),
            jax.ShapeDtypeStruct((rows, width), jnp.bfloat16),
            jax.ShapeDtypeStruct((1, width), jnp.float32),
            jax.ShapeDtypeStruct((shards, rows, part), jnp.bfloat16),
        ),
        scratch_shapes=[
            pltpu.VMEM((shards, rows, part), jnp.bfloat16),
            pltpu.SemaphoreType.DMA((4,)),
            pltpu.SemaphoreType.DMA((4,)),
            pltpu.SemaphoreType.DMA((1,)),
        ],
        compiler_params=pltpu.CompilerParams(
            collective_id=5, has_side_effects=True, vmem_limit_bytes=40 * MIB
        ),
        cost_estimate=pl.CostEstimate(
            flops=2 * rows * width * width, bytes_accessed=40 * MIB, transcendentals=0
        ),
    )(hidden, grad, out_grad, gain, weight)


def closing_kernel(
    shards, planes, normed_grad, out_total, qkv_grad, out_grad, tokens, hidden_grad, hidden, gain, router, vectors,
    input_grad, mixed_out, query_out, key_out, value_out, weight_out, gain_out, router_out, vectors_out,
    held, came, diag, side, held2, came2, diag2, side2,
    norm_land, out_land, qkv_land, weight_land, gain_mine, gain_land, gain_line, router_land, router_sum, router_line,
    vector_land, vector_sum, vector_line, send, recv, local,
):
    wires = Wires(send, recv)
    device, shard = wires.device, wires.shard
    rows, width = tokens.shape
    block = query_out.shape[0]
    part = width // shards
    lines = router_out.shape[0]
    line_peers = [wires.peer(step=step, shards=shards) for step in range(1, shards)]
    plane_peers = [wires.peer(bits) for bits in range(1, planes)]
    greet(line_peers + plane_peers)

    def rel(source):
        return lambda chip, core: source.at[device ^ (2 * chip + core)]

    norms = LineSum(wires, shards, lambda t: normed_grad.at[t], lambda s: norm_land.at[s])
    values = LineSum(
        wires, shards, lambda t: out_total.at[aligned(t, rows)], lambda s: out_land.at[s]
    )
    qkv = PlaneSum(wires, rel(qkv_grad), held, came, diag, side, local, 0)
    weight = PlaneSum(wires, rel(out_grad), held2, came2, diag2, side2, local, 4)
    qkv_line = LineSum(
        wires, shards, lambda t: held.at[0, aligned(t, block)], lambda s: qkv_land.at[s]
    )
    weight_line = LineSum(
        wires, shards, lambda t: held2.at[0, aligned(t, block)], lambda s: weight_land.at[s]
    )
    norms.begin()
    own_norm = pltpu.make_async_copy(normed_grad.at[shard], norm_land.at[shard], local.at[8])
    own_norm.start()
    own_value = pltpu.make_async_copy(
        out_total.at[aligned(shard, rows)], out_land.at[shard], local.at[9]
    )
    own_value.start()
    sent = []

    def spread(slots, source, landing):
        for bits in range(1, planes):
            copy = wires.copy(
                source(device ^ bits), landing.at[device], slots[bits - 1], wires.peer(bits)
            )
            copy.start()
            sent.append(copy)

    def collect(slots, landing):
        for bits in range(1, planes):
            place = landing.at[device ^ bits]
            wires.copy(place, place, slots[bits - 1], wires.peer(bits)).wait_recv()
        total = landing[0]
        for other in range(1, planes):
            total = total + landing[other]
        return total

    router_slots = [wires.slot() for _ in range(1, planes)]
    vector_slots = [wires.slot() for _ in range(1, planes)]
    gain_slots = [wires.slot() for _ in range(1, planes)]
    spread(router_slots, lambda e: router.at[aligned(e, shards * lines)], router_land)
    spread(vector_slots, lambda e: vectors, vector_land)
    qkv.begin()
    weight.begin()
    qkv.send_corner()
    qkv.add_cores()
    weight.send_corner()
    router_land[device] = router[aligned(device, shards * lines), :]
    vector_land[device] = vectors[...]
    router_sum[...] = collect(router_slots, router_land)
    vector_sum[...] = collect(vector_slots, vector_land)
    router_pass = LineSum(
        wires, shards, lambda t: router_sum.at[aligned(t, lines)], lambda s: router_line.at[s]
    )
    vector_pass = LineSum(wires, shards, lambda t: vector_sum, lambda s: vector_line.at[s])
    router_pass.begin()
    vector_pass.begin()
    qkv.send_sides()
    weight.add_cores()
    own_norm.wait()
    norms.arrive()
    values.begin()
    grad = line_total(norm_land, shards)
    given = tokens[...].astype(jnp.float32)
    factor = norm_factor(given)
    gain_mine[...] = jnp.sum(grad * given * factor, axis=0, keepdims=True)
    spread(gain_slots, lambda e: gain_mine, gain_land)
    scaled = grad * gain[...]
    inner = jnp.mean(scaled * given, axis=-1, keepdims=True)
    total = hidden_grad[...] + factor * scaled - given * (factor * factor * factor) * inner
    input_grad[...] = total.astype(jnp.bfloat16)
    qkv.end()
    qkv_line.begin()
    weight.send_sides()
    gain_land[device] = gain_mine[...]
    gain_mine2 = collect(gain_slots, gain_land)
    gain_line[shard] = gain_mine2
    gain_pass = LineSum(wires, shards, lambda t: gain_line.at[shard], lambda s: gain_line.at[s])
    gain_pass.begin()
    weight.end()
    weight_line.begin()
    router_line[shard] = router_sum[aligned(shard, lines), :]
    vector_line[shard] = vector_sum[...]
    router_pass.arrive()
    router_out[...] = line_total(router_line, shards)
    vector_pass.arrive()
    vectors_out[...] = line_total(vector_line, shards)
    own_value.wait()
    values.arrive()
    mixed_out[...] = (hidden[...] + line_total(out_land, shards)).astype(jnp.bfloat16)
    qkv_land[shard] = held[0, aligned(shard, block), :]
    qkv_line.arrive()
    for source in range(shards):
        for which, result in enumerate((query_out, key_out, value_out)):
            result[:, pl.ds(source * part, part)] = qkv_land[
                source, :, pl.ds(which * part, part)
            ].astype(jnp.float32)
    gain_pass.arrive()
    gain_out[...] = line_total(gain_line, shards)
    weight_land[shard] = held2[0, aligned(shard, block), :]
    weight_line.arrive()
    weight_out[...] = line_total(weight_land, shards)
    for copy in sent:
        copy.wait_send()
    groups = (norms, values, qkv, weight, qkv_line, weight_line, router_pass, vector_pass)
    for group in groups + (gain_pass,):
        group.drain()


def closing_call(
    normed_grad, out_total, qkv_grad, out_grad, tokens, hidden_grad, hidden, gain, router, vectors
):
    shards, rows, width = normed_grad.shape
    planes, each, lanes = qkv_grad.shape
    block = each // shards
    lines = router.shape[0] // (planes * shards)
    hbm = pl.BlockSpec(memory_space=pltpu.HBM)
    vmem = pl.BlockSpec(memory_space=pltpu.VMEM)
    low, full = jnp.bfloat16, jnp.float32

    def work(wide):
        return [
            pltpu.VMEM((4, each, wide), low),
            pltpu.VMEM((4, each, wide), low),
            pltpu.VMEM((2, each // 2, wide), low),
            pltpu.VMEM((2, each, wide), low),
        ]

    weight_shape = jax.ShapeDtypeStruct((block, width), full)
    return pl.pallas_call(
        functools.partial(closing_kernel, shards, planes),
        in_specs=[hbm] * 4 + [vmem] * 6,
        out_specs=[vmem] * 9,
        out_shape=(
            jax.ShapeDtypeStruct((rows, width), low),
            jax.ShapeDtypeStruct((rows, width), low),
            weight_shape,
            weight_shape,
            weight_shape,
            weight_shape,
            jax.ShapeDtypeStruct((1, width), full),
            jax.ShapeDtypeStruct((lines, 128), full),
            jax.ShapeDtypeStruct(vectors.shape, full),
        ),
        scratch_shapes=work(lanes)
        + work(width)
        + [
            pltpu.VMEM((shards, rows, width), low),
            pltpu.VMEM((shards, rows, width), low),
            pltpu.VMEM((shards, block, lanes), low),
            pltpu.VMEM((shards, block, width), low),
            pltpu.VMEM((1, width), full),
            pltpu.VMEM((planes, 1, width), full),
            pltpu.VMEM((shards, 1, width), full),
            pltpu.VMEM((planes, shards * lines, 128), full),
            pltpu.VMEM((shards * lines, 128), full),
            pltpu.VMEM((shards, lines, 128), full),
            pltpu.VMEM((planes,) + vectors.shape, full),
            pltpu.VMEM(vectors.shape, full),
            pltpu.VMEM((shards,) + vectors.shape, full),
            pltpu.SemaphoreType.DMA((72,)),
            pltpu.SemaphoreType.DMA((72,)),
            pltpu.SemaphoreType.DMA((10,)),
        ],
        compiler_params=pltpu.CompilerParams(
            collective_id=6, has_side_effects=True, vmem_limit_bytes=58 * MIB
        ),
        cost_estimate=pl.CostEstimate(flops=0, bytes_accessed=300 * MIB, transcendentals=0),
    )(normed_grad, out_total, qkv_grad, out_grad, tokens, hidden_grad, hidden, gain, router, vectors)


LOW = jnp.bfloat16
WIDE = jnp.float32


def swap(value, bits):
    count = lax.axis_size(EXPERT)
    return lax.ppermute(value, EXPERT, [(i, i ^ bits) for i in range(count)])


def shard_exchange(pieces, shard):
    size = lax.axis_size(SHARD)
    result = pieces
    for step in range(1, size):
        target = (shard + step) % size
        sent = lax.dynamic_index_in_dim(pieces, target, 0, keepdims=True)
        got = lax.ppermute(sent, SHARD, [(i, (i + step) % size) for i in range(size)])
        result = lax.dynamic_update_slice_in_dim(result, got, (shard - step) % size, 0)
    return result


def fast_local(
    tokens,
    segment_ids,
    routes,
    pair_order,
    attn_gain,
    w_query,
    w_key,
    w_value,
    query_gain,
    key_gain,
    w_out,
    ffn_gain,
    w_router,
    w_gate,
    w_up,
    w_down,
    out_grad,
):
    rows, width = tokens.shape
    top_count = routes.shape[1]
    planes = lax.axis_size(EXPERT)
    shards = lax.axis_size(SHARD)
    own_experts = w_gate.shape[0]
    experts = own_experts * planes
    capacity = 5 * rows * top_count // (4 * own_experts)
    seq = segment_ids.shape[0]
    device = lax.axis_index(EXPERT)
    shard = lax.axis_index(SHARD)
    part = width // shards

    gains = jnp.concatenate([attn_gain, ffn_gain, query_gain, key_gain])
    gains = jnp.pad(gains, (0, -gains.size % (16 * 128))).reshape(-1, 128)
    router_pad = jnp.pad(w_router, ((0, 0), (0, 128 - experts)))
    small, router_w, qkv_w, tokens_seq, out_block, grad_seq = opening_call(
        routes,
        pair_order.reshape(rows, top_count),
        gains,
        router_pad,
        w_query,
        w_key,
        w_value,
        tokens,
        w_out,
        out_grad,
        experts,
        planes,
        shards,
    )
    router_w = router_w.reshape(width, 128)
    gains = small[:, 2 * experts :].reshape(planes * shards, -1).astype(WIDE)
    fields, at = [], 0
    for size in (attn_gain.size, ffn_gain.size, query_gain.size, key_gain.size):
        fields.append(gains[:, at : at + size].reshape(1, -1))
        at += size
    attn_row, ffn_row, query_row, key_row = fields
    digits = [
        lax.dynamic_slice_in_dim(small, start + device * own_experts, own_experts, 1)
        for start in (0, experts)
    ]
    high, low_digit = [value.transpose(1, 0, 2) for value in digits]
    most = planes * shards * rows * top_count
    kept = keep_call(high, low_digit, capacity, most, planes, shards)

    tables = turn_tables(seq)
    seg_row, seg_col = segment_ids.reshape(1, seq), segment_ids.reshape(seq, 1)
    normed_low, raw, low, mixed_own, total = attend_call(
        tokens_seq, attn_row, qkv_w, query_row, key_row, tables, seg_row, seg_col
    )
    mixed, out_w = middle_call(mixed_own, out_block, planes, shards)
    hidden_seq, normed_seq = join_call(mixed, out_w, tokens_seq, ffn_row)

    token_all, grad_all, wide_w, down_w = meeting_call(
        normed_seq, grad_seq, w_gate, w_up, w_down, planes, shards
    )
    wide_w = wide_w.reshape(width, -1)
    own_ids = device * own_experts + jnp.arange(own_experts, dtype=jnp.int32)
    own_hot = (own_ids[:, None] == jnp.arange(128, dtype=jnp.int32)[None, :]).astype(WIDE)
    out_parts, in_parts, wide_message, router_grad, down_message = expert_call(
        token_all, grad_all, kept, wide_w, router_w, down_w, own_hot, experts
    )
    normed_two_grad, out_total, wide_pieces = returning_call(
        in_parts, out_parts, wide_message.reshape(shards, part, -1), shards
    )
    hidden = lax.dynamic_slice_in_dim(hidden_seq, shard * rows, rows)

    hidden_grad, attn_low, ffn_scale_grad, mixed_grad = turn_back_call(
        hidden, normed_two_grad, out_grad, ffn_row, out_w, shards
    )
    mixed_grad = mixed_grad.reshape(seq, part)
    down_message, _ = lax.optimization_barrier((down_message, mixed_grad))
    down_pieces = shard_exchange(down_message, shard)
    qkv_grad, normed_grad, query_scale_grad, key_scale_grad = attend_back_call(
        mixed_grad, raw, low, total, qkv_w, query_row, key_row, tables, seg_row, seg_col
    )
    normed_grad = normed_grad.reshape(shards, rows, width)

    qkv_w_grad = matmul_tn(normed_low, qkv_grad).astype(LOW).reshape(planes, -1, 3 * part)
    own_mixed = lax.dynamic_slice_in_dim(mixed, shard * rows, rows, 1)
    own_mixed = own_mixed.transpose(1, 0, 2).reshape(rows, width)
    out_w_grad = matmul_tn(own_mixed, attn_low).astype(LOW).reshape(planes, -1, width)
    router_table = router_grad[:, :experts].reshape(-1, 128)
    vectors = jnp.concatenate(
        [ffn_scale_grad.reshape(-1, 128), query_scale_grad, key_scale_grad], axis=0
    )
    vectors = jnp.pad(vectors, ((0, -vectors.shape[0] % 8), (0, 0)))
    closed = closing_call(
        normed_grad,
        out_total,
        qkv_w_grad,
        out_w_grad,
        tokens,
        hidden_grad,
        hidden,
        attn_row,
        router_table,
        vectors,
    )
    input_grad, mixed_out, query_w_grad, key_w_grad, value_w_grad, out_w_grad = closed[:6]
    attn_scale_grad, router_out, vectors = closed[6:]
    gate_grad, up_grad, down_grad = unpack_units(wide_pieces, down_pieces, own_experts)
    index = device * shards + shard
    flat = vectors.reshape(-1)

    def own_piece(values, start, size):
        return lax.dynamic_slice_in_dim(values, start + index * size, size)

    return (
        mixed_out,
        input_grad,
        own_piece(attn_scale_grad.reshape(-1), 0, attn_gain.size),
        query_w_grad,
        key_w_grad,
        value_w_grad,
        own_piece(flat, width, query_gain.size),
        own_piece(flat, width + HD, key_gain.size),
        out_w_grad,
        own_piece(flat, 0, ffn_gain.size),
        router_out.reshape(-1, experts),
        gate_grad,
        up_grad,
        down_grad,
    )


def solution(mesh):
    local = fast_local if mesh.shape[EXPERT] == 8 else general_local
    return jax.shard_map(
        local,
        mesh=mesh,
        in_specs=(
            P(BOTH, None),
            P(EXPERT),
            P(BOTH, None),
            P(BOTH),
            P(BOTH),
            P(BOTH, None),
            P(BOTH, None),
            P(BOTH, None),
            P(BOTH),
            P(BOTH),
            P(BOTH, None),
            P(BOTH),
            P(BOTH, None),
            P(EXPERT, SHARD, None),
            P(EXPERT, SHARD, None),
            P(EXPERT, None, SHARD),
            P(BOTH, None),
        ),
        out_specs=(
            P(BOTH, None),
            P(BOTH, None),
            P(BOTH),
            P(BOTH, None),
            P(BOTH, None),
            P(BOTH, None),
            P(BOTH),
            P(BOTH),
            P(BOTH, None),
            P(BOTH),
            P(BOTH, None),
            P(EXPERT, SHARD, None),
            P(EXPERT, SHARD, None),
            P(EXPERT, None, SHARD),
        ),
        check_vma=False,
    )
```

```python
import functools

import jax
import jax.numpy as jnp
import numpy as np
from jax import lax
from jax.experimental import pallas as pl
from jax.experimental.pallas import tpu as pltpu
from jax.sharding import PartitionSpec as P

HEADS = 16
HD = 128


EXPERT = "expert"
SHARD = "wshard"
BOTH = (EXPERT, SHARD)

SUM_QHD_KHD_HQK = "qhd,khd->hqk"
SUM_HQK_KHD_QHD = "hqk,khd->qhd"
SUM_ECD_EDF_ECF = "ecd,edf->ecf"
SUM_ECF_EFD_ECD = "ecf,efd->ecd"
SUM_TK_TKD_TD = "tk,tkd->td"
SUM_TD_TKD_TK = "td,tkd->tk"
SUM_ECD_EFD_ECF = "ecd,efd->ecf"
SUM_ECF_ECD_EFD = "ecf,ecd->efd"
SUM_ECD_ECF_EDF = "ecd,ecf->edf"
SUM_ECF_EDF_ECD = "ecf,edf->ecd"
SUM_HQK_QHD_KHD = "hqk,qhd->khd"
EPSILON = 1e-06
THETA = 10000.0


def matmul(left, right):
    return jnp.dot(left, right, preferred_element_type=jnp.float32)


def matmul_tn(left, right):
    return lax.dot_general(
        left, right, (((0,), (0,)), ((), ())), preferred_element_type=jnp.float32
    )


def matmul_nt(left, right):
    return lax.dot_general(
        left, right, (((1,), (1,)), ((), ())), preferred_element_type=jnp.float32
    )


def rms_scale(values, scale_gain):
    factor = lax.rsqrt(jnp.mean(values * values, axis=-1, keepdims=True) + EPSILON)
    return values * factor * scale_gain


def rope_tables(positions):
    exponent = jnp.arange(HD // 2, dtype=jnp.float32) * (2.0 / HD)
    frequency = jnp.power(jnp.float32(THETA), -exponent)
    angles = positions.astype(jnp.float32)[:, None] * frequency[None, :]
    return (jnp.cos(angles), jnp.sin(angles))


def rotate(values, cosine, sine):
    first_half = values[..., : HD // 2]
    second_half = values[..., HD // 2 :]
    cos_part = cosine[:, None, :]
    sin_part = sine[:, None, :]
    return jnp.concatenate(
        [
            first_half * cos_part - second_half * sin_part,
            second_half * cos_part + first_half * sin_part,
        ],
        axis=-1,
    )


def padded_rows(rows):
    return jnp.concatenate([jnp.zeros((1,) + rows.shape[1:], rows.dtype), rows], axis=0)


def masked_scores(query_rot, key_rot, query_segment, key_segment):
    scores = jnp.einsum(SUM_QHD_KHD_HQK, query_rot, key_rot, preferred_element_type=jnp.float32)
    allowed = query_segment[:, None] == key_segment[None, :]
    return jnp.where(allowed[None], scores, -1e30)


def swiglu_fn(gate_in, up_in):
    return jax.nn.silu(gate_in) * up_in


def general_local(
    tokens,
    segment_ids,
    routes,
    pair_order,
    attn_gain,
    w_query,
    w_key,
    w_value,
    query_gain,
    key_gain,
    w_out,
    ffn_gain,
    w_router,
    w_gate,
    w_up,
    w_down,
    out_grad,
):
    tok_rows, width = tokens.shape
    top_count = routes.shape[1]
    expert_devs = lax.axis_size(EXPERT)
    shard_devs = lax.axis_size(SHARD)
    local_experts = w_gate.shape[0]
    expert_count = local_experts * expert_devs
    most_rows = 2 * tok_rows * top_count // expert_count
    capacity = 5 * tok_rows * top_count // (4 * local_experts)
    seq_length = segment_ids.shape[0]
    device_expert = lax.axis_index(EXPERT)
    device_shard = lax.axis_index(SHARD)
    low_type = jnp.bfloat16
    wide_type = jnp.float32
    gathered = (
        lax.all_gather(attn_gain, BOTH, axis=0, tiled=True),
        lax.all_gather(w_query, BOTH, axis=0, tiled=True),
        lax.all_gather(w_key, BOTH, axis=0, tiled=True),
        lax.all_gather(w_value, BOTH, axis=0, tiled=True),
        lax.all_gather(query_gain, BOTH, axis=0, tiled=True),
        lax.all_gather(key_gain, BOTH, axis=0, tiled=True),
        lax.all_gather(w_out, BOTH, axis=0, tiled=True),
        lax.all_gather(ffn_gain, BOTH, axis=0, tiled=True),
        lax.all_gather(w_router, BOTH, axis=0, tiled=True),
    )
    attn_scale = gathered[0].astype(wide_type)
    query_w, key_w, value_w = (gathered[1], gathered[2], gathered[3])
    query_scale = gathered[4].astype(wide_type)
    key_scale = gathered[5].astype(wide_type)
    out_w = gathered[6]
    ffn_scale = gathered[7].astype(wide_type)
    router_w = gathered[8]
    inputs = tokens.astype(wide_type)
    normed, norm_one_pull = jax.vjp(rms_scale, inputs, attn_scale)
    normed_low = normed.astype(low_type)
    query_raw = matmul(normed_low, query_w)
    key_raw = matmul(normed_low, key_w)
    value_low = matmul(normed_low, value_w).astype(low_type)
    positions = device_shard * tok_rows + jnp.arange(tok_rows, dtype=jnp.int32)
    cosine, sine = rope_tables(positions)

    def prepare(query_in, key_in, query_g, key_g):
        query_heads = rms_scale(query_in.reshape(tok_rows, HEADS, HD), query_g)
        key_heads = rms_scale(key_in.reshape(tok_rows, HEADS, HD), key_g)
        return (rotate(query_heads, cosine, sine) * HD ** (-0.5), rotate(key_heads, cosine, sine))

    rotated, prepare_pull = jax.vjp(prepare, query_raw, key_raw, query_scale, key_scale)
    query_low = rotated[0].astype(low_type)
    key_low = rotated[1].astype(low_type).reshape(tok_rows, width)
    seq_keys, seq_values = (
        lax.all_gather(key_low, SHARD, axis=0, tiled=True),
        lax.all_gather(value_low, SHARD, axis=0, tiled=True),
    )
    query_segment = lax.dynamic_slice_in_dim(segment_ids, device_shard * tok_rows, tok_rows)
    scores = masked_scores(
        query_low, seq_keys.reshape(seq_length, HEADS, HD), query_segment, segment_ids
    )
    row_max = jnp.max(scores, axis=-1, keepdims=True)
    shifted = jnp.exp(scores - row_max)
    totals = jnp.sum(shifted, axis=-1, keepdims=True)
    log_total = row_max + jnp.log(totals)
    probs_low = (shifted / totals).astype(low_type)
    mixed = jnp.einsum(
        SUM_HQK_KHD_QHD,
        probs_low,
        seq_values.reshape(seq_length, HEADS, HD),
        preferred_element_type=wide_type,
    )
    mixed_low = mixed.reshape(tok_rows, width).astype(low_type)
    hidden = inputs + matmul(mixed_low, out_w)
    normed_two, norm_two_pull = jax.vjp(rms_scale, hidden, ffn_scale)
    normed_two_low = normed_two.astype(low_type)
    logits = matmul(normed_two_low, router_w)

    def router_weights(logit_values):
        return jnp.take_along_axis(jax.nn.softmax(logit_values, axis=-1), routes, axis=1)

    route_weight, route_pull = jax.vjp(router_weights, logits)
    group_routes, group_order = (
        lax.all_gather(routes, EXPERT, axis=0, tiled=True),
        lax.all_gather(pair_order, EXPERT, axis=0, tiled=True),
    )
    per_source = tok_rows * top_count
    group_pairs = per_source * expert_devs
    expert_of = group_routes.reshape(-1)
    pair_index = jnp.arange(group_pairs, dtype=jnp.int32)
    source_of = pair_index // per_source
    expert_ids = jnp.arange(expert_count, dtype=jnp.int32)
    onehot = (expert_of.reshape(expert_devs, per_source, 1) == expert_ids).astype(jnp.int32)
    position_of = (jnp.sum(jnp.cumsum(onehot, axis=1) * onehot, axis=-1) - 1).reshape(-1)
    order_span = group_pairs * shard_devs
    sort_keys = expert_of * order_span + group_order
    sorted_pairs = jnp.argsort(sort_keys)
    placement = jnp.zeros((group_pairs,), jnp.int32).at[sorted_pairs].set(pair_index)
    expert_counts = jnp.sum(onehot, axis=(0, 1))
    expert_start = jnp.cumsum(expert_counts) - expert_counts
    start_of = jnp.sum(onehot.reshape(group_pairs, expert_count) * expert_start[None, :], axis=-1)
    slot_rank = placement - start_of
    retained = slot_rank < capacity
    own_expert = routes.reshape(-1)
    own_position = lax.dynamic_slice_in_dim(position_of, device_expert * per_source, per_source)
    send_slot = own_expert * most_rows + own_position
    send_pair = (
        jnp.zeros((expert_count * most_rows,), jnp.int32)
        .at[send_slot]
        .set(jnp.arange(per_source, dtype=jnp.int32) + 1)
    )
    send_token = jnp.where(send_pair > 0, (send_pair - 1) // top_count + 1, 0)
    owner_local = expert_of % local_experts
    is_mine = expert_of // local_experts == device_expert
    recv_row = source_of * (local_experts * most_rows) + owner_local * most_rows + position_of
    slot_target = jnp.where(
        is_mine & retained, owner_local * capacity + slot_rank, local_experts * capacity
    )
    slot_source = (
        jnp.zeros((local_experts * capacity,), jnp.int32)
        .at[slot_target]
        .set(recv_row + 1, mode="drop")
    )
    back_room = expert_devs * local_experts * most_rows
    back_target = jnp.where(is_mine, recv_row, back_room)
    back_source = (
        jnp.zeros((back_room,), jnp.int32)
        .at[back_target]
        .set(jnp.where(retained, owner_local * capacity + slot_rank + 1, 0), mode="drop")
    )
    send_rows = padded_rows(normed_two_low)[send_token].reshape(
        expert_devs, local_experts * most_rows, width
    )
    recv_rows = lax.all_to_all(
        send_rows, EXPERT, split_axis=0, concat_axis=0, tiled=True
    ).reshape(-1, width)
    slot_rows = padded_rows(recv_rows)[slot_source].reshape(local_experts, capacity, width)
    full_gate, full_up, full_down = (
        lax.all_gather(w_gate, SHARD, axis=1, tiled=True),
        lax.all_gather(w_up, SHARD, axis=1, tiled=True),
        lax.all_gather(w_down, SHARD, axis=2, tiled=True),
    )
    gate_act = jnp.einsum(SUM_ECD_EDF_ECF, slot_rows, full_gate, preferred_element_type=wide_type)
    up_act = jnp.einsum(SUM_ECD_EDF_ECF, slot_rows, full_up, preferred_element_type=wide_type)
    swiglu_out, swiglu_pull = jax.vjp(swiglu_fn, gate_act, up_act)
    swiglu_low = swiglu_out.astype(low_type)
    expert_out = jnp.einsum(
        SUM_ECF_EFD_ECD, swiglu_low, full_down, preferred_element_type=wide_type
    ).astype(low_type)
    back_rows = padded_rows(expert_out.reshape(-1, width))[back_source].reshape(
        expert_devs, local_experts * most_rows, width
    )
    returned = lax.all_to_all(back_rows, EXPERT, split_axis=0, concat_axis=0, tiled=True).reshape(
        -1, width
    )
    pair_rows = returned[send_slot].reshape(tok_rows, top_count, width)
    combined = jnp.einsum(SUM_TK_TKD_TD, route_weight, pair_rows, preferred_element_type=wide_type)
    mixed_out = (hidden + combined).astype(low_type)
    result_grad = out_grad.astype(wide_type)
    weight_grad = jnp.einsum(SUM_TD_TKD_TK, result_grad, pair_rows, preferred_element_type=wide_type)
    pair_grad = (
        (route_weight[:, :, None] * result_grad[:, None, :])
        .astype(low_type)
        .reshape(per_source, width)
    )
    send_grad = padded_rows(pair_grad)[send_pair].reshape(
        expert_devs, local_experts * most_rows, width
    )
    recv_grad = lax.all_to_all(
        send_grad, EXPERT, split_axis=0, concat_axis=0, tiled=True
    ).reshape(-1, width)
    slot_grad = padded_rows(recv_grad)[slot_source].reshape(local_experts, capacity, width)
    act_grad = jnp.einsum(SUM_ECD_EFD_ECF, slot_grad, full_down, preferred_element_type=wide_type)
    down_grad = jnp.einsum(SUM_ECF_ECD_EFD, swiglu_low, slot_grad, preferred_element_type=wide_type)
    gate_grad, up_grad = swiglu_pull(act_grad)
    gate_low = gate_grad.astype(low_type)
    up_low = up_grad.astype(low_type)
    gate_w_grad = jnp.einsum(SUM_ECD_ECF_EDF, slot_rows, gate_low, preferred_element_type=wide_type)
    up_w_grad = jnp.einsum(SUM_ECD_ECF_EDF, slot_rows, up_low, preferred_element_type=wide_type)
    slot_in_grad = jnp.einsum(SUM_ECF_EDF_ECD, gate_low, full_gate, preferred_element_type=wide_type)
    slot_in_grad = (
        slot_in_grad + jnp.einsum(SUM_ECF_EDF_ECD, up_low, full_up, preferred_element_type=wide_type)
    ).astype(low_type)
    gate_shard, up_shard, down_shard = (
        lax.psum_scatter(
            gate_w_grad.astype(jnp.bfloat16), SHARD, scatter_dimension=1, tiled=True
        ).astype(jnp.float32),
        lax.psum_scatter(
            up_w_grad.astype(jnp.bfloat16), SHARD, scatter_dimension=1, tiled=True
        ).astype(jnp.float32),
        lax.psum_scatter(
            down_grad.astype(jnp.bfloat16), SHARD, scatter_dimension=2, tiled=True
        ).astype(jnp.float32),
    )
    back_grad = padded_rows(slot_in_grad.reshape(-1, width))[back_source].reshape(
        expert_devs, local_experts * most_rows, width
    )
    returned_grad = lax.all_to_all(
        back_grad, EXPERT, split_axis=0, concat_axis=0, tiled=True
    ).reshape(-1, width)
    expert_in_grad = jnp.sum(
        returned_grad[send_slot].reshape(tok_rows, top_count, width).astype(wide_type), axis=1
    )
    logit_grad = route_pull(weight_grad)[0]
    logit_low = logit_grad.astype(low_type)
    router_grad = matmul_tn(normed_two_low, logit_low)
    normed_two_grad = expert_in_grad + matmul_nt(logit_low, router_w)
    hidden_norm_grad, ffn_scale_grad = norm_two_pull(normed_two_grad)
    hidden_grad = result_grad + hidden_norm_grad
    attn_low = hidden_grad.astype(low_type)
    out_w_grad = matmul_tn(mixed_low, attn_low)
    mixed_grad = matmul_nt(attn_low, out_w).astype(low_type).reshape(tok_rows, HEADS, HD)
    back_keys, back_values = (seq_keys, seq_values)
    key_heads = back_keys.reshape(seq_length, HEADS, HD)
    value_heads = back_values.reshape(seq_length, HEADS, HD)
    scores_again = masked_scores(query_low, key_heads, query_segment, segment_ids)
    probs_again = jnp.exp(scores_again - log_total)
    probs_again_low = probs_again.astype(low_type)
    prob_grad = jnp.einsum(
        SUM_QHD_KHD_HQK, mixed_grad, value_heads, preferred_element_type=wide_type
    )
    value_part = jnp.einsum(
        SUM_HQK_QHD_KHD, probs_again_low, mixed_grad, preferred_element_type=wide_type
    )
    row_inner = jnp.sum(probs_again * prob_grad, axis=-1, keepdims=True)
    score_low = (probs_again * (prob_grad - row_inner)).astype(low_type)
    query_rot_grad = jnp.einsum(
        SUM_HQK_KHD_QHD, score_low, key_heads, preferred_element_type=wide_type
    )
    key_part = jnp.einsum(SUM_HQK_QHD_KHD, score_low, query_low, preferred_element_type=wide_type)
    key_rot_grad, value_grad = (
        lax.psum_scatter(
            key_part.reshape(seq_length, width).astype(jnp.bfloat16),
            SHARD,
            scatter_dimension=0,
            tiled=True,
        ).astype(jnp.float32),
        lax.psum_scatter(
            value_part.reshape(seq_length, width).astype(jnp.bfloat16),
            SHARD,
            scatter_dimension=0,
            tiled=True,
        ).astype(jnp.float32),
    )
    query_raw_grad, key_raw_grad, query_scale_grad, key_scale_grad = prepare_pull(
        (query_rot_grad, key_rot_grad.reshape(tok_rows, HEADS, HD))
    )
    query_grad_low = query_raw_grad.astype(low_type)
    key_grad_low = key_raw_grad.astype(low_type)
    value_grad_low = value_grad.astype(low_type)
    query_w_grad = matmul_tn(normed_low, query_grad_low)
    key_w_grad = matmul_tn(normed_low, key_grad_low)
    value_w_grad = matmul_tn(normed_low, value_grad_low)
    normed_grad = (
        matmul_nt(query_grad_low, query_w)
        + matmul_nt(key_grad_low, key_w)
        + matmul_nt(value_grad_low, value_w)
    )
    input_norm_grad, attn_scale_grad = norm_one_pull(normed_grad)
    input_grad = (hidden_grad + input_norm_grad).astype(low_type)
    summed = (
        lax.psum_scatter(attn_scale_grad, BOTH, scatter_dimension=0, tiled=True),
        lax.psum_scatter(query_w_grad, BOTH, scatter_dimension=0, tiled=True),
        lax.psum_scatter(key_w_grad, BOTH, scatter_dimension=0, tiled=True),
        lax.psum_scatter(value_w_grad, BOTH, scatter_dimension=0, tiled=True),
        lax.psum_scatter(query_scale_grad, BOTH, scatter_dimension=0, tiled=True),
        lax.psum_scatter(key_scale_grad, BOTH, scatter_dimension=0, tiled=True),
        lax.psum_scatter(out_w_grad, BOTH, scatter_dimension=0, tiled=True),
        lax.psum_scatter(ffn_scale_grad, BOTH, scatter_dimension=0, tiled=True),
        lax.psum_scatter(router_grad, BOTH, scatter_dimension=0, tiled=True),
    )
    return (
        mixed_out,
        input_grad,
        summed[0],
        summed[1],
        summed[2],
        summed[3],
        summed[4],
        summed[5],
        summed[6],
        summed[7],
        summed[8],
        gate_shard,
        up_shard,
        down_shard,
    )


MIB = 1 << 20


def nt_dot(left, right):
    return lax.dot_general(
        left, right, (((1,), (1,)), ((), ())), preferred_element_type=jnp.float32
    )


def tn_dot(left, right):
    return lax.dot_general(
        left, right, (((0,), (0,)), ((), ())), preferred_element_type=jnp.float32
    )


def vmem_params(mib):
    return pltpu.CompilerParams(vmem_limit_bytes=mib * MIB)


def turn_tables(length):
    exponent = np.arange(HD // 2, dtype=np.float32) * np.float32(2.0 / HD)
    frequency = np.power(np.float32(THETA), -exponent).astype(np.float32)
    angles = np.arange(length, dtype=np.float32)[:, None] * frequency[None, :]
    cosine, sine = np.cos(angles), np.sin(angles)
    return (
        jnp.asarray(np.concatenate([cosine, cosine], axis=1), jnp.float32),
        jnp.asarray(np.concatenate([-sine, sine], axis=1), jnp.float32),
    )


def norm_factor(values):
    return lax.rsqrt(jnp.mean(values * values, axis=-1, keepdims=True) + EPSILON)


def attend_kernel(
    tokens, gain, weight, query_gain, key_gain, cosine, sine, seg_row, seg_col,
    normed_out, raw_out, low_out, mixed_out, total_out, qkv,
):
    part = mixed_out.shape[1]
    values = tokens[...].astype(jnp.float32)
    normed = (values * norm_factor(values) * gain[...]).astype(jnp.bfloat16)
    normed_out[...] = normed
    qkv[...] = jnp.dot(normed, weight[...], preferred_element_type=jnp.float32)
    raw_out[...] = qkv[:, : 2 * part]
    low_out[:, 2 * part :] = qkv[:, 2 * part :].astype(jnp.bfloat16)
    allowed = seg_col[...] == seg_row[...]
    for head in range(part // HD):
        span = pl.ds(head * HD, HD)
        for offset, scale_gain, scale in ((0, query_gain, HD ** (-0.5)), (part, key_gain, 1.0)):
            raw = qkv[:, pl.ds(offset + head * HD, HD)]
            unit = raw * norm_factor(raw) * scale_gain[...]
            turned = unit * cosine[...] + pltpu.roll(unit, HD // 2, 1) * sine[...]
            low_out[:, pl.ds(offset + head * HD, HD)] = (turned * scale).astype(jnp.bfloat16)
        query, key = low_out[:, span], low_out[:, pl.ds(part + head * HD, HD)]
        scores = jnp.where(allowed, nt_dot(query, key), -1e30)
        top = jnp.max(scores, axis=-1, keepdims=True)
        shifted = jnp.exp(scores - top)
        total = jnp.sum(shifted, axis=-1, keepdims=True)
        probs = (shifted / total).astype(jnp.bfloat16)
        mixed = jnp.dot(
            probs, low_out[:, pl.ds(2 * part + head * HD, HD)], preferred_element_type=jnp.float32
        )
        mixed_out[:, span] = mixed.astype(jnp.bfloat16)
        total_out[:, head : head + 1] = top + jnp.log(total)


def attend_call(tokens, gain, weight, query_gain, key_gain, tables, seg_row, seg_col):
    seq, width = tokens.shape
    part = weight.shape[1] // 3
    return pl.pallas_call(
        attend_kernel,
        out_shape=(
            jax.ShapeDtypeStruct((seq, width), jnp.bfloat16),
            jax.ShapeDtypeStruct((seq, 2 * part), jnp.float32),
            jax.ShapeDtypeStruct((seq, 3 * part), jnp.bfloat16),
            jax.ShapeDtypeStruct((seq, part), jnp.bfloat16),
            jax.ShapeDtypeStruct((seq, 128), jnp.float32),
        ),
        scratch_shapes=[pltpu.VMEM((seq, 3 * part), jnp.float32)],
        compiler_params=vmem_params(28),
        cost_estimate=pl.CostEstimate(
            flops=2 * seq * width * 3 * part, bytes_accessed=16 * MIB, transcendentals=seq * seq * 4
        ),
    )(tokens, gain, weight, query_gain, key_gain, *tables, seg_row, seg_col)


def join_kernel(mixed, weight, tokens, gain, hidden_out, normed_out):
    shards, _, part = mixed.shape
    total = tokens[...].astype(jnp.float32)
    for shard in range(shards):
        total = total + jnp.dot(
            mixed[shard], weight[pl.ds(shard * part, part), :], preferred_element_type=jnp.float32
        )
    hidden_out[...] = total
    normed_out[...] = (total * norm_factor(total) * gain[...]).astype(jnp.bfloat16)


def join_call(mixed, weight, tokens, gain):
    shards, seq, part = mixed.shape
    width = weight.shape[1]
    tile = seq // 2
    return pl.pallas_call(
        join_kernel,
        grid=(2,),
        in_specs=[
            pl.BlockSpec((shards, tile, part), lambda i: (0, i, 0)),
            pl.BlockSpec(weight.shape, lambda i: (0, 0), pipeline_mode=pl.Buffered(1)),
            pl.BlockSpec((tile, width), lambda i: (i, 0)),
            pl.BlockSpec((1, width), lambda i: (0, 0)),
        ],
        out_specs=[
            pl.BlockSpec((tile, width), lambda i: (i, 0)),
            pl.BlockSpec((tile, width), lambda i: (i, 0)),
        ],
        out_shape=(
            jax.ShapeDtypeStruct((seq, width), jnp.float32),
            jax.ShapeDtypeStruct((seq, width), jnp.bfloat16),
        ),
        compiler_params=vmem_params(26),
        cost_estimate=pl.CostEstimate(
            flops=2 * seq * width * width, bytes_accessed=18 * MIB, transcendentals=0
        ),
    )(mixed, weight, tokens, gain)


def unpack_kernel(gate0, gate1, up0, up1, down0, down1, gate_out, up_out, down_out):
    for index, group in enumerate(((gate0, up0, down0), (gate1, up1, down1))):

        @pl.when(pl.program_id(0) == index)
        def _(group=group):
            for source, result in zip(group, (gate_out, up_out, down_out), strict=True):
                result[...] = source[...].astype(result.dtype)


def unpack_units(wides, downs):
    shards, part, lanes = wides[0].shape
    each = lanes // 2

    def held(index, e, s):
        return jnp.where(e == index, s, (shards - 1) * (1 - index))

    def wide_spec(index, which):
        return pl.BlockSpec((1, part, each), lambda e, s: (held(index, e, s), 0, which))

    def down_spec(index):
        return pl.BlockSpec((1, each, part), lambda e, s: (held(index, e, s), 0, 0))

    wide_out = pl.BlockSpec((1, part, each), lambda e, s: (e, 0, s))
    shape = jax.ShapeDtypeStruct((2, part, shards * each), jnp.float32)
    return pl.pallas_call(
        unpack_kernel,
        grid=(2, shards),
        in_specs=[wide_spec(index, which) for which in range(2) for index in range(2)]
        + [down_spec(index) for index in range(2)],
        out_specs=[wide_out, wide_out, pl.BlockSpec((1, each, part), lambda e, s: (e, s, 0))],
        out_shape=[shape, shape, jax.ShapeDtypeStruct((2, shards * each, part), jnp.float32)],
        compiler_params=vmem_params(24),
    )(wides[0], wides[1], wides[0], wides[1], *downs)


def keep_kernel(capacity, bits, shards, high, low, keep_out):
    own, _, rows = high.shape
    for index in range(own):
        order = high[index].astype(jnp.float32) * 256.0 + low[index].astype(jnp.float32)
        there = order > 0.0
        row = lax.broadcasted_iota(jnp.int32, order.shape, 0)
        group = lax.rem(row, shards)
        bound = jnp.zeros_like(order)
        for bit in reversed(range(bits)):
            trial = bound + float(1 << bit)
            within = jnp.where(there & (order <= trial), 1.0, 0.0)
            for shard in range(shards):
                here = group == shard
                count = jnp.sum(jnp.where(here, within, 0.0), keepdims=True)
                bound = jnp.where(here & (count <= float(capacity)), trial, bound)
        kept = jnp.where(there & (order <= bound), 1.0, 0.0).T
        for block in range(order.shape[0]):
            place = keep_out.at[block // shards, pl.ds(block % shards * rows, rows)]
            place[:, index : index + 1] = kept[:, block : block + 1]


def keep_call(high, low, capacity, most, planes, shards):
    own, _, rows = high.shape
    return pl.pallas_call(
        functools.partial(keep_kernel, capacity, most.bit_length(), shards),
        out_shape=jax.ShapeDtypeStruct((planes, shards * rows, own), jnp.float32),
        compiler_params=vmem_params(8),
    )(high, low)


CORE, XBIT, YBIT = 1, 2, 4


MESH = pl.DeviceIdType.MESH


def held_in_hbm(*values):
    return [pltpu.with_memory_space_constraint(value, pltpu.HBM) for value in values]


class Wires:
    def __init__(self, send, recv):
        self.send, self.recv, self.used = send, recv, 0
        self.device, self.shard = lax.axis_index(EXPERT), lax.axis_index(SHARD)

    def slot(self):
        self.used += 1
        return self.used - 1

    def peer(self, bits=0, step=0, shards=1):
        shard = lax.rem(self.shard + step, shards) if step else self.shard
        return (self.device ^ bits, shard)

    def copy(self, source, target, slot, peer):
        return pltpu.make_async_remote_copy(
            src_ref=source,
            dst_ref=target,
            send_sem=self.send.at[slot],
            recv_sem=self.recv.at[slot],
            device_id=peer,
            device_id_type=MESH,
        )


def greet(peers):
    barrier = pltpu.get_barrier_semaphore()
    for peer in peers:
        pl.semaphore_signal(barrier, inc=1, device_id=peer, device_id_type=MESH)
    pl.semaphore_wait(barrier, len(peers))


class Relay:
    def __init__(self, wires, shards, views):
        self.wires, self.shards, self.views = wires, shards, views
        self.slots = [[[wires.slot() for _ in views] for _ in range(shards - 1)] for _ in range(2)]

    def copies(self, way, step, block):
        wires = self.wires
        peer = (wires.device, wires.shard + (1 if way == 0 else -1))
        return [
            wires.copy(view(block), view(block), slot, peer)
            for view, slot in zip(self.views, self.slots[way][step], strict=True)
        ]

    def has(self, way, step):
        shard = self.wires.shard
        return shard - step >= 0 if way == 0 else shard + step < self.shards

    def sends(self, way, step):
        shard = self.wires.shard
        edge = shard < self.shards - 1 if way == 0 else shard > 0
        return jnp.logical_and(edge, self.has(way, step))

    def block(self, way, step):
        return self.wires.shard + (-step if way == 0 else step)

    def run(self, step, first=None):
        wires = self.wires
        for index, view in enumerate(self.views):
            for way in range(2):
                block = self.block(way, step)
                peer = (wires.device, wires.shard + (1 if way == 0 else -1))
                if step > 0:

                    @pl.when(self.has(way, step))
                    def _(way=way, block=block, index=index, view=view, peer=peer):
                        slot = self.slots[way][step - 1][index]
                        wires.copy(view(block), view(block), slot, peer).wait_recv()

                if step < self.shards - 1:

                    @pl.when(self.sends(way, step))
                    def _(way=way, block=block, index=index, view=view, peer=peer):
                        source = view(block) if first is None else first[index]
                        slot = self.slots[way][step][index]
                        wires.copy(source, view(block), slot, peer).start()

    def drain(self):
        for way in range(2):
            for step in range(self.shards - 1):

                @pl.when(self.sends(way, step))
                def _(way=way, step=step):
                    for copy in self.copies(way, step, self.block(way, step)):
                        copy.wait_send()


class Plane:
    def __init__(self, wires, views, whole):
        self.wires, self.views, self.whole = wires, views, whole
        count = len(views)
        self.first = [[wires.slot() for _ in range(count)] for _ in range(2)]
        self.second = [[[wires.slot() for _ in range(count)] for _ in range(2)] for _ in range(2)]
        self.last = [[wires.slot() for _ in range(count)] for _ in range(4)]
        self.sent = []

    def start(self, copies):
        for copy in copies:
            copy.start()
        self.sent += copies

    def one(self, owner, half, bits, slots):
        wires = self.wires
        return [
            wires.copy(view(owner, half), view(owner, half), slot, wires.peer(bits))
            for view, slot in zip(self.views, slots, strict=True)
        ]

    def step_one(self):
        me = self.wires.device
        for half, bits in enumerate((XBIT, YBIT)):
            self.start(self.one(me, half, bits, self.first[half]))

    def step_two(self):
        me = self.wires.device
        for half, bits in enumerate((XBIT, YBIT)):
            for copy in self.one(me ^ bits, half, bits, self.first[half]):
                copy.wait_recv()
        for half, bits in enumerate((XBIT, YBIT)):
            other = (XBIT | YBIT) ^ bits
            self.start(self.one(me, half, other, self.second[half][0]))
            self.start(self.one(me ^ bits, half, other, self.second[half][1]))

    def cores(self, index):
        wires = self.wires
        owner = wires.device ^ (0, XBIT, YBIT, XBIT | YBIT)[index]
        return [
            wires.copy(place(owner), place(owner), slot, wires.peer(CORE))
            for place, slot in zip(self.whole, self.last[index], strict=True)
        ]

    def step_three(self):
        me = self.wires.device
        for half, bits in enumerate((XBIT, YBIT)):
            other = (XBIT | YBIT) ^ bits
            for owner, slots in ((me ^ other, 0), (me ^ other ^ bits, 1)):
                for copy in self.one(owner, half, other, self.second[half][slots]):
                    copy.wait_recv()
        for index in range(1, 4):
            self.start(self.cores(index))

    def finish(self):
        for index, bits in enumerate((0, XBIT, YBIT, XBIT | YBIT)):
            owner = self.wires.device ^ CORE ^ bits
            for place, slot in zip(self.whole, self.last[index], strict=True):
                self.wires.copy(
                    place(owner), place(owner), slot, self.wires.peer(CORE)
                ).wait_recv()
        for copy in self.sent:
            copy.wait_send()


def opening_kernel(
    shards, experts, routes, order, gains, router, w_query, w_key, w_value, tokens, w_out, out_grad,
    small_all, router_all, qkv_w, tokens_all, out_block, grad_all, small, send, recv, local,
):
    wires = Wires(send, recv)
    device, shard = wires.device, wires.shard
    weights = (w_query, w_key, w_value)
    block, width = w_query.shape
    rows = tokens.shape[0]
    part = width // shards
    greet(
        [wires.peer(step=step, shards=shards) for step in range(1, shards)]
        + [wires.peer(XBIT), wires.peer(YBIT), wires.peer(CORE)]
    )

    def place(source_shard, which):
        start = pl.multiple_of((device * shards + source_shard) * block, block)
        return qkv_w.at[pl.ds(start, block), pl.ds(which * part, part)]

    def cut(which, target):
        return weights[which].at[:, pl.ds(pl.multiple_of(target * part, part), part)]

    mine = device * shards + shard

    def token_rows(ref):
        return lambda b: ref.at[pl.ds(pl.multiple_of(b * rows, rows), rows)]

    def grad_block(owner, source):
        return (owner * shards + source) * rows

    def grad_rows(owner, source):
        return grad_all.at[pl.ds(pl.multiple_of(grad_block(owner, source), rows), rows)]

    def grad_half(source):
        def view(owner, half):
            start = grad_block(owner, source) + half * (rows // 2)
            return grad_all.at[pl.ds(pl.multiple_of(start, rows // 2), rows // 2)]

        return view

    grad_line = Relay(wires, shards, [lambda b: grad_rows(device, b)])
    line = Relay(
        wires,
        shards,
        [
            token_rows(tokens_all),
            lambda b: out_block.at[pl.ds(pl.multiple_of(b * block, block), block)],
        ],
    )
    grad_line.run(0, (out_grad,))
    own = [
        pltpu.make_async_copy(cut(which, shard), place(shard, which), local.at[which])
        for which in range(3)
    ]
    own += [
        pltpu.make_async_copy(router, router_all.at[mine], local.at[3]),
        pltpu.make_async_copy(tokens, token_rows(tokens_all)(shard), local.at[4]),
        pltpu.make_async_copy(
            w_out, out_block.at[pl.ds(pl.multiple_of(shard * block, block), block)], local.at[5]
        ),
        pltpu.make_async_copy(out_grad, grad_rows(device, shard), local.at[6]),
    ]
    for copy in own:
        copy.start()
    turns = [shard] + [
        sum(jnp.where(shard == index, source, 0) for index, source in enumerate(row))
        for row in ((1, 0, 1, 2), (2, 2, 3, 1), (3, 3, 0, 0))
    ]
    stages = [
        Plane(wires, [grad_half(source)], [lambda owner, source=source: grad_rows(owner, source)])
        for source in turns
    ]
    own[6].wait()
    stages[0].step_one()
    stages[0].start(stages[0].cores(0))
    column = lax.broadcasted_iota(jnp.int32, (rows, 128), 1)
    dense = jnp.zeros((rows, 128), jnp.int32)
    for choice in range(routes.shape[1]):
        named = routes[:, choice : choice + 1] == column
        dense = dense + jnp.where(named, order[:, choice : choice + 1] + 1, 0)
    high = lax.shift_right_logical(dense, 8)
    for start, digits in ((0, high), (experts, dense - high * 256)):
        turned = digits.astype(jnp.float32).T
        small[pl.ds(start, experts), :] = turned[:experts, :].astype(small.dtype)
    small[pl.ds(2 * experts, gains.shape[0]), :] = gains[...]
    own.append(pltpu.make_async_copy(small, small_all.at[mine], local.at[7]))
    own[-1].start()
    stages[0].step_two()
    grad_line.run(1)
    stages[1].step_one()
    stages[1].start(stages[1].cores(0))
    exchange = [[wires.slot() for _ in range(5)] for _ in range(1, shards)]
    sent = []
    for step in range(1, shards):
        peer = wires.peer(step=step, shards=shards)
        slots = exchange[step - 1]
        copies = [
            wires.copy(router, router_all.at[mine], slots[4], peer),
            wires.copy(small, small_all.at[mine], slots[3], peer),
        ]
        copies += [
            wires.copy(cut(which, peer[1]), place(shard, which), slots[which], peer)
            for which in range(3)
        ]
        for copy in copies:
            copy.start()
        sent += copies
    stages[0].step_three()
    stages[1].step_two()
    grad_line.run(2)
    line.run(0, (tokens, w_out))
    stages[2].step_one()
    stages[2].start(stages[2].cores(0))
    stages[1].step_three()
    for index, copy in enumerate(own):
        if index != 6:
            copy.wait()
    for step in range(1, shards):
        peer = wires.peer(step=shards - step, shards=shards)
        source = peer[1]
        slots = exchange[step - 1]
        wires.copy(small, small_all.at[device * shards + source], slots[3], peer).wait_recv()
        wires.copy(router, router_all.at[device * shards + source], slots[4], peer).wait_recv()
        for which in range(3):
            wires.copy(place(source, which), place(source, which), slots[which], peer).wait_recv()

    each = shards * block // 2

    def rows_of(owner, half):
        return qkv_w.at[pl.ds(pl.multiple_of((owner * 2 + half) * each, each), each)]

    def small_of(owner, half):
        return small_all.at[pl.ds((owner * 2 + half) * (shards // 2), shards // 2)]

    def router_of(owner, half):
        return router_all.at[pl.ds((owner * 2 + half) * (shards // 2), shards // 2)]

    plane = Plane(
        wires,
        [rows_of, small_of, router_of],
        [
            lambda owner: qkv_w.at[pl.ds(pl.multiple_of(owner * 2 * each, 2 * each), 2 * each)],
            lambda owner: small_all.at[pl.ds(owner * shards, shards)],
            lambda owner: router_all.at[pl.ds(owner * shards, shards)],
        ],
    )
    plane.step_one()
    plane.start(plane.cores(0))
    stages[2].step_two()
    grad_line.run(3)
    stages[3].step_one()
    stages[3].start(stages[3].cores(0))
    plane.step_two()
    stages[2].step_three()
    line.run(1)
    stages[3].step_two()
    plane.step_three()
    line.run(2)
    stages[3].step_three()
    line.run(3)
    for group in (*stages, plane):
        group.finish()
    for copy in sent:
        copy.wait_send()
    line.drain()
    grad_line.drain()


def opening_call(
    routes, order, gains, router, w_query, w_key, w_value, tokens, w_out, out_grad, experts, planes, shards
):
    block, width = w_query.shape
    rows = tokens.shape[0]
    hbm = pl.BlockSpec(memory_space=pltpu.HBM)
    vmem = pl.BlockSpec(memory_space=pltpu.VMEM)
    slots = 112
    small = (2 * experts + gains.shape[0], 128)
    return pl.pallas_call(
        functools.partial(opening_kernel, shards, experts),
        in_specs=[vmem] * 3 + [hbm] * 7,
        out_specs=[hbm] * 6,
        out_shape=(
            jax.ShapeDtypeStruct((planes * shards,) + small, gains.dtype),
            jax.ShapeDtypeStruct((planes * shards,) + router.shape, router.dtype),
            jax.ShapeDtypeStruct((planes * shards * block, 3 * width // shards), w_query.dtype),
            jax.ShapeDtypeStruct((shards * rows, width), tokens.dtype),
            jax.ShapeDtypeStruct((shards * block, width), w_out.dtype),
            jax.ShapeDtypeStruct((planes * shards * rows, width), out_grad.dtype),
        ),
        scratch_shapes=[
            pltpu.VMEM(small, gains.dtype),
            pltpu.SemaphoreType.DMA((slots,)),
            pltpu.SemaphoreType.DMA((slots,)),
            pltpu.SemaphoreType.DMA((8,)),
        ],
        compiler_params=pltpu.CompilerParams(
            collective_id=1, has_side_effects=True, vmem_limit_bytes=4 * MIB
        ),
        cost_estimate=pl.CostEstimate(flops=0, bytes_accessed=200 * MIB, transcendentals=0),
    )(routes, order, gains, router, w_query, w_key, w_value, tokens, w_out, out_grad)


def middle_kernel(shards, mixed, out_block, mixed_all, out_w, send, recv, local):
    wires = Wires(send, recv)
    device, shard = wires.device, wires.shard
    greet(
        [wires.peer(step=step, shards=shards) for step in range(1, shards)]
        + [wires.peer(XBIT), wires.peer(YBIT), wires.peer(CORE)]
    )
    each = out_block.shape[0] // 2
    line = Relay(wires, shards, [lambda b: mixed_all.at[b]])
    line.run(0, (mixed,))
    own = [
        pltpu.make_async_copy(
            out_block,
            out_w.at[pl.ds(pl.multiple_of(device * 2 * each, 2 * each), 2 * each)],
            local.at[0],
        ),
        pltpu.make_async_copy(mixed, mixed_all.at[shard], local.at[1]),
    ]
    for copy in own:
        copy.start()
    for copy in own:
        copy.wait()
    plane = Plane(
        wires,
        [lambda owner, half: out_w.at[pl.ds(pl.multiple_of((owner * 2 + half) * each, each), each)]],
        [lambda owner: out_w.at[pl.ds(pl.multiple_of(owner * 2 * each, 2 * each), 2 * each)]],
    )
    plane.step_one()
    plane.start(plane.cores(0))
    line.run(1)
    plane.step_two()
    line.run(2)
    for step in range(3, shards):
        line.run(step)
    plane.step_three()
    plane.finish()
    line.drain()


def middle_call(mixed, out_block, planes, shards):
    hbm = pl.BlockSpec(memory_space=pltpu.HBM)
    slots = 32
    return pl.pallas_call(
        functools.partial(middle_kernel, shards),
        in_specs=[hbm] * 2,
        out_specs=[hbm] * 2,
        out_shape=(
            jax.ShapeDtypeStruct((shards,) + mixed.shape, mixed.dtype),
            jax.ShapeDtypeStruct((planes * out_block.shape[0], out_block.shape[1]), mixed.dtype),
        ),
        scratch_shapes=[
            pltpu.SemaphoreType.DMA((slots,)),
            pltpu.SemaphoreType.DMA((slots,)),
            pltpu.SemaphoreType.DMA((2,)),
        ],
        compiler_params=pltpu.CompilerParams(
            collective_id=2, has_side_effects=True, vmem_limit_bytes=4 * MIB
        ),
        cost_estimate=pl.CostEstimate(flops=0, bytes_accessed=150 * MIB, transcendentals=0),
    )(mixed, out_block)


class Units:
    def __init__(self, wires, shards, index, gate, up, down, wide_w, down_w, local, base):
        self.wires, self.shards, self.index = wires, shards, index
        self.gate, self.up, self.down, self.wide_w, self.down_w = gate, up, down, wide_w, down_w
        self.local, self.base = local, base
        self.slots = [[wires.slot() for _ in range(3)] for _ in range(1, shards)]

    def pairs(self, source, target):
        each = self.down_w.shape[1]
        span = pl.ds(pl.multiple_of(target * each, each), each)
        return [
            (self.gate.at[self.index, :, span], self.wide_w.at[source, :, pl.ds(0, each)]),
            (self.up.at[self.index, :, span], self.wide_w.at[source, :, pl.ds(each, each)]),
            (self.down.at[self.index, span, :], self.down_w.at[source]),
        ]

    def own(self):
        shard = self.wires.shard
        return [
            pltpu.make_async_copy(source, place, self.local.at[self.base + slot])
            for slot, (source, place) in enumerate(self.pairs(shard, shard))
        ]

    def sends(self):
        wires = self.wires
        for step in range(1, self.shards):
            peer = wires.peer(step=step, shards=self.shards)
            pairs = self.pairs(wires.shard, peer[1])
            for slot, (source, place) in zip(self.slots[step - 1], pairs, strict=True):
                yield wires.copy(source, place, slot, peer)

    def begin(self):
        for copy in self.own():
            copy.start()
        for copy in self.sends():
            copy.start()

    def end(self):
        wires = self.wires
        for copy in self.own():
            copy.wait()
        for step in range(1, self.shards):
            back = wires.peer(step=self.shards - step, shards=self.shards)
            pairs = self.pairs(back[1], wires.shard)
            for slot, (_, place) in zip(self.slots[step - 1], pairs, strict=True):
                wires.copy(place, place, slot, back).wait_recv()
        for copy in self.sends():
            copy.wait_send()


def meeting_kernel(
    shards, normed, gate, up, down, normed_all, wide_w, down_w, send, recv, local
):
    wires = Wires(send, recv)
    device = wires.device
    half = normed.shape[0] // 2
    greet(
        [wires.peer(step=step, shards=shards) for step in range(1, shards)]
        + [wires.peer(XBIT), wires.peer(YBIT), wires.peer(CORE)]
    )
    plane = Plane(
        wires,
        [lambda owner, part_of: normed_all.at[owner, pl.ds(part_of * half, half)]],
        [lambda owner: normed_all.at[owner]],
    )
    units = Units(wires, shards, 0, gate, up, down, wide_w, down_w, local, 1)
    own = pltpu.make_async_copy(normed, normed_all.at[device], local.at[0])
    own.start()
    own.wait()
    plane.step_one()
    units.begin()
    plane.start(plane.cores(0))
    plane.step_two()
    plane.step_three()
    plane.finish()
    units.end()


def unit_shapes(gate, shards):
    _, part, hidden_units = gate.shape
    each = hidden_units // shards
    return (
        jax.ShapeDtypeStruct((shards, part, 2 * each), gate.dtype),
        jax.ShapeDtypeStruct((shards, each, part), gate.dtype),
    )


def meeting_call(normed, gate, up, down, planes, shards):
    hbm = pl.BlockSpec(memory_space=pltpu.HBM)
    slots = 24
    return pl.pallas_call(
        functools.partial(meeting_kernel, shards),
        in_specs=[hbm] * 4,
        out_specs=[hbm] * 3,
        out_shape=(jax.ShapeDtypeStruct((planes,) + normed.shape, normed.dtype),)
        + unit_shapes(gate, shards),
        scratch_shapes=[
            pltpu.SemaphoreType.DMA((slots,)),
            pltpu.SemaphoreType.DMA((slots,)),
            pltpu.SemaphoreType.DMA((4,)),
        ],
        compiler_params=pltpu.CompilerParams(
            collective_id=3, has_side_effects=True, vmem_limit_bytes=4 * MIB
        ),
        cost_estimate=pl.CostEstimate(flops=0, bytes_accessed=300 * MIB, transcendentals=0),
    )(normed, gate, up, down)


def add_rows(target, sources, lines):
    rows = target.shape[0]

    def body(index, carry):
        span = pl.ds(pl.multiple_of(index * lines, lines), lines)
        total = target[span, :].astype(jnp.float32)
        for source in sources:
            total = total + source[span, :].astype(jnp.float32)
        target[span, :] = total.astype(target.dtype)
        return carry

    lax.fori_loop(0, rows // lines, body, 0)


class PlaneSum:
    def __init__(self, wires, part, held, came, diag, side, local, base):
        self.wires, self.part, self.local, self.base = wires, part, local, base
        self.held, self.came, self.diag, self.side = held, came, diag, side
        self.half = held.shape[1] // 2
        self.core = [wires.slot() for _ in range(4)]
        self.corner = [wires.slot() for _ in range(2)]
        self.edge = [wires.slot() for _ in range(2)]
        self.sent = []

    def start(self, copy):
        copy.start()
        self.sent.append(copy)

    def load(self, chip):
        return pltpu.make_async_copy(
            self.part(chip, 0), self.held.at[chip], self.local.at[self.base + chip]
        )

    def give(self, chip):
        self.start(
            self.wires.copy(
                self.held.at[chip], self.came.at[chip], self.core[chip], self.wires.peer(CORE)
            )
        )

    def begin(self):
        for chip in (3, 1, 2, 0):
            self.load(chip).start()
            self.start(
                self.wires.copy(
                    self.part(chip, 1), self.came.at[chip], self.core[chip], self.wires.peer(CORE)
                )
            )

    def add_core(self, chip):
        if self.part is not None:
            self.load(chip).wait()
        place = self.came.at[chip]
        self.wires.copy(place, place, self.core[chip], self.wires.peer(CORE)).wait_recv()
        add_rows(self.held.at[chip], [place], 64)

    def part_of_corner(self, which):
        return self.held.at[3, pl.ds(which * self.half, self.half)]

    def send_corner(self):
        self.add_core(3)
        for which, bits in enumerate((XBIT, YBIT)):
            self.start(
                self.wires.copy(
                    self.part_of_corner(which),
                    self.diag.at[which],
                    self.corner[which],
                    self.wires.peer(bits),
                )
            )

    def add_cores(self):
        for chip in (1, 2, 0):
            self.add_core(chip)

    def send_sides(self):
        for which, (bits, chip) in enumerate(((XBIT, 2), (YBIT, 1))):
            place = self.diag.at[which]
            self.wires.copy(place, place, self.corner[which], self.wires.peer(bits)).wait_recv()
            add_rows(self.held.at[chip, pl.ds(which * self.half, self.half)], [place], 64)
            self.start(
                self.wires.copy(
                    self.held.at[chip],
                    self.side.at[1 - which],
                    self.edge[1 - which],
                    self.wires.peer((XBIT | YBIT) ^ bits),
                )
            )

    def end(self):
        for which, bits in enumerate((XBIT, YBIT)):
            place = self.side.at[which]
            self.wires.copy(place, place, self.edge[which], self.wires.peer(bits)).wait_recv()
        add_rows(self.held.at[0], [self.side.at[0], self.side.at[1]], 64)

    def drain(self):
        for copy in self.sent:
            copy.wait_send()


class LineSum:
    def __init__(self, wires, shards, source, landing):
        self.wires, self.shards, self.source, self.landing = wires, shards, source, landing
        self.slots = [wires.slot() for _ in range(shards - 1)]

    def sends(self):
        wires = self.wires
        for step in range(1, self.shards):
            peer = wires.peer(step=step, shards=self.shards)
            yield wires.copy(
                self.source(peer[1]), self.landing(wires.shard), self.slots[step - 1], peer
            )

    def begin(self):
        for copy in self.sends():
            copy.start()

    def arrive(self):
        wires = self.wires
        for step in range(1, self.shards):
            peer = wires.peer(step=self.shards - step, shards=self.shards)
            place = self.landing(peer[1])
            wires.copy(place, place, self.slots[step - 1], peer).wait_recv()

    def drain(self):
        for copy in self.sends():
            copy.wait_send()


def line_total(landing, shards):
    total = landing[0].astype(jnp.float32)
    for shard in range(1, shards):
        total = total + landing[shard].astype(jnp.float32)
    return total


def aligned(index, size):
    return pl.ds(pl.multiple_of(index * size, size), size)


def expert_kernel(
    index, experts, shards, x, g, keep, wide_w, router_w, down_w, hot, *refs
):
    if index == 0:
        gate, up, down, out, grad, pull, wide_sum, down_sum, next_wide, next_down = refs[:10]
        acc, dacc, wide_out, down_out, send, recv, local, sems = refs[10:]
    else:
        old_out, old_grad, old_pull, wide_sent, down_sent = refs[:5]
        out, grad, wide_sum, down_sum, router_sum, wide_came, down_came = refs[5:12]
        acc, racc, dacc, wide_out, down_out, send, recv, local, sems = refs[12:]
    step, steps = pl.program_id(0), pl.num_programs(0)
    wires = Wires(send, recv)
    if index == 0:
        travel = [Units(wires, shards, 1, gate, up, down, next_wide, next_down, local, 0)]
    else:
        travel = [
            LineSum(wires, shards, lambda t: wide_sent.at[t], lambda s: wide_came.at[s]),
            LineSum(wires, shards, lambda t: down_sent.at[t], lambda s: down_came.at[s]),
        ]
        stay = [
            pltpu.make_async_copy(
                sent.at[wires.shard], came.at[wires.shard], local.at[place]
            )
            for place, (sent, came) in enumerate(((wide_sent, wide_came), (down_sent, down_came)))
        ]

    @pl.when(step == 0)
    def _():
        greet([wires.peer(step=hop, shards=shards) for hop in range(1, shards)])
        for group in travel:
            group.begin()
        acc[...] = jnp.zeros_like(acc)
        dacc[...] = jnp.zeros_like(dacc)
        if index == 1:
            for copy in stay:
                copy.start()
            racc[...] = jnp.zeros_like(racc)

    _, each, part = down_w.shape
    wide = jnp.dot(x[...], wide_w[...], preferred_element_type=jnp.float32)
    logits = jnp.dot(x[...], router_w[...], preferred_element_type=jnp.float32)
    back = nt_dot(g[:, :part], down_w[0])
    for shard in range(1, shards):
        back = back + nt_dot(g[:, shard * part : (shard + 1) * part], down_w[shard])
    lane = lax.broadcasted_iota(jnp.int32, logits.shape, 1)
    logits = jnp.where(lane < experts, logits, -1e30)
    shifted = jnp.exp(logits - jnp.max(logits, axis=-1, keepdims=True))
    probs = shifted / jnp.sum(shifted, axis=-1, keepdims=True)
    mark = hot[index : index + 1, :]
    kept = keep[:, index : index + 1]
    route = jnp.sum(probs * mark, axis=-1, keepdims=True) * kept
    gated, lifted = wide[:, :each], wide[:, each:]
    sigma = 1.0 / (1.0 + jnp.exp(-gated))
    silu = gated * sigma
    act = silu * lifted
    pulled = jnp.sum(act * back, axis=-1, keepdims=True) * kept
    act_low = (act * route).astype(jnp.bfloat16)
    act_grad = back * route
    wide_low = jnp.concatenate(
        [
            (act_grad * lifted * sigma * (1.0 + gated * (1.0 - sigma))).astype(jnp.bfloat16),
            (act_grad * silu).astype(jnp.bfloat16),
        ],
        axis=1,
    )
    result = nt_dot(wide_low, wide_w[...])
    if index == 0:
        pull[...] = pulled
    else:
        dense = pulled * mark + old_pull[...] * hot[0:1, :]
        logit_grad = probs * (dense - jnp.sum(probs * dense, axis=-1, keepdims=True))
        logit_low = logit_grad.astype(jnp.bfloat16)
        result = result + nt_dot(logit_low, router_w[...]) + old_grad[...].astype(jnp.float32)
        racc[...] += tn_dot(x[...], logit_low)
    grad[...] = result.astype(jnp.bfloat16)
    for shard in range(shards):
        span = slice(shard * part, (shard + 1) * part)
        value = jnp.dot(act_low, down_w[shard], preferred_element_type=jnp.float32)
        if index == 1:
            value = value + old_out[:, span].astype(jnp.float32)
        out[:, span] = value.astype(jnp.bfloat16)
        dacc[shard] += tn_dot(act_low, g[:, span])
    acc[...] += tn_dot(x[...], wide_low)

    @pl.when(step == steps - 1)
    def _():
        wide_out[...] = acc[...].astype(jnp.bfloat16)
        wide_copy = pltpu.make_async_copy(wide_out, wide_sum, sems.at[0])
        wide_copy.start()
        down_out[...] = dacc[...].astype(jnp.bfloat16)
        down_copy = pltpu.make_async_copy(down_out, down_sum, sems.at[1])
        down_copy.start()
        if index == 1:
            router_copy = pltpu.make_async_copy(racc, router_sum, sems.at[2])
            router_copy.start()
            router_copy.wait()
        wide_copy.wait()
        down_copy.wait()
        if index == 0:
            travel[0].end()
        else:
            for copy in stay:
                copy.wait()
            for group in travel:
                group.arrive()
                group.drain()


def expert_call(index, x_all, g_all, keep, wide_w, router_w, down_w, hot, experts, weights, before):
    planes, rows, width = x_all.shape
    shards = down_w.shape[0]
    tile = 512
    per = rows // tile
    hbm = pl.BlockSpec(memory_space=pltpu.HBM)

    def whole(value):
        zeros = (0,) * value.ndim
        return pl.BlockSpec(value.shape, lambda i: zeros, pipeline_mode=pl.Buffered(1))

    def rowwise(lanes):
        return pl.BlockSpec((None, tile, lanes), lambda i: (i // per, i % per, 0))

    low = jnp.bfloat16
    tall = pltpu.HBM((planes, rows, width), low)
    narrow = pltpu.HBM((planes, rows, 1), jnp.float32)
    wide_shape = pltpu.HBM(wide_w.shape, low)
    down_shape = pltpu.HBM(down_w.shape, low)
    came = pltpu.HBM((shards, width // shards, wide_w.shape[1]), low)
    if index == 0:
        extra = [hbm] * 3
        out_specs = [rowwise(width)] * 2 + [rowwise(1)] + [hbm] * 4
        shapes = (tall, tall, narrow, wide_shape, down_shape, came, down_shape)
        operands = held_in_hbm(*weights)
    else:
        extra = [rowwise(width)] * 2 + [rowwise(1)] + [hbm] * 2
        out_specs = [rowwise(width)] * 2 + [hbm] * 5
        router_shape = pltpu.HBM(router_w.shape, jnp.float32)
        shapes = (tall, tall, wide_shape, down_shape, router_shape, came, down_shape)
        operands = held_in_hbm(*before)
    return pl.pallas_call(
        functools.partial(expert_kernel, index, experts, shards),
        grid=(planes * per,),
        in_specs=[
            rowwise(width),
            rowwise(width),
            rowwise(keep.shape[2]),
            whole(wide_w),
            whole(router_w),
            whole(down_w),
            whole(hot),
        ]
        + extra,
        out_specs=out_specs,
        scratch_shapes=[pltpu.VMEM(wide_w.shape, jnp.float32)]
        + ([] if index == 0 else [pltpu.VMEM(router_w.shape, jnp.float32)])
        + [
            pltpu.VMEM(down_w.shape, jnp.float32),
            pltpu.VMEM(wide_w.shape, low),
            pltpu.VMEM(down_w.shape, low),
            pltpu.SemaphoreType.DMA((12,)),
            pltpu.SemaphoreType.DMA((12,)),
            pltpu.SemaphoreType.DMA((3,)),
            pltpu.SemaphoreType.DMA((3,)),
        ],
        out_shape=shapes,
        compiler_params=pltpu.CompilerParams(
            collective_id=7 + index, has_side_effects=True, vmem_limit_bytes=52 * MIB
        ),
        cost_estimate=pl.CostEstimate(
            flops=planes * rows * width * 12 * down_w.shape[1],
            bytes_accessed=100 * MIB,
            transcendentals=planes * rows * down_w.shape[1],
        ),
    )(*held_in_hbm(x_all, g_all), keep, wide_w, router_w, down_w, hot, *operands)


def returning_kernel(
    shards, ins, outs, wide, down, in_total, out_total, wide_all, down_all,
    held, came, diag, side, held2, came2, diag2, side2, landing, send, recv, local,
):
    wires = Wires(send, recv)
    device, shard = wires.device, wires.shard
    rows = in_total.shape[0]
    greet(
        [wires.peer(step=step, shards=shards) for step in range(1, shards)]
        + [wires.peer(XBIT), wires.peer(YBIT), wires.peer(CORE)]
    )

    def rel(source):
        return lambda chip, core: source.at[device ^ (2 * chip + core)]

    grads = PlaneSum(wires, rel(ins), held, came, diag, side, local, 0)
    values = PlaneSum(wires, rel(outs), held2, came2, diag2, side2, local, 6)
    weights = [
        LineSum(wires, shards, lambda t: wide.at[t], lambda s: wide_all.at[s]),
        LineSum(wires, shards, lambda t: down.at[t], lambda s: down_all.at[s]),
    ]
    line = LineSum(
        wires, shards, lambda t: held.at[0, aligned(t, rows)], lambda s: landing.at[s]
    )
    grads.begin()
    for group in weights:
        group.begin()
    own = [
        pltpu.make_async_copy(wide.at[shard], wide_all.at[shard], local.at[4]),
        pltpu.make_async_copy(down.at[shard], down_all.at[shard], local.at[5]),
    ]
    for copy in own:
        copy.start()
    grads.send_corner()
    values.begin()
    grads.add_cores()
    grads.send_sides()
    values.send_corner()
    values.add_cores()
    grads.end()
    line.begin()
    values.send_sides()
    landing[shard] = held[0, aligned(shard, rows), :]
    line.arrive()
    in_total[...] = line_total(landing, shards)
    values.end()
    back = pltpu.make_async_copy(held2.at[0], out_total, local.at[10])
    back.start()
    for copy in own:
        copy.wait()
    back.wait()
    for group in weights:
        group.arrive()
    for group in (grads, values, line, *weights):
        group.drain()


def sum_work(rows, lanes):
    low = jnp.bfloat16
    return [
        pltpu.VMEM((4, rows, lanes), low),
        pltpu.VMEM((4, rows, lanes), low),
        pltpu.VMEM((2, rows // 2, lanes), low),
        pltpu.VMEM((2, rows, lanes), low),
    ]


def returning_call(ins, outs, wide, down):
    _, seq, width = ins.shape
    shards = wide.shape[0]
    rows = seq // shards
    hbm = pl.BlockSpec(memory_space=pltpu.HBM)
    vmem = pl.BlockSpec(memory_space=pltpu.VMEM)
    return pl.pallas_call(
        functools.partial(returning_kernel, shards),
        in_specs=[hbm] * 4,
        out_specs=[vmem, hbm, hbm, hbm],
        out_shape=(
            jax.ShapeDtypeStruct((rows, width), jnp.float32),
            jax.ShapeDtypeStruct((seq, width), jnp.bfloat16),
            pltpu.HBM(wide.shape, wide.dtype),
            pltpu.HBM(down.shape, down.dtype),
        ),
        scratch_shapes=sum_work(seq, width)
        + sum_work(seq, width)
        + [
            pltpu.VMEM((shards, rows, width), jnp.bfloat16),
            pltpu.SemaphoreType.DMA((36,)),
            pltpu.SemaphoreType.DMA((36,)),
            pltpu.SemaphoreType.DMA((11,)),
        ],
        compiler_params=pltpu.CompilerParams(
            collective_id=4, has_side_effects=True, vmem_limit_bytes=56 * MIB
        ),
        cost_estimate=pl.CostEstimate(flops=0, bytes_accessed=300 * MIB, transcendentals=0),
    )(*held_in_hbm(ins, outs, wide, down))


def back_through_heads(
    mixed_grad, raw, low, total, query_gain, key_gain, cosine, sine, allowed, qkv_grad
):
    part = raw.shape[1] // 2
    gain_sums = [None, None]
    for head in range(part // HD):
        span = pl.ds(head * HD, HD)
        query, key = low[:, span], low[:, pl.ds(part + head * HD, HD)]
        value = low[:, pl.ds(2 * part + head * HD, HD)]
        out_grad = mixed_grad[:, span]
        scores = jnp.where(allowed, nt_dot(query, key), -1e30)
        probs = jnp.exp(scores - total[:, head : head + 1])
        prob_grad = nt_dot(out_grad, value)
        value_grad = tn_dot(probs.astype(jnp.bfloat16), out_grad)
        qkv_grad[:, pl.ds(2 * part + head * HD, HD)] = value_grad.astype(jnp.bfloat16)
        inner = jnp.sum(probs * prob_grad, axis=-1, keepdims=True)
        score_grad = (probs * (prob_grad - inner)).astype(jnp.bfloat16)
        rotated = (
            jnp.dot(score_grad, key, preferred_element_type=jnp.float32) * HD ** (-0.5),
            tn_dot(score_grad, query),
        )
        for which, (offset, scale_gain) in enumerate(((0, query_gain), (part, key_gain))):
            grad = rotated[which]
            grad = grad * cosine[...] - pltpu.roll(grad, HD // 2, 1) * sine[...]
            source = raw[:, pl.ds(offset + head * HD, HD)]
            factor = norm_factor(source)
            gain_sum = jnp.sum(grad * source * factor, axis=0, keepdims=True)
            gain_sums[which] = gain_sum if head == 0 else gain_sums[which] + gain_sum
            scaled = grad * scale_gain[...]
            inner = jnp.mean(scaled * source, axis=-1, keepdims=True)
            result = factor * scaled - source * (factor * factor * factor) * inner
            qkv_grad[:, pl.ds(offset + head * HD, HD)] = result.astype(jnp.bfloat16)
    return gain_sums


def closing_kernel(
    shards, planes,
    hidden, grad, out_grad, ffn_gain, raw, low, total, query_gain, key_gain, cosine, sine, seg_row, seg_col,
    tokens, gain, own_mixed, normed, router, out_w, qkv_w, out_total,
    input_grad, mixed_out, query_out, key_out, value_out, weight_out, gain_out, router_out, vectors_out,
    held, came, diag, side, held2, came2, diag2, side2,
    weights, hidden_grad, attn_low, message, message_land, qkv_grad, normed_grad, vectors,
    norm_land, out_land, qkv_land, weight_land, gain_mine, gain_land, gain_line, router_land, router_sum, router_line,
    vector_land, vector_sum, vector_line, send, recv, local,
):
    wires = Wires(send, recv)
    device, shard = wires.device, wires.shard
    rows, width = tokens.shape
    block = query_out.shape[0]
    part = width // shards
    lines = router_out.shape[0]
    lanes = qkv_w.shape[1]
    line_peers = [wires.peer(step=step, shards=shards) for step in range(1, shards)]
    plane_peers = [wires.peer(bits) for bits in range(1, planes)]
    load_out = pltpu.make_async_copy(out_w, weights, local.at[0])
    load_out.start()
    greet(line_peers + plane_peers)

    back = LineSum(
        wires, shards, lambda t: message.at[t], lambda s: message_land.at[aligned(s, rows)]
    )
    norms = LineSum(wires, shards, lambda t: normed_grad.at[aligned(t, rows)], lambda s: norm_land.at[s])
    values = LineSum(
        wires, shards, lambda t: out_total.at[aligned(t, rows)], lambda s: out_land.at[s]
    )
    qkv = PlaneSum(wires, None, held, came, diag, side, local, 0)
    weight = PlaneSum(wires, None, held2, came2, diag2, side2, local, 0)
    qkv_line = LineSum(
        wires, shards, lambda t: held.at[0, aligned(t, block)], lambda s: qkv_land.at[s]
    )
    weight_line = LineSum(
        wires, shards, lambda t: held2.at[0, aligned(t, block)], lambda s: weight_land.at[s]
    )
    sent = []

    def spread(slots, source, landing):
        for bits in range(1, planes):
            copy = wires.copy(
                source(device ^ bits), landing.at[device], slots[bits - 1], wires.peer(bits)
            )
            copy.start()
            sent.append(copy)

    def collect(slots, landing):
        for bits in range(1, planes):
            place = landing.at[device ^ bits]
            wires.copy(place, place, slots[bits - 1], wires.peer(bits)).wait_recv()
        total = landing[0]
        for other in range(1, planes):
            total = total + landing[other]
        return total

    router_slots = [wires.slot() for _ in range(1, planes)]
    vector_slots = [wires.slot() for _ in range(1, planes)]
    gain_slots = [wires.slot() for _ in range(1, planes)]
    spread(router_slots, lambda e: router.at[aligned(e, shards * lines)], router_land)
    router_land[device] = router[aligned(device, shards * lines), :]

    factor = norm_factor(hidden[...])
    vectors[:, :width] = jnp.sum(grad[...] * hidden[...] * factor, axis=0, keepdims=True)
    scaled = grad[...] * ffn_gain[...]
    inner = jnp.mean(scaled * hidden[...], axis=-1, keepdims=True)
    change = out_grad[...].astype(jnp.float32) + factor * scaled
    change = change - hidden[...] * (factor * factor * factor) * inner
    hidden_grad[...] = change
    attn_low[...] = change.astype(jnp.bfloat16)
    load_out.wait()
    for target in range(shards):
        message[target] = nt_dot(attn_low[...], weights[pl.ds(target * part, part), :]).astype(
            jnp.bfloat16
        )
    back.begin()
    values.begin()
    load_qkv = pltpu.make_async_copy(qkv_w, weights.at[:, pl.ds(0, lanes)], local.at[1])
    load_qkv.start()
    own_value = pltpu.make_async_copy(
        out_total.at[aligned(shard, rows)], out_land.at[shard], local.at[2]
    )
    own_value.start()
    message_land[aligned(shard, rows), :] = message[shard]

    def addends(group, left, right):
        for core in (1, 0):
            for chip in (3, 1, 2, 0):
                owner = device ^ (2 * chip + core)
                columns = pl.ds(pl.multiple_of(owner * shards * block, shards * block), shards * block)
                if core == 0:
                    group.sent[(3, 1, 2, 0).index(chip)].wait_send()
                group.held[chip] = tn_dot(left[:, columns], right[...]).astype(jnp.bfloat16)
                if core == 1:
                    group.give(chip)
        group.sent = []

    addends(weight, own_mixed, attn_low)
    weight.send_corner()
    weight.add_cores()
    router_sum[...] = collect(router_slots, router_land)
    router_pass = LineSum(
        wires, shards, lambda t: router_sum.at[aligned(t, lines)], lambda s: router_line.at[s]
    )

    back.arrive()
    allowed = seg_col[...] == seg_row[...]
    query_sum, key_sum = back_through_heads(
        message_land, raw, low, total, query_gain, key_gain, cosine, sine, allowed, qkv_grad
    )
    vectors[:, pl.ds(width, HD)] = query_sum
    vectors[:, pl.ds(width + HD, HD)] = key_sum
    load_qkv.wait()
    normed_grad[...] = nt_dot(qkv_grad[...], weights[:, pl.ds(0, lanes)]).astype(jnp.bfloat16)
    norms.begin()
    norm_land[shard] = normed_grad[aligned(shard, rows), :]
    router_pass.begin()
    spread(vector_slots, lambda e: vectors, vector_land)
    vector_land[device] = vectors[...]
    weight.send_sides()
    addends(qkv, normed, qkv_grad)
    qkv.send_corner()
    qkv.add_cores()
    vector_sum[...] = collect(vector_slots, vector_land)
    vector_pass = LineSum(wires, shards, lambda t: vector_sum, lambda s: vector_line.at[s])
    vector_pass.begin()
    vector_line[shard] = vector_sum[...]
    router_line[shard] = router_sum[aligned(shard, lines), :]
    qkv.send_sides()
    weight.end()
    weight_line.begin()
    weight_land[shard] = held2[0, aligned(shard, block), :]
    out_land_ready = own_value
    out_land_ready.wait()
    values.arrive()
    mixed_out[...] = (hidden[...] + line_total(out_land, shards)).astype(jnp.bfloat16)

    norms.arrive()
    change = line_total(norm_land, shards)
    given = tokens[...].astype(jnp.float32)
    factor = norm_factor(given)
    gain_mine[...] = jnp.sum(change * given * factor, axis=0, keepdims=True)
    spread(gain_slots, lambda e: gain_mine, gain_land)
    scaled = change * gain[...]
    inner = jnp.mean(scaled * given, axis=-1, keepdims=True)
    result = hidden_grad[...] + factor * scaled - given * (factor * factor * factor) * inner
    input_grad[...] = result.astype(jnp.bfloat16)
    qkv.end()
    qkv_line.begin()
    qkv_land[shard] = held[0, aligned(shard, block), :]
    gain_land[device] = gain_mine[...]
    gain_line[shard] = collect(gain_slots, gain_land)
    gain_pass = LineSum(wires, shards, lambda t: gain_line.at[shard], lambda s: gain_line.at[s])
    gain_pass.begin()
    router_pass.arrive()
    router_out[...] = line_total(router_line, shards)
    vector_pass.arrive()
    vectors_out[...] = line_total(vector_line, shards)
    weight_line.arrive()
    weight_out[...] = line_total(weight_land, shards)
    qkv_line.arrive()
    for source in range(shards):
        for which, result_out in enumerate((query_out, key_out, value_out)):
            result_out[:, pl.ds(source * part, part)] = qkv_land[
                source, :, pl.ds(which * part, part)
            ].astype(jnp.float32)
    gain_pass.arrive()
    gain_out[...] = line_total(gain_line, shards)
    for copy in sent:
        copy.wait_send()
    groups = (back, norms, values, qkv, weight, qkv_line, weight_line, router_pass, vector_pass)
    for group in (*groups, gain_pass):
        group.drain()


def closing_call(
    hidden, grad, out_grad, ffn_gain, raw, low, total, query_gain, key_gain, tables, seg_row, seg_col,
    tokens, gain, own_mixed, normed, router, out_w, qkv_w, out_total, planes, shards,
):
    rows, width = tokens.shape
    seq, lanes = low.shape
    each = width // planes
    block = each // shards
    lines = router.shape[0] // (planes * shards)
    hbm = pl.BlockSpec(memory_space=pltpu.HBM)
    vmem = pl.BlockSpec(memory_space=pltpu.VMEM)
    half, full = jnp.bfloat16, jnp.float32
    weight_shape = jax.ShapeDtypeStruct((block, width), full)
    vector = width + 2 * HD
    return pl.pallas_call(
        functools.partial(closing_kernel, shards, planes),
        in_specs=[vmem] * 18 + [hbm] * 3,
        out_specs=[vmem] * 9,
        out_shape=(
            jax.ShapeDtypeStruct((rows, width), half),
            jax.ShapeDtypeStruct((rows, width), half),
            weight_shape,
            weight_shape,
            weight_shape,
            weight_shape,
            jax.ShapeDtypeStruct((1, width), full),
            jax.ShapeDtypeStruct((lines, 128), full),
            jax.ShapeDtypeStruct((1, vector), full),
        ),
        scratch_shapes=sum_work(each, lanes)
        + sum_work(each, width)
        + [
            pltpu.VMEM((width, width), half),
            pltpu.VMEM((rows, width), full),
            pltpu.VMEM((rows, width), half),
            pltpu.VMEM((shards, rows, width // shards), half),
            pltpu.VMEM((seq, width // shards), half),
            pltpu.VMEM((seq, lanes), half),
            pltpu.VMEM((seq, width), half),
            pltpu.VMEM((1, vector), full),
            pltpu.VMEM((shards, rows, width), half),
            pltpu.VMEM((shards, rows, width), half),
            pltpu.VMEM((shards, block, lanes), half),
            pltpu.VMEM((shards, block, width), half),
            pltpu.VMEM((1, width), full),
            pltpu.VMEM((planes, 1, width), full),
            pltpu.VMEM((shards, 1, width), full),
            pltpu.VMEM((planes, shards * lines, 128), full),
            pltpu.VMEM((shards * lines, 128), full),
            pltpu.VMEM((shards, lines, 128), full),
            pltpu.VMEM((planes, 1, vector), full),
            pltpu.VMEM((1, vector), full),
            pltpu.VMEM((shards, 1, vector), full),
            pltpu.SemaphoreType.DMA((72,)),
            pltpu.SemaphoreType.DMA((72,)),
            pltpu.SemaphoreType.DMA((3,)),
        ],
        compiler_params=pltpu.CompilerParams(
            collective_id=6, has_side_effects=True, vmem_limit_bytes=60 * MIB
        ),
        cost_estimate=pl.CostEstimate(flops=0, bytes_accessed=300 * MIB, transcendentals=0),
    )(
        hidden, grad, out_grad, ffn_gain, raw, low, total, query_gain, key_gain, *tables, seg_row, seg_col,
        tokens, gain, own_mixed, normed, router, *held_in_hbm(out_w, qkv_w, out_total),
    )


LOW = jnp.bfloat16
WIDE = jnp.float32


def fast_local(
    tokens,
    segment_ids,
    routes,
    pair_order,
    attn_gain,
    w_query,
    w_key,
    w_value,
    query_gain,
    key_gain,
    w_out,
    ffn_gain,
    w_router,
    w_gate,
    w_up,
    w_down,
    out_grad,
):
    rows, width = tokens.shape
    top_count = routes.shape[1]
    planes = lax.axis_size(EXPERT)
    shards = lax.axis_size(SHARD)
    own_experts = w_gate.shape[0]
    experts = own_experts * planes
    capacity = 5 * rows * top_count // (4 * own_experts)
    seq = segment_ids.shape[0]
    device = lax.axis_index(EXPERT)
    shard = lax.axis_index(SHARD)
    part = width // shards

    gains = jnp.concatenate([attn_gain, ffn_gain, query_gain, key_gain])
    gains = jnp.pad(gains, (0, -gains.size % (16 * 128))).reshape(-1, 128)
    router_pad = jnp.pad(w_router, ((0, 0), (0, 128 - experts)))
    small, router_w, qkv_w, tokens_seq, out_block, grad_all = opening_call(
        routes,
        pair_order.reshape(rows, top_count),
        gains,
        router_pad,
        w_query,
        w_key,
        w_value,
        tokens,
        w_out,
        out_grad,
        experts,
        planes,
        shards,
    )
    router_w = router_w.reshape(width, 128)
    gains = small[:, 2 * experts :].reshape(planes * shards, -1).astype(WIDE)
    fields, at = [], 0
    for size in (attn_gain.size, ffn_gain.size, query_gain.size, key_gain.size):
        fields.append(gains[:, at : at + size].reshape(1, -1))
        at += size
    attn_row, ffn_row, query_row, key_row = fields
    digits = [
        lax.dynamic_slice_in_dim(small, start + device * own_experts, own_experts, 1)
        for start in (0, experts)
    ]
    high, low_digit = [value.transpose(1, 0, 2) for value in digits]
    most = planes * shards * rows * top_count
    kept = keep_call(high, low_digit, capacity, most, planes, shards)

    tables = turn_tables(seq)
    seg_row, seg_col = segment_ids.reshape(1, seq), segment_ids.reshape(seq, 1)
    normed_low, raw, low, mixed_own, total = attend_call(
        tokens_seq, attn_row, qkv_w, query_row, key_row, tables, seg_row, seg_col
    )
    mixed, out_w = middle_call(mixed_own, out_block, planes, shards)
    hidden_seq, normed_seq = join_call(mixed, out_w, tokens_seq, ffn_row)

    token_all, wide_w, down_w = meeting_call(normed_seq, w_gate, w_up, w_down, planes, shards)
    grad_all = grad_all.reshape(planes, seq, width)
    own_ids = device * own_experts + jnp.arange(own_experts, dtype=jnp.int32)
    own_hot = (own_ids[:, None] == jnp.arange(128, dtype=jnp.int32)[None, :]).astype(WIDE)
    out_first, in_first, pull, wide_sum, down_sum, wide_next, down_next = expert_call(
        0,
        token_all,
        grad_all,
        kept,
        wide_w.reshape(width, -1),
        router_w,
        down_w,
        own_hot,
        experts,
        (w_gate, w_up, w_down),
        None,
    )
    before = (out_first, in_first, pull, wide_sum.reshape(shards, part, -1), down_sum)
    out_parts, in_parts, wide_sum, down_sum, router_grad, wide0, down0 = expert_call(
        1,
        token_all,
        grad_all,
        kept,
        wide_next.reshape(width, -1),
        router_w,
        down_next,
        own_hot,
        experts,
        None,
        before,
    )
    normed_two_grad, out_total, wide1, down1 = returning_call(
        in_parts, out_parts, wide_sum.reshape(shards, part, -1), down_sum
    )
    hidden = lax.dynamic_slice_in_dim(hidden_seq, shard * rows, rows)
    own_mixed = lax.dynamic_slice_in_dim(mixed, shard * rows, rows, 1)
    own_mixed = own_mixed.transpose(1, 0, 2).reshape(rows, width)
    closed = closing_call(
        hidden,
        normed_two_grad,
        out_grad,
        ffn_row,
        raw,
        low,
        total,
        query_row,
        key_row,
        tables,
        seg_row,
        seg_col,
        tokens,
        attn_row,
        own_mixed,
        normed_low,
        router_grad[:, :experts].reshape(-1, 128),
        out_w,
        qkv_w,
        out_total,
        planes,
        shards,
    )
    input_grad, mixed_out, query_w_grad, key_w_grad, value_w_grad, out_w_grad = closed[:6]
    attn_scale_grad, router_out, vectors = closed[6:]
    gate_grad, up_grad, down_grad = unpack_units((wide0, wide1), (down0, down1))
    index = device * shards + shard
    flat = vectors.reshape(-1)

    def own_piece(values, start, size):
        return lax.dynamic_slice_in_dim(values, start + index * size, size)

    return (
        mixed_out,
        input_grad,
        own_piece(attn_scale_grad.reshape(-1), 0, attn_gain.size),
        query_w_grad,
        key_w_grad,
        value_w_grad,
        own_piece(flat, width, query_gain.size),
        own_piece(flat, width + HD, key_gain.size),
        out_w_grad,
        own_piece(flat, 0, ffn_gain.size),
        router_out.reshape(-1, experts),
        gate_grad,
        up_grad,
        down_grad,
    )


def solution(mesh):
    local = fast_local if mesh.shape[EXPERT] == 8 else general_local
    return jax.shard_map(
        local,
        mesh=mesh,
        in_specs=(
            P(BOTH, None),
            P(EXPERT),
            P(BOTH, None),
            P(BOTH),
            P(BOTH),
            P(BOTH, None),
            P(BOTH, None),
            P(BOTH, None),
            P(BOTH),
            P(BOTH),
            P(BOTH, None),
            P(BOTH),
            P(BOTH, None),
            P(EXPERT, SHARD, None),
            P(EXPERT, SHARD, None),
            P(EXPERT, None, SHARD),
            P(BOTH, None),
        ),
        out_specs=(
            P(BOTH, None),
            P(BOTH, None),
            P(BOTH),
            P(BOTH, None),
            P(BOTH, None),
            P(BOTH, None),
            P(BOTH),
            P(BOTH),
            P(BOTH, None),
            P(BOTH),
            P(BOTH, None),
            P(EXPERT, SHARD, None),
            P(EXPERT, SHARD, None),
            P(EXPERT, None, SHARD),
        ),
        check_vma=False,
    )
```

```python
import functools

import jax
import jax.numpy as jnp
import numpy as np
from jax import lax
from jax.experimental import pallas as pl
from jax.experimental.pallas import tpu as pltpu
from jax.sharding import PartitionSpec as P

HEADS = 16
HD = 128


EXPERT = "expert"
SHARD = "wshard"
BOTH = (EXPERT, SHARD)

SUM_QHD_KHD_HQK = "qhd,khd->hqk"
SUM_HQK_KHD_QHD = "hqk,khd->qhd"
SUM_ECD_EDF_ECF = "ecd,edf->ecf"
SUM_ECF_EFD_ECD = "ecf,efd->ecd"
SUM_TK_TKD_TD = "tk,tkd->td"
SUM_TD_TKD_TK = "td,tkd->tk"
SUM_ECD_EFD_ECF = "ecd,efd->ecf"
SUM_ECF_ECD_EFD = "ecf,ecd->efd"
SUM_ECD_ECF_EDF = "ecd,ecf->edf"
SUM_ECF_EDF_ECD = "ecf,edf->ecd"
SUM_HQK_QHD_KHD = "hqk,qhd->khd"
EPSILON = 1e-06
THETA = 10000.0


def matmul(left, right):
    return jnp.dot(left, right, preferred_element_type=jnp.float32)


def matmul_tn(left, right):
    return lax.dot_general(
        left, right, (((0,), (0,)), ((), ())), preferred_element_type=jnp.float32
    )


def matmul_nt(left, right):
    return lax.dot_general(
        left, right, (((1,), (1,)), ((), ())), preferred_element_type=jnp.float32
    )


def rms_scale(values, scale_gain):
    factor = lax.rsqrt(jnp.mean(values * values, axis=-1, keepdims=True) + EPSILON)
    return values * factor * scale_gain


def rope_tables(positions):
    exponent = jnp.arange(HD // 2, dtype=jnp.float32) * (2.0 / HD)
    frequency = jnp.power(jnp.float32(THETA), -exponent)
    angles = positions.astype(jnp.float32)[:, None] * frequency[None, :]
    return (jnp.cos(angles), jnp.sin(angles))


def rotate(values, cosine, sine):
    first_half = values[..., : HD // 2]
    second_half = values[..., HD // 2 :]
    cos_part = cosine[:, None, :]
    sin_part = sine[:, None, :]
    return jnp.concatenate(
        [
            first_half * cos_part - second_half * sin_part,
            second_half * cos_part + first_half * sin_part,
        ],
        axis=-1,
    )


def padded_rows(rows):
    return jnp.concatenate([jnp.zeros((1,) + rows.shape[1:], rows.dtype), rows], axis=0)


def masked_scores(query_rot, key_rot, query_segment, key_segment):
    scores = jnp.einsum(SUM_QHD_KHD_HQK, query_rot, key_rot, preferred_element_type=jnp.float32)
    allowed = query_segment[:, None] == key_segment[None, :]
    return jnp.where(allowed[None], scores, -1e30)


def swiglu_fn(gate_in, up_in):
    return jax.nn.silu(gate_in) * up_in


def general_local(
    tokens,
    segment_ids,
    routes,
    pair_order,
    attn_gain,
    w_query,
    w_key,
    w_value,
    query_gain,
    key_gain,
    w_out,
    ffn_gain,
    w_router,
    w_gate,
    w_up,
    w_down,
    out_grad,
):
    tok_rows, width = tokens.shape
    top_count = routes.shape[1]
    expert_devs = lax.axis_size(EXPERT)
    shard_devs = lax.axis_size(SHARD)
    local_experts = w_gate.shape[0]
    expert_count = local_experts * expert_devs
    most_rows = 2 * tok_rows * top_count // expert_count
    capacity = 5 * tok_rows * top_count // (4 * local_experts)
    seq_length = segment_ids.shape[0]
    device_expert = lax.axis_index(EXPERT)
    device_shard = lax.axis_index(SHARD)
    low_type = jnp.bfloat16
    wide_type = jnp.float32
    gathered = (
        lax.all_gather(attn_gain, BOTH, axis=0, tiled=True),
        lax.all_gather(w_query, BOTH, axis=0, tiled=True),
        lax.all_gather(w_key, BOTH, axis=0, tiled=True),
        lax.all_gather(w_value, BOTH, axis=0, tiled=True),
        lax.all_gather(query_gain, BOTH, axis=0, tiled=True),
        lax.all_gather(key_gain, BOTH, axis=0, tiled=True),
        lax.all_gather(w_out, BOTH, axis=0, tiled=True),
        lax.all_gather(ffn_gain, BOTH, axis=0, tiled=True),
        lax.all_gather(w_router, BOTH, axis=0, tiled=True),
    )
    attn_scale = gathered[0].astype(wide_type)
    query_w, key_w, value_w = (gathered[1], gathered[2], gathered[3])
    query_scale = gathered[4].astype(wide_type)
    key_scale = gathered[5].astype(wide_type)
    out_w = gathered[6]
    ffn_scale = gathered[7].astype(wide_type)
    router_w = gathered[8]
    inputs = tokens.astype(wide_type)
    normed, norm_one_pull = jax.vjp(rms_scale, inputs, attn_scale)
    normed_low = normed.astype(low_type)
    query_raw = matmul(normed_low, query_w)
    key_raw = matmul(normed_low, key_w)
    value_low = matmul(normed_low, value_w).astype(low_type)
    positions = device_shard * tok_rows + jnp.arange(tok_rows, dtype=jnp.int32)
    cosine, sine = rope_tables(positions)

    def prepare(query_in, key_in, query_g, key_g):
        query_heads = rms_scale(query_in.reshape(tok_rows, HEADS, HD), query_g)
        key_heads = rms_scale(key_in.reshape(tok_rows, HEADS, HD), key_g)
        return (rotate(query_heads, cosine, sine) * HD ** (-0.5), rotate(key_heads, cosine, sine))

    rotated, prepare_pull = jax.vjp(prepare, query_raw, key_raw, query_scale, key_scale)
    query_low = rotated[0].astype(low_type)
    key_low = rotated[1].astype(low_type).reshape(tok_rows, width)
    seq_keys, seq_values = (
        lax.all_gather(key_low, SHARD, axis=0, tiled=True),
        lax.all_gather(value_low, SHARD, axis=0, tiled=True),
    )
    query_segment = lax.dynamic_slice_in_dim(segment_ids, device_shard * tok_rows, tok_rows)
    scores = masked_scores(
        query_low, seq_keys.reshape(seq_length, HEADS, HD), query_segment, segment_ids
    )
    row_max = jnp.max(scores, axis=-1, keepdims=True)
    shifted = jnp.exp(scores - row_max)
    totals = jnp.sum(shifted, axis=-1, keepdims=True)
    log_total = row_max + jnp.log(totals)
    probs_low = (shifted / totals).astype(low_type)
    mixed = jnp.einsum(
        SUM_HQK_KHD_QHD,
        probs_low,
        seq_values.reshape(seq_length, HEADS, HD),
        preferred_element_type=wide_type,
    )
    mixed_low = mixed.reshape(tok_rows, width).astype(low_type)
    hidden = inputs + matmul(mixed_low, out_w)
    normed_two, norm_two_pull = jax.vjp(rms_scale, hidden, ffn_scale)
    normed_two_low = normed_two.astype(low_type)
    logits = matmul(normed_two_low, router_w)

    def router_weights(logit_values):
        return jnp.take_along_axis(jax.nn.softmax(logit_values, axis=-1), routes, axis=1)

    route_weight, route_pull = jax.vjp(router_weights, logits)
    group_routes, group_order = (
        lax.all_gather(routes, EXPERT, axis=0, tiled=True),
        lax.all_gather(pair_order, EXPERT, axis=0, tiled=True),
    )
    per_source = tok_rows * top_count
    group_pairs = per_source * expert_devs
    expert_of = group_routes.reshape(-1)
    pair_index = jnp.arange(group_pairs, dtype=jnp.int32)
    source_of = pair_index // per_source
    expert_ids = jnp.arange(expert_count, dtype=jnp.int32)
    onehot = (expert_of.reshape(expert_devs, per_source, 1) == expert_ids).astype(jnp.int32)
    position_of = (jnp.sum(jnp.cumsum(onehot, axis=1) * onehot, axis=-1) - 1).reshape(-1)
    order_span = group_pairs * shard_devs
    sort_keys = expert_of * order_span + group_order
    sorted_pairs = jnp.argsort(sort_keys)
    placement = jnp.zeros((group_pairs,), jnp.int32).at[sorted_pairs].set(pair_index)
    expert_counts = jnp.sum(onehot, axis=(0, 1))
    expert_start = jnp.cumsum(expert_counts) - expert_counts
    start_of = jnp.sum(onehot.reshape(group_pairs, expert_count) * expert_start[None, :], axis=-1)
    slot_rank = placement - start_of
    retained = slot_rank < capacity
    own_expert = routes.reshape(-1)
    own_position = lax.dynamic_slice_in_dim(position_of, device_expert * per_source, per_source)
    send_slot = own_expert * most_rows + own_position
    send_pair = (
        jnp.zeros((expert_count * most_rows,), jnp.int32)
        .at[send_slot]
        .set(jnp.arange(per_source, dtype=jnp.int32) + 1)
    )
    send_token = jnp.where(send_pair > 0, (send_pair - 1) // top_count + 1, 0)
    owner_local = expert_of % local_experts
    is_mine = expert_of // local_experts == device_expert
    recv_row = source_of * (local_experts * most_rows) + owner_local * most_rows + position_of
    slot_target = jnp.where(
        is_mine & retained, owner_local * capacity + slot_rank, local_experts * capacity
    )
    slot_source = (
        jnp.zeros((local_experts * capacity,), jnp.int32)
        .at[slot_target]
        .set(recv_row + 1, mode="drop")
    )
    back_room = expert_devs * local_experts * most_rows
    back_target = jnp.where(is_mine, recv_row, back_room)
    back_source = (
        jnp.zeros((back_room,), jnp.int32)
        .at[back_target]
        .set(jnp.where(retained, owner_local * capacity + slot_rank + 1, 0), mode="drop")
    )
    send_rows = padded_rows(normed_two_low)[send_token].reshape(
        expert_devs, local_experts * most_rows, width
    )
    recv_rows = lax.all_to_all(
        send_rows, EXPERT, split_axis=0, concat_axis=0, tiled=True
    ).reshape(-1, width)
    slot_rows = padded_rows(recv_rows)[slot_source].reshape(local_experts, capacity, width)
    full_gate, full_up, full_down = (
        lax.all_gather(w_gate, SHARD, axis=1, tiled=True),
        lax.all_gather(w_up, SHARD, axis=1, tiled=True),
        lax.all_gather(w_down, SHARD, axis=2, tiled=True),
    )
    gate_act = jnp.einsum(SUM_ECD_EDF_ECF, slot_rows, full_gate, preferred_element_type=wide_type)
    up_act = jnp.einsum(SUM_ECD_EDF_ECF, slot_rows, full_up, preferred_element_type=wide_type)
    swiglu_out, swiglu_pull = jax.vjp(swiglu_fn, gate_act, up_act)
    swiglu_low = swiglu_out.astype(low_type)
    expert_out = jnp.einsum(
        SUM_ECF_EFD_ECD, swiglu_low, full_down, preferred_element_type=wide_type
    ).astype(low_type)
    back_rows = padded_rows(expert_out.reshape(-1, width))[back_source].reshape(
        expert_devs, local_experts * most_rows, width
    )
    returned = lax.all_to_all(back_rows, EXPERT, split_axis=0, concat_axis=0, tiled=True).reshape(
        -1, width
    )
    pair_rows = returned[send_slot].reshape(tok_rows, top_count, width)
    combined = jnp.einsum(SUM_TK_TKD_TD, route_weight, pair_rows, preferred_element_type=wide_type)
    mixed_out = (hidden + combined).astype(low_type)
    result_grad = out_grad.astype(wide_type)
    weight_grad = jnp.einsum(SUM_TD_TKD_TK, result_grad, pair_rows, preferred_element_type=wide_type)
    pair_grad = (
        (route_weight[:, :, None] * result_grad[:, None, :])
        .astype(low_type)
        .reshape(per_source, width)
    )
    send_grad = padded_rows(pair_grad)[send_pair].reshape(
        expert_devs, local_experts * most_rows, width
    )
    recv_grad = lax.all_to_all(
        send_grad, EXPERT, split_axis=0, concat_axis=0, tiled=True
    ).reshape(-1, width)
    slot_grad = padded_rows(recv_grad)[slot_source].reshape(local_experts, capacity, width)
    act_grad = jnp.einsum(SUM_ECD_EFD_ECF, slot_grad, full_down, preferred_element_type=wide_type)
    down_grad = jnp.einsum(SUM_ECF_ECD_EFD, swiglu_low, slot_grad, preferred_element_type=wide_type)
    gate_grad, up_grad = swiglu_pull(act_grad)
    gate_low = gate_grad.astype(low_type)
    up_low = up_grad.astype(low_type)
    gate_w_grad = jnp.einsum(SUM_ECD_ECF_EDF, slot_rows, gate_low, preferred_element_type=wide_type)
    up_w_grad = jnp.einsum(SUM_ECD_ECF_EDF, slot_rows, up_low, preferred_element_type=wide_type)
    slot_in_grad = jnp.einsum(SUM_ECF_EDF_ECD, gate_low, full_gate, preferred_element_type=wide_type)
    slot_in_grad = (
        slot_in_grad + jnp.einsum(SUM_ECF_EDF_ECD, up_low, full_up, preferred_element_type=wide_type)
    ).astype(low_type)
    gate_shard, up_shard, down_shard = (
        lax.psum_scatter(
            gate_w_grad.astype(jnp.bfloat16), SHARD, scatter_dimension=1, tiled=True
        ).astype(jnp.float32),
        lax.psum_scatter(
            up_w_grad.astype(jnp.bfloat16), SHARD, scatter_dimension=1, tiled=True
        ).astype(jnp.float32),
        lax.psum_scatter(
            down_grad.astype(jnp.bfloat16), SHARD, scatter_dimension=2, tiled=True
        ).astype(jnp.float32),
    )
    back_grad = padded_rows(slot_in_grad.reshape(-1, width))[back_source].reshape(
        expert_devs, local_experts * most_rows, width
    )
    returned_grad = lax.all_to_all(
        back_grad, EXPERT, split_axis=0, concat_axis=0, tiled=True
    ).reshape(-1, width)
    expert_in_grad = jnp.sum(
        returned_grad[send_slot].reshape(tok_rows, top_count, width).astype(wide_type), axis=1
    )
    logit_grad = route_pull(weight_grad)[0]
    logit_low = logit_grad.astype(low_type)
    router_grad = matmul_tn(normed_two_low, logit_low)
    normed_two_grad = expert_in_grad + matmul_nt(logit_low, router_w)
    hidden_norm_grad, ffn_scale_grad = norm_two_pull(normed_two_grad)
    hidden_grad = result_grad + hidden_norm_grad
    attn_low = hidden_grad.astype(low_type)
    out_w_grad = matmul_tn(mixed_low, attn_low)
    mixed_grad = matmul_nt(attn_low, out_w).astype(low_type).reshape(tok_rows, HEADS, HD)
    back_keys, back_values = (seq_keys, seq_values)
    key_heads = back_keys.reshape(seq_length, HEADS, HD)
    value_heads = back_values.reshape(seq_length, HEADS, HD)
    scores_again = masked_scores(query_low, key_heads, query_segment, segment_ids)
    probs_again = jnp.exp(scores_again - log_total)
    probs_again_low = probs_again.astype(low_type)
    prob_grad = jnp.einsum(
        SUM_QHD_KHD_HQK, mixed_grad, value_heads, preferred_element_type=wide_type
    )
    value_part = jnp.einsum(
        SUM_HQK_QHD_KHD, probs_again_low, mixed_grad, preferred_element_type=wide_type
    )
    row_inner = jnp.sum(probs_again * prob_grad, axis=-1, keepdims=True)
    score_low = (probs_again * (prob_grad - row_inner)).astype(low_type)
    query_rot_grad = jnp.einsum(
        SUM_HQK_KHD_QHD, score_low, key_heads, preferred_element_type=wide_type
    )
    key_part = jnp.einsum(SUM_HQK_QHD_KHD, score_low, query_low, preferred_element_type=wide_type)
    key_rot_grad, value_grad = (
        lax.psum_scatter(
            key_part.reshape(seq_length, width).astype(jnp.bfloat16),
            SHARD,
            scatter_dimension=0,
            tiled=True,
        ).astype(jnp.float32),
        lax.psum_scatter(
            value_part.reshape(seq_length, width).astype(jnp.bfloat16),
            SHARD,
            scatter_dimension=0,
            tiled=True,
        ).astype(jnp.float32),
    )
    query_raw_grad, key_raw_grad, query_scale_grad, key_scale_grad = prepare_pull(
        (query_rot_grad, key_rot_grad.reshape(tok_rows, HEADS, HD))
    )
    query_grad_low = query_raw_grad.astype(low_type)
    key_grad_low = key_raw_grad.astype(low_type)
    value_grad_low = value_grad.astype(low_type)
    query_w_grad = matmul_tn(normed_low, query_grad_low)
    key_w_grad = matmul_tn(normed_low, key_grad_low)
    value_w_grad = matmul_tn(normed_low, value_grad_low)
    normed_grad = (
        matmul_nt(query_grad_low, query_w)
        + matmul_nt(key_grad_low, key_w)
        + matmul_nt(value_grad_low, value_w)
    )
    input_norm_grad, attn_scale_grad = norm_one_pull(normed_grad)
    input_grad = (hidden_grad + input_norm_grad).astype(low_type)
    summed = (
        lax.psum_scatter(attn_scale_grad, BOTH, scatter_dimension=0, tiled=True),
        lax.psum_scatter(query_w_grad, BOTH, scatter_dimension=0, tiled=True),
        lax.psum_scatter(key_w_grad, BOTH, scatter_dimension=0, tiled=True),
        lax.psum_scatter(value_w_grad, BOTH, scatter_dimension=0, tiled=True),
        lax.psum_scatter(query_scale_grad, BOTH, scatter_dimension=0, tiled=True),
        lax.psum_scatter(key_scale_grad, BOTH, scatter_dimension=0, tiled=True),
        lax.psum_scatter(out_w_grad, BOTH, scatter_dimension=0, tiled=True),
        lax.psum_scatter(ffn_scale_grad, BOTH, scatter_dimension=0, tiled=True),
        lax.psum_scatter(router_grad, BOTH, scatter_dimension=0, tiled=True),
    )
    return (
        mixed_out,
        input_grad,
        summed[0],
        summed[1],
        summed[2],
        summed[3],
        summed[4],
        summed[5],
        summed[6],
        summed[7],
        summed[8],
        gate_shard,
        up_shard,
        down_shard,
    )


MIB = 1 << 20


def nt_dot(left, right):
    return lax.dot_general(
        left, right, (((1,), (1,)), ((), ())), preferred_element_type=jnp.float32
    )


def tn_dot(left, right):
    return lax.dot_general(
        left, right, (((0,), (0,)), ((), ())), preferred_element_type=jnp.float32
    )


def vmem_params(mib):
    return pltpu.CompilerParams(vmem_limit_bytes=mib * MIB)


def turn_tables(length):
    exponent = np.arange(HD // 2, dtype=np.float32) * np.float32(2.0 / HD)
    frequency = np.power(np.float32(THETA), -exponent).astype(np.float32)
    angles = np.arange(length, dtype=np.float32)[:, None] * frequency[None, :]
    cosine, sine = np.cos(angles), np.sin(angles)
    return (
        jnp.asarray(np.concatenate([cosine, cosine], axis=1), jnp.float32),
        jnp.asarray(np.concatenate([-sine, sine], axis=1), jnp.float32),
    )


def norm_factor(values):
    return lax.rsqrt(jnp.mean(values * values, axis=-1, keepdims=True) + EPSILON)


def attend(
    tokens, gain, weight, query_gain, key_gain, cosine, sine, seg_row, seg_col,
    normed_out, raw_out, low_out, mixed_out, total_out, qkv,
):
    part = mixed_out.shape[1]
    values = tokens[...].astype(jnp.float32)
    normed = (values * norm_factor(values) * gain[...]).astype(jnp.bfloat16)
    normed_out[...] = normed
    qkv[...] = jnp.dot(normed, weight[...], preferred_element_type=jnp.float32)
    raw_out[...] = qkv[:, : 2 * part]
    low_out[:, 2 * part :] = qkv[:, 2 * part :].astype(jnp.bfloat16)
    allowed = seg_col[...] == seg_row[...]
    for head in range(part // HD):
        span = pl.ds(head * HD, HD)
        for offset, scale_gain, scale in ((0, query_gain, HD ** (-0.5)), (part, key_gain, 1.0)):
            raw = qkv[:, pl.ds(offset + head * HD, HD)]
            unit = raw * norm_factor(raw) * scale_gain[...]
            turned = unit * cosine[...] + pltpu.roll(unit, HD // 2, 1) * sine[...]
            low_out[:, pl.ds(offset + head * HD, HD)] = (turned * scale).astype(jnp.bfloat16)
        query, key = low_out[:, span], low_out[:, pl.ds(part + head * HD, HD)]
        scores = jnp.where(allowed, nt_dot(query, key), -1e30)
        top = jnp.max(scores, axis=-1, keepdims=True)
        shifted = jnp.exp(scores - top)
        total = jnp.sum(shifted, axis=-1, keepdims=True)
        probs = (shifted / total).astype(jnp.bfloat16)
        mixed = jnp.dot(
            probs, low_out[:, pl.ds(2 * part + head * HD, HD)], preferred_element_type=jnp.float32
        )
        mixed_out[:, span] = mixed.astype(jnp.bfloat16)
        total_out[:, head : head + 1] = top + jnp.log(total)


def unpack_kernel(gate0, gate1, up0, up1, down0, down1, gate_out, up_out, down_out):
    for index, group in enumerate(((gate0, up0, down0), (gate1, up1, down1))):

        @pl.when(pl.program_id(0) == index)
        def _(group=group):
            for source, result in zip(group, (gate_out, up_out, down_out), strict=True):
                result[...] = source[...].astype(result.dtype)


def unpack_units(wides, downs):
    shards, part, lanes = wides[0].shape
    each = lanes // 2

    def held(index, e, s):
        return jnp.where(e == index, s, (shards - 1) * (1 - index))

    def wide_spec(index, which):
        return pl.BlockSpec((1, part, each), lambda e, s: (held(index, e, s), 0, which))

    def down_spec(index):
        return pl.BlockSpec((1, each, part), lambda e, s: (held(index, e, s), 0, 0))

    wide_out = pl.BlockSpec((1, part, each), lambda e, s: (e, 0, s))
    shape = jax.ShapeDtypeStruct((2, part, shards * each), jnp.float32)
    return pl.pallas_call(
        unpack_kernel,
        grid=(2, shards),
        in_specs=[wide_spec(index, which) for which in range(2) for index in range(2)]
        + [down_spec(index) for index in range(2)],
        out_specs=[wide_out, wide_out, pl.BlockSpec((1, each, part), lambda e, s: (e, s, 0))],
        out_shape=[shape, shape, jax.ShapeDtypeStruct((2, shards * each, part), jnp.float32)],
        compiler_params=vmem_params(24),
    )(wides[0], wides[1], wides[0], wides[1], *downs)


def mark_kept(small_all, first, experts, own, capacity, bits, shards, keep_out):
    devices, _, rows = small_all.shape
    row = lax.broadcasted_iota(jnp.int32, (devices, rows), 0)
    group = lax.rem(row, shards)
    for index in range(own):
        order = jnp.zeros((devices, rows), jnp.float32)
        for expert in range(experts):
            high = small_all[:, expert, :].astype(jnp.float32)
            low = small_all[:, experts + expert, :].astype(jnp.float32)
            order = order + jnp.where(first + index == expert, high * 256.0 + low, 0.0)
        there = order > 0.0
        bound = jnp.zeros_like(order)
        for bit in reversed(range(bits)):
            trial = bound + float(1 << bit)
            within = jnp.where(there & (order <= trial), 1.0, 0.0)
            for shard in range(shards):
                here = group == shard
                count = jnp.sum(jnp.where(here, within, 0.0), keepdims=True)
                bound = jnp.where(here & (count <= float(capacity)), trial, bound)
        kept = jnp.where(there & (order <= bound), 1.0, 0.0).T
        for block in range(devices):
            place = keep_out.at[block // shards, pl.ds(block % shards * rows, rows)]
            place[:, index : index + 1] = kept[:, block : block + 1]


CORE, XBIT, YBIT = 1, 2, 4


MESH = pl.DeviceIdType.MESH


def held_in_hbm(*values):
    return [pltpu.with_memory_space_constraint(value, pltpu.HBM) for value in values]


class Wires:
    def __init__(self, send, recv):
        self.send, self.recv, self.used = send, recv, 0
        self.device, self.shard = lax.axis_index(EXPERT), lax.axis_index(SHARD)

    def slot(self):
        self.used += 1
        return self.used - 1

    def peer(self, bits=0, step=0, shards=1):
        shard = lax.rem(self.shard + step, shards) if step else self.shard
        return (self.device ^ bits, shard)

    def copy(self, source, target, slot, peer):
        return pltpu.make_async_remote_copy(
            src_ref=source,
            dst_ref=target,
            send_sem=self.send.at[slot],
            recv_sem=self.recv.at[slot],
            device_id=peer,
            device_id_type=MESH,
        )


def greet(peers):
    barrier = pltpu.get_barrier_semaphore()
    for peer in peers:
        pl.semaphore_signal(barrier, inc=1, device_id=peer, device_id_type=MESH)
    pl.semaphore_wait(barrier, len(peers))


class Relay:
    def __init__(self, wires, shards, views):
        self.wires, self.shards, self.views = wires, shards, views
        self.slots = [[[wires.slot() for _ in views] for _ in range(shards - 1)] for _ in range(2)]

    def copies(self, way, step, block):
        wires = self.wires
        peer = (wires.device, wires.shard + (1 if way == 0 else -1))
        return [
            wires.copy(view(block), view(block), slot, peer)
            for view, slot in zip(self.views, self.slots[way][step], strict=True)
        ]

    def has(self, way, step):
        shard = self.wires.shard
        return shard - step >= 0 if way == 0 else shard + step < self.shards

    def sends(self, way, step):
        shard = self.wires.shard
        edge = shard < self.shards - 1 if way == 0 else shard > 0
        return jnp.logical_and(edge, self.has(way, step))

    def block(self, way, step):
        return self.wires.shard + (-step if way == 0 else step)

    def run(self, step, first=None):
        wires = self.wires
        for index, view in enumerate(self.views):
            for way in range(2):
                block = self.block(way, step)
                peer = (wires.device, wires.shard + (1 if way == 0 else -1))
                if step > 0:

                    @pl.when(self.has(way, step))
                    def _(way=way, block=block, index=index, view=view, peer=peer):
                        slot = self.slots[way][step - 1][index]
                        wires.copy(view(block), view(block), slot, peer).wait_recv()

                if step < self.shards - 1:

                    @pl.when(self.sends(way, step))
                    def _(way=way, block=block, index=index, view=view, peer=peer):
                        source = view(block) if first is None else first[index]
                        slot = self.slots[way][step][index]
                        wires.copy(source, view(block), slot, peer).start()

    def drain(self):
        for way in range(2):
            for step in range(self.shards - 1):

                @pl.when(self.sends(way, step))
                def _(way=way, step=step):
                    for copy in self.copies(way, step, self.block(way, step)):
                        copy.wait_send()


class Plane:
    def __init__(self, wires, views, whole):
        self.wires, self.views, self.whole = wires, views, whole
        count = len(views)
        self.first = [[wires.slot() for _ in range(count)] for _ in range(2)]
        self.second = [[[wires.slot() for _ in range(count)] for _ in range(2)] for _ in range(2)]
        self.last = [[wires.slot() for _ in range(count)] for _ in range(4)]
        self.sent = []

    def start(self, copies):
        for copy in copies:
            copy.start()
        self.sent += copies

    def one(self, owner, half, bits, slots):
        wires = self.wires
        return [
            wires.copy(view(owner, half), view(owner, half), slot, wires.peer(bits))
            for view, slot in zip(self.views, slots, strict=True)
        ]

    def step_one(self):
        me = self.wires.device
        for half, bits in enumerate((XBIT, YBIT)):
            self.start(self.one(me, half, bits, self.first[half]))

    def step_two(self):
        me = self.wires.device
        for half, bits in enumerate((XBIT, YBIT)):
            for copy in self.one(me ^ bits, half, bits, self.first[half]):
                copy.wait_recv()
        for half, bits in enumerate((XBIT, YBIT)):
            other = (XBIT | YBIT) ^ bits
            self.start(self.one(me, half, other, self.second[half][0]))
            self.start(self.one(me ^ bits, half, other, self.second[half][1]))

    def cores(self, index):
        wires = self.wires
        owner = wires.device ^ (0, XBIT, YBIT, XBIT | YBIT)[index]
        return [
            wires.copy(place(owner), place(owner), slot, wires.peer(CORE))
            for place, slot in zip(self.whole, self.last[index], strict=True)
        ]

    def step_three(self):
        me = self.wires.device
        for half, bits in enumerate((XBIT, YBIT)):
            other = (XBIT | YBIT) ^ bits
            for owner, slots in ((me ^ other, 0), (me ^ other ^ bits, 1)):
                for copy in self.one(owner, half, other, self.second[half][slots]):
                    copy.wait_recv()
        for index in range(1, 4):
            self.start(self.cores(index))

    def finish(self):
        for index, bits in enumerate((0, XBIT, YBIT, XBIT | YBIT)):
            owner = self.wires.device ^ CORE ^ bits
            for place, slot in zip(self.whole, self.last[index], strict=True):
                self.wires.copy(
                    place(owner), place(owner), slot, self.wires.peer(CORE)
                ).wait_recv()
        for copy in self.sent:
            copy.wait_send()


def opening_kernel(
    shards, planes, experts, own_experts, capacity, bits,
    routes, order, gains, seg_row, seg_col, cosine, sine,
    router, w_query, w_key, w_value, tokens, w_out, out_grad,
    kept_out, attn_row, ffn_row, query_row, key_row, normed_out, raw_out, low_out, total_out, mixed_all,
    router_all, qkv_w_out, tokens_all, out_w_out, grad_out,
    small, small_all, grad_all, qkv_w, out_w, mixed, qkv, send, recv, local, store,
):
    wires = Wires(send, recv)
    device, shard = wires.device, wires.shard
    weights = (w_query, w_key, w_value)
    block, width = w_query.shape
    rows = tokens.shape[0]
    part = width // shards
    mine = device * shards + shard
    greet(
        [wires.peer(step=step, shards=shards) for step in range(1, shards)]
        + [wires.peer(XBIT), wires.peer(YBIT), wires.peer(CORE)]
    )

    def place(source_shard, which):
        start = pl.multiple_of((device * shards + source_shard) * block, block)
        return qkv_w.at[pl.ds(start, block), pl.ds(which * part, part)]

    def cut(which, target):
        return weights[which].at[:, pl.ds(pl.multiple_of(target * part, part), part)]

    def token_rows(b):
        return tokens_all.at[pl.ds(pl.multiple_of(b * rows, rows), rows)]

    def out_rows(owner, source):
        return out_w.at[pl.ds(pl.multiple_of((owner * shards + source) * block, block), block)]

    def grad_block(owner, source):
        return (owner * shards + source) * rows

    def grad_rows(owner, source):
        return grad_all.at[pl.ds(pl.multiple_of(grad_block(owner, source), rows), rows)]

    def grad_half(source):
        def view(owner, half):
            start = grad_block(owner, source) + half * (rows // 2)
            return grad_all.at[pl.ds(pl.multiple_of(start, rows // 2), rows // 2)]

        return view

    exchange = [[wires.slot() for _ in range(5)] for _ in range(1, shards)]
    sent = []
    for step in range(1, shards):
        peer = wires.peer(step=step, shards=shards)
        slots = exchange[step - 1]
        copies = [
            wires.copy(cut(which, peer[1]), place(shard, which), slots[which], peer)
            for which in range(3)
        ]
        copies.append(wires.copy(router, router_all.at[mine], slots[4], peer))
        for copy in copies:
            copy.start()
        sent += copies
    grad_line = Relay(wires, shards, [lambda b: grad_rows(device, b)])
    token_line = Relay(wires, shards, [token_rows])
    out_line = Relay(wires, shards, [lambda b: out_rows(device, b)])
    mixed_line = Relay(wires, shards, [lambda b: mixed_all.at[b]])
    own = [
        pltpu.make_async_copy(out_grad, grad_rows(device, shard), local.at[0]),
        pltpu.make_async_copy(router, router_all.at[mine], local.at[1]),
        pltpu.make_async_copy(tokens, token_rows(shard), local.at[2]),
        pltpu.make_async_copy(w_out, out_rows(device, shard), local.at[3]),
    ]
    own += [
        pltpu.make_async_copy(cut(which, shard), place(shard, which), local.at[4 + which])
        for which in range(3)
    ]
    for copy in own:
        copy.start()
    turns = [shard] + [
        sum(jnp.where(shard == index, source, 0) for index, source in enumerate(row))
        for row in ((1, 0, 1, 2), (2, 2, 3, 1), (3, 3, 0, 0))
    ]
    stages = [
        Plane(wires, [grad_half(source)], [lambda owner, source=source: grad_rows(owner, source)])
        for source in turns
    ]
    stored = []

    def begin(stage):
        stage.step_one()
        stage.start(stage.cores(0))

    def keep(turn):
        stages[turn].finish()
        for owner in range(planes):
            start = pl.multiple_of(grad_block(owner, turns[turn]), rows)
            copy = pltpu.make_async_copy(
                grad_rows(owner, turns[turn]),
                grad_out.at[pl.ds(start, rows)],
                store.at[turn * planes + owner],
            )
            copy.start()
            stored.append(copy)

    own[0].wait()
    begin(stages[0])
    column = lax.broadcasted_iota(jnp.int32, (rows, 128), 1)
    dense = jnp.zeros((rows, 128), jnp.int32)
    for choice in range(routes.shape[1]):
        named = routes[:, choice : choice + 1] == column
        dense = dense + jnp.where(named, order[:, choice : choice + 1] + 1, 0)
    high = lax.shift_right_logical(dense, 8)
    for start, digits in ((0, high), (experts, dense - high * 256)):
        turned = digits.astype(jnp.float32).T
        small[pl.ds(start, experts), :] = turned[:experts, :].astype(small.dtype)
    small[pl.ds(2 * experts, gains.shape[0]), :] = gains[...]
    small_all[mine] = small[...]
    for step in range(1, shards):
        peer = wires.peer(step=step, shards=shards)
        copy = wires.copy(small, small_all.at[mine], exchange[step - 1][3], peer)
        copy.start()
        sent.append(copy)
    out_line.run(0, (w_out,))
    token_line.run(0, (tokens,))
    stages[0].step_two()
    for copy in own[1:]:
        copy.wait()
    for step in range(1, shards):
        peer = wires.peer(step=shards - step, shards=shards)
        source = peer[1]
        slots = exchange[step - 1]
        for which in range(3):
            wires.copy(place(source, which), place(source, which), slots[which], peer).wait_recv()
        wires.copy(router, router_all.at[device * shards + source], slots[4], peer).wait_recv()
        wires.copy(small, small_all.at[device * shards + source], slots[3], peer).wait_recv()

    each = shards * block // 2

    def rows_of(owner, half):
        return qkv_w.at[pl.ds(pl.multiple_of((owner * 2 + half) * each, each), each)]

    def small_of(owner, half):
        return small_all.at[pl.ds((owner * 2 + half) * (shards // 2), shards // 2)]

    def router_of(owner, half):
        return router_all.at[pl.ds((owner * 2 + half) * (shards // 2), shards // 2)]

    plane = Plane(
        wires,
        [rows_of, small_of, router_of],
        [
            lambda owner: qkv_w.at[pl.ds(pl.multiple_of(owner * 2 * each, 2 * each), 2 * each)],
            lambda owner: small_all.at[pl.ds(owner * shards, shards)],
            lambda owner: router_all.at[pl.ds(owner * shards, shards)],
        ],
    )
    outs = [
        Plane(
            wires,
            [
                lambda owner, side, index=index: out_w.at[
                    pl.ds(
                        pl.multiple_of(owner * 2 * each + index * each + side * (each // 2), each // 2),
                        each // 2,
                    )
                ]
            ],
            [
                lambda owner, index=index: out_w.at[
                    pl.ds(pl.multiple_of((owner * 2 + index) * each, each), each)
                ]
            ],
        )
        for index in range(2)
    ]
    begin(plane)
    stages[0].step_three()
    out_line.run(1)
    token_line.run(1)
    plane.step_two()
    out_line.run(2)
    token_line.run(2)
    grad_line.run(0, (out_grad,))
    plane.step_three()
    keep(0)
    out_line.run(3)
    for stage in outs:
        begin(stage)
    plane.finish()

    count = width // 128
    start = 2 * experts
    summed = small_all[0, pl.ds(start, gains.shape[0]), :].astype(jnp.float32)
    for other in range(1, planes * shards):
        summed = summed + small_all[other, pl.ds(start, gains.shape[0]), :].astype(jnp.float32)
    attn_row[...] = jnp.concatenate([summed[i : i + 1] for i in range(count)], axis=1)
    ffn_row[...] = jnp.concatenate([summed[count + i : count + i + 1] for i in range(count)], axis=1)
    query_row[...] = summed[2 * count : 2 * count + 1]
    key_row[...] = summed[2 * count + 1 : 2 * count + 2]
    for stage in outs:
        stage.step_two()
    token_line.run(3)
    attend(
        tokens_all, attn_row, qkv_w, query_row, key_row, cosine, sine, seg_row, seg_col,
        normed_out, raw_out, low_out, mixed, total_out, qkv,
    )
    mixed_line.run(0, (mixed,))
    mixed_all[shard] = mixed[...]
    save_qkv = pltpu.make_async_copy(qkv_w, qkv_w_out, local.at[7])
    save_qkv.start()
    grad_line.run(1)
    begin(stages[1])
    for stage in outs:
        stage.step_three()
    mixed_line.run(1)
    stages[1].step_two()
    grad_line.run(2)
    begin(stages[2])
    for stage in outs:
        stage.finish()
    save_out = pltpu.make_async_copy(out_w, out_w_out, local.at[8])
    save_out.start()
    mixed_line.run(2)
    stages[1].step_three()
    stages[2].step_two()
    mark_kept(
        small_all, device * own_experts, experts, own_experts, capacity, bits, shards, kept_out
    )
    grad_line.run(3)
    begin(stages[3])
    stages[2].step_three()
    keep(1)
    mixed_line.run(3)
    stages[3].step_two()
    keep(2)
    stages[3].step_three()
    keep(3)
    for copy in sent:
        copy.wait_send()
    for group in (token_line, grad_line, out_line, mixed_line):
        group.drain()
    for copy in stored:
        copy.wait()
    save_qkv.wait()
    save_out.wait()


def opening_call(
    routes, order, gains, seg_row, seg_col, tables, router, w_query, w_key, w_value, tokens, w_out, out_grad,
    experts, own_experts, capacity, planes, shards,
):
    block, width = w_query.shape
    rows, top_count = routes.shape
    seq, part = shards * rows, width // shards
    hbm = pl.BlockSpec(memory_space=pltpu.HBM)
    vmem = pl.BlockSpec(memory_space=pltpu.VMEM)
    place = pl.BlockSpec(memory_space=pl.ANY)
    slots = 144
    low, full = tokens.dtype, jnp.float32
    small = (2 * experts + gains.shape[0], 128)
    most = planes * shards * rows * top_count
    return pl.pallas_call(
        functools.partial(
            opening_kernel, shards, planes, experts, own_experts, capacity, most.bit_length()
        ),
        in_specs=[vmem] * 7 + [place] * 7,
        out_specs=[vmem] * 10 + [place, hbm, vmem, hbm, hbm],
        out_shape=(
            jax.ShapeDtypeStruct((planes, seq, own_experts), full),
            jax.ShapeDtypeStruct((1, width), full),
            jax.ShapeDtypeStruct((1, width), full),
            jax.ShapeDtypeStruct((1, HD), full),
            jax.ShapeDtypeStruct((1, HD), full),
            jax.ShapeDtypeStruct((seq, width), low),
            jax.ShapeDtypeStruct((seq, 2 * part), full),
            jax.ShapeDtypeStruct((seq, 3 * part), low),
            jax.ShapeDtypeStruct((seq, 128), full),
            jax.ShapeDtypeStruct((shards, seq, part), low),
            jax.ShapeDtypeStruct((planes * shards,) + router.shape, router.dtype),
            pltpu.HBM((width, 3 * part), low),
            jax.ShapeDtypeStruct((seq, width), low),
            pltpu.HBM((width, width), low),
            pltpu.HBM((planes * seq, width), low),
        ),
        scratch_shapes=[
            pltpu.VMEM(small, gains.dtype),
            pltpu.VMEM((planes * shards,) + small, gains.dtype),
            pltpu.VMEM((planes * seq, width), low),
            pltpu.VMEM((width, 3 * part), low),
            pltpu.VMEM((width, width), low),
            pltpu.VMEM((seq, part), low),
            pltpu.VMEM((seq, 3 * part), full),
            pltpu.SemaphoreType.DMA((slots,)),
            pltpu.SemaphoreType.DMA((slots,)),
            pltpu.SemaphoreType.DMA((9,)),
            pltpu.SemaphoreType.DMA((planes * shards,)),
        ],
        compiler_params=pltpu.CompilerParams(
            collective_id=1, has_side_effects=True, vmem_limit_bytes=60 * MIB
        ),
        cost_estimate=pl.CostEstimate(flops=0, bytes_accessed=200 * MIB, transcendentals=0),
    )(
        routes, order, gains, seg_row, seg_col, *tables, router, w_query, w_key, w_value, tokens, w_out, out_grad
    )


class Units:
    def __init__(self, wires, shards, index, gate, up, down, wide_w, down_w, local, base):
        self.wires, self.shards, self.index = wires, shards, index
        self.gate, self.up, self.down, self.wide_w, self.down_w = gate, up, down, wide_w, down_w
        self.local, self.base = local, base
        self.slots = [[wires.slot() for _ in range(3)] for _ in range(1, shards)]

    def pairs(self, source, target):
        each = self.down_w.shape[1]
        span = pl.ds(pl.multiple_of(target * each, each), each)
        return [
            (self.gate.at[self.index, :, span], self.wide_w.at[source, :, pl.ds(0, each)]),
            (self.up.at[self.index, :, span], self.wide_w.at[source, :, pl.ds(each, each)]),
            (self.down.at[self.index, span, :], self.down_w.at[source]),
        ]

    def own(self):
        shard = self.wires.shard
        return [
            pltpu.make_async_copy(source, place, self.local.at[self.base + slot])
            for slot, (source, place) in enumerate(self.pairs(shard, shard))
        ]

    def sends(self):
        wires = self.wires
        for step in range(1, self.shards):
            peer = wires.peer(step=step, shards=self.shards)
            pairs = self.pairs(wires.shard, peer[1])
            for slot, (source, place) in zip(self.slots[step - 1], pairs, strict=True):
                yield wires.copy(source, place, slot, peer)

    def begin(self):
        for copy in self.own():
            copy.start()
        for copy in self.sends():
            copy.start()

    def end(self):
        wires = self.wires
        for copy in self.own():
            copy.wait()
        for step in range(1, self.shards):
            back = wires.peer(step=self.shards - step, shards=self.shards)
            pairs = self.pairs(back[1], wires.shard)
            for slot, (_, place) in zip(self.slots[step - 1], pairs, strict=True):
                wires.copy(place, place, slot, back).wait_recv()
        for copy in self.sends():
            copy.wait_send()


def meeting_kernel(
    shards, planes, tokens, gain, mixed_all, out_w, gate, up, down,
    hidden_out, mixed_own, normed_out, wide_w, down_w, normed_all, send, recv, local, store,
):
    wires = Wires(send, recv)
    device, shard = wires.device, wires.shard
    seq, _ = tokens.shape
    rows, part = hidden_out.shape[0], mixed_all.shape[2]
    half = seq // 2
    greet(
        [wires.peer(step=step, shards=shards) for step in range(1, shards)]
        + [wires.peer(XBIT), wires.peer(YBIT), wires.peer(CORE)]
    )
    units = Units(wires, shards, 0, gate, up, down, wide_w, down_w, local, 0)
    units.begin()

    def stage(index):
        def view(owner, start, size):
            return normed_all.at[owner, pl.ds(start, size)]

        return Plane(
            wires,
            [lambda owner, side: view(owner, index * half + side * (half // 2), half // 2)],
            [lambda owner: view(owner, index * half, half)],
        )

    stages = [stage(index) for index in range(2)]
    for side in range(2):
        span = pl.ds(side * half, half)
        total = tokens[span, :].astype(jnp.float32)
        for source in range(shards):
            total = total + jnp.dot(
                mixed_all[source, span, :],
                out_w[pl.ds(source * part, part), :],
                preferred_element_type=jnp.float32,
            )
        normed_all[device, span, :] = (total * norm_factor(total) * gain[...]).astype(
            normed_all.dtype
        )
        stages[side].step_one()
        stages[side].start(stages[side].cores(0))
        for inner in range(half // rows):

            @pl.when(shard == side * (half // rows) + inner)
            def _(total=total, inner=inner):
                hidden_out[...] = total[inner * rows : (inner + 1) * rows, :]

    stored = []

    def keep(owner, side):
        span = pl.ds(side * half, half)
        copy = pltpu.make_async_copy(
            normed_all.at[owner, span], normed_out.at[owner, span], store.at[len(stored)]
        )
        copy.start()
        stored.append(copy)

    for source in range(shards):
        mixed_own[:, pl.ds(source * part, part)] = mixed_all[
            source, pl.ds(pl.multiple_of(shard * rows, rows), rows), :
        ]
    for plane in stages:
        plane.step_two()
    for side, plane in enumerate(stages):
        plane.step_three()
        for chip in range(4):
            keep(device ^ (2 * chip), side)
    for side, plane in enumerate(stages):
        plane.finish()
        for chip in range(4):
            keep(device ^ (2 * chip + 1), side)
    units.end()
    for copy in stored:
        copy.wait()


def unit_shapes(gate, shards):
    _, part, hidden_units = gate.shape
    each = hidden_units // shards
    return (
        jax.ShapeDtypeStruct((shards, part, 2 * each), gate.dtype),
        jax.ShapeDtypeStruct((shards, each, part), gate.dtype),
    )


def meeting_call(tokens, gain, mixed_all, out_w, gate, up, down, planes, shards):
    hbm = pl.BlockSpec(memory_space=pltpu.HBM)
    vmem = pl.BlockSpec(memory_space=pltpu.VMEM)
    seq, width = tokens.shape
    rows = seq // shards
    slots = 32
    low = tokens.dtype
    return pl.pallas_call(
        functools.partial(meeting_kernel, shards, planes),
        in_specs=[vmem] * 4 + [hbm] * 3,
        out_specs=[vmem] * 2 + [hbm] * 3,
        out_shape=(
            jax.ShapeDtypeStruct((rows, width), jnp.float32),
            jax.ShapeDtypeStruct((rows, width), low),
            pltpu.HBM((planes, seq, width), low),
        )
        + unit_shapes(gate, shards),
        scratch_shapes=[
            pltpu.VMEM((planes, seq, width), low),
            pltpu.SemaphoreType.DMA((slots,)),
            pltpu.SemaphoreType.DMA((slots,)),
            pltpu.SemaphoreType.DMA((3,)),
            pltpu.SemaphoreType.DMA((2 * planes,)),
        ],
        compiler_params=pltpu.CompilerParams(
            collective_id=3, has_side_effects=True, vmem_limit_bytes=40 * MIB
        ),
        cost_estimate=pl.CostEstimate(
            flops=2 * seq * width * width, bytes_accessed=300 * MIB, transcendentals=0
        ),
    )(tokens, gain, mixed_all, out_w, gate, up, down)


def add_rows(target, sources, lines):
    rows = target.shape[0]

    def body(index, carry):
        span = pl.ds(pl.multiple_of(index * lines, lines), lines)
        total = target[span, :].astype(jnp.float32)
        for source in sources:
            total = total + source[span, :].astype(jnp.float32)
        target[span, :] = total.astype(target.dtype)
        return carry

    lax.fori_loop(0, rows // lines, body, 0)


class PlaneSum:
    def __init__(self, wires, part, held, came, diag, side, local, base):
        self.wires, self.part, self.local, self.base = wires, part, local, base
        self.held, self.came, self.diag, self.side = held, came, diag, side
        self.half = held.shape[1] // 2
        self.core = [wires.slot() for _ in range(4)]
        self.corner = [wires.slot() for _ in range(2)]
        self.edge = [wires.slot() for _ in range(2)]
        self.sent = []

    def start(self, copy):
        copy.start()
        self.sent.append(copy)

    def load(self, chip):
        return pltpu.make_async_copy(
            self.part(chip, 0), self.held.at[chip], self.local.at[self.base + chip]
        )

    def give(self, chip):
        self.start(
            self.wires.copy(
                self.held.at[chip], self.came.at[chip], self.core[chip], self.wires.peer(CORE)
            )
        )

    def begin(self):
        for chip in (3, 1, 2, 0):
            self.load(chip).start()
            self.start(
                self.wires.copy(
                    self.part(chip, 1), self.came.at[chip], self.core[chip], self.wires.peer(CORE)
                )
            )

    def add_core(self, chip):
        if self.part is not None:
            self.load(chip).wait()
        place = self.came.at[chip]
        self.wires.copy(place, place, self.core[chip], self.wires.peer(CORE)).wait_recv()
        add_rows(self.held.at[chip], [place], 64)

    def part_of_corner(self, which):
        return self.held.at[3, pl.ds(which * self.half, self.half)]

    def send_corner(self):
        self.add_core(3)
        for which, bits in enumerate((XBIT, YBIT)):
            self.start(
                self.wires.copy(
                    self.part_of_corner(which),
                    self.diag.at[which],
                    self.corner[which],
                    self.wires.peer(bits),
                )
            )

    def add_cores(self):
        for chip in (1, 2, 0):
            self.add_core(chip)

    def send_sides(self):
        for which, (bits, chip) in enumerate(((XBIT, 2), (YBIT, 1))):
            place = self.diag.at[which]
            self.wires.copy(place, place, self.corner[which], self.wires.peer(bits)).wait_recv()
            add_rows(self.held.at[chip, pl.ds(which * self.half, self.half)], [place], 64)
            self.start(
                self.wires.copy(
                    self.held.at[chip],
                    self.side.at[1 - which],
                    self.edge[1 - which],
                    self.wires.peer((XBIT | YBIT) ^ bits),
                )
            )

    def end(self):
        for which, bits in enumerate((XBIT, YBIT)):
            place = self.side.at[which]
            self.wires.copy(place, place, self.edge[which], self.wires.peer(bits)).wait_recv()
        add_rows(self.held.at[0], [self.side.at[0], self.side.at[1]], 64)

    def drain(self):
        for copy in self.sent:
            copy.wait_send()


class LineSum:
    def __init__(self, wires, shards, source, landing):
        self.wires, self.shards, self.source, self.landing = wires, shards, source, landing
        self.slots = [wires.slot() for _ in range(shards - 1)]

    def sends(self):
        wires = self.wires
        for step in range(1, self.shards):
            peer = wires.peer(step=step, shards=self.shards)
            yield wires.copy(
                self.source(peer[1]), self.landing(wires.shard), self.slots[step - 1], peer
            )

    def begin(self):
        for copy in self.sends():
            copy.start()

    def arrive(self):
        wires = self.wires
        for step in range(1, self.shards):
            peer = wires.peer(step=self.shards - step, shards=self.shards)
            place = self.landing(peer[1])
            wires.copy(place, place, self.slots[step - 1], peer).wait_recv()

    def drain(self):
        for copy in self.sends():
            copy.wait_send()


def line_total(landing, shards):
    total = landing[0].astype(jnp.float32)
    for shard in range(1, shards):
        total = total + landing[shard].astype(jnp.float32)
    return total


def aligned(index, size):
    return pl.ds(pl.multiple_of(index * size, size), size)


def expert_kernel(
    index, experts, shards, x, g, keep, wide_w, router_w, down_w, hot, *refs
):
    if index == 0:
        gate, up, down, out, grad, pull, wide_sum, down_sum, next_wide, next_down = refs[:10]
        acc, dacc, wide_out, down_out, send, recv, local, sems = refs[10:]
    else:
        old_out, old_grad, old_pull, wide_sent, down_sent = refs[:5]
        out, grad, wide_sum, down_sum, router_sum, wide_came, down_came = refs[5:12]
        acc, racc, dacc, wide_out, down_out, send, recv, local, sems = refs[12:]
    step, steps = pl.program_id(0), pl.num_programs(0)
    wires = Wires(send, recv)
    if index == 0:
        travel = [Units(wires, shards, 1, gate, up, down, next_wide, next_down, local, 0)]
    else:
        travel = [
            LineSum(wires, shards, lambda t: wide_sent.at[t], lambda s: wide_came.at[s]),
            LineSum(wires, shards, lambda t: down_sent.at[t], lambda s: down_came.at[s]),
        ]
        stay = [
            pltpu.make_async_copy(
                sent.at[wires.shard], came.at[wires.shard], local.at[place]
            )
            for place, (sent, came) in enumerate(((wide_sent, wide_came), (down_sent, down_came)))
        ]

    @pl.when(step == 0)
    def _():
        greet([wires.peer(step=hop, shards=shards) for hop in range(1, shards)])
        for group in travel:
            group.begin()
        acc[...] = jnp.zeros_like(acc)
        dacc[...] = jnp.zeros_like(dacc)
        if index == 1:
            for copy in stay:
                copy.start()
            racc[...] = jnp.zeros_like(racc)

    _, each, part = down_w.shape
    wide = jnp.dot(x[...], wide_w[...], preferred_element_type=jnp.float32)
    back = nt_dot(g[:, :part], down_w[0])
    for shard in range(1, shards):
        back = back + nt_dot(g[:, shard * part : (shard + 1) * part], down_w[shard])
    if index == 0:
        logits = jnp.dot(x[...], router_w[...], preferred_element_type=jnp.float32)
        lane = lax.broadcasted_iota(jnp.int32, logits.shape, 1)
        logits = jnp.where(lane < experts, logits, -1e30)
        shifted = jnp.exp(logits - jnp.max(logits, axis=-1, keepdims=True))
        probs = shifted / jnp.sum(shifted, axis=-1, keepdims=True)
    else:
        lane = lax.broadcasted_iota(jnp.int32, old_pull.shape, 1)
        probs = jnp.where(lane < experts, old_pull[...], 0.0)
    mark = hot[index : index + 1, :]
    kept = keep[:, index : index + 1]
    route = jnp.sum(probs * mark, axis=-1, keepdims=True) * kept
    gated, lifted = wide[:, :each], wide[:, each:]
    sigma = 1.0 / (1.0 + jnp.exp(-gated))
    silu = gated * sigma
    act = silu * lifted
    pulled = jnp.sum(act * back, axis=-1, keepdims=True) * kept
    act_low = (act * route).astype(jnp.bfloat16)
    act_grad = back * route
    wide_low = jnp.concatenate(
        [
            (act_grad * lifted * sigma * (1.0 + gated * (1.0 - sigma))).astype(jnp.bfloat16),
            (act_grad * silu).astype(jnp.bfloat16),
        ],
        axis=1,
    )
    result = nt_dot(wide_low, wide_w[...])
    if index == 0:
        pull[...] = jnp.where(lane < experts, probs, jnp.where(lane == 127, pulled, 0.0))
    else:
        dense = pulled * mark + old_pull[:, 127:] * hot[0:1, :]
        logit_grad = probs * (dense - jnp.sum(probs * dense, axis=-1, keepdims=True))
        logit_low = logit_grad.astype(jnp.bfloat16)
        result = result + nt_dot(logit_low, router_w[...]) + old_grad[...].astype(jnp.float32)
        racc[...] += tn_dot(x[...], logit_low)
    grad[...] = result.astype(jnp.bfloat16)
    for shard in range(shards):
        span = slice(shard * part, (shard + 1) * part)
        value = jnp.dot(act_low, down_w[shard], preferred_element_type=jnp.float32)
        if index == 1:
            value = value + old_out[:, span].astype(jnp.float32)
        out[:, span] = value.astype(jnp.bfloat16)
        dacc[shard] += tn_dot(act_low, g[:, span])
    acc[...] += tn_dot(x[...], wide_low)

    @pl.when(step == steps - 1)
    def _():
        wide_out[...] = acc[...].astype(jnp.bfloat16)
        wide_copy = pltpu.make_async_copy(wide_out, wide_sum, sems.at[0])
        wide_copy.start()
        down_out[...] = dacc[...].astype(jnp.bfloat16)
        down_copy = pltpu.make_async_copy(down_out, down_sum, sems.at[1])
        down_copy.start()
        if index == 1:
            router_copy = pltpu.make_async_copy(racc, router_sum, sems.at[2])
            router_copy.start()
            router_copy.wait()
        wide_copy.wait()
        down_copy.wait()
        if index == 0:
            travel[0].end()
        else:
            for copy in stay:
                copy.wait()
            for group in travel:
                group.arrive()
                group.drain()


def expert_call(index, x_all, g_all, keep, wide_w, router_w, down_w, hot, experts, weights, before):
    planes, rows, width = x_all.shape
    shards = down_w.shape[0]
    tile = 512
    per = rows // tile
    hbm = pl.BlockSpec(memory_space=pltpu.HBM)

    def whole(value):
        zeros = (0,) * value.ndim
        return pl.BlockSpec(value.shape, lambda i: zeros, pipeline_mode=pl.Buffered(1))

    def rowwise(lanes):
        return pl.BlockSpec((None, tile, lanes), lambda i: (i // per, i % per, 0))

    low = jnp.bfloat16
    tall = pltpu.HBM((planes, rows, width), low)
    narrow = pltpu.HBM((planes, rows, 128), jnp.float32)
    wide_shape = pltpu.HBM(wide_w.shape, low)
    down_shape = pltpu.HBM(down_w.shape, low)
    came = pltpu.HBM((shards, width // shards, wide_w.shape[1]), low)
    if index == 0:
        extra = [hbm] * 3
        out_specs = [rowwise(width)] * 2 + [rowwise(128)] + [hbm] * 4
        shapes = (tall, tall, narrow, wide_shape, down_shape, came, down_shape)
        operands = held_in_hbm(*weights)
    else:
        extra = [rowwise(width)] * 2 + [rowwise(128)] + [hbm] * 2
        out_specs = [rowwise(width)] * 2 + [hbm] * 5
        router_shape = pltpu.HBM(router_w.shape, jnp.float32)
        shapes = (tall, tall, wide_shape, down_shape, router_shape, came, down_shape)
        operands = held_in_hbm(*before)
    return pl.pallas_call(
        functools.partial(expert_kernel, index, experts, shards),
        grid=(planes * per,),
        in_specs=[
            rowwise(width),
            rowwise(width),
            rowwise(keep.shape[2]),
            whole(wide_w),
            whole(router_w),
            whole(down_w),
            whole(hot),
        ]
        + extra,
        out_specs=out_specs,
        scratch_shapes=[pltpu.VMEM(wide_w.shape, jnp.float32)]
        + ([] if index == 0 else [pltpu.VMEM(router_w.shape, jnp.float32)])
        + [
            pltpu.VMEM(down_w.shape, jnp.float32),
            pltpu.VMEM(wide_w.shape, low),
            pltpu.VMEM(down_w.shape, low),
            pltpu.SemaphoreType.DMA((12,)),
            pltpu.SemaphoreType.DMA((12,)),
            pltpu.SemaphoreType.DMA((3,)),
            pltpu.SemaphoreType.DMA((3,)),
        ],
        out_shape=shapes,
        compiler_params=pltpu.CompilerParams(
            collective_id=7 + index, has_side_effects=True, vmem_limit_bytes=52 * MIB
        ),
        cost_estimate=pl.CostEstimate(
            flops=planes * rows * width * 12 * down_w.shape[1],
            bytes_accessed=100 * MIB,
            transcendentals=planes * rows * down_w.shape[1],
        ),
    )(*held_in_hbm(x_all, g_all), keep, wide_w, router_w, down_w, hot, *operands)


def returning_kernel(
    shards, ins, outs, wide, down, in_total, out_total, wide_all, down_all,
    held, came, diag, side, held2, came2, diag2, side2, landing, send, recv, local,
):
    wires = Wires(send, recv)
    device, shard = wires.device, wires.shard
    rows = in_total.shape[0]
    greet(
        [wires.peer(step=step, shards=shards) for step in range(1, shards)]
        + [wires.peer(XBIT), wires.peer(YBIT), wires.peer(CORE)]
    )

    def rel(source):
        return lambda chip, core: source.at[device ^ (2 * chip + core)]

    grads = PlaneSum(wires, rel(ins), held, came, diag, side, local, 0)
    values = PlaneSum(wires, rel(outs), held2, came2, diag2, side2, local, 6)
    weights = [
        LineSum(wires, shards, lambda t: wide.at[t], lambda s: wide_all.at[s]),
        LineSum(wires, shards, lambda t: down.at[t], lambda s: down_all.at[s]),
    ]
    line = LineSum(
        wires, shards, lambda t: held.at[0, aligned(t, rows)], lambda s: landing.at[s]
    )
    grads.begin()
    for group in weights:
        group.begin()
    own = [
        pltpu.make_async_copy(wide.at[shard], wide_all.at[shard], local.at[4]),
        pltpu.make_async_copy(down.at[shard], down_all.at[shard], local.at[5]),
    ]
    for copy in own:
        copy.start()
    grads.send_corner()
    values.begin()
    grads.add_cores()
    grads.send_sides()
    values.send_corner()
    values.add_cores()
    grads.end()
    line.begin()
    values.send_sides()
    landing[shard] = held[0, aligned(shard, rows), :]
    line.arrive()
    in_total[...] = line_total(landing, shards)
    values.end()
    back = pltpu.make_async_copy(held2.at[0], out_total, local.at[10])
    back.start()
    for copy in own:
        copy.wait()
    back.wait()
    for group in weights:
        group.arrive()
    for group in (grads, values, line, *weights):
        group.drain()


def sum_work(rows, lanes):
    low = jnp.bfloat16
    return [
        pltpu.VMEM((4, rows, lanes), low),
        pltpu.VMEM((4, rows, lanes), low),
        pltpu.VMEM((2, rows // 2, lanes), low),
        pltpu.VMEM((2, rows, lanes), low),
    ]


def returning_call(ins, outs, wide, down):
    _, seq, width = ins.shape
    shards = wide.shape[0]
    rows = seq // shards
    hbm = pl.BlockSpec(memory_space=pltpu.HBM)
    vmem = pl.BlockSpec(memory_space=pltpu.VMEM)
    return pl.pallas_call(
        functools.partial(returning_kernel, shards),
        in_specs=[hbm] * 4,
        out_specs=[vmem, hbm, hbm, hbm],
        out_shape=(
            jax.ShapeDtypeStruct((rows, width), jnp.float32),
            jax.ShapeDtypeStruct((seq, width), jnp.bfloat16),
            pltpu.HBM(wide.shape, wide.dtype),
            pltpu.HBM(down.shape, down.dtype),
        ),
        scratch_shapes=sum_work(seq, width)
        + sum_work(seq, width)
        + [
            pltpu.VMEM((shards, rows, width), jnp.bfloat16),
            pltpu.SemaphoreType.DMA((36,)),
            pltpu.SemaphoreType.DMA((36,)),
            pltpu.SemaphoreType.DMA((11,)),
        ],
        compiler_params=pltpu.CompilerParams(
            collective_id=4, has_side_effects=True, vmem_limit_bytes=56 * MIB
        ),
        cost_estimate=pl.CostEstimate(flops=0, bytes_accessed=300 * MIB, transcendentals=0),
    )(*held_in_hbm(ins, outs, wide, down))


def back_through_heads(
    mixed_grad, raw, low, total, query_gain, key_gain, cosine, sine, allowed, qkv_grad
):
    part = raw.shape[1] // 2
    gain_sums = [None, None]
    for head in range(part // HD):
        span = pl.ds(head * HD, HD)
        query, key = low[:, span], low[:, pl.ds(part + head * HD, HD)]
        value = low[:, pl.ds(2 * part + head * HD, HD)]
        out_grad = mixed_grad[:, span]
        scores = jnp.where(allowed, nt_dot(query, key), -1e30)
        probs = jnp.exp(scores - total[:, head : head + 1])
        prob_grad = nt_dot(out_grad, value)
        value_grad = tn_dot(probs.astype(jnp.bfloat16), out_grad)
        qkv_grad[:, pl.ds(2 * part + head * HD, HD)] = value_grad.astype(jnp.bfloat16)
        inner = jnp.sum(probs * prob_grad, axis=-1, keepdims=True)
        score_grad = (probs * (prob_grad - inner)).astype(jnp.bfloat16)
        rotated = (
            jnp.dot(score_grad, key, preferred_element_type=jnp.float32) * HD ** (-0.5),
            tn_dot(score_grad, query),
        )
        for which, (offset, scale_gain) in enumerate(((0, query_gain), (part, key_gain))):
            grad = rotated[which]
            grad = grad * cosine[...] - pltpu.roll(grad, HD // 2, 1) * sine[...]
            source = raw[:, pl.ds(offset + head * HD, HD)]
            factor = norm_factor(source)
            gain_sum = jnp.sum(grad * source * factor, axis=0, keepdims=True)
            gain_sums[which] = gain_sum if head == 0 else gain_sums[which] + gain_sum
            scaled = grad * scale_gain[...]
            inner = jnp.mean(scaled * source, axis=-1, keepdims=True)
            result = factor * scaled - source * (factor * factor * factor) * inner
            qkv_grad[:, pl.ds(offset + head * HD, HD)] = result.astype(jnp.bfloat16)
    return gain_sums


def closing_kernel(
    shards, planes,
    hidden, grad, out_grad, ffn_gain, raw, low, total, query_gain, key_gain, cosine, sine, seg_row, seg_col,
    tokens, gain, own_mixed, normed, router, out_w, qkv_w, out_total,
    input_grad, mixed_out, query_out, key_out, value_out, weight_out, gain_out, router_out, vectors_out,
    held, came, diag, side, held2, came2, diag2, side2,
    weights, hidden_grad, attn_low, message, message_land, qkv_grad, normed_grad, vectors,
    norm_land, out_land, qkv_land, weight_land, gain_mine, gain_land, gain_line, router_land, router_sum, router_line,
    vector_land, vector_sum, vector_line, send, recv, local,
):
    wires = Wires(send, recv)
    device, shard = wires.device, wires.shard
    rows, width = tokens.shape
    block = query_out.shape[0]
    part = width // shards
    lines = router_out.shape[0]
    lanes = qkv_w.shape[1]
    line_peers = [wires.peer(step=step, shards=shards) for step in range(1, shards)]
    plane_peers = [wires.peer(bits) for bits in range(1, planes)]
    load_out = pltpu.make_async_copy(out_w, weights, local.at[0])
    load_out.start()
    greet(line_peers + plane_peers)

    back = LineSum(
        wires, shards, lambda t: message.at[t], lambda s: message_land.at[aligned(s, rows)]
    )
    norms = LineSum(wires, shards, lambda t: normed_grad.at[aligned(t, rows)], lambda s: norm_land.at[s])
    values = LineSum(
        wires, shards, lambda t: out_total.at[aligned(t, rows)], lambda s: out_land.at[s]
    )
    qkv = PlaneSum(wires, None, held, came, diag, side, local, 0)
    weight = PlaneSum(wires, None, held2, came2, diag2, side2, local, 0)
    qkv_line = LineSum(
        wires, shards, lambda t: held.at[0, aligned(t, block)], lambda s: qkv_land.at[s]
    )
    weight_line = LineSum(
        wires, shards, lambda t: held2.at[0, aligned(t, block)], lambda s: weight_land.at[s]
    )
    sent = []

    def spread(slots, source, landing):
        for bits in range(1, planes):
            copy = wires.copy(
                source(device ^ bits), landing.at[device], slots[bits - 1], wires.peer(bits)
            )
            copy.start()
            sent.append(copy)

    def collect(slots, landing):
        for bits in range(1, planes):
            place = landing.at[device ^ bits]
            wires.copy(place, place, slots[bits - 1], wires.peer(bits)).wait_recv()
        total = landing[0]
        for other in range(1, planes):
            total = total + landing[other]
        return total

    router_slots = [wires.slot() for _ in range(1, planes)]
    vector_slots = [wires.slot() for _ in range(1, planes)]
    gain_slots = [wires.slot() for _ in range(1, planes)]
    spread(router_slots, lambda e: router.at[aligned(e, shards * lines)], router_land)
    router_land[device] = router[aligned(device, shards * lines), :]

    factor = norm_factor(hidden[...])
    vectors[:, :width] = jnp.sum(grad[...] * hidden[...] * factor, axis=0, keepdims=True)
    scaled = grad[...] * ffn_gain[...]
    inner = jnp.mean(scaled * hidden[...], axis=-1, keepdims=True)
    change = out_grad[...].astype(jnp.float32) + factor * scaled
    change = change - hidden[...] * (factor * factor * factor) * inner
    hidden_grad[...] = change
    attn_low[...] = change.astype(jnp.bfloat16)
    load_out.wait()
    for target in range(shards):
        message[target] = nt_dot(attn_low[...], weights[pl.ds(target * part, part), :]).astype(
            jnp.bfloat16
        )
    back.begin()
    values.begin()
    load_qkv = pltpu.make_async_copy(qkv_w, weights.at[:, pl.ds(0, lanes)], local.at[1])
    load_qkv.start()
    own_value = pltpu.make_async_copy(
        out_total.at[aligned(shard, rows)], out_land.at[shard], local.at[2]
    )
    own_value.start()
    message_land[aligned(shard, rows), :] = message[shard]

    def addends(group, left, right):
        for core in (1, 0):
            for chip in (3, 1, 2, 0):
                owner = device ^ (2 * chip + core)
                columns = pl.ds(pl.multiple_of(owner * shards * block, shards * block), shards * block)
                if core == 0:
                    group.sent[(3, 1, 2, 0).index(chip)].wait_send()
                group.held[chip] = tn_dot(left[:, columns], right[...]).astype(jnp.bfloat16)
                if core == 1:
                    group.give(chip)
        group.sent = []

    addends(weight, own_mixed, attn_low)
    weight.send_corner()
    weight.add_cores()
    router_sum[...] = collect(router_slots, router_land)
    router_pass = LineSum(
        wires, shards, lambda t: router_sum.at[aligned(t, lines)], lambda s: router_line.at[s]
    )

    back.arrive()
    allowed = seg_col[...] == seg_row[...]
    query_sum, key_sum = back_through_heads(
        message_land, raw, low, total, query_gain, key_gain, cosine, sine, allowed, qkv_grad
    )
    vectors[:, pl.ds(width, HD)] = query_sum
    vectors[:, pl.ds(width + HD, HD)] = key_sum
    load_qkv.wait()
    normed_grad[...] = nt_dot(qkv_grad[...], weights[:, pl.ds(0, lanes)]).astype(jnp.bfloat16)
    norms.begin()
    norm_land[shard] = normed_grad[aligned(shard, rows), :]
    router_pass.begin()
    spread(vector_slots, lambda e: vectors, vector_land)
    vector_land[device] = vectors[...]
    weight.send_sides()
    addends(qkv, normed, qkv_grad)
    qkv.send_corner()
    qkv.add_cores()
    vector_sum[...] = collect(vector_slots, vector_land)
    vector_pass = LineSum(wires, shards, lambda t: vector_sum, lambda s: vector_line.at[s])
    vector_pass.begin()
    vector_line[shard] = vector_sum[...]
    router_line[shard] = router_sum[aligned(shard, lines), :]
    qkv.send_sides()
    weight.end()
    weight_line.begin()
    weight_land[shard] = held2[0, aligned(shard, block), :]
    out_land_ready = own_value
    out_land_ready.wait()
    values.arrive()
    mixed_out[...] = (hidden[...] + line_total(out_land, shards)).astype(jnp.bfloat16)

    norms.arrive()
    change = line_total(norm_land, shards)
    given = tokens[...].astype(jnp.float32)
    factor = norm_factor(given)
    gain_mine[...] = jnp.sum(change * given * factor, axis=0, keepdims=True)
    spread(gain_slots, lambda e: gain_mine, gain_land)
    scaled = change * gain[...]
    inner = jnp.mean(scaled * given, axis=-1, keepdims=True)
    result = hidden_grad[...] + factor * scaled - given * (factor * factor * factor) * inner
    input_grad[...] = result.astype(jnp.bfloat16)
    qkv.end()
    qkv_line.begin()
    qkv_land[shard] = held[0, aligned(shard, block), :]
    gain_land[device] = gain_mine[...]
    gain_line[shard] = collect(gain_slots, gain_land)
    gain_pass = LineSum(wires, shards, lambda t: gain_line.at[shard], lambda s: gain_line.at[s])
    gain_pass.begin()
    router_pass.arrive()
    router_out[...] = line_total(router_line, shards)
    vector_pass.arrive()
    vectors_out[...] = line_total(vector_line, shards)
    weight_line.arrive()
    weight_out[...] = line_total(weight_land, shards)
    qkv_line.arrive()
    for source in range(shards):
        for which, result_out in enumerate((query_out, key_out, value_out)):
            result_out[:, pl.ds(source * part, part)] = qkv_land[
                source, :, pl.ds(which * part, part)
            ].astype(jnp.float32)
    gain_pass.arrive()
    gain_out[...] = line_total(gain_line, shards)
    for copy in sent:
        copy.wait_send()
    groups = (back, norms, values, qkv, weight, qkv_line, weight_line, router_pass, vector_pass)
    for group in (*groups, gain_pass):
        group.drain()


def closing_call(
    hidden, grad, out_grad, ffn_gain, raw, low, total, query_gain, key_gain, tables, seg_row, seg_col,
    tokens, gain, own_mixed, normed, router, out_w, qkv_w, out_total, planes, shards,
):
    rows, width = tokens.shape
    seq, lanes = low.shape
    each = width // planes
    block = each // shards
    lines = router.shape[0] // (planes * shards)
    hbm = pl.BlockSpec(memory_space=pltpu.HBM)
    vmem = pl.BlockSpec(memory_space=pltpu.VMEM)
    half, full = jnp.bfloat16, jnp.float32
    weight_shape = jax.ShapeDtypeStruct((block, width), full)
    vector = width + 2 * HD
    return pl.pallas_call(
        functools.partial(closing_kernel, shards, planes),
        in_specs=[vmem] * 18 + [hbm] * 3,
        out_specs=[vmem] * 9,
        out_shape=(
            jax.ShapeDtypeStruct((rows, width), half),
            jax.ShapeDtypeStruct((rows, width), half),
            weight_shape,
            weight_shape,
            weight_shape,
            weight_shape,
            jax.ShapeDtypeStruct((1, width), full),
            jax.ShapeDtypeStruct((lines, 128), full),
            jax.ShapeDtypeStruct((1, vector), full),
        ),
        scratch_shapes=sum_work(each, lanes)
        + sum_work(each, width)
        + [
            pltpu.VMEM((width, width), half),
            pltpu.VMEM((rows, width), full),
            pltpu.VMEM((rows, width), half),
            pltpu.VMEM((shards, rows, width // shards), half),
            pltpu.VMEM((seq, width // shards), half),
            pltpu.VMEM((seq, lanes), half),
            pltpu.VMEM((seq, width), half),
            pltpu.VMEM((1, vector), full),
            pltpu.VMEM((shards, rows, width), half),
            pltpu.VMEM((shards, rows, width), half),
            pltpu.VMEM((shards, block, lanes), half),
            pltpu.VMEM((shards, block, width), half),
            pltpu.VMEM((1, width), full),
            pltpu.VMEM((planes, 1, width), full),
            pltpu.VMEM((shards, 1, width), full),
            pltpu.VMEM((planes, shards * lines, 128), full),
            pltpu.VMEM((shards * lines, 128), full),
            pltpu.VMEM((shards, lines, 128), full),
            pltpu.VMEM((planes, 1, vector), full),
            pltpu.VMEM((1, vector), full),
            pltpu.VMEM((shards, 1, vector), full),
            pltpu.SemaphoreType.DMA((72,)),
            pltpu.SemaphoreType.DMA((72,)),
            pltpu.SemaphoreType.DMA((3,)),
        ],
        compiler_params=pltpu.CompilerParams(
            collective_id=6, has_side_effects=True, vmem_limit_bytes=60 * MIB
        ),
        cost_estimate=pl.CostEstimate(flops=0, bytes_accessed=300 * MIB, transcendentals=0),
    )(
        hidden, grad, out_grad, ffn_gain, raw, low, total, query_gain, key_gain, *tables, seg_row, seg_col,
        tokens, gain, own_mixed, normed, router, *held_in_hbm(out_w, qkv_w, out_total),
    )


LOW = jnp.bfloat16
WIDE = jnp.float32


def fast_local(
    tokens,
    segment_ids,
    routes,
    pair_order,
    attn_gain,
    w_query,
    w_key,
    w_value,
    query_gain,
    key_gain,
    w_out,
    ffn_gain,
    w_router,
    w_gate,
    w_up,
    w_down,
    out_grad,
):
    rows, width = tokens.shape
    top_count = routes.shape[1]
    planes = lax.axis_size(EXPERT)
    shards = lax.axis_size(SHARD)
    own_experts = w_gate.shape[0]
    experts = own_experts * planes
    capacity = 5 * rows * top_count // (4 * own_experts)
    seq = segment_ids.shape[0]
    device = lax.axis_index(EXPERT)
    shard = lax.axis_index(SHARD)
    part = width // shards

    index = device * shards + shard

    def placed(values, size):
        zeros = jnp.zeros((size,), values.dtype)
        return lax.dynamic_update_slice_in_dim(zeros, values, index * values.size, 0)

    gains = [placed(attn_gain, width), placed(ffn_gain, width)]
    gains += [placed(query_gain, HD), placed(key_gain, HD)]
    gains = jnp.concatenate(gains)
    gains = jnp.pad(gains, (0, -gains.size % (16 * 128))).reshape(-1, 128)
    router_pad = jnp.pad(w_router, ((0, 0), (0, 128 - experts)))
    tables = turn_tables(seq)
    seg_row, seg_col = segment_ids.reshape(1, seq), segment_ids.reshape(seq, 1)
    opened = opening_call(
        routes,
        pair_order.reshape(rows, top_count),
        gains,
        seg_row,
        seg_col,
        tables,
        router_pad,
        w_query,
        w_key,
        w_value,
        tokens,
        w_out,
        out_grad,
        experts,
        own_experts,
        capacity,
        planes,
        shards,
    )
    kept, attn_row, ffn_row, query_row, key_row, normed_low, raw, low, total, mixed_all = opened[:10]
    router_w, qkv_w, tokens_seq, out_w, grad_all = opened[10:]
    router_w = router_w.reshape(width, 128)
    hidden, own_mixed, token_all, wide_w, down_w = meeting_call(
        tokens_seq, ffn_row, mixed_all, out_w, w_gate, w_up, w_down, planes, shards
    )
    grad_all = grad_all.reshape(planes, seq, width)
    own_ids = device * own_experts + jnp.arange(own_experts, dtype=jnp.int32)
    own_hot = (own_ids[:, None] == jnp.arange(128, dtype=jnp.int32)[None, :]).astype(WIDE)
    out_first, in_first, pull, wide_sum, down_sum, wide_next, down_next = expert_call(
        0,
        token_all,
        grad_all,
        kept,
        wide_w.reshape(width, -1),
        router_w,
        down_w,
        own_hot,
        experts,
        (w_gate, w_up, w_down),
        None,
    )
    before = (out_first, in_first, pull, wide_sum.reshape(shards, part, -1), down_sum)
    out_parts, in_parts, wide_sum, down_sum, router_grad, wide0, down0 = expert_call(
        1,
        token_all,
        grad_all,
        kept,
        wide_next.reshape(width, -1),
        router_w,
        down_next,
        own_hot,
        experts,
        None,
        before,
    )
    normed_two_grad, out_total, wide1, down1 = returning_call(
        in_parts, out_parts, wide_sum.reshape(shards, part, -1), down_sum
    )
    closed = closing_call(
        hidden,
        normed_two_grad,
        out_grad,
        ffn_row,
        raw,
        low,
        total,
        query_row,
        key_row,
        tables,
        seg_row,
        seg_col,
        tokens,
        attn_row,
        own_mixed,
        normed_low,
        router_grad[:, :experts].reshape(-1, 128),
        out_w,
        qkv_w,
        out_total,
        planes,
        shards,
    )
    input_grad, mixed_out, query_w_grad, key_w_grad, value_w_grad, out_w_grad = closed[:6]
    attn_scale_grad, router_out, vectors = closed[6:]
    gate_grad, up_grad, down_grad = unpack_units((wide0, wide1), (down0, down1))
    flat = vectors.reshape(-1)

    def own_piece(values, start, size):
        return lax.dynamic_slice_in_dim(values, start + index * size, size)

    return (
        mixed_out,
        input_grad,
        own_piece(attn_scale_grad.reshape(-1), 0, attn_gain.size),
        query_w_grad,
        key_w_grad,
        value_w_grad,
        own_piece(flat, width, query_gain.size),
        own_piece(flat, width + HD, key_gain.size),
        out_w_grad,
        own_piece(flat, 0, ffn_gain.size),
        router_out.reshape(-1, experts),
        gate_grad,
        up_grad,
        down_grad,
    )


def solution(mesh):
    local = fast_local if mesh.shape[EXPERT] == 8 else general_local
    return jax.shard_map(
        local,
        mesh=mesh,
        in_specs=(
            P(BOTH, None),
            P(EXPERT),
            P(BOTH, None),
            P(BOTH),
            P(BOTH),
            P(BOTH, None),
            P(BOTH, None),
            P(BOTH, None),
            P(BOTH),
            P(BOTH),
            P(BOTH, None),
            P(BOTH),
            P(BOTH, None),
            P(EXPERT, SHARD, None),
            P(EXPERT, SHARD, None),
            P(EXPERT, None, SHARD),
            P(BOTH, None),
        ),
        out_specs=(
            P(BOTH, None),
            P(BOTH, None),
            P(BOTH),
            P(BOTH, None),
            P(BOTH, None),
            P(BOTH, None),
            P(BOTH),
            P(BOTH),
            P(BOTH, None),
            P(BOTH),
            P(BOTH, None),
            P(EXPERT, SHARD, None),
            P(EXPERT, SHARD, None),
            P(EXPERT, None, SHARD),
        ),
        check_vma=False,
    )
```

```python
import functools

import jax
import jax.numpy as jnp
import numpy as np
from jax import lax
from jax.experimental import pallas as pl
from jax.experimental.pallas import tpu as pltpu
from jax.sharding import PartitionSpec as P

HEADS = 16
HD = 128


EXPERT = "expert"
SHARD = "wshard"
BOTH = (EXPERT, SHARD)

SUM_QHD_KHD_HQK = "qhd,khd->hqk"
SUM_HQK_KHD_QHD = "hqk,khd->qhd"
SUM_ECD_EDF_ECF = "ecd,edf->ecf"
SUM_ECF_EFD_ECD = "ecf,efd->ecd"
SUM_TK_TKD_TD = "tk,tkd->td"
SUM_TD_TKD_TK = "td,tkd->tk"
SUM_ECD_EFD_ECF = "ecd,efd->ecf"
SUM_ECF_ECD_EFD = "ecf,ecd->efd"
SUM_ECD_ECF_EDF = "ecd,ecf->edf"
SUM_ECF_EDF_ECD = "ecf,edf->ecd"
SUM_HQK_QHD_KHD = "hqk,qhd->khd"
EPSILON = 1e-06
THETA = 10000.0


def matmul(left, right):
    return jnp.dot(left, right, preferred_element_type=jnp.float32)


def matmul_tn(left, right):
    return lax.dot_general(
        left, right, (((0,), (0,)), ((), ())), preferred_element_type=jnp.float32
    )


def matmul_nt(left, right):
    return lax.dot_general(
        left, right, (((1,), (1,)), ((), ())), preferred_element_type=jnp.float32
    )


def rms_scale(values, scale_gain):
    factor = lax.rsqrt(jnp.mean(values * values, axis=-1, keepdims=True) + EPSILON)
    return values * factor * scale_gain


def rope_tables(positions):
    exponent = jnp.arange(HD // 2, dtype=jnp.float32) * (2.0 / HD)
    frequency = jnp.power(jnp.float32(THETA), -exponent)
    angles = positions.astype(jnp.float32)[:, None] * frequency[None, :]
    return (jnp.cos(angles), jnp.sin(angles))


def rotate(values, cosine, sine):
    first_half = values[..., : HD // 2]
    second_half = values[..., HD // 2 :]
    cos_part = cosine[:, None, :]
    sin_part = sine[:, None, :]
    return jnp.concatenate(
        [
            first_half * cos_part - second_half * sin_part,
            second_half * cos_part + first_half * sin_part,
        ],
        axis=-1,
    )


def padded_rows(rows):
    return jnp.concatenate([jnp.zeros((1,) + rows.shape[1:], rows.dtype), rows], axis=0)


def masked_scores(query_rot, key_rot, query_segment, key_segment):
    scores = jnp.einsum(SUM_QHD_KHD_HQK, query_rot, key_rot, preferred_element_type=jnp.float32)
    allowed = query_segment[:, None] == key_segment[None, :]
    return jnp.where(allowed[None], scores, -1e30)


def swiglu_fn(gate_in, up_in):
    return jax.nn.silu(gate_in) * up_in


def general_local(
    tokens,
    segment_ids,
    routes,
    pair_order,
    attn_gain,
    w_query,
    w_key,
    w_value,
    query_gain,
    key_gain,
    w_out,
    ffn_gain,
    w_router,
    w_gate,
    w_up,
    w_down,
    out_grad,
):
    tok_rows, width = tokens.shape
    top_count = routes.shape[1]
    expert_devs = lax.axis_size(EXPERT)
    shard_devs = lax.axis_size(SHARD)
    local_experts = w_gate.shape[0]
    expert_count = local_experts * expert_devs
    most_rows = 2 * tok_rows * top_count // expert_count
    capacity = 5 * tok_rows * top_count // (4 * local_experts)
    seq_length = segment_ids.shape[0]
    device_expert = lax.axis_index(EXPERT)
    device_shard = lax.axis_index(SHARD)
    low_type = jnp.bfloat16
    wide_type = jnp.float32
    gathered = (
        lax.all_gather(attn_gain, BOTH, axis=0, tiled=True),
        lax.all_gather(w_query, BOTH, axis=0, tiled=True),
        lax.all_gather(w_key, BOTH, axis=0, tiled=True),
        lax.all_gather(w_value, BOTH, axis=0, tiled=True),
        lax.all_gather(query_gain, BOTH, axis=0, tiled=True),
        lax.all_gather(key_gain, BOTH, axis=0, tiled=True),
        lax.all_gather(w_out, BOTH, axis=0, tiled=True),
        lax.all_gather(ffn_gain, BOTH, axis=0, tiled=True),
        lax.all_gather(w_router, BOTH, axis=0, tiled=True),
    )
    attn_scale = gathered[0].astype(wide_type)
    query_w, key_w, value_w = (gathered[1], gathered[2], gathered[3])
    query_scale = gathered[4].astype(wide_type)
    key_scale = gathered[5].astype(wide_type)
    out_w = gathered[6]
    ffn_scale = gathered[7].astype(wide_type)
    router_w = gathered[8]
    inputs = tokens.astype(wide_type)
    normed, norm_one_pull = jax.vjp(rms_scale, inputs, attn_scale)
    normed_low = normed.astype(low_type)
    query_raw = matmul(normed_low, query_w)
    key_raw = matmul(normed_low, key_w)
    value_low = matmul(normed_low, value_w).astype(low_type)
    positions = device_shard * tok_rows + jnp.arange(tok_rows, dtype=jnp.int32)
    cosine, sine = rope_tables(positions)

    def prepare(query_in, key_in, query_g, key_g):
        query_heads = rms_scale(query_in.reshape(tok_rows, HEADS, HD), query_g)
        key_heads = rms_scale(key_in.reshape(tok_rows, HEADS, HD), key_g)
        return (rotate(query_heads, cosine, sine) * HD ** (-0.5), rotate(key_heads, cosine, sine))

    rotated, prepare_pull = jax.vjp(prepare, query_raw, key_raw, query_scale, key_scale)
    query_low = rotated[0].astype(low_type)
    key_low = rotated[1].astype(low_type).reshape(tok_rows, width)
    seq_keys, seq_values = (
        lax.all_gather(key_low, SHARD, axis=0, tiled=True),
        lax.all_gather(value_low, SHARD, axis=0, tiled=True),
    )
    query_segment = lax.dynamic_slice_in_dim(segment_ids, device_shard * tok_rows, tok_rows)
    scores = masked_scores(
        query_low, seq_keys.reshape(seq_length, HEADS, HD), query_segment, segment_ids
    )
    row_max = jnp.max(scores, axis=-1, keepdims=True)
    shifted = jnp.exp(scores - row_max)
    totals = jnp.sum(shifted, axis=-1, keepdims=True)
    log_total = row_max + jnp.log(totals)
    probs_low = (shifted / totals).astype(low_type)
    mixed = jnp.einsum(
        SUM_HQK_KHD_QHD,
        probs_low,
        seq_values.reshape(seq_length, HEADS, HD),
        preferred_element_type=wide_type,
    )
    mixed_low = mixed.reshape(tok_rows, width).astype(low_type)
    hidden = inputs + matmul(mixed_low, out_w)
    normed_two, norm_two_pull = jax.vjp(rms_scale, hidden, ffn_scale)
    normed_two_low = normed_two.astype(low_type)
    logits = matmul(normed_two_low, router_w)

    def router_weights(logit_values):
        return jnp.take_along_axis(jax.nn.softmax(logit_values, axis=-1), routes, axis=1)

    route_weight, route_pull = jax.vjp(router_weights, logits)
    group_routes, group_order = (
        lax.all_gather(routes, EXPERT, axis=0, tiled=True),
        lax.all_gather(pair_order, EXPERT, axis=0, tiled=True),
    )
    per_source = tok_rows * top_count
    group_pairs = per_source * expert_devs
    expert_of = group_routes.reshape(-1)
    pair_index = jnp.arange(group_pairs, dtype=jnp.int32)
    source_of = pair_index // per_source
    expert_ids = jnp.arange(expert_count, dtype=jnp.int32)
    onehot = (expert_of.reshape(expert_devs, per_source, 1) == expert_ids).astype(jnp.int32)
    position_of = (jnp.sum(jnp.cumsum(onehot, axis=1) * onehot, axis=-1) - 1).reshape(-1)
    order_span = group_pairs * shard_devs
    sort_keys = expert_of * order_span + group_order
    sorted_pairs = jnp.argsort(sort_keys)
    placement = jnp.zeros((group_pairs,), jnp.int32).at[sorted_pairs].set(pair_index)
    expert_counts = jnp.sum(onehot, axis=(0, 1))
    expert_start = jnp.cumsum(expert_counts) - expert_counts
    start_of = jnp.sum(onehot.reshape(group_pairs, expert_count) * expert_start[None, :], axis=-1)
    slot_rank = placement - start_of
    retained = slot_rank < capacity
    own_expert = routes.reshape(-1)
    own_position = lax.dynamic_slice_in_dim(position_of, device_expert * per_source, per_source)
    send_slot = own_expert * most_rows + own_position
    send_pair = (
        jnp.zeros((expert_count * most_rows,), jnp.int32)
        .at[send_slot]
        .set(jnp.arange(per_source, dtype=jnp.int32) + 1)
    )
    send_token = jnp.where(send_pair > 0, (send_pair - 1) // top_count + 1, 0)
    owner_local = expert_of % local_experts
    is_mine = expert_of // local_experts == device_expert
    recv_row = source_of * (local_experts * most_rows) + owner_local * most_rows + position_of
    slot_target = jnp.where(
        is_mine & retained, owner_local * capacity + slot_rank, local_experts * capacity
    )
    slot_source = (
        jnp.zeros((local_experts * capacity,), jnp.int32)
        .at[slot_target]
        .set(recv_row + 1, mode="drop")
    )
    back_room = expert_devs * local_experts * most_rows
    back_target = jnp.where(is_mine, recv_row, back_room)
    back_source = (
        jnp.zeros((back_room,), jnp.int32)
        .at[back_target]
        .set(jnp.where(retained, owner_local * capacity + slot_rank + 1, 0), mode="drop")
    )
    send_rows = padded_rows(normed_two_low)[send_token].reshape(
        expert_devs, local_experts * most_rows, width
    )
    recv_rows = lax.all_to_all(
        send_rows, EXPERT, split_axis=0, concat_axis=0, tiled=True
    ).reshape(-1, width)
    slot_rows = padded_rows(recv_rows)[slot_source].reshape(local_experts, capacity, width)
    full_gate, full_up, full_down = (
        lax.all_gather(w_gate, SHARD, axis=1, tiled=True),
        lax.all_gather(w_up, SHARD, axis=1, tiled=True),
        lax.all_gather(w_down, SHARD, axis=2, tiled=True),
    )
    gate_act = jnp.einsum(SUM_ECD_EDF_ECF, slot_rows, full_gate, preferred_element_type=wide_type)
    up_act = jnp.einsum(SUM_ECD_EDF_ECF, slot_rows, full_up, preferred_element_type=wide_type)
    swiglu_out, swiglu_pull = jax.vjp(swiglu_fn, gate_act, up_act)
    swiglu_low = swiglu_out.astype(low_type)
    expert_out = jnp.einsum(
        SUM_ECF_EFD_ECD, swiglu_low, full_down, preferred_element_type=wide_type
    ).astype(low_type)
    back_rows = padded_rows(expert_out.reshape(-1, width))[back_source].reshape(
        expert_devs, local_experts * most_rows, width
    )
    returned = lax.all_to_all(back_rows, EXPERT, split_axis=0, concat_axis=0, tiled=True).reshape(
        -1, width
    )
    pair_rows = returned[send_slot].reshape(tok_rows, top_count, width)
    combined = jnp.einsum(SUM_TK_TKD_TD, route_weight, pair_rows, preferred_element_type=wide_type)
    mixed_out = (hidden + combined).astype(low_type)
    result_grad = out_grad.astype(wide_type)
    weight_grad = jnp.einsum(SUM_TD_TKD_TK, result_grad, pair_rows, preferred_element_type=wide_type)
    pair_grad = (
        (route_weight[:, :, None] * result_grad[:, None, :])
        .astype(low_type)
        .reshape(per_source, width)
    )
    send_grad = padded_rows(pair_grad)[send_pair].reshape(
        expert_devs, local_experts * most_rows, width
    )
    recv_grad = lax.all_to_all(
        send_grad, EXPERT, split_axis=0, concat_axis=0, tiled=True
    ).reshape(-1, width)
    slot_grad = padded_rows(recv_grad)[slot_source].reshape(local_experts, capacity, width)
    act_grad = jnp.einsum(SUM_ECD_EFD_ECF, slot_grad, full_down, preferred_element_type=wide_type)
    down_grad = jnp.einsum(SUM_ECF_ECD_EFD, swiglu_low, slot_grad, preferred_element_type=wide_type)
    gate_grad, up_grad = swiglu_pull(act_grad)
    gate_low = gate_grad.astype(low_type)
    up_low = up_grad.astype(low_type)
    gate_w_grad = jnp.einsum(SUM_ECD_ECF_EDF, slot_rows, gate_low, preferred_element_type=wide_type)
    up_w_grad = jnp.einsum(SUM_ECD_ECF_EDF, slot_rows, up_low, preferred_element_type=wide_type)
    slot_in_grad = jnp.einsum(SUM_ECF_EDF_ECD, gate_low, full_gate, preferred_element_type=wide_type)
    slot_in_grad = (
        slot_in_grad + jnp.einsum(SUM_ECF_EDF_ECD, up_low, full_up, preferred_element_type=wide_type)
    ).astype(low_type)
    gate_shard, up_shard, down_shard = (
        lax.psum_scatter(
            gate_w_grad.astype(jnp.bfloat16), SHARD, scatter_dimension=1, tiled=True
        ).astype(jnp.float32),
        lax.psum_scatter(
            up_w_grad.astype(jnp.bfloat16), SHARD, scatter_dimension=1, tiled=True
        ).astype(jnp.float32),
        lax.psum_scatter(
            down_grad.astype(jnp.bfloat16), SHARD, scatter_dimension=2, tiled=True
        ).astype(jnp.float32),
    )
    back_grad = padded_rows(slot_in_grad.reshape(-1, width))[back_source].reshape(
        expert_devs, local_experts * most_rows, width
    )
    returned_grad = lax.all_to_all(
        back_grad, EXPERT, split_axis=0, concat_axis=0, tiled=True
    ).reshape(-1, width)
    expert_in_grad = jnp.sum(
        returned_grad[send_slot].reshape(tok_rows, top_count, width).astype(wide_type), axis=1
    )
    logit_grad = route_pull(weight_grad)[0]
    logit_low = logit_grad.astype(low_type)
    router_grad = matmul_tn(normed_two_low, logit_low)
    normed_two_grad = expert_in_grad + matmul_nt(logit_low, router_w)
    hidden_norm_grad, ffn_scale_grad = norm_two_pull(normed_two_grad)
    hidden_grad = result_grad + hidden_norm_grad
    attn_low = hidden_grad.astype(low_type)
    out_w_grad = matmul_tn(mixed_low, attn_low)
    mixed_grad = matmul_nt(attn_low, out_w).astype(low_type).reshape(tok_rows, HEADS, HD)
    back_keys, back_values = (seq_keys, seq_values)
    key_heads = back_keys.reshape(seq_length, HEADS, HD)
    value_heads = back_values.reshape(seq_length, HEADS, HD)
    scores_again = masked_scores(query_low, key_heads, query_segment, segment_ids)
    probs_again = jnp.exp(scores_again - log_total)
    probs_again_low = probs_again.astype(low_type)
    prob_grad = jnp.einsum(
        SUM_QHD_KHD_HQK, mixed_grad, value_heads, preferred_element_type=wide_type
    )
    value_part = jnp.einsum(
        SUM_HQK_QHD_KHD, probs_again_low, mixed_grad, preferred_element_type=wide_type
    )
    row_inner = jnp.sum(probs_again * prob_grad, axis=-1, keepdims=True)
    score_low = (probs_again * (prob_grad - row_inner)).astype(low_type)
    query_rot_grad = jnp.einsum(
        SUM_HQK_KHD_QHD, score_low, key_heads, preferred_element_type=wide_type
    )
    key_part = jnp.einsum(SUM_HQK_QHD_KHD, score_low, query_low, preferred_element_type=wide_type)
    key_rot_grad, value_grad = (
        lax.psum_scatter(
            key_part.reshape(seq_length, width).astype(jnp.bfloat16),
            SHARD,
            scatter_dimension=0,
            tiled=True,
        ).astype(jnp.float32),
        lax.psum_scatter(
            value_part.reshape(seq_length, width).astype(jnp.bfloat16),
            SHARD,
            scatter_dimension=0,
            tiled=True,
        ).astype(jnp.float32),
    )
    query_raw_grad, key_raw_grad, query_scale_grad, key_scale_grad = prepare_pull(
        (query_rot_grad, key_rot_grad.reshape(tok_rows, HEADS, HD))
    )
    query_grad_low = query_raw_grad.astype(low_type)
    key_grad_low = key_raw_grad.astype(low_type)
    value_grad_low = value_grad.astype(low_type)
    query_w_grad = matmul_tn(normed_low, query_grad_low)
    key_w_grad = matmul_tn(normed_low, key_grad_low)
    value_w_grad = matmul_tn(normed_low, value_grad_low)
    normed_grad = (
        matmul_nt(query_grad_low, query_w)
        + matmul_nt(key_grad_low, key_w)
        + matmul_nt(value_grad_low, value_w)
    )
    input_norm_grad, attn_scale_grad = norm_one_pull(normed_grad)
    input_grad = (hidden_grad + input_norm_grad).astype(low_type)
    summed = (
        lax.psum_scatter(attn_scale_grad, BOTH, scatter_dimension=0, tiled=True),
        lax.psum_scatter(query_w_grad, BOTH, scatter_dimension=0, tiled=True),
        lax.psum_scatter(key_w_grad, BOTH, scatter_dimension=0, tiled=True),
        lax.psum_scatter(value_w_grad, BOTH, scatter_dimension=0, tiled=True),
        lax.psum_scatter(query_scale_grad, BOTH, scatter_dimension=0, tiled=True),
        lax.psum_scatter(key_scale_grad, BOTH, scatter_dimension=0, tiled=True),
        lax.psum_scatter(out_w_grad, BOTH, scatter_dimension=0, tiled=True),
        lax.psum_scatter(ffn_scale_grad, BOTH, scatter_dimension=0, tiled=True),
        lax.psum_scatter(router_grad, BOTH, scatter_dimension=0, tiled=True),
    )
    return (
        mixed_out,
        input_grad,
        summed[0],
        summed[1],
        summed[2],
        summed[3],
        summed[4],
        summed[5],
        summed[6],
        summed[7],
        summed[8],
        gate_shard,
        up_shard,
        down_shard,
    )


MIB = 1 << 20


def nt_dot(left, right):
    return lax.dot_general(
        left, right, (((1,), (1,)), ((), ())), preferred_element_type=jnp.float32
    )


def tn_dot(left, right):
    return lax.dot_general(
        left, right, (((0,), (0,)), ((), ())), preferred_element_type=jnp.float32
    )


def vmem_params(mib):
    return pltpu.CompilerParams(vmem_limit_bytes=mib * MIB)


def turn_tables(length):
    exponent = np.arange(HD // 2, dtype=np.float32) * np.float32(2.0 / HD)
    frequency = np.power(np.float32(THETA), -exponent).astype(np.float32)
    angles = np.arange(length, dtype=np.float32)[:, None] * frequency[None, :]
    cosine, sine = np.cos(angles), np.sin(angles)
    return (
        jnp.asarray(np.concatenate([cosine, cosine], axis=1), jnp.float32),
        jnp.asarray(np.concatenate([-sine, sine], axis=1), jnp.float32),
    )


def norm_factor(values):
    return lax.rsqrt(jnp.mean(values * values, axis=-1, keepdims=True) + EPSILON)


def attend(
    tokens, gain, weight, query_gain, key_gain, cosine, sine, seg_row, seg_col,
    normed_out, raw_out, low_out, mixed_out, total_out, qkv,
):
    part = mixed_out.shape[1]
    values = tokens[...].astype(jnp.float32)
    normed = (values * norm_factor(values) * gain[...]).astype(jnp.bfloat16)
    normed_out[...] = normed
    qkv[...] = jnp.dot(normed, weight[...], preferred_element_type=jnp.float32)
    raw_out[...] = qkv[:, : 2 * part]
    low_out[:, 2 * part :] = qkv[:, 2 * part :].astype(jnp.bfloat16)
    allowed = seg_col[...] == seg_row[...]
    for head in range(part // HD):
        span = pl.ds(head * HD, HD)
        for offset, scale_gain, scale in ((0, query_gain, HD ** (-0.5)), (part, key_gain, 1.0)):
            raw = qkv[:, pl.ds(offset + head * HD, HD)]
            unit = raw * norm_factor(raw) * scale_gain[...]
            turned = unit * cosine[...] + pltpu.roll(unit, HD // 2, 1) * sine[...]
            low_out[:, pl.ds(offset + head * HD, HD)] = (turned * scale).astype(jnp.bfloat16)
        query, key = low_out[:, span], low_out[:, pl.ds(part + head * HD, HD)]
        scores = jnp.where(allowed, nt_dot(query, key), -1e30)
        top = jnp.max(scores, axis=-1, keepdims=True)
        shifted = jnp.exp(scores - top)
        total = jnp.sum(shifted, axis=-1, keepdims=True)
        probs = (shifted / total).astype(jnp.bfloat16)
        mixed = jnp.dot(
            probs, low_out[:, pl.ds(2 * part + head * HD, HD)], preferred_element_type=jnp.float32
        )
        mixed_out[:, span] = mixed.astype(jnp.bfloat16)
        total_out[:, head : head + 1] = top + jnp.log(total)


def unpack_kernel(gate0, gate1, up0, up1, down0, down1, gate_out, up_out, down_out):
    for index, group in enumerate(((gate0, up0, down0), (gate1, up1, down1))):

        @pl.when(pl.program_id(0) == index)
        def _(group=group):
            for source, result in zip(group, (gate_out, up_out, down_out), strict=True):
                result[...] = source[...].astype(result.dtype)


def unpack_units(wides, downs):
    shards, part, lanes = wides[0].shape
    each = lanes // 2

    def held(index, e, s):
        return jnp.where(e == index, s, (shards - 1) * (1 - index))

    def wide_spec(index, which):
        return pl.BlockSpec((1, part, each), lambda e, s: (held(index, e, s), 0, which))

    def down_spec(index):
        return pl.BlockSpec((1, each, part), lambda e, s: (held(index, e, s), 0, 0))

    wide_out = pl.BlockSpec((1, part, each), lambda e, s: (e, 0, s))
    shape = jax.ShapeDtypeStruct((2, part, shards * each), jnp.float32)
    return pl.pallas_call(
        unpack_kernel,
        grid=(2, shards),
        in_specs=[wide_spec(index, which) for which in range(2) for index in range(2)]
        + [down_spec(index) for index in range(2)],
        out_specs=[wide_out, wide_out, pl.BlockSpec((1, each, part), lambda e, s: (e, s, 0))],
        out_shape=[shape, shape, jax.ShapeDtypeStruct((2, shards * each, part), jnp.float32)],
        compiler_params=vmem_params(24),
    )(wides[0], wides[1], wides[0], wides[1], *downs)


def mark_kept(small_all, first, experts, own, capacity, bits, shards, keep_out):
    devices, _, rows = small_all.shape
    row = lax.broadcasted_iota(jnp.int32, (devices, rows), 0)
    group = lax.rem(row, shards)
    for index in range(own):
        order = jnp.zeros((devices, rows), jnp.float32)
        for expert in range(experts):
            high = small_all[:, expert, :].astype(jnp.float32)
            low = small_all[:, experts + expert, :].astype(jnp.float32)
            order = order + jnp.where(first + index == expert, high * 256.0 + low, 0.0)
        there = order > 0.0
        bound = jnp.zeros_like(order)
        for bit in reversed(range(bits)):
            trial = bound + float(1 << bit)
            within = jnp.where(there & (order <= trial), 1.0, 0.0)
            for shard in range(shards):
                here = group == shard
                count = jnp.sum(jnp.where(here, within, 0.0), keepdims=True)
                bound = jnp.where(here & (count <= float(capacity)), trial, bound)
        kept = jnp.where(there & (order <= bound), 1.0, 0.0).T
        for block in range(devices):
            place = keep_out.at[block // shards, pl.ds(block % shards * rows, rows)]
            place[:, index : index + 1] = kept[:, block : block + 1]


CORE, XBIT, YBIT = 1, 2, 4


MESH = pl.DeviceIdType.MESH


def held_in_hbm(*values):
    return [pltpu.with_memory_space_constraint(value, pltpu.HBM) for value in values]


class Wires:
    def __init__(self, send, recv):
        self.send, self.recv, self.used = send, recv, 0
        self.device, self.shard = lax.axis_index(EXPERT), lax.axis_index(SHARD)

    def slot(self):
        self.used += 1
        return self.used - 1

    def peer(self, bits=0, step=0, shards=1):
        shard = lax.rem(self.shard + step, shards) if step else self.shard
        return (self.device ^ bits, shard)

    def copy(self, source, target, slot, peer):
        return pltpu.make_async_remote_copy(
            src_ref=source,
            dst_ref=target,
            send_sem=self.send.at[slot],
            recv_sem=self.recv.at[slot],
            device_id=peer,
            device_id_type=MESH,
        )


def greet(peers):
    barrier = pltpu.get_barrier_semaphore()
    for peer in peers:
        pl.semaphore_signal(barrier, inc=1, device_id=peer, device_id_type=MESH)
    pl.semaphore_wait(barrier, len(peers))


class Relay:
    def __init__(self, wires, shards, views):
        self.wires, self.shards, self.views = wires, shards, views
        self.slots = [[[wires.slot() for _ in views] for _ in range(shards - 1)] for _ in range(2)]

    def copies(self, way, step, block):
        wires = self.wires
        peer = (wires.device, wires.shard + (1 if way == 0 else -1))
        return [
            wires.copy(view(block), view(block), slot, peer)
            for view, slot in zip(self.views, self.slots[way][step], strict=True)
        ]

    def has(self, way, step):
        shard = self.wires.shard
        return shard - step >= 0 if way == 0 else shard + step < self.shards

    def sends(self, way, step):
        shard = self.wires.shard
        edge = shard < self.shards - 1 if way == 0 else shard > 0
        return jnp.logical_and(edge, self.has(way, step))

    def block(self, way, step):
        return self.wires.shard + (-step if way == 0 else step)

    def run(self, step, first=None):
        wires = self.wires
        for index, view in enumerate(self.views):
            for way in range(2):
                block = self.block(way, step)
                peer = (wires.device, wires.shard + (1 if way == 0 else -1))
                if step > 0:

                    @pl.when(self.has(way, step))
                    def _(way=way, block=block, index=index, view=view, peer=peer):
                        slot = self.slots[way][step - 1][index]
                        wires.copy(view(block), view(block), slot, peer).wait_recv()

                if step < self.shards - 1:

                    @pl.when(self.sends(way, step))
                    def _(way=way, block=block, index=index, view=view, peer=peer):
                        source = view(block) if first is None else first[index]
                        slot = self.slots[way][step][index]
                        wires.copy(source, view(block), slot, peer).start()

    def drain(self):
        for way in range(2):
            for step in range(self.shards - 1):

                @pl.when(self.sends(way, step))
                def _(way=way, step=step):
                    for copy in self.copies(way, step, self.block(way, step)):
                        copy.wait_send()


class Plane:
    def __init__(self, wires, views, whole):
        self.wires, self.views, self.whole = wires, views, whole
        count = len(views)
        self.first = [[wires.slot() for _ in range(count)] for _ in range(2)]
        self.second = [[[wires.slot() for _ in range(count)] for _ in range(2)] for _ in range(2)]
        self.last = [[wires.slot() for _ in range(count)] for _ in range(4)]
        self.sent = []

    def start(self, copies):
        for copy in copies:
            copy.start()
        self.sent += copies

    def one(self, owner, half, bits, slots):
        wires = self.wires
        return [
            wires.copy(view(owner, half), view(owner, half), slot, wires.peer(bits))
            for view, slot in zip(self.views, slots, strict=True)
        ]

    def step_one(self):
        me = self.wires.device
        for half, bits in enumerate((XBIT, YBIT)):
            self.start(self.one(me, half, bits, self.first[half]))

    def step_two(self):
        me = self.wires.device
        for half, bits in enumerate((XBIT, YBIT)):
            for copy in self.one(me ^ bits, half, bits, self.first[half]):
                copy.wait_recv()
        for half, bits in enumerate((XBIT, YBIT)):
            other = (XBIT | YBIT) ^ bits
            self.start(self.one(me, half, other, self.second[half][0]))
            self.start(self.one(me ^ bits, half, other, self.second[half][1]))

    def cores(self, index):
        wires = self.wires
        owner = wires.device ^ (0, XBIT, YBIT, XBIT | YBIT)[index]
        return [
            wires.copy(place(owner), place(owner), slot, wires.peer(CORE))
            for place, slot in zip(self.whole, self.last[index], strict=True)
        ]

    def step_three(self):
        me = self.wires.device
        for half, bits in enumerate((XBIT, YBIT)):
            other = (XBIT | YBIT) ^ bits
            for owner, slots in ((me ^ other, 0), (me ^ other ^ bits, 1)):
                for copy in self.one(owner, half, other, self.second[half][slots]):
                    copy.wait_recv()
        for index in range(1, 4):
            self.start(self.cores(index))

    def finish(self):
        for index, bits in enumerate((0, XBIT, YBIT, XBIT | YBIT)):
            owner = self.wires.device ^ CORE ^ bits
            for place, slot in zip(self.whole, self.last[index], strict=True):
                self.wires.copy(
                    place(owner), place(owner), slot, self.wires.peer(CORE)
                ).wait_recv()
        for copy in self.sent:
            copy.wait_send()


def opening_kernel(
    shards, planes, experts, own_experts, capacity, bits,
    routes, order, gains, seg_row, seg_col, cosine, sine,
    router, w_query, w_key, w_value, tokens, w_out, out_grad,
    kept_out, attn_row, ffn_row, query_row, key_row, normed_out, raw_out, low_out, total_out, mixed_all,
    router_all, qkv_w_out, tokens_all, out_w_out, grad_out,
    small, small_all, grad_all, qkv_w, out_w, mixed, qkv, send, recv, local, store,
):
    wires = Wires(send, recv)
    device, shard = wires.device, wires.shard
    weights = (w_query, w_key, w_value)
    block, width = w_query.shape
    rows = tokens.shape[0]
    part = width // shards
    mine = device * shards + shard
    greet(
        [wires.peer(step=step, shards=shards) for step in range(1, shards)]
        + [wires.peer(XBIT), wires.peer(YBIT), wires.peer(CORE)]
    )

    def place(source_shard, which):
        start = pl.multiple_of((device * shards + source_shard) * block, block)
        return qkv_w.at[pl.ds(start, block), pl.ds(which * part, part)]

    def cut(which, target):
        return weights[which].at[:, pl.ds(pl.multiple_of(target * part, part), part)]

    def token_rows(b):
        return tokens_all.at[pl.ds(pl.multiple_of(b * rows, rows), rows)]

    def out_rows(owner, source):
        return out_w.at[pl.ds(pl.multiple_of((owner * shards + source) * block, block), block)]

    def grad_block(owner, source):
        return (owner * shards + source) * rows

    def grad_rows(owner, source):
        return grad_all.at[pl.ds(pl.multiple_of(grad_block(owner, source), rows), rows)]

    def grad_half(source):
        def view(owner, half):
            start = grad_block(owner, source) + half * (rows // 2)
            return grad_all.at[pl.ds(pl.multiple_of(start, rows // 2), rows // 2)]

        return view

    exchange = [[wires.slot() for _ in range(5)] for _ in range(1, shards)]
    sent = []
    for step in range(1, shards):
        peer = wires.peer(step=step, shards=shards)
        slots = exchange[step - 1]
        copies = [
            wires.copy(cut(which, peer[1]), place(shard, which), slots[which], peer)
            for which in range(3)
        ]
        copies.append(wires.copy(router, router_all.at[mine], slots[4], peer))
        for copy in copies:
            copy.start()
        sent += copies
    grad_line = Relay(wires, shards, [lambda b: grad_rows(device, b)])
    token_line = Relay(wires, shards, [token_rows])
    out_line = Relay(wires, shards, [lambda b: out_rows(device, b)])
    mixed_line = Relay(wires, shards, [lambda b: mixed_all.at[b]])
    own = [
        pltpu.make_async_copy(out_grad, grad_rows(device, shard), local.at[0]),
        pltpu.make_async_copy(router, router_all.at[mine], local.at[1]),
        pltpu.make_async_copy(tokens, token_rows(shard), local.at[2]),
        pltpu.make_async_copy(w_out, out_rows(device, shard), local.at[3]),
    ]
    own += [
        pltpu.make_async_copy(cut(which, shard), place(shard, which), local.at[4 + which])
        for which in range(3)
    ]
    for copy in own:
        copy.start()
    turns = [shard] + [
        sum(jnp.where(shard == index, source, 0) for index, source in enumerate(row))
        for row in ((1, 0, 1, 2), (2, 2, 3, 1), (3, 3, 0, 0))
    ]
    stages = [
        Plane(wires, [grad_half(source)], [lambda owner, source=source: grad_rows(owner, source)])
        for source in turns
    ]
    stored = []

    def begin(stage):
        stage.step_one()
        stage.start(stage.cores(0))

    def keep(turn):
        stages[turn].finish()
        for owner in range(planes):
            start = pl.multiple_of(grad_block(owner, turns[turn]), rows)
            copy = pltpu.make_async_copy(
                grad_rows(owner, turns[turn]),
                grad_out.at[pl.ds(start, rows)],
                store.at[turn * planes + owner],
            )
            copy.start()
            stored.append(copy)

    own[0].wait()
    begin(stages[0])
    column = lax.broadcasted_iota(jnp.int32, (rows, 128), 1)
    dense = jnp.zeros((rows, 128), jnp.int32)
    for choice in range(routes.shape[1]):
        named = routes[:, choice : choice + 1] == column
        dense = dense + jnp.where(named, order[:, choice : choice + 1] + 1, 0)
    high = lax.shift_right_logical(dense, 8)
    for start, digits in ((0, high), (experts, dense - high * 256)):
        turned = digits.astype(jnp.float32).T
        small[pl.ds(start, experts), :] = turned[:experts, :].astype(small.dtype)
    small[pl.ds(2 * experts, gains.shape[0]), :] = gains[...]
    small_all[mine] = small[...]
    for step in range(1, shards):
        peer = wires.peer(step=step, shards=shards)
        copy = wires.copy(small, small_all.at[mine], exchange[step - 1][3], peer)
        copy.start()
        sent.append(copy)
    out_line.run(0, (w_out,))
    token_line.run(0, (tokens,))
    stages[0].step_two()
    for copy in own[1:]:
        copy.wait()
    for step in range(1, shards):
        peer = wires.peer(step=shards - step, shards=shards)
        source = peer[1]
        slots = exchange[step - 1]
        for which in range(3):
            wires.copy(place(source, which), place(source, which), slots[which], peer).wait_recv()
        wires.copy(router, router_all.at[device * shards + source], slots[4], peer).wait_recv()
        wires.copy(small, small_all.at[device * shards + source], slots[3], peer).wait_recv()

    each = shards * block // 2

    def rows_of(owner, half):
        return qkv_w.at[pl.ds(pl.multiple_of((owner * 2 + half) * each, each), each)]

    def small_of(owner, half):
        return small_all.at[pl.ds((owner * 2 + half) * (shards // 2), shards // 2)]

    def router_of(owner, half):
        return router_all.at[pl.ds((owner * 2 + half) * (shards // 2), shards // 2)]

    plane = Plane(
        wires,
        [rows_of, small_of, router_of],
        [
            lambda owner: qkv_w.at[pl.ds(pl.multiple_of(owner * 2 * each, 2 * each), 2 * each)],
            lambda owner: small_all.at[pl.ds(owner * shards, shards)],
            lambda owner: router_all.at[pl.ds(owner * shards, shards)],
        ],
    )
    outs = [
        Plane(
            wires,
            [
                lambda owner, side, index=index: out_w.at[
                    pl.ds(
                        pl.multiple_of(owner * 2 * each + index * each + side * (each // 2), each // 2),
                        each // 2,
                    )
                ]
            ],
            [
                lambda owner, index=index: out_w.at[
                    pl.ds(pl.multiple_of((owner * 2 + index) * each, each), each)
                ]
            ],
        )
        for index in range(2)
    ]
    begin(plane)
    stages[0].step_three()
    out_line.run(1)
    token_line.run(1)
    plane.step_two()
    out_line.run(2)
    token_line.run(2)
    grad_line.run(0, (out_grad,))
    plane.step_three()
    keep(0)
    out_line.run(3)
    for stage in outs:
        begin(stage)
    plane.finish()

    count = width // 128
    start = 2 * experts
    summed = small_all[0, pl.ds(start, gains.shape[0]), :].astype(jnp.float32)
    for other in range(1, planes * shards):
        summed = summed + small_all[other, pl.ds(start, gains.shape[0]), :].astype(jnp.float32)
    attn_row[...] = jnp.concatenate([summed[i : i + 1] for i in range(count)], axis=1)
    ffn_row[...] = jnp.concatenate([summed[count + i : count + i + 1] for i in range(count)], axis=1)
    query_row[...] = summed[2 * count : 2 * count + 1]
    key_row[...] = summed[2 * count + 1 : 2 * count + 2]
    for stage in outs:
        stage.step_two()
    token_line.run(3)
    attend(
        tokens_all, attn_row, qkv_w, query_row, key_row, cosine, sine, seg_row, seg_col,
        normed_out, raw_out, low_out, mixed, total_out, qkv,
    )
    mixed_line.run(0, (mixed,))
    mixed_all[shard] = mixed[...]
    save_qkv = pltpu.make_async_copy(qkv_w, qkv_w_out, local.at[7])
    save_qkv.start()
    grad_line.run(1)
    begin(stages[1])
    for stage in outs:
        stage.step_three()
    mixed_line.run(1)
    stages[1].step_two()
    grad_line.run(2)
    begin(stages[2])
    for stage in outs:
        stage.finish()
    save_out = pltpu.make_async_copy(out_w, out_w_out, local.at[8])
    save_out.start()
    mixed_line.run(2)
    stages[1].step_three()
    stages[2].step_two()
    mark_kept(
        small_all, device * own_experts, experts, own_experts, capacity, bits, shards, kept_out
    )
    grad_line.run(3)
    begin(stages[3])
    stages[2].step_three()
    keep(1)
    mixed_line.run(3)
    stages[3].step_two()
    keep(2)
    stages[3].step_three()
    keep(3)
    for copy in sent:
        copy.wait_send()
    for group in (token_line, grad_line, out_line, mixed_line):
        group.drain()
    for copy in stored:
        copy.wait()
    save_qkv.wait()
    save_out.wait()


def opening_call(
    routes, order, gains, seg_row, seg_col, tables, router, w_query, w_key, w_value, tokens, w_out, out_grad,
    experts, own_experts, capacity, planes, shards,
):
    block, width = w_query.shape
    rows, top_count = routes.shape
    seq, part = shards * rows, width // shards
    hbm = pl.BlockSpec(memory_space=pltpu.HBM)
    vmem = pl.BlockSpec(memory_space=pltpu.VMEM)
    place = pl.BlockSpec(memory_space=pl.ANY)
    slots = 144
    low, full = tokens.dtype, jnp.float32
    small = (2 * experts + gains.shape[0], 128)
    most = planes * shards * rows * top_count
    return pl.pallas_call(
        functools.partial(
            opening_kernel, shards, planes, experts, own_experts, capacity, most.bit_length()
        ),
        in_specs=[vmem] * 7 + [place] * 7,
        out_specs=[vmem] * 10 + [place, hbm, vmem, hbm, hbm],
        out_shape=(
            jax.ShapeDtypeStruct((planes, seq, own_experts), full),
            jax.ShapeDtypeStruct((1, width), full),
            jax.ShapeDtypeStruct((1, width), full),
            jax.ShapeDtypeStruct((1, HD), full),
            jax.ShapeDtypeStruct((1, HD), full),
            jax.ShapeDtypeStruct((seq, width), low),
            jax.ShapeDtypeStruct((seq, 2 * part), full),
            jax.ShapeDtypeStruct((seq, 3 * part), low),
            jax.ShapeDtypeStruct((seq, 128), full),
            jax.ShapeDtypeStruct((shards, seq, part), low),
            jax.ShapeDtypeStruct((planes * shards,) + router.shape, router.dtype),
            pltpu.HBM((width, 3 * part), low),
            jax.ShapeDtypeStruct((seq, width), low),
            pltpu.HBM((width, width), low),
            pltpu.HBM((planes * seq, width), low),
        ),
        scratch_shapes=[
            pltpu.VMEM(small, gains.dtype),
            pltpu.VMEM((planes * shards,) + small, gains.dtype),
            pltpu.VMEM((planes * seq, width), low),
            pltpu.VMEM((width, 3 * part), low),
            pltpu.VMEM((width, width), low),
            pltpu.VMEM((seq, part), low),
            pltpu.VMEM((seq, 3 * part), full),
            pltpu.SemaphoreType.DMA((slots,)),
            pltpu.SemaphoreType.DMA((slots,)),
            pltpu.SemaphoreType.DMA((9,)),
            pltpu.SemaphoreType.DMA((planes * shards,)),
        ],
        compiler_params=pltpu.CompilerParams(
            collective_id=1, has_side_effects=True, vmem_limit_bytes=60 * MIB
        ),
        cost_estimate=pl.CostEstimate(flops=0, bytes_accessed=200 * MIB, transcendentals=0),
    )(
        routes, order, gains, seg_row, seg_col, *tables, router, w_query, w_key, w_value, tokens, w_out, out_grad
    )


class Units:
    def __init__(self, wires, shards, index, gate, up, down, wide_w, down_w, local, base):
        self.wires, self.shards, self.index = wires, shards, index
        self.gate, self.up, self.down, self.wide_w, self.down_w = gate, up, down, wide_w, down_w
        self.local, self.base = local, base
        self.slots = [[wires.slot() for _ in range(3)] for _ in range(1, shards)]

    def pairs(self, source, target):
        each = self.down_w.shape[1]
        span = pl.ds(pl.multiple_of(target * each, each), each)
        return [
            (self.gate.at[self.index, :, span], self.wide_w.at[source, :, pl.ds(0, each)]),
            (self.up.at[self.index, :, span], self.wide_w.at[source, :, pl.ds(each, each)]),
            (self.down.at[self.index, span, :], self.down_w.at[source]),
        ]

    def own(self):
        shard = self.wires.shard
        return [
            pltpu.make_async_copy(source, place, self.local.at[self.base + slot])
            for slot, (source, place) in enumerate(self.pairs(shard, shard))
        ]

    def sends(self):
        wires = self.wires
        for step in range(1, self.shards):
            peer = wires.peer(step=step, shards=self.shards)
            pairs = self.pairs(wires.shard, peer[1])
            for slot, (source, place) in zip(self.slots[step - 1], pairs, strict=True):
                yield wires.copy(source, place, slot, peer)

    def begin(self):
        for copy in self.own():
            copy.start()
        for copy in self.sends():
            copy.start()

    def end(self):
        wires = self.wires
        for copy in self.own():
            copy.wait()
        for step in range(1, self.shards):
            back = wires.peer(step=self.shards - step, shards=self.shards)
            pairs = self.pairs(back[1], wires.shard)
            for slot, (_, place) in zip(self.slots[step - 1], pairs, strict=True):
                wires.copy(place, place, slot, back).wait_recv()
        for copy in self.sends():
            copy.wait_send()


def meeting_kernel(
    shards, planes, tokens, gain, mixed_all, out_w, gate, up, down,
    hidden_out, mixed_own, normed_out, wide_w, down_w, normed_all, send, recv, local, store,
):
    wires = Wires(send, recv)
    device, shard = wires.device, wires.shard
    seq, _ = tokens.shape
    rows, part = hidden_out.shape[0], mixed_all.shape[2]
    half = seq // 2
    greet(
        [wires.peer(step=step, shards=shards) for step in range(1, shards)]
        + [wires.peer(XBIT), wires.peer(YBIT), wires.peer(CORE)]
    )
    units = Units(wires, shards, 0, gate, up, down, wide_w, down_w, local, 0)
    units.begin()

    def stage(index):
        def view(owner, start, size):
            return normed_all.at[owner, pl.ds(start, size)]

        return Plane(
            wires,
            [lambda owner, side: view(owner, index * half + side * (half // 2), half // 2)],
            [lambda owner: view(owner, index * half, half)],
        )

    stages = [stage(index) for index in range(2)]
    for side in range(2):
        span = pl.ds(side * half, half)
        total = tokens[span, :].astype(jnp.float32)
        for source in range(shards):
            total = total + jnp.dot(
                mixed_all[source, span, :],
                out_w[pl.ds(source * part, part), :],
                preferred_element_type=jnp.float32,
            )
        normed_all[device, span, :] = (total * norm_factor(total) * gain[...]).astype(
            normed_all.dtype
        )
        stages[side].step_one()
        stages[side].start(stages[side].cores(0))
        for inner in range(half // rows):

            @pl.when(shard == side * (half // rows) + inner)
            def _(total=total, inner=inner):
                hidden_out[...] = total[inner * rows : (inner + 1) * rows, :]

    stored = []

    def keep(owner, side):
        span = pl.ds(side * half, half)
        copy = pltpu.make_async_copy(
            normed_all.at[owner, span], normed_out.at[owner, span], store.at[len(stored)]
        )
        copy.start()
        stored.append(copy)

    for source in range(shards):
        mixed_own[:, pl.ds(source * part, part)] = mixed_all[
            source, pl.ds(pl.multiple_of(shard * rows, rows), rows), :
        ]
    for plane in stages:
        plane.step_two()
    for side, plane in enumerate(stages):
        plane.step_three()
        for chip in range(4):
            keep(device ^ (2 * chip), side)
    for side, plane in enumerate(stages):
        plane.finish()
        for chip in range(4):
            keep(device ^ (2 * chip + 1), side)
    units.end()
    for copy in stored:
        copy.wait()


def unit_shapes(gate, shards):
    _, part, hidden_units = gate.shape
    each = hidden_units // shards
    return (
        jax.ShapeDtypeStruct((shards, part, 2 * each), gate.dtype),
        jax.ShapeDtypeStruct((shards, each, part), gate.dtype),
    )


def meeting_call(tokens, gain, mixed_all, out_w, gate, up, down, planes, shards):
    hbm = pl.BlockSpec(memory_space=pltpu.HBM)
    vmem = pl.BlockSpec(memory_space=pltpu.VMEM)
    seq, width = tokens.shape
    rows = seq // shards
    slots = 32
    low = tokens.dtype
    return pl.pallas_call(
        functools.partial(meeting_kernel, shards, planes),
        in_specs=[vmem] * 4 + [hbm] * 3,
        out_specs=[vmem] * 2 + [hbm] * 3,
        out_shape=(
            jax.ShapeDtypeStruct((rows, width), jnp.float32),
            jax.ShapeDtypeStruct((rows, width), low),
            pltpu.HBM((planes, seq + 16, width), low),
        )
        + unit_shapes(gate, shards),
        scratch_shapes=[
            pltpu.VMEM((planes, seq, width), low),
            pltpu.SemaphoreType.DMA((slots,)),
            pltpu.SemaphoreType.DMA((slots,)),
            pltpu.SemaphoreType.DMA((3,)),
            pltpu.SemaphoreType.DMA((2 * planes,)),
        ],
        compiler_params=pltpu.CompilerParams(
            collective_id=3, has_side_effects=True, vmem_limit_bytes=40 * MIB
        ),
        cost_estimate=pl.CostEstimate(
            flops=2 * seq * width * width, bytes_accessed=300 * MIB, transcendentals=0
        ),
    )(tokens, gain, mixed_all, out_w, gate, up, down)


def add_rows(target, sources, lines):
    rows = target.shape[0]

    def body(index, carry):
        span = pl.ds(pl.multiple_of(index * lines, lines), lines)
        total = target[span, :].astype(jnp.float32)
        for source in sources:
            total = total + source[span, :].astype(jnp.float32)
        target[span, :] = total.astype(target.dtype)
        return carry

    lax.fori_loop(0, rows // lines, body, 0)


class PlaneSum:
    def __init__(self, wires, part, held, came, diag, side, local, base):
        self.wires, self.part, self.local, self.base = wires, part, local, base
        self.held, self.came, self.diag, self.side = held, came, diag, side
        self.half = held.shape[1] // 2
        self.core = [wires.slot() for _ in range(4)]
        self.corner = [wires.slot() for _ in range(2)]
        self.edge = [wires.slot() for _ in range(2)]
        self.sent = []

    def start(self, copy):
        copy.start()
        self.sent.append(copy)

    def load(self, chip):
        return pltpu.make_async_copy(
            self.part(chip, 0), self.held.at[chip], self.local.at[self.base + chip]
        )

    def give(self, chip):
        self.start(
            self.wires.copy(
                self.held.at[chip], self.came.at[chip], self.core[chip], self.wires.peer(CORE)
            )
        )

    def begin(self):
        for chip in (3, 1, 2, 0):
            self.load(chip).start()
            self.start(
                self.wires.copy(
                    self.part(chip, 1), self.came.at[chip], self.core[chip], self.wires.peer(CORE)
                )
            )

    def add_core(self, chip):
        if self.part is not None:
            self.load(chip).wait()
        place = self.came.at[chip]
        self.wires.copy(place, place, self.core[chip], self.wires.peer(CORE)).wait_recv()
        add_rows(self.held.at[chip], [place], 64)

    def part_of_corner(self, which):
        return self.held.at[3, pl.ds(which * self.half, self.half)]

    def send_corner(self):
        self.add_core(3)
        for which, bits in enumerate((XBIT, YBIT)):
            self.start(
                self.wires.copy(
                    self.part_of_corner(which),
                    self.diag.at[which],
                    self.corner[which],
                    self.wires.peer(bits),
                )
            )

    def add_cores(self):
        for chip in (1, 2, 0):
            self.add_core(chip)

    def send_sides(self):
        for which, (bits, chip) in enumerate(((XBIT, 2), (YBIT, 1))):
            place = self.diag.at[which]
            self.wires.copy(place, place, self.corner[which], self.wires.peer(bits)).wait_recv()
            add_rows(self.held.at[chip, pl.ds(which * self.half, self.half)], [place], 64)
            self.start(
                self.wires.copy(
                    self.held.at[chip],
                    self.side.at[1 - which],
                    self.edge[1 - which],
                    self.wires.peer((XBIT | YBIT) ^ bits),
                )
            )

    def end(self):
        for which, bits in enumerate((XBIT, YBIT)):
            place = self.side.at[which]
            self.wires.copy(place, place, self.edge[which], self.wires.peer(bits)).wait_recv()
        add_rows(self.held.at[0], [self.side.at[0], self.side.at[1]], 64)

    def drain(self):
        for copy in self.sent:
            copy.wait_send()


class LineSum:
    def __init__(self, wires, shards, source, landing):
        self.wires, self.shards, self.source, self.landing = wires, shards, source, landing
        self.slots = [wires.slot() for _ in range(shards - 1)]

    def sends(self):
        wires = self.wires
        for step in range(1, self.shards):
            peer = wires.peer(step=step, shards=self.shards)
            yield wires.copy(
                self.source(peer[1]), self.landing(wires.shard), self.slots[step - 1], peer
            )

    def begin(self):
        for copy in self.sends():
            copy.start()

    def arrive(self):
        wires = self.wires
        for step in range(1, self.shards):
            peer = wires.peer(step=self.shards - step, shards=self.shards)
            place = self.landing(peer[1])
            wires.copy(place, place, self.slots[step - 1], peer).wait_recv()

    def drain(self):
        for copy in self.sends():
            copy.wait_send()


class LineFlow:
    def __init__(self, wires, shards, own, flow):
        self.wires, self.shards, self.own, self.flow = wires, shards, own, flow
        self.slots = [[wires.slot() for _ in range(shards)] for _ in range(2)]
        self.order = [
            (way, (shards - 1 - step) if way == 0 else step)
            for step in range(shards - 1)
            for way in range(2)
        ]

    def copy(self, way, block, source):
        wires = self.wires
        peer = (wires.device, wires.shard + (1 if way == 0 else -1))
        return wires.copy(source, self.flow.at[way, block], self.slots[way][block], peer)

    def first(self, way):
        return self.wires.shard == (0 if way == 0 else self.shards - 1)

    def passes(self, way, block):
        shard = self.wires.shard
        inner = jnp.logical_and(shard > 0, shard < block)
        if way == 1:
            inner = jnp.logical_and(shard < self.shards - 1, shard > block)
        return inner

    def begin(self):
        for way, block in self.order:

            @pl.when(self.first(way))
            def _(way=way, block=block):
                self.copy(way, block, self.own(block)).start()

    def forward(self, way, block):
        @pl.when(self.passes(way, block))
        def _():
            place = self.flow.at[way, block]
            self.copy(way, block, place).wait_recv()
            add_rows(place, [self.own(block)], 64)
            self.copy(way, block, place).start()

    def end(self):
        shard = self.wires.shard
        for block in range(self.shards):

            @pl.when(shard == block)
            def _(block=block):
                sources = []
                for way in range(2):
                    if block != (0 if way == 0 else self.shards - 1):
                        place = self.flow.at[way, block]
                        self.copy(way, block, place).wait_recv()
                        sources.append(place)
                add_rows(self.own(block), sources, 64)

    def drain(self):
        for way, block in self.order:
            sends = jnp.logical_or(self.first(way), self.passes(way, block))

            @pl.when(sends)
            def _(way=way, block=block):
                self.copy(way, block, self.own(block)).wait_send()


def line_total(landing, shards):
    total = landing[0].astype(jnp.float32)
    for shard in range(1, shards):
        total = total + landing[shard].astype(jnp.float32)
    return total


def aligned(index, size):
    return pl.ds(pl.multiple_of(index * size, size), size)


def expert_kernel(
    index, experts, shards, x, g, keep, wide_w, router_w, down_w, hot, *refs
):
    if index == 0:
        gate, up, down, out, grad, pull, wide_sum, down_sum, next_wide, next_down = refs[:10]
        acc, dacc, wide_out, down_out, send, recv, local, sems = refs[10:]
    else:
        old_out, old_grad, old_pull, wide_sent, down_sent = refs[:5]
        out, grad, wide_sum, down_sum, router_sum, wide_came, down_came = refs[5:12]
        acc, racc, dacc, wide_out, down_out, send, recv, local, sems = refs[12:]
    step, steps = pl.program_id(0), pl.num_programs(0)
    wires = Wires(send, recv)
    if index == 0:
        travel = [Units(wires, shards, 1, gate, up, down, next_wide, next_down, local, 0)]
    else:
        travel = [
            LineSum(wires, shards, lambda t: wide_sent.at[t], lambda s: wide_came.at[s]),
            LineSum(wires, shards, lambda t: down_sent.at[t], lambda s: down_came.at[s]),
        ]
        stay = [
            pltpu.make_async_copy(
                sent.at[wires.shard], came.at[wires.shard], local.at[place]
            )
            for place, (sent, came) in enumerate(((wide_sent, wide_came), (down_sent, down_came)))
        ]

    @pl.when(step == 0)
    def _():
        greet([wires.peer(step=hop, shards=shards) for hop in range(1, shards)])
        for group in travel:
            group.begin()
        acc[...] = jnp.zeros_like(acc)
        dacc[...] = jnp.zeros_like(dacc)
        if index == 1:
            for copy in stay:
                copy.start()
            racc[...] = jnp.zeros_like(racc)

    _, each, part = down_w.shape
    wide = jnp.dot(x[...], wide_w[...], preferred_element_type=jnp.float32)
    back = nt_dot(g[:, :part], down_w[0])
    for shard in range(1, shards):
        back = back + nt_dot(g[:, shard * part : (shard + 1) * part], down_w[shard])
    if index == 0:
        logits = jnp.dot(x[...], router_w[...], preferred_element_type=jnp.float32)
        lane = lax.broadcasted_iota(jnp.int32, logits.shape, 1)
        logits = jnp.where(lane < experts, logits, -1e30)
        shifted = jnp.exp(logits - jnp.max(logits, axis=-1, keepdims=True))
        probs = shifted / jnp.sum(shifted, axis=-1, keepdims=True)
    else:
        lane = lax.broadcasted_iota(jnp.int32, old_pull.shape, 1)
        probs = jnp.where(lane < experts, old_pull[...], 0.0)
    mark = hot[index : index + 1, :]
    kept = keep[:, index : index + 1]
    route = jnp.sum(probs * mark, axis=-1, keepdims=True) * kept
    gated, lifted = wide[:, :each], wide[:, each:]
    sigma = 1.0 / (1.0 + jnp.exp(-gated))
    silu = gated * sigma
    act = silu * lifted
    pulled = jnp.sum(act * back, axis=-1, keepdims=True) * kept
    act_low = (act * route).astype(jnp.bfloat16)
    act_grad = back * route
    wide_low = jnp.concatenate(
        [
            (act_grad * lifted * sigma * (1.0 + gated * (1.0 - sigma))).astype(jnp.bfloat16),
            (act_grad * silu).astype(jnp.bfloat16),
        ],
        axis=1,
    )
    result = nt_dot(wide_low, wide_w[...])
    if index == 0:
        pull[...] = jnp.where(lane < experts, probs, jnp.where(lane == 127, pulled, 0.0))
    else:
        dense = pulled * mark + old_pull[:, 127:] * hot[0:1, :]
        logit_grad = probs * (dense - jnp.sum(probs * dense, axis=-1, keepdims=True))
        logit_low = logit_grad.astype(jnp.bfloat16)
        result = result + nt_dot(logit_low, router_w[...]) + old_grad[...].astype(jnp.float32)
        racc[...] += tn_dot(x[...], logit_low)
    grad[...] = result.astype(jnp.bfloat16)
    for shard in range(shards):
        span = slice(shard * part, (shard + 1) * part)
        value = jnp.dot(act_low, down_w[shard], preferred_element_type=jnp.float32)
        if index == 1:
            value = value + old_out[:, span].astype(jnp.float32)
        out[:, span] = value.astype(jnp.bfloat16)
        dacc[shard] += tn_dot(act_low, g[:, span])
    acc[...] += tn_dot(x[...], wide_low)

    @pl.when(step == steps - 1)
    def _():
        wide_out[...] = acc[...].astype(jnp.bfloat16)
        wide_copy = pltpu.make_async_copy(wide_out, wide_sum, sems.at[0])
        wide_copy.start()
        down_out[...] = dacc[...].astype(jnp.bfloat16)
        down_copy = pltpu.make_async_copy(down_out, down_sum, sems.at[1])
        down_copy.start()
        if index == 1:
            router_copy = pltpu.make_async_copy(racc, router_sum, sems.at[2])
            router_copy.start()
            router_copy.wait()
        wide_copy.wait()
        down_copy.wait()
        if index == 0:
            travel[0].end()
        else:
            for copy in stay:
                copy.wait()
            for group in travel:
                group.arrive()
                group.drain()


def expert_call(index, x_all, g_all, keep, wide_w, router_w, down_w, hot, experts, weights, before):
    planes, _, width = x_all.shape
    rows = keep.shape[1]
    shards = down_w.shape[0]
    tile = 512
    per = rows // tile
    hbm = pl.BlockSpec(memory_space=pltpu.HBM)

    def whole(value):
        zeros = (0,) * value.ndim
        return pl.BlockSpec(value.shape, lambda i: zeros, pipeline_mode=pl.Buffered(1))

    def rowwise(lanes):
        return pl.BlockSpec((None, tile, lanes), lambda i: (i // per, i % per, 0))

    low = jnp.bfloat16
    tall = pltpu.HBM((planes, rows, width), low)
    narrow = pltpu.HBM((planes, rows, 128), jnp.float32)
    wide_shape = pltpu.HBM(wide_w.shape, low)
    down_shape = pltpu.HBM(down_w.shape, low)
    came = pltpu.HBM((shards, width // shards, wide_w.shape[1]), low)
    if index == 0:
        others = [hbm] * 3
        out_specs = [rowwise(width)] * 2 + [rowwise(128)] + [hbm] * 4
        spare = [pltpu.HBM((planes, rows + extra, width), low) for extra in (32, 48)]
        shapes = (*spare, narrow, wide_shape, down_shape, came, down_shape)
        operands = held_in_hbm(*weights)
    else:
        others = [rowwise(width)] * 2 + [rowwise(128)] + [hbm] * 2
        out_specs = [rowwise(width)] * 2 + [hbm] * 5
        router_shape = pltpu.HBM(router_w.shape, jnp.float32)
        shapes = (tall, tall, wide_shape, down_shape, router_shape, came, down_shape)
        operands = held_in_hbm(*before)
    return pl.pallas_call(
        functools.partial(expert_kernel, index, experts, shards),
        grid=(planes * per,),
        in_specs=[
            rowwise(width),
            rowwise(width),
            rowwise(keep.shape[2]),
            whole(wide_w),
            whole(router_w),
            whole(down_w),
            whole(hot),
        ]
        + others,
        out_specs=out_specs,
        scratch_shapes=[pltpu.VMEM(wide_w.shape, jnp.float32)]
        + ([] if index == 0 else [pltpu.VMEM(router_w.shape, jnp.float32)])
        + [
            pltpu.VMEM(down_w.shape, jnp.float32),
            pltpu.VMEM(wide_w.shape, low),
            pltpu.VMEM(down_w.shape, low),
            pltpu.SemaphoreType.DMA((12,)),
            pltpu.SemaphoreType.DMA((12,)),
            pltpu.SemaphoreType.DMA((3,)),
            pltpu.SemaphoreType.DMA((3,)),
        ],
        out_shape=shapes,
        compiler_params=pltpu.CompilerParams(
            collective_id=7 + index, has_side_effects=True, vmem_limit_bytes=52 * MIB
        ),
        cost_estimate=pl.CostEstimate(
            flops=planes * rows * width * 12 * down_w.shape[1],
            bytes_accessed=100 * MIB,
            transcendentals=planes * rows * down_w.shape[1],
        ),
    )(*held_in_hbm(x_all, g_all), keep, wide_w, router_w, down_w, hot, *operands)


def returning_kernel(
    shards, ins, outs, wide, down, in_total, out_total, wide_all, down_all,
    held, came, diag, side, held2, came2, diag2, side2, landing, send, recv, local,
):
    wires = Wires(send, recv)
    device, shard = wires.device, wires.shard
    rows = in_total.shape[0]
    greet(
        [wires.peer(step=step, shards=shards) for step in range(1, shards)]
        + [wires.peer(XBIT), wires.peer(YBIT), wires.peer(CORE)]
    )

    def rel(source):
        return lambda chip, core: source.at[device ^ (2 * chip + core)]

    grads = PlaneSum(wires, rel(ins), held, came, diag, side, local, 0)
    values = PlaneSum(wires, rel(outs), held2, came2, diag2, side2, local, 6)
    weights = [
        LineSum(wires, shards, lambda t: wide.at[t], lambda s: wide_all.at[s]),
        LineSum(wires, shards, lambda t: down.at[t], lambda s: down_all.at[s]),
    ]
    line = LineSum(
        wires, shards, lambda t: held.at[0, aligned(t, rows)], lambda s: landing.at[s]
    )
    grads.begin()
    for group in weights:
        group.begin()
    own = [
        pltpu.make_async_copy(wide.at[shard], wide_all.at[shard], local.at[4]),
        pltpu.make_async_copy(down.at[shard], down_all.at[shard], local.at[5]),
    ]
    for copy in own:
        copy.start()
    grads.send_corner()
    values.begin()
    grads.add_cores()
    grads.send_sides()
    values.send_corner()
    values.add_cores()
    grads.end()
    line.begin()
    values.send_sides()
    landing[shard] = held[0, aligned(shard, rows), :]
    line.arrive()
    in_total[...] = line_total(landing, shards)
    values.end()
    back = pltpu.make_async_copy(held2.at[0], out_total, local.at[10])
    back.start()
    for copy in own:
        copy.wait()
    back.wait()
    for group in weights:
        group.arrive()
    for group in (grads, values, line, *weights):
        group.drain()


def sum_work(rows, lanes):
    low = jnp.bfloat16
    return [
        pltpu.VMEM((4, rows, lanes), low),
        pltpu.VMEM((4, rows, lanes), low),
        pltpu.VMEM((2, rows // 2, lanes), low),
        pltpu.VMEM((2, rows, lanes), low),
    ]


def returning_call(ins, outs, wide, down):
    _, seq, width = ins.shape
    shards = wide.shape[0]
    rows = seq // shards
    hbm = pl.BlockSpec(memory_space=pltpu.HBM)
    vmem = pl.BlockSpec(memory_space=pltpu.VMEM)
    return pl.pallas_call(
        functools.partial(returning_kernel, shards),
        in_specs=[hbm] * 4,
        out_specs=[vmem, hbm, hbm, hbm],
        out_shape=(
            jax.ShapeDtypeStruct((rows, width), jnp.float32),
            jax.ShapeDtypeStruct((seq, width), jnp.bfloat16),
            pltpu.HBM(wide.shape, wide.dtype),
            pltpu.HBM(down.shape, down.dtype),
        ),
        scratch_shapes=sum_work(seq, width)
        + sum_work(seq, width)
        + [
            pltpu.VMEM((shards, rows, width), jnp.bfloat16),
            pltpu.SemaphoreType.DMA((36,)),
            pltpu.SemaphoreType.DMA((36,)),
            pltpu.SemaphoreType.DMA((11,)),
        ],
        compiler_params=pltpu.CompilerParams(
            collective_id=4, has_side_effects=True, vmem_limit_bytes=56 * MIB
        ),
        cost_estimate=pl.CostEstimate(flops=0, bytes_accessed=300 * MIB, transcendentals=0),
    )(*held_in_hbm(ins, outs, wide, down))


def back_through_heads(
    mixed_grad, raw, low, total, query_gain, key_gain, cosine, sine, allowed, qkv_grad
):
    part = raw.shape[1] // 2
    gain_sums = [None, None]
    for head in range(part // HD):
        span = pl.ds(head * HD, HD)
        query, key = low[:, span], low[:, pl.ds(part + head * HD, HD)]
        value = low[:, pl.ds(2 * part + head * HD, HD)]
        out_grad = mixed_grad[:, span]
        scores = jnp.where(allowed, nt_dot(query, key), -1e30)
        probs = jnp.exp(scores - total[:, head : head + 1])
        prob_grad = nt_dot(out_grad, value)
        value_grad = tn_dot(probs.astype(jnp.bfloat16), out_grad)
        qkv_grad[:, pl.ds(2 * part + head * HD, HD)] = value_grad.astype(jnp.bfloat16)
        inner = jnp.sum(probs * prob_grad, axis=-1, keepdims=True)
        score_grad = (probs * (prob_grad - inner)).astype(jnp.bfloat16)
        rotated = (
            jnp.dot(score_grad, key, preferred_element_type=jnp.float32) * HD ** (-0.5),
            tn_dot(score_grad, query),
        )
        for which, (offset, scale_gain) in enumerate(((0, query_gain), (part, key_gain))):
            grad = rotated[which]
            grad = grad * cosine[...] - pltpu.roll(grad, HD // 2, 1) * sine[...]
            source = raw[:, pl.ds(offset + head * HD, HD)]
            factor = norm_factor(source)
            gain_sum = jnp.sum(grad * source * factor, axis=0, keepdims=True)
            gain_sums[which] = gain_sum if head == 0 else gain_sums[which] + gain_sum
            scaled = grad * scale_gain[...]
            inner = jnp.mean(scaled * source, axis=-1, keepdims=True)
            result = factor * scaled - source * (factor * factor * factor) * inner
            qkv_grad[:, pl.ds(offset + head * HD, HD)] = result.astype(jnp.bfloat16)
    return gain_sums


def closing_kernel(
    shards, planes,
    hidden, grad, out_grad, ffn_gain, raw, low, total, query_gain, key_gain, cosine, sine, seg_row, seg_col,
    tokens, gain, own_mixed, normed, router, out_w, qkv_w, out_total,
    input_grad, mixed_out, query_out, key_out, value_out, weight_out, gain_out, router_out, vectors_out,
    held, came, diag, side, held2, came2, diag2, side2,
    weights, hidden_grad, attn_low, message, message_land, qkv_grad, normed_grad, vectors,
    out_own, norm_land, out_land, qkv_land, weight_land, gain_mine, gain_land, gain_line, router_land, router_sum, router_line,
    vector_land, vector_sum, vector_line, send, recv, local,
):
    wires = Wires(send, recv)
    device, shard = wires.device, wires.shard
    rows, width = tokens.shape
    block = query_out.shape[0]
    part = width // shards
    lines = router_out.shape[0]
    lanes = qkv_w.shape[1]
    line_peers = [wires.peer(step=step, shards=shards) for step in range(1, shards)]
    plane_peers = [wires.peer(bits) for bits in range(1, planes)]
    load_out = pltpu.make_async_copy(out_w, weights, local.at[0])
    load_out.start()
    load_value = pltpu.make_async_copy(out_total, out_own, local.at[2])
    load_value.start()
    greet(line_peers + plane_peers)

    back = LineSum(
        wires, shards, lambda t: message.at[t], lambda s: message_land.at[aligned(s, rows)]
    )
    norms = LineFlow(wires, shards, lambda b: normed_grad.at[aligned(b, rows)], norm_land)
    values = LineFlow(wires, shards, lambda b: out_own.at[aligned(b, rows)], out_land)
    qkv = PlaneSum(wires, None, held, came, diag, side, local, 0)
    weight = PlaneSum(wires, None, held2, came2, diag2, side2, local, 0)
    qkv_line = LineSum(
        wires, shards, lambda t: held.at[0, aligned(t, block)], lambda s: qkv_land.at[s]
    )
    weight_line = LineSum(
        wires, shards, lambda t: held2.at[0, aligned(t, block)], lambda s: weight_land.at[s]
    )
    sent = []

    def spread(slots, source, landing):
        for bits in range(1, planes):
            copy = wires.copy(
                source(device ^ bits), landing.at[device], slots[bits - 1], wires.peer(bits)
            )
            copy.start()
            sent.append(copy)

    def collect(slots, landing):
        for bits in range(1, planes):
            place = landing.at[device ^ bits]
            wires.copy(place, place, slots[bits - 1], wires.peer(bits)).wait_recv()
        total = landing[0]
        for other in range(1, planes):
            total = total + landing[other]
        return total

    router_slots = [wires.slot() for _ in range(1, planes)]
    vector_slots = [wires.slot() for _ in range(1, planes)]
    gain_slots = [wires.slot() for _ in range(1, planes)]
    spread(router_slots, lambda e: router.at[aligned(e, shards * lines)], router_land)
    router_land[device] = router[aligned(device, shards * lines), :]

    factor = norm_factor(hidden[...])
    vectors[:, :width] = jnp.sum(grad[...] * hidden[...] * factor, axis=0, keepdims=True)
    scaled = grad[...] * ffn_gain[...]
    inner = jnp.mean(scaled * hidden[...], axis=-1, keepdims=True)
    change = out_grad[...].astype(jnp.float32) + factor * scaled
    change = change - hidden[...] * (factor * factor * factor) * inner
    hidden_grad[...] = change
    attn_low[...] = change.astype(jnp.bfloat16)
    load_out.wait()
    for target in range(shards):
        message[target] = nt_dot(attn_low[...], weights[pl.ds(target * part, part), :]).astype(
            jnp.bfloat16
        )
    back.begin()
    load_value.wait()
    values.begin()
    load_qkv = pltpu.make_async_copy(qkv_w, weights.at[:, pl.ds(0, lanes)], local.at[1])
    load_qkv.start()
    message_land[aligned(shard, rows), :] = message[shard]

    def addends(group, left, right):
        for core in (1, 0):
            for chip in (3, 1, 2, 0):
                owner = device ^ (2 * chip + core)
                columns = pl.ds(pl.multiple_of(owner * shards * block, shards * block), shards * block)
                if core == 0:
                    group.sent[(3, 1, 2, 0).index(chip)].wait_send()
                group.held[chip] = tn_dot(left[:, columns], right[...]).astype(jnp.bfloat16)
                if core == 1:
                    group.give(chip)
        group.sent = []

    addends(weight, own_mixed, attn_low)
    weight.send_corner()
    weight.add_cores()
    far = shards - 1
    values.forward(0, far)
    values.forward(1, 0)
    router_sum[...] = collect(router_slots, router_land)
    router_pass = LineSum(
        wires, shards, lambda t: router_sum.at[aligned(t, lines)], lambda s: router_line.at[s]
    )

    back.arrive()
    allowed = seg_col[...] == seg_row[...]
    query_sum, key_sum = back_through_heads(
        message_land, raw, low, total, query_gain, key_gain, cosine, sine, allowed, qkv_grad
    )
    vectors[:, pl.ds(width, HD)] = query_sum
    vectors[:, pl.ds(width + HD, HD)] = key_sum
    load_qkv.wait()
    normed_grad[...] = nt_dot(qkv_grad[...], weights[:, pl.ds(0, lanes)]).astype(jnp.bfloat16)
    norms.begin()
    for step in range(1, shards - 1):
        values.forward(0, far - step)
        values.forward(1, step)
    router_pass.begin()
    spread(vector_slots, lambda e: vectors, vector_land)
    vector_land[device] = vectors[...]
    weight.send_sides()
    addends(qkv, normed, qkv_grad)
    norms.forward(0, far)
    norms.forward(1, 0)
    qkv.send_corner()
    qkv.add_cores()
    for step in range(1, shards - 1):
        norms.forward(0, far - step)
        norms.forward(1, step)
    vector_sum[...] = collect(vector_slots, vector_land)
    vector_pass = LineSum(wires, shards, lambda t: vector_sum, lambda s: vector_line.at[s])
    vector_pass.begin()
    vector_line[shard] = vector_sum[...]
    router_line[shard] = router_sum[aligned(shard, lines), :]
    qkv.send_sides()
    weight.end()
    weight_line.begin()
    weight_land[shard] = held2[0, aligned(shard, block), :]
    values.end()
    mine = aligned(shard, rows)
    mixed_out[...] = (hidden[...] + out_own[mine, :].astype(jnp.float32)).astype(jnp.bfloat16)

    norms.end()
    change = normed_grad[mine, :].astype(jnp.float32)
    given = tokens[...].astype(jnp.float32)
    factor = norm_factor(given)
    gain_mine[...] = jnp.sum(change * given * factor, axis=0, keepdims=True)
    spread(gain_slots, lambda e: gain_mine, gain_land)
    scaled = change * gain[...]
    inner = jnp.mean(scaled * given, axis=-1, keepdims=True)
    result = hidden_grad[...] + factor * scaled - given * (factor * factor * factor) * inner
    input_grad[...] = result.astype(jnp.bfloat16)
    qkv.end()
    qkv_line.begin()
    qkv_land[shard] = held[0, aligned(shard, block), :]
    gain_land[device] = gain_mine[...]
    gain_line[shard] = collect(gain_slots, gain_land)
    gain_pass = LineSum(wires, shards, lambda t: gain_line.at[shard], lambda s: gain_line.at[s])
    gain_pass.begin()
    router_pass.arrive()
    router_out[...] = line_total(router_line, shards)
    vector_pass.arrive()
    vectors_out[...] = line_total(vector_line, shards)
    weight_line.arrive()
    weight_out[...] = line_total(weight_land, shards)
    qkv_line.arrive()
    for source in range(shards):
        for which, result_out in enumerate((query_out, key_out, value_out)):
            result_out[:, pl.ds(source * part, part)] = qkv_land[
                source, :, pl.ds(which * part, part)
            ].astype(jnp.float32)
    gain_pass.arrive()
    gain_out[...] = line_total(gain_line, shards)
    for copy in sent:
        copy.wait_send()
    groups = (back, norms, values, qkv, weight, qkv_line, weight_line, router_pass, vector_pass)
    for group in (*groups, gain_pass):
        group.drain()


def closing_call(
    hidden, grad, out_grad, ffn_gain, raw, low, total, query_gain, key_gain, tables, seg_row, seg_col,
    tokens, gain, own_mixed, normed, router, out_w, qkv_w, out_total, planes, shards,
):
    rows, width = tokens.shape
    seq, lanes = low.shape
    each = width // planes
    block = each // shards
    lines = router.shape[0] // (planes * shards)
    hbm = pl.BlockSpec(memory_space=pltpu.HBM)
    vmem = pl.BlockSpec(memory_space=pltpu.VMEM)
    half, full = jnp.bfloat16, jnp.float32
    weight_shape = jax.ShapeDtypeStruct((block, width), full)
    vector = width + 2 * HD
    return pl.pallas_call(
        functools.partial(closing_kernel, shards, planes),
        in_specs=[vmem] * 18 + [hbm] * 3,
        out_specs=[vmem] * 9,
        out_shape=(
            jax.ShapeDtypeStruct((rows, width), half),
            jax.ShapeDtypeStruct((rows, width), half),
            weight_shape,
            weight_shape,
            weight_shape,
            weight_shape,
            jax.ShapeDtypeStruct((1, width), full),
            jax.ShapeDtypeStruct((lines, 128), full),
            jax.ShapeDtypeStruct((1, vector), full),
        ),
        scratch_shapes=sum_work(each, lanes)
        + sum_work(each, width)
        + [
            pltpu.VMEM((width, width), half),
            pltpu.VMEM((rows, width), full),
            pltpu.VMEM((rows, width), half),
            pltpu.VMEM((shards, rows, width // shards), half),
            pltpu.VMEM((seq, width // shards), half),
            pltpu.VMEM((seq, lanes), half),
            pltpu.VMEM((seq, width), half),
            pltpu.VMEM((1, vector), full),
            pltpu.VMEM((seq, width), half),
            pltpu.VMEM((2, shards, rows, width), half),
            pltpu.VMEM((2, shards, rows, width), half),
            pltpu.VMEM((shards, block, lanes), half),
            pltpu.VMEM((shards, block, width), half),
            pltpu.VMEM((1, width), full),
            pltpu.VMEM((planes, 1, width), full),
            pltpu.VMEM((shards, 1, width), full),
            pltpu.VMEM((planes, shards * lines, 128), full),
            pltpu.VMEM((shards * lines, 128), full),
            pltpu.VMEM((shards, lines, 128), full),
            pltpu.VMEM((planes, 1, vector), full),
            pltpu.VMEM((1, vector), full),
            pltpu.VMEM((shards, 1, vector), full),
            pltpu.SemaphoreType.DMA((80,)),
            pltpu.SemaphoreType.DMA((80,)),
            pltpu.SemaphoreType.DMA((3,)),
        ],
        compiler_params=pltpu.CompilerParams(
            collective_id=6, has_side_effects=True, vmem_limit_bytes=62 * MIB
        ),
        cost_estimate=pl.CostEstimate(flops=0, bytes_accessed=300 * MIB, transcendentals=0),
    )(
        hidden, grad, out_grad, ffn_gain, raw, low, total, query_gain, key_gain, *tables, seg_row, seg_col,
        tokens, gain, own_mixed, normed, router, *held_in_hbm(out_w, qkv_w, out_total),
    )


LOW = jnp.bfloat16
WIDE = jnp.float32


def fast_local(
    tokens,
    segment_ids,
    routes,
    pair_order,
    attn_gain,
    w_query,
    w_key,
    w_value,
    query_gain,
    key_gain,
    w_out,
    ffn_gain,
    w_router,
    w_gate,
    w_up,
    w_down,
    out_grad,
):
    rows, width = tokens.shape
    top_count = routes.shape[1]
    planes = lax.axis_size(EXPERT)
    shards = lax.axis_size(SHARD)
    own_experts = w_gate.shape[0]
    experts = own_experts * planes
    capacity = 5 * rows * top_count // (4 * own_experts)
    seq = segment_ids.shape[0]
    device = lax.axis_index(EXPERT)
    shard = lax.axis_index(SHARD)
    part = width // shards

    index = device * shards + shard

    def placed(values, size):
        zeros = jnp.zeros((size,), values.dtype)
        return lax.dynamic_update_slice_in_dim(zeros, values, index * values.size, 0)

    gains = [placed(attn_gain, width), placed(ffn_gain, width)]
    gains += [placed(query_gain, HD), placed(key_gain, HD)]
    gains = jnp.concatenate(gains)
    gains = jnp.pad(gains, (0, -gains.size % (16 * 128))).reshape(-1, 128)
    router_pad = jnp.pad(w_router, ((0, 0), (0, 128 - experts)))
    tables = turn_tables(seq)
    seg_row, seg_col = segment_ids.reshape(1, seq), segment_ids.reshape(seq, 1)
    opened = opening_call(
        routes,
        pair_order.reshape(rows, top_count),
        gains,
        seg_row,
        seg_col,
        tables,
        router_pad,
        w_query,
        w_key,
        w_value,
        tokens,
        w_out,
        out_grad,
        experts,
        own_experts,
        capacity,
        planes,
        shards,
    )
    kept, attn_row, ffn_row, query_row, key_row, normed_low, raw, low, total, mixed_all = opened[:10]
    router_w, qkv_w, tokens_seq, out_w, grad_all = opened[10:]
    router_w = router_w.reshape(width, 128)
    hidden, own_mixed, token_all, wide_w, down_w = meeting_call(
        tokens_seq, ffn_row, mixed_all, out_w, w_gate, w_up, w_down, planes, shards
    )
    grad_all = grad_all.reshape(planes, seq, width)
    own_ids = device * own_experts + jnp.arange(own_experts, dtype=jnp.int32)
    own_hot = (own_ids[:, None] == jnp.arange(128, dtype=jnp.int32)[None, :]).astype(WIDE)
    out_first, in_first, pull, wide_sum, down_sum, wide_next, down_next = expert_call(
        0,
        token_all,
        grad_all,
        kept,
        wide_w.reshape(width, -1),
        router_w,
        down_w,
        own_hot,
        experts,
        (w_gate, w_up, w_down),
        None,
    )
    before = (out_first, in_first, pull, wide_sum.reshape(shards, part, -1), down_sum)
    out_parts, in_parts, wide_sum, down_sum, router_grad, wide0, down0 = expert_call(
        1,
        token_all,
        grad_all,
        kept,
        wide_next.reshape(width, -1),
        router_w,
        down_next,
        own_hot,
        experts,
        None,
        before,
    )
    normed_two_grad, out_total, wide1, down1 = returning_call(
        in_parts, out_parts, wide_sum.reshape(shards, part, -1), down_sum
    )
    closed = closing_call(
        hidden,
        normed_two_grad,
        out_grad,
        ffn_row,
        raw,
        low,
        total,
        query_row,
        key_row,
        tables,
        seg_row,
        seg_col,
        tokens,
        attn_row,
        own_mixed,
        normed_low,
        router_grad[:, :experts].reshape(-1, 128),
        out_w,
        qkv_w,
        out_total,
        planes,
        shards,
    )
    input_grad, mixed_out, query_w_grad, key_w_grad, value_w_grad, out_w_grad = closed[:6]
    attn_scale_grad, router_out, vectors = closed[6:]
    gate_grad, up_grad, down_grad = unpack_units((wide0, wide1), (down0, down1))
    flat = vectors.reshape(-1)

    def own_piece(values, start, size):
        return lax.dynamic_slice_in_dim(values, start + index * size, size)

    return (
        mixed_out,
        input_grad,
        own_piece(attn_scale_grad.reshape(-1), 0, attn_gain.size),
        query_w_grad,
        key_w_grad,
        value_w_grad,
        own_piece(flat, width, query_gain.size),
        own_piece(flat, width + HD, key_gain.size),
        out_w_grad,
        own_piece(flat, 0, ffn_gain.size),
        router_out.reshape(-1, experts),
        gate_grad,
        up_grad,
        down_grad,
    )


def solution(mesh):
    local = fast_local if mesh.shape[EXPERT] == 8 else general_local
    return jax.shard_map(
        local,
        mesh=mesh,
        in_specs=(
            P(BOTH, None),
            P(EXPERT),
            P(BOTH, None),
            P(BOTH),
            P(BOTH),
            P(BOTH, None),
            P(BOTH, None),
            P(BOTH, None),
            P(BOTH),
            P(BOTH),
            P(BOTH, None),
            P(BOTH),
            P(BOTH, None),
            P(EXPERT, SHARD, None),
            P(EXPERT, SHARD, None),
            P(EXPERT, None, SHARD),
            P(BOTH, None),
        ),
        out_specs=(
            P(BOTH, None),
            P(BOTH, None),
            P(BOTH),
            P(BOTH, None),
            P(BOTH, None),
            P(BOTH, None),
            P(BOTH),
            P(BOTH),
            P(BOTH, None),
            P(BOTH),
            P(BOTH, None),
            P(EXPERT, SHARD, None),
            P(EXPERT, SHARD, None),
            P(EXPERT, None, SHARD),
        ),
        check_vma=False,
    )
```

```python
import functools

import jax
import jax.numpy as jnp
import numpy as np
from jax import lax
from jax.experimental import pallas as pl
from jax.experimental.pallas import tpu as pltpu
from jax.sharding import PartitionSpec as P

HEADS = 16
HD = 128


EXPERT = "expert"
SHARD = "wshard"
BOTH = (EXPERT, SHARD)

SUM_QHD_KHD_HQK = "qhd,khd->hqk"
SUM_HQK_KHD_QHD = "hqk,khd->qhd"
SUM_ECD_EDF_ECF = "ecd,edf->ecf"
SUM_ECF_EFD_ECD = "ecf,efd->ecd"
SUM_TK_TKD_TD = "tk,tkd->td"
SUM_TD_TKD_TK = "td,tkd->tk"
SUM_ECD_EFD_ECF = "ecd,efd->ecf"
SUM_ECF_ECD_EFD = "ecf,ecd->efd"
SUM_ECD_ECF_EDF = "ecd,ecf->edf"
SUM_ECF_EDF_ECD = "ecf,edf->ecd"
SUM_HQK_QHD_KHD = "hqk,qhd->khd"
EPSILON = 1e-06
THETA = 10000.0


def matmul(left, right):
    return jnp.dot(left, right, preferred_element_type=jnp.float32)


def matmul_tn(left, right):
    return lax.dot_general(
        left, right, (((0,), (0,)), ((), ())), preferred_element_type=jnp.float32
    )


def matmul_nt(left, right):
    return lax.dot_general(
        left, right, (((1,), (1,)), ((), ())), preferred_element_type=jnp.float32
    )


def rms_scale(values, scale_gain):
    factor = lax.rsqrt(jnp.mean(values * values, axis=-1, keepdims=True) + EPSILON)
    return values * factor * scale_gain


def rope_tables(positions):
    exponent = jnp.arange(HD // 2, dtype=jnp.float32) * (2.0 / HD)
    frequency = jnp.power(jnp.float32(THETA), -exponent)
    angles = positions.astype(jnp.float32)[:, None] * frequency[None, :]
    return (jnp.cos(angles), jnp.sin(angles))


def rotate(values, cosine, sine):
    first_half = values[..., : HD // 2]
    second_half = values[..., HD // 2 :]
    cos_part = cosine[:, None, :]
    sin_part = sine[:, None, :]
    return jnp.concatenate(
        [
            first_half * cos_part - second_half * sin_part,
            second_half * cos_part + first_half * sin_part,
        ],
        axis=-1,
    )


def padded_rows(rows):
    return jnp.concatenate([jnp.zeros((1,) + rows.shape[1:], rows.dtype), rows], axis=0)


def masked_scores(query_rot, key_rot, query_segment, key_segment):
    scores = jnp.einsum(SUM_QHD_KHD_HQK, query_rot, key_rot, preferred_element_type=jnp.float32)
    allowed = query_segment[:, None] == key_segment[None, :]
    return jnp.where(allowed[None], scores, -1e30)


def swiglu_fn(gate_in, up_in):
    return jax.nn.silu(gate_in) * up_in


def general_local(
    tokens,
    segment_ids,
    routes,
    pair_order,
    attn_gain,
    w_query,
    w_key,
    w_value,
    query_gain,
    key_gain,
    w_out,
    ffn_gain,
    w_router,
    w_gate,
    w_up,
    w_down,
    out_grad,
):
    tok_rows, width = tokens.shape
    top_count = routes.shape[1]
    expert_devs = lax.axis_size(EXPERT)
    shard_devs = lax.axis_size(SHARD)
    local_experts = w_gate.shape[0]
    expert_count = local_experts * expert_devs
    most_rows = 2 * tok_rows * top_count // expert_count
    capacity = 5 * tok_rows * top_count // (4 * local_experts)
    seq_length = segment_ids.shape[0]
    device_expert = lax.axis_index(EXPERT)
    device_shard = lax.axis_index(SHARD)
    low_type = jnp.bfloat16
    wide_type = jnp.float32
    gathered = (
        lax.all_gather(attn_gain, BOTH, axis=0, tiled=True),
        lax.all_gather(w_query, BOTH, axis=0, tiled=True),
        lax.all_gather(w_key, BOTH, axis=0, tiled=True),
        lax.all_gather(w_value, BOTH, axis=0, tiled=True),
        lax.all_gather(query_gain, BOTH, axis=0, tiled=True),
        lax.all_gather(key_gain, BOTH, axis=0, tiled=True),
        lax.all_gather(w_out, BOTH, axis=0, tiled=True),
        lax.all_gather(ffn_gain, BOTH, axis=0, tiled=True),
        lax.all_gather(w_router, BOTH, axis=0, tiled=True),
    )
    attn_scale = gathered[0].astype(wide_type)
    query_w, key_w, value_w = (gathered[1], gathered[2], gathered[3])
    query_scale = gathered[4].astype(wide_type)
    key_scale = gathered[5].astype(wide_type)
    out_w = gathered[6]
    ffn_scale = gathered[7].astype(wide_type)
    router_w = gathered[8]
    inputs = tokens.astype(wide_type)
    normed, norm_one_pull = jax.vjp(rms_scale, inputs, attn_scale)
    normed_low = normed.astype(low_type)
    query_raw = matmul(normed_low, query_w)
    key_raw = matmul(normed_low, key_w)
    value_low = matmul(normed_low, value_w).astype(low_type)
    positions = device_shard * tok_rows + jnp.arange(tok_rows, dtype=jnp.int32)
    cosine, sine = rope_tables(positions)

    def prepare(query_in, key_in, query_g, key_g):
        query_heads = rms_scale(query_in.reshape(tok_rows, HEADS, HD), query_g)
        key_heads = rms_scale(key_in.reshape(tok_rows, HEADS, HD), key_g)
        return (rotate(query_heads, cosine, sine) * HD ** (-0.5), rotate(key_heads, cosine, sine))

    rotated, prepare_pull = jax.vjp(prepare, query_raw, key_raw, query_scale, key_scale)
    query_low = rotated[0].astype(low_type)
    key_low = rotated[1].astype(low_type).reshape(tok_rows, width)
    seq_keys, seq_values = (
        lax.all_gather(key_low, SHARD, axis=0, tiled=True),
        lax.all_gather(value_low, SHARD, axis=0, tiled=True),
    )
    query_segment = lax.dynamic_slice_in_dim(segment_ids, device_shard * tok_rows, tok_rows)
    scores = masked_scores(
        query_low, seq_keys.reshape(seq_length, HEADS, HD), query_segment, segment_ids
    )
    row_max = jnp.max(scores, axis=-1, keepdims=True)
    shifted = jnp.exp(scores - row_max)
    totals = jnp.sum(shifted, axis=-1, keepdims=True)
    log_total = row_max + jnp.log(totals)
    probs_low = (shifted / totals).astype(low_type)
    mixed = jnp.einsum(
        SUM_HQK_KHD_QHD,
        probs_low,
        seq_values.reshape(seq_length, HEADS, HD),
        preferred_element_type=wide_type,
    )
    mixed_low = mixed.reshape(tok_rows, width).astype(low_type)
    hidden = inputs + matmul(mixed_low, out_w)
    normed_two, norm_two_pull = jax.vjp(rms_scale, hidden, ffn_scale)
    normed_two_low = normed_two.astype(low_type)
    logits = matmul(normed_two_low, router_w)

    def router_weights(logit_values):
        return jnp.take_along_axis(jax.nn.softmax(logit_values, axis=-1), routes, axis=1)

    route_weight, route_pull = jax.vjp(router_weights, logits)
    group_routes, group_order = (
        lax.all_gather(routes, EXPERT, axis=0, tiled=True),
        lax.all_gather(pair_order, EXPERT, axis=0, tiled=True),
    )
    per_source = tok_rows * top_count
    group_pairs = per_source * expert_devs
    expert_of = group_routes.reshape(-1)
    pair_index = jnp.arange(group_pairs, dtype=jnp.int32)
    source_of = pair_index // per_source
    expert_ids = jnp.arange(expert_count, dtype=jnp.int32)
    onehot = (expert_of.reshape(expert_devs, per_source, 1) == expert_ids).astype(jnp.int32)
    position_of = (jnp.sum(jnp.cumsum(onehot, axis=1) * onehot, axis=-1) - 1).reshape(-1)
    order_span = group_pairs * shard_devs
    sort_keys = expert_of * order_span + group_order
    sorted_pairs = jnp.argsort(sort_keys)
    placement = jnp.zeros((group_pairs,), jnp.int32).at[sorted_pairs].set(pair_index)
    expert_counts = jnp.sum(onehot, axis=(0, 1))
    expert_start = jnp.cumsum(expert_counts) - expert_counts
    start_of = jnp.sum(onehot.reshape(group_pairs, expert_count) * expert_start[None, :], axis=-1)
    slot_rank = placement - start_of
    retained = slot_rank < capacity
    own_expert = routes.reshape(-1)
    own_position = lax.dynamic_slice_in_dim(position_of, device_expert * per_source, per_source)
    send_slot = own_expert * most_rows + own_position
    send_pair = (
        jnp.zeros((expert_count * most_rows,), jnp.int32)
        .at[send_slot]
        .set(jnp.arange(per_source, dtype=jnp.int32) + 1)
    )
    send_token = jnp.where(send_pair > 0, (send_pair - 1) // top_count + 1, 0)
    owner_local = expert_of % local_experts
    is_mine = expert_of // local_experts == device_expert
    recv_row = source_of * (local_experts * most_rows) + owner_local * most_rows + position_of
    slot_target = jnp.where(
        is_mine & retained, owner_local * capacity + slot_rank, local_experts * capacity
    )
    slot_source = (
        jnp.zeros((local_experts * capacity,), jnp.int32)
        .at[slot_target]
        .set(recv_row + 1, mode="drop")
    )
    back_room = expert_devs * local_experts * most_rows
    back_target = jnp.where(is_mine, recv_row, back_room)
    back_source = (
        jnp.zeros((back_room,), jnp.int32)
        .at[back_target]
        .set(jnp.where(retained, owner_local * capacity + slot_rank + 1, 0), mode="drop")
    )
    send_rows = padded_rows(normed_two_low)[send_token].reshape(
        expert_devs, local_experts * most_rows, width
    )
    recv_rows = lax.all_to_all(
        send_rows, EXPERT, split_axis=0, concat_axis=0, tiled=True
    ).reshape(-1, width)
    slot_rows = padded_rows(recv_rows)[slot_source].reshape(local_experts, capacity, width)
    full_gate, full_up, full_down = (
        lax.all_gather(w_gate, SHARD, axis=1, tiled=True),
        lax.all_gather(w_up, SHARD, axis=1, tiled=True),
        lax.all_gather(w_down, SHARD, axis=2, tiled=True),
    )
    gate_act = jnp.einsum(SUM_ECD_EDF_ECF, slot_rows, full_gate, preferred_element_type=wide_type)
    up_act = jnp.einsum(SUM_ECD_EDF_ECF, slot_rows, full_up, preferred_element_type=wide_type)
    swiglu_out, swiglu_pull = jax.vjp(swiglu_fn, gate_act, up_act)
    swiglu_low = swiglu_out.astype(low_type)
    expert_out = jnp.einsum(
        SUM_ECF_EFD_ECD, swiglu_low, full_down, preferred_element_type=wide_type
    ).astype(low_type)
    back_rows = padded_rows(expert_out.reshape(-1, width))[back_source].reshape(
        expert_devs, local_experts * most_rows, width
    )
    returned = lax.all_to_all(back_rows, EXPERT, split_axis=0, concat_axis=0, tiled=True).reshape(
        -1, width
    )
    pair_rows = returned[send_slot].reshape(tok_rows, top_count, width)
    combined = jnp.einsum(SUM_TK_TKD_TD, route_weight, pair_rows, preferred_element_type=wide_type)
    mixed_out = (hidden + combined).astype(low_type)
    result_grad = out_grad.astype(wide_type)
    weight_grad = jnp.einsum(SUM_TD_TKD_TK, result_grad, pair_rows, preferred_element_type=wide_type)
    pair_grad = (
        (route_weight[:, :, None] * result_grad[:, None, :])
        .astype(low_type)
        .reshape(per_source, width)
    )
    send_grad = padded_rows(pair_grad)[send_pair].reshape(
        expert_devs, local_experts * most_rows, width
    )
    recv_grad = lax.all_to_all(
        send_grad, EXPERT, split_axis=0, concat_axis=0, tiled=True
    ).reshape(-1, width)
    slot_grad = padded_rows(recv_grad)[slot_source].reshape(local_experts, capacity, width)
    act_grad = jnp.einsum(SUM_ECD_EFD_ECF, slot_grad, full_down, preferred_element_type=wide_type)
    down_grad = jnp.einsum(SUM_ECF_ECD_EFD, swiglu_low, slot_grad, preferred_element_type=wide_type)
    gate_grad, up_grad = swiglu_pull(act_grad)
    gate_low = gate_grad.astype(low_type)
    up_low = up_grad.astype(low_type)
    gate_w_grad = jnp.einsum(SUM_ECD_ECF_EDF, slot_rows, gate_low, preferred_element_type=wide_type)
    up_w_grad = jnp.einsum(SUM_ECD_ECF_EDF, slot_rows, up_low, preferred_element_type=wide_type)
    slot_in_grad = jnp.einsum(SUM_ECF_EDF_ECD, gate_low, full_gate, preferred_element_type=wide_type)
    slot_in_grad = (
        slot_in_grad + jnp.einsum(SUM_ECF_EDF_ECD, up_low, full_up, preferred_element_type=wide_type)
    ).astype(low_type)
    gate_shard, up_shard, down_shard = (
        lax.psum_scatter(
            gate_w_grad.astype(jnp.bfloat16), SHARD, scatter_dimension=1, tiled=True
        ).astype(jnp.float32),
        lax.psum_scatter(
            up_w_grad.astype(jnp.bfloat16), SHARD, scatter_dimension=1, tiled=True
        ).astype(jnp.float32),
        lax.psum_scatter(
            down_grad.astype(jnp.bfloat16), SHARD, scatter_dimension=2, tiled=True
        ).astype(jnp.float32),
    )
    back_grad = padded_rows(slot_in_grad.reshape(-1, width))[back_source].reshape(
        expert_devs, local_experts * most_rows, width
    )
    returned_grad = lax.all_to_all(
        back_grad, EXPERT, split_axis=0, concat_axis=0, tiled=True
    ).reshape(-1, width)
    expert_in_grad = jnp.sum(
        returned_grad[send_slot].reshape(tok_rows, top_count, width).astype(wide_type), axis=1
    )
    logit_grad = route_pull(weight_grad)[0]
    logit_low = logit_grad.astype(low_type)
    router_grad = matmul_tn(normed_two_low, logit_low)
    normed_two_grad = expert_in_grad + matmul_nt(logit_low, router_w)
    hidden_norm_grad, ffn_scale_grad = norm_two_pull(normed_two_grad)
    hidden_grad = result_grad + hidden_norm_grad
    attn_low = hidden_grad.astype(low_type)
    out_w_grad = matmul_tn(mixed_low, attn_low)
    mixed_grad = matmul_nt(attn_low, out_w).astype(low_type).reshape(tok_rows, HEADS, HD)
    back_keys, back_values = (seq_keys, seq_values)
    key_heads = back_keys.reshape(seq_length, HEADS, HD)
    value_heads = back_values.reshape(seq_length, HEADS, HD)
    scores_again = masked_scores(query_low, key_heads, query_segment, segment_ids)
    probs_again = jnp.exp(scores_again - log_total)
    probs_again_low = probs_again.astype(low_type)
    prob_grad = jnp.einsum(
        SUM_QHD_KHD_HQK, mixed_grad, value_heads, preferred_element_type=wide_type
    )
    value_part = jnp.einsum(
        SUM_HQK_QHD_KHD, probs_again_low, mixed_grad, preferred_element_type=wide_type
    )
    row_inner = jnp.sum(probs_again * prob_grad, axis=-1, keepdims=True)
    score_low = (probs_again * (prob_grad - row_inner)).astype(low_type)
    query_rot_grad = jnp.einsum(
        SUM_HQK_KHD_QHD, score_low, key_heads, preferred_element_type=wide_type
    )
    key_part = jnp.einsum(SUM_HQK_QHD_KHD, score_low, query_low, preferred_element_type=wide_type)
    key_rot_grad, value_grad = (
        lax.psum_scatter(
            key_part.reshape(seq_length, width).astype(jnp.bfloat16),
            SHARD,
            scatter_dimension=0,
            tiled=True,
        ).astype(jnp.float32),
        lax.psum_scatter(
            value_part.reshape(seq_length, width).astype(jnp.bfloat16),
            SHARD,
            scatter_dimension=0,
            tiled=True,
        ).astype(jnp.float32),
    )
    query_raw_grad, key_raw_grad, query_scale_grad, key_scale_grad = prepare_pull(
        (query_rot_grad, key_rot_grad.reshape(tok_rows, HEADS, HD))
    )
    query_grad_low = query_raw_grad.astype(low_type)
    key_grad_low = key_raw_grad.astype(low_type)
    value_grad_low = value_grad.astype(low_type)
    query_w_grad = matmul_tn(normed_low, query_grad_low)
    key_w_grad = matmul_tn(normed_low, key_grad_low)
    value_w_grad = matmul_tn(normed_low, value_grad_low)
    normed_grad = (
        matmul_nt(query_grad_low, query_w)
        + matmul_nt(key_grad_low, key_w)
        + matmul_nt(value_grad_low, value_w)
    )
    input_norm_grad, attn_scale_grad = norm_one_pull(normed_grad)
    input_grad = (hidden_grad + input_norm_grad).astype(low_type)
    summed = (
        lax.psum_scatter(attn_scale_grad, BOTH, scatter_dimension=0, tiled=True),
        lax.psum_scatter(query_w_grad, BOTH, scatter_dimension=0, tiled=True),
        lax.psum_scatter(key_w_grad, BOTH, scatter_dimension=0, tiled=True),
        lax.psum_scatter(value_w_grad, BOTH, scatter_dimension=0, tiled=True),
        lax.psum_scatter(query_scale_grad, BOTH, scatter_dimension=0, tiled=True),
        lax.psum_scatter(key_scale_grad, BOTH, scatter_dimension=0, tiled=True),
        lax.psum_scatter(out_w_grad, BOTH, scatter_dimension=0, tiled=True),
        lax.psum_scatter(ffn_scale_grad, BOTH, scatter_dimension=0, tiled=True),
        lax.psum_scatter(router_grad, BOTH, scatter_dimension=0, tiled=True),
    )
    return (
        mixed_out,
        input_grad,
        summed[0],
        summed[1],
        summed[2],
        summed[3],
        summed[4],
        summed[5],
        summed[6],
        summed[7],
        summed[8],
        gate_shard,
        up_shard,
        down_shard,
    )


MIB = 1 << 20


def nt_dot(left, right):
    return lax.dot_general(
        left, right, (((1,), (1,)), ((), ())), preferred_element_type=jnp.float32
    )


def tn_dot(left, right):
    return lax.dot_general(
        left, right, (((0,), (0,)), ((), ())), preferred_element_type=jnp.float32
    )


def vmem_params(mib):
    return pltpu.CompilerParams(vmem_limit_bytes=mib * MIB)


def turn_tables(length):
    exponent = np.arange(HD // 2, dtype=np.float32) * np.float32(2.0 / HD)
    frequency = np.power(np.float32(THETA), -exponent).astype(np.float32)
    angles = np.arange(length, dtype=np.float32)[:, None] * frequency[None, :]
    cosine, sine = np.cos(angles), np.sin(angles)
    return (
        jnp.asarray(np.concatenate([cosine, cosine], axis=1), jnp.float32),
        jnp.asarray(np.concatenate([-sine, sine], axis=1), jnp.float32),
    )


def norm_factor(values):
    return lax.rsqrt(jnp.mean(values * values, axis=-1, keepdims=True) + EPSILON)


def same_document(seg_row):
    row = seg_row[...].astype(jnp.float32)
    column = jnp.broadcast_to(row, (128, row.shape[1])).T[:, :1]
    return column == row


def attend(
    tokens, gain, weight, query_gain, key_gain, cosine, sine, allowed,
    normed_out, raw_out, low_out, mixed_out, total_out, qkv,
):
    part = mixed_out.shape[1]
    values = tokens[...].astype(jnp.float32)
    normed = (values * norm_factor(values) * gain[...]).astype(jnp.bfloat16)
    normed_out[...] = normed
    qkv[...] = jnp.dot(normed, weight[...], preferred_element_type=jnp.float32)
    raw_out[...] = qkv[:, : 2 * part]
    low_out[:, 2 * part :] = qkv[:, 2 * part :].astype(jnp.bfloat16)
    for head in range(part // HD):
        span = pl.ds(head * HD, HD)
        for offset, scale_gain, scale in ((0, query_gain, HD ** (-0.5)), (part, key_gain, 1.0)):
            raw = qkv[:, pl.ds(offset + head * HD, HD)]
            unit = raw * norm_factor(raw) * scale_gain[...]
            turned = unit * cosine[...] + pltpu.roll(unit, HD // 2, 1) * sine[...]
            low_out[:, pl.ds(offset + head * HD, HD)] = (turned * scale).astype(jnp.bfloat16)
        query, key = low_out[:, span], low_out[:, pl.ds(part + head * HD, HD)]
        scores = jnp.where(allowed, nt_dot(query, key), -1e30)
        top = jnp.max(scores, axis=-1, keepdims=True)
        shifted = jnp.exp(scores - top)
        total = jnp.sum(shifted, axis=-1, keepdims=True)
        probs = (shifted / total).astype(jnp.bfloat16)
        mixed = jnp.dot(
            probs, low_out[:, pl.ds(2 * part + head * HD, HD)], preferred_element_type=jnp.float32
        )
        mixed_out[:, span] = mixed.astype(jnp.bfloat16)
        total_out[:, head : head + 1] = top + jnp.log(total)


def unpack_kernel(gate0, gate1, up0, up1, down0, down1, gate_out, up_out, down_out):
    for index, group in enumerate(((gate0, up0, down0), (gate1, up1, down1))):

        @pl.when(pl.program_id(0) == index)
        def _(group=group):
            for source, result in zip(group, (gate_out, up_out, down_out), strict=True):
                result[...] = source[...].astype(result.dtype)


def unpack_units(wides, downs):
    shards, part, lanes = wides[0].shape
    each = lanes // 2

    def held(index, e, s):
        return jnp.where(e == index, s, (shards - 1) * (1 - index))

    def wide_spec(index, which):
        return pl.BlockSpec((1, part, each), lambda e, s: (held(index, e, s), 0, which))

    def down_spec(index):
        return pl.BlockSpec((1, each, part), lambda e, s: (held(index, e, s), 0, 0))

    wide_out = pl.BlockSpec((1, part, each), lambda e, s: (e, 0, s))
    shape = jax.ShapeDtypeStruct((2, part, shards * each), jnp.float32)
    return pl.pallas_call(
        unpack_kernel,
        grid=(2, shards),
        in_specs=[wide_spec(index, which) for which in range(2) for index in range(2)]
        + [down_spec(index) for index in range(2)],
        out_specs=[wide_out, wide_out, pl.BlockSpec((1, each, part), lambda e, s: (e, s, 0))],
        out_shape=[shape, shape, jax.ShapeDtypeStruct((2, shards * each, part), jnp.float32)],
        compiler_params=vmem_params(24),
    )(wides[0], wides[1], wides[0], wides[1], *downs)


def mark_kept(small_all, first, experts, own, capacity, bits, shards, keep_out):
    devices, _, rows = small_all.shape
    row = lax.broadcasted_iota(jnp.int32, (devices, rows), 0)
    group = lax.rem(row, shards)
    for index in range(own):
        order = jnp.zeros((devices, rows), jnp.float32)
        for expert in range(experts):
            high = small_all[:, expert, :].astype(jnp.float32)
            low = small_all[:, experts + expert, :].astype(jnp.float32)
            order = order + jnp.where(first + index == expert, high * 256.0 + low, 0.0)
        there = order > 0.0
        bound = jnp.zeros_like(order)
        for bit in reversed(range(bits)):
            trial = bound + float(1 << bit)
            within = jnp.where(there & (order <= trial), 1.0, 0.0)
            for shard in range(shards):
                here = group == shard
                count = jnp.sum(jnp.where(here, within, 0.0), keepdims=True)
                bound = jnp.where(here & (count <= float(capacity)), trial, bound)
        kept = jnp.where(there & (order <= bound), 1.0, 0.0).T
        for block in range(devices):
            place = keep_out.at[block // shards, pl.ds(block % shards * rows, rows)]
            place[:, index : index + 1] = kept[:, block : block + 1]


CORE, XBIT, YBIT = 1, 2, 4


MESH = pl.DeviceIdType.MESH


def held_in_hbm(*values):
    return [pltpu.with_memory_space_constraint(value, pltpu.HBM) for value in values]


class Wires:
    def __init__(self, send, recv):
        self.send, self.recv, self.used = send, recv, 0
        self.device, self.shard = lax.axis_index(EXPERT), lax.axis_index(SHARD)

    def slot(self):
        self.used += 1
        return self.used - 1

    def peer(self, bits=0, step=0, shards=1):
        shard = lax.rem(self.shard + step, shards) if step else self.shard
        return (self.device ^ bits, shard)

    def copy(self, source, target, slot, peer):
        return pltpu.make_async_remote_copy(
            src_ref=source,
            dst_ref=target,
            send_sem=self.send.at[slot],
            recv_sem=self.recv.at[slot],
            device_id=peer,
            device_id_type=MESH,
        )


def greet(peers):
    barrier = pltpu.get_barrier_semaphore()
    for peer in peers:
        pl.semaphore_signal(barrier, inc=1, device_id=peer, device_id_type=MESH)
    pl.semaphore_wait(barrier, len(peers))


class Relay:
    def __init__(self, wires, shards, views):
        self.wires, self.shards, self.views = wires, shards, views
        self.slots = [[[wires.slot() for _ in views] for _ in range(shards - 1)] for _ in range(2)]

    def copies(self, way, step, block):
        wires = self.wires
        peer = (wires.device, wires.shard + (1 if way == 0 else -1))
        return [
            wires.copy(view(block), view(block), slot, peer)
            for view, slot in zip(self.views, self.slots[way][step], strict=True)
        ]

    def has(self, way, step):
        shard = self.wires.shard
        return shard - step >= 0 if way == 0 else shard + step < self.shards

    def sends(self, way, step):
        shard = self.wires.shard
        edge = shard < self.shards - 1 if way == 0 else shard > 0
        return jnp.logical_and(edge, self.has(way, step))

    def block(self, way, step):
        return self.wires.shard + (-step if way == 0 else step)

    def run(self, step, first=None):
        wires = self.wires
        for index, view in enumerate(self.views):
            for way in range(2):
                block = self.block(way, step)
                peer = (wires.device, wires.shard + (1 if way == 0 else -1))
                if step > 0:

                    @pl.when(self.has(way, step))
                    def _(way=way, block=block, index=index, view=view, peer=peer):
                        slot = self.slots[way][step - 1][index]
                        wires.copy(view(block), view(block), slot, peer).wait_recv()

                if step < self.shards - 1:

                    @pl.when(self.sends(way, step))
                    def _(way=way, block=block, index=index, view=view, peer=peer):
                        source = view(block) if first is None else first[index]
                        slot = self.slots[way][step][index]
                        wires.copy(source, view(block), slot, peer).start()

    def drain(self):
        for way in range(2):
            for step in range(self.shards - 1):

                @pl.when(self.sends(way, step))
                def _(way=way, step=step):
                    for copy in self.copies(way, step, self.block(way, step)):
                        copy.wait_send()


class Plane:
    def __init__(self, wires, views, whole):
        self.wires, self.views, self.whole = wires, views, whole
        count = len(views)
        self.first = [[wires.slot() for _ in range(count)] for _ in range(2)]
        self.second = [[[wires.slot() for _ in range(count)] for _ in range(2)] for _ in range(2)]
        self.last = [[wires.slot() for _ in range(count)] for _ in range(4)]
        self.sent = []

    def start(self, copies):
        for copy in copies:
            copy.start()
        self.sent += copies

    def one(self, owner, half, bits, slots):
        wires = self.wires
        return [
            wires.copy(view(owner, half), view(owner, half), slot, wires.peer(bits))
            for view, slot in zip(self.views, slots, strict=True)
        ]

    def step_one(self):
        me = self.wires.device
        for half, bits in enumerate((XBIT, YBIT)):
            self.start(self.one(me, half, bits, self.first[half]))

    def step_two(self):
        me = self.wires.device
        for half, bits in enumerate((XBIT, YBIT)):
            for copy in self.one(me ^ bits, half, bits, self.first[half]):
                copy.wait_recv()
        for half, bits in enumerate((XBIT, YBIT)):
            other = (XBIT | YBIT) ^ bits
            self.start(self.one(me, half, other, self.second[half][0]))
            self.start(self.one(me ^ bits, half, other, self.second[half][1]))

    def cores(self, index):
        wires = self.wires
        owner = wires.device ^ (0, XBIT, YBIT, XBIT | YBIT)[index]
        return [
            wires.copy(place(owner), place(owner), slot, wires.peer(CORE))
            for place, slot in zip(self.whole, self.last[index], strict=True)
        ]

    def step_three(self):
        me = self.wires.device
        for half, bits in enumerate((XBIT, YBIT)):
            other = (XBIT | YBIT) ^ bits
            for owner, slots in ((me ^ other, 0), (me ^ other ^ bits, 1)):
                for copy in self.one(owner, half, other, self.second[half][slots]):
                    copy.wait_recv()
        for index in range(1, 4):
            self.start(self.cores(index))

    def finish(self):
        for index, bits in enumerate((0, XBIT, YBIT, XBIT | YBIT)):
            owner = self.wires.device ^ CORE ^ bits
            for place, slot in zip(self.whole, self.last[index], strict=True):
                self.wires.copy(
                    place(owner), place(owner), slot, self.wires.peer(CORE)
                ).wait_recv()
        for copy in self.sent:
            copy.wait_send()


def opening_kernel(
    shards, planes, experts, own_experts, capacity, bits,
    routes, order, gains, seg_row, cosine, sine,
    router, w_query, w_key, w_value, tokens, w_out, out_grad,
    kept_out, attn_row, ffn_row, query_row, key_row, normed_out, raw_out, low_out, total_out, mixed_all,
    router_all, qkv_w_out, tokens_all, out_w_out, grad_out,
    small, small_all, grad_all, qkv_w, out_w, mixed, qkv, send, recv, local, store,
):
    wires = Wires(send, recv)
    device, shard = wires.device, wires.shard
    weights = (w_query, w_key, w_value)
    block, width = w_query.shape
    rows = tokens.shape[0]
    part = width // shards
    mine = device * shards + shard
    greet(
        [wires.peer(step=step, shards=shards) for step in range(1, shards)]
        + [wires.peer(XBIT), wires.peer(YBIT), wires.peer(CORE)]
    )

    def place(source_shard, which):
        start = pl.multiple_of((device * shards + source_shard) * block, block)
        return qkv_w.at[pl.ds(start, block), pl.ds(which * part, part)]

    def cut(which, target):
        return weights[which].at[:, pl.ds(pl.multiple_of(target * part, part), part)]

    def token_rows(b):
        return tokens_all.at[pl.ds(pl.multiple_of(b * rows, rows), rows)]

    def out_rows(owner, source):
        return out_w.at[pl.ds(pl.multiple_of((owner * shards + source) * block, block), block)]

    def grad_block(owner, source):
        return (owner * shards + source) * rows

    def grad_rows(owner, source):
        return grad_all.at[pl.ds(pl.multiple_of(grad_block(owner, source), rows), rows)]

    def grad_half(source):
        def view(owner, half):
            start = grad_block(owner, source) + half * (rows // 2)
            return grad_all.at[pl.ds(pl.multiple_of(start, rows // 2), rows // 2)]

        return view

    exchange = [[wires.slot() for _ in range(5)] for _ in range(1, shards)]
    sent = []
    for step in range(1, shards):
        peer = wires.peer(step=step, shards=shards)
        slots = exchange[step - 1]
        copies = [
            wires.copy(cut(which, peer[1]), place(shard, which), slots[which], peer)
            for which in range(3)
        ]
        copies.append(wires.copy(router, router_all.at[mine], slots[4], peer))
        for copy in copies:
            copy.start()
        sent += copies
    grad_line = Relay(wires, shards, [lambda b: grad_rows(device, b)])
    token_line = Relay(wires, shards, [token_rows])
    out_line = Relay(wires, shards, [lambda b: out_rows(device, b)])
    mixed_line = Relay(wires, shards, [lambda b: mixed_all.at[b]])
    own = [
        pltpu.make_async_copy(out_grad, grad_rows(device, shard), local.at[0]),
        pltpu.make_async_copy(router, router_all.at[mine], local.at[1]),
        pltpu.make_async_copy(tokens, token_rows(shard), local.at[2]),
        pltpu.make_async_copy(w_out, out_rows(device, shard), local.at[3]),
    ]
    own += [
        pltpu.make_async_copy(cut(which, shard), place(shard, which), local.at[4 + which])
        for which in range(3)
    ]
    for copy in own:
        copy.start()
    turns = [shard] + [
        sum(jnp.where(shard == index, source, 0) for index, source in enumerate(row))
        for row in ((1, 0, 1, 2), (2, 2, 3, 1), (3, 3, 0, 0))
    ]
    stages = [
        Plane(wires, [grad_half(source)], [lambda owner, source=source: grad_rows(owner, source)])
        for source in turns
    ]
    stored = []

    def begin(stage):
        stage.step_one()
        stage.start(stage.cores(0))

    def keep(turn):
        stages[turn].finish()
        for owner in range(planes):
            start = pl.multiple_of(grad_block(owner, turns[turn]), rows)
            copy = pltpu.make_async_copy(
                grad_rows(owner, turns[turn]),
                grad_out.at[pl.ds(start, rows)],
                store.at[turn * planes + owner],
            )
            copy.start()
            stored.append(copy)

    own[0].wait()
    begin(stages[0])
    expert = lax.broadcasted_iota(jnp.int32, (experts, rows), 0)
    dense = jnp.zeros((experts, rows), jnp.int32)
    for choice in range(routes.shape[0]):
        named = routes[choice : choice + 1, :] == expert
        dense = dense + jnp.where(named, order[choice : choice + 1, :] + 1, 0)
    high = lax.shift_right_logical(dense, 8)
    for start, digits in ((0, high), (experts, dense - high * 256)):
        small[pl.ds(start, experts), :] = digits.astype(jnp.float32).astype(small.dtype)
    small[pl.ds(2 * experts, gains.shape[0]), :] = gains[...]
    small_all[mine] = small[...]
    for step in range(1, shards):
        peer = wires.peer(step=step, shards=shards)
        copy = wires.copy(small, small_all.at[mine], exchange[step - 1][3], peer)
        copy.start()
        sent.append(copy)
    out_line.run(0, (w_out,))
    token_line.run(0, (tokens,))
    stages[0].step_two()
    for copy in own[1:]:
        copy.wait()
    for step in range(1, shards):
        peer = wires.peer(step=shards - step, shards=shards)
        source = peer[1]
        slots = exchange[step - 1]
        for which in range(3):
            wires.copy(place(source, which), place(source, which), slots[which], peer).wait_recv()
        wires.copy(router, router_all.at[device * shards + source], slots[4], peer).wait_recv()
        wires.copy(small, small_all.at[device * shards + source], slots[3], peer).wait_recv()

    each = shards * block // 2

    def rows_of(owner, half):
        return qkv_w.at[pl.ds(pl.multiple_of((owner * 2 + half) * each, each), each)]

    def small_of(owner, half):
        return small_all.at[pl.ds((owner * 2 + half) * (shards // 2), shards // 2)]

    def router_of(owner, half):
        return router_all.at[pl.ds((owner * 2 + half) * (shards // 2), shards // 2)]

    plane = Plane(
        wires,
        [rows_of, small_of, router_of],
        [
            lambda owner: qkv_w.at[pl.ds(pl.multiple_of(owner * 2 * each, 2 * each), 2 * each)],
            lambda owner: small_all.at[pl.ds(owner * shards, shards)],
            lambda owner: router_all.at[pl.ds(owner * shards, shards)],
        ],
    )
    outs = [
        Plane(
            wires,
            [
                lambda owner, side, index=index: out_w.at[
                    pl.ds(
                        pl.multiple_of(owner * 2 * each + index * each + side * (each // 2), each // 2),
                        each // 2,
                    )
                ]
            ],
            [
                lambda owner, index=index: out_w.at[
                    pl.ds(pl.multiple_of((owner * 2 + index) * each, each), each)
                ]
            ],
        )
        for index in range(2)
    ]
    begin(plane)
    stages[0].step_three()
    out_line.run(1)
    token_line.run(1)
    plane.step_two()
    out_line.run(2)
    token_line.run(2)
    grad_line.run(0, (out_grad,))
    plane.step_three()
    keep(0)
    out_line.run(3)
    for stage in outs:
        begin(stage)
    plane.finish()

    count = width // 128
    start = 2 * experts
    summed = small_all[0, pl.ds(start, gains.shape[0]), :].astype(jnp.float32)
    for other in range(1, planes * shards):
        summed = summed + small_all[other, pl.ds(start, gains.shape[0]), :].astype(jnp.float32)
    attn_row[...] = jnp.concatenate([summed[i : i + 1] for i in range(count)], axis=1)
    ffn_row[...] = jnp.concatenate([summed[count + i : count + i + 1] for i in range(count)], axis=1)
    query_row[...] = summed[2 * count : 2 * count + 1]
    key_row[...] = summed[2 * count + 1 : 2 * count + 2]
    for stage in outs:
        stage.step_two()
    token_line.run(3)
    attend(
        tokens_all, attn_row, qkv_w, query_row, key_row, cosine, sine, same_document(seg_row),
        normed_out, raw_out, low_out, mixed, total_out, qkv,
    )
    mixed_line.run(0, (mixed,))
    mixed_all[shard] = mixed[...]
    save_qkv = pltpu.make_async_copy(qkv_w, qkv_w_out, local.at[7])
    save_qkv.start()
    grad_line.run(1)
    begin(stages[1])
    for stage in outs:
        stage.step_three()
    mixed_line.run(1)
    stages[1].step_two()
    grad_line.run(2)
    begin(stages[2])
    for stage in outs:
        stage.finish()
    save_out = pltpu.make_async_copy(out_w, out_w_out, local.at[8])
    save_out.start()
    mixed_line.run(2)
    stages[1].step_three()
    stages[2].step_two()
    mark_kept(
        small_all, device * own_experts, experts, own_experts, capacity, bits, shards, kept_out
    )
    grad_line.run(3)
    begin(stages[3])
    stages[2].step_three()
    keep(1)
    mixed_line.run(3)
    stages[3].step_two()
    keep(2)
    stages[3].step_three()
    keep(3)
    for copy in sent:
        copy.wait_send()
    for group in (token_line, grad_line, out_line, mixed_line):
        group.drain()
    for copy in stored:
        copy.wait()
    save_qkv.wait()
    save_out.wait()


def opening_call(
    routes, order, gains, seg_row, tables, router, w_query, w_key, w_value, tokens, w_out, out_grad,
    experts, own_experts, capacity, planes, shards,
):
    block, width = w_query.shape
    top_count, rows = routes.shape
    seq, part = shards * rows, width // shards
    hbm = pl.BlockSpec(memory_space=pltpu.HBM)
    vmem = pl.BlockSpec(memory_space=pltpu.VMEM)
    place = pl.BlockSpec(memory_space=pl.ANY)
    slots = 144
    low, full = tokens.dtype, jnp.float32
    small = (2 * experts + gains.shape[0], 128)
    most = planes * shards * rows * top_count
    return pl.pallas_call(
        functools.partial(
            opening_kernel, shards, planes, experts, own_experts, capacity, most.bit_length()
        ),
        in_specs=[vmem] * 6 + [place] * 7,
        out_specs=[vmem] * 10 + [place, hbm, vmem, hbm, hbm],
        out_shape=(
            jax.ShapeDtypeStruct((planes, seq, own_experts), full),
            jax.ShapeDtypeStruct((1, width), full),
            jax.ShapeDtypeStruct((1, width), full),
            jax.ShapeDtypeStruct((1, HD), full),
            jax.ShapeDtypeStruct((1, HD), full),
            jax.ShapeDtypeStruct((seq, width), low),
            jax.ShapeDtypeStruct((seq, 2 * part), full),
            jax.ShapeDtypeStruct((seq, 3 * part), low),
            jax.ShapeDtypeStruct((seq, 128), full),
            jax.ShapeDtypeStruct((shards, seq, part), low),
            jax.ShapeDtypeStruct((planes * shards,) + router.shape, router.dtype),
            pltpu.HBM((width, 3 * part), low),
            jax.ShapeDtypeStruct((seq, width), low),
            pltpu.HBM((width, width), low),
            pltpu.HBM((planes * seq, width), low),
        ),
        scratch_shapes=[
            pltpu.VMEM(small, gains.dtype),
            pltpu.VMEM((planes * shards,) + small, gains.dtype),
            pltpu.VMEM((planes * seq, width), low),
            pltpu.VMEM((width, 3 * part), low),
            pltpu.VMEM((width, width), low),
            pltpu.VMEM((seq, part), low),
            pltpu.VMEM((seq, 3 * part), full),
            pltpu.SemaphoreType.DMA((slots,)),
            pltpu.SemaphoreType.DMA((slots,)),
            pltpu.SemaphoreType.DMA((9,)),
            pltpu.SemaphoreType.DMA((planes * shards,)),
        ],
        compiler_params=pltpu.CompilerParams(
            collective_id=1, has_side_effects=True, vmem_limit_bytes=60 * MIB
        ),
        cost_estimate=pl.CostEstimate(flops=0, bytes_accessed=200 * MIB, transcendentals=0),
    )(
        routes, order, gains, seg_row, *tables, router, w_query, w_key, w_value, tokens, w_out, out_grad
    )


class Units:
    def __init__(self, wires, shards, index, gate, up, down, wide_w, down_w, local, base, piece=(0, 1)):
        self.wires, self.shards, self.index = wires, shards, index
        self.gate, self.up, self.down, self.wide_w, self.down_w = gate, up, down, wide_w, down_w
        self.local, self.base, self.piece = local, base, piece
        count = (0 if wide_w is None else 2) + (0 if down_w is None else 1)
        self.slots = [[wires.slot() for _ in range(count)] for _ in range(1, shards)]

    def pairs(self, source, target):
        each = self.gate.shape[2] // self.shards
        span = pl.ds(pl.multiple_of(target * each, each), each)
        result = []
        if self.wide_w is not None:
            result += [
                (self.gate.at[self.index, :, span], self.wide_w.at[source, :, pl.ds(0, each)]),
                (self.up.at[self.index, :, span], self.wide_w.at[source, :, pl.ds(each, each)]),
            ]
        if self.down_w is not None:
            number, pieces = self.piece
            size = each // pieces
            start = pl.multiple_of(target * each + number * size, size)
            place = self.down_w.at[source, pl.ds(number * size, size), :]
            result.append((self.down.at[self.index, pl.ds(start, size), :], place))
        return result

    def own(self):
        shard = self.wires.shard
        return [
            pltpu.make_async_copy(source, place, self.local.at[self.base + slot])
            for slot, (source, place) in enumerate(self.pairs(shard, shard))
        ]

    def sends(self):
        wires = self.wires
        for step in range(1, self.shards):
            peer = wires.peer(step=step, shards=self.shards)
            pairs = self.pairs(wires.shard, peer[1])
            for slot, (source, place) in zip(self.slots[step - 1], pairs, strict=True):
                yield wires.copy(source, place, slot, peer)

    def begin(self):
        for copy in self.own():
            copy.start()
        for copy in self.sends():
            copy.start()

    def end(self):
        wires = self.wires
        for copy in self.own():
            copy.wait()
        for step in range(1, self.shards):
            back = wires.peer(step=self.shards - step, shards=self.shards)
            pairs = self.pairs(back[1], wires.shard)
            for slot, (_, place) in zip(self.slots[step - 1], pairs, strict=True):
                wires.copy(place, place, slot, back).wait_recv()
        for copy in self.sends():
            copy.wait_send()


def meeting_kernel(
    shards, planes, tokens, gain, mixed_all, out_w, gate, up, down,
    hidden_out, mixed_own, normed_out, wide_w, down_w, down_next, normed_all, send, recv, local, store,
):
    wires = Wires(send, recv)
    device, shard = wires.device, wires.shard
    seq, _ = tokens.shape
    rows, part = hidden_out.shape[0], mixed_all.shape[2]
    half = seq // 2
    greet(
        [wires.peer(step=step, shards=shards) for step in range(1, shards)]
        + [wires.peer(XBIT), wires.peer(YBIT), wires.peer(CORE)]
    )
    units = [
        Units(wires, shards, 0, gate, up, down, wide_w, down_w, local, 0),
        Units(wires, shards, 1, gate, up, down, None, down_next, local, 3, (0, 2)),
    ]
    for group in units:
        group.begin()

    def stage(index):
        def view(owner, start, size):
            return normed_all.at[owner, pl.ds(start, size)]

        return Plane(
            wires,
            [lambda owner, side: view(owner, index * half + side * (half // 2), half // 2)],
            [lambda owner: view(owner, index * half, half)],
        )

    stages = [stage(index) for index in range(2)]
    for side in range(2):
        span = pl.ds(side * half, half)
        total = tokens[span, :].astype(jnp.float32)
        for source in range(shards):
            total = total + jnp.dot(
                mixed_all[source, span, :],
                out_w[pl.ds(source * part, part), :],
                preferred_element_type=jnp.float32,
            )
        normed_all[device, span, :] = (total * norm_factor(total) * gain[...]).astype(
            normed_all.dtype
        )
        stages[side].step_one()
        stages[side].start(stages[side].cores(0))
        for inner in range(half // rows):

            @pl.when(shard == side * (half // rows) + inner)
            def _(total=total, inner=inner):
                hidden_out[...] = total[inner * rows : (inner + 1) * rows, :]

    stored = []

    def keep(owner, side):
        span = pl.ds(side * half, half)
        copy = pltpu.make_async_copy(
            normed_all.at[owner, span], normed_out.at[owner, span], store.at[len(stored)]
        )
        copy.start()
        stored.append(copy)

    for source in range(shards):
        mixed_own[:, pl.ds(source * part, part)] = mixed_all[
            source, pl.ds(pl.multiple_of(shard * rows, rows), rows), :
        ]
    for plane in stages:
        plane.step_two()
    for side, plane in enumerate(stages):
        plane.step_three()
        for chip in range(4):
            keep(device ^ (2 * chip), side)
    for side, plane in enumerate(stages):
        plane.finish()
        for chip in range(4):
            keep(device ^ (2 * chip + 1), side)
    for group in units:
        group.end()
    for copy in stored:
        copy.wait()


def unit_shapes(gate, shards):
    _, part, hidden_units = gate.shape
    each = hidden_units // shards
    return (
        jax.ShapeDtypeStruct((shards, part, 2 * each), gate.dtype),
        jax.ShapeDtypeStruct((shards, each, part), gate.dtype),
    )


def meeting_call(tokens, gain, mixed_all, out_w, gate, up, down, planes, shards):
    hbm = pl.BlockSpec(memory_space=pltpu.HBM)
    vmem = pl.BlockSpec(memory_space=pltpu.VMEM)
    seq, width = tokens.shape
    rows = seq // shards
    slots = 32
    low = tokens.dtype
    return pl.pallas_call(
        functools.partial(meeting_kernel, shards, planes),
        in_specs=[vmem] * 4 + [hbm] * 3,
        out_specs=[vmem] * 2 + [hbm] * 4,
        out_shape=(
            pltpu.HBM((rows, width), jnp.float32),
            pltpu.HBM((rows, width), low),
            pltpu.HBM((planes, seq + 16, width), low),
        )
        + unit_shapes(gate, shards)
        + unit_shapes(gate, shards)[1:],
        scratch_shapes=[
            pltpu.VMEM((planes, seq, width), low),
            pltpu.SemaphoreType.DMA((slots,)),
            pltpu.SemaphoreType.DMA((slots,)),
            pltpu.SemaphoreType.DMA((4,)),
            pltpu.SemaphoreType.DMA((2 * planes,)),
        ],
        compiler_params=pltpu.CompilerParams(
            collective_id=3, has_side_effects=True, vmem_limit_bytes=40 * MIB
        ),
        cost_estimate=pl.CostEstimate(
            flops=2 * seq * width * width, bytes_accessed=300 * MIB, transcendentals=0
        ),
    )(tokens, gain, mixed_all, out_w, *held_in_hbm(gate, up, down))


def add_rows(target, sources, lines):
    rows = target.shape[0]

    def body(index, carry):
        span = pl.ds(pl.multiple_of(index * lines, lines), lines)
        total = target[span, :].astype(jnp.float32)
        for source in sources:
            total = total + source[span, :].astype(jnp.float32)
        target[span, :] = total.astype(target.dtype)
        return carry

    lax.fori_loop(0, rows // lines, body, 0)


class PlaneSum:
    def __init__(self, wires, part, held, came, diag, side, local, base):
        self.wires, self.part, self.local, self.base = wires, part, local, base
        self.held, self.came, self.diag, self.side = held, came, diag, side
        self.half = held.shape[1] // 2
        self.core = [wires.slot() for _ in range(4)]
        self.corner = [wires.slot() for _ in range(2)]
        self.edge = [wires.slot() for _ in range(2)]
        self.sent = []

    def start(self, copy):
        copy.start()
        self.sent.append(copy)

    def load(self, chip):
        return pltpu.make_async_copy(
            self.part(chip, 0), self.held.at[chip], self.local.at[self.base + chip]
        )

    def give(self, chip):
        self.start(
            self.wires.copy(
                self.held.at[chip], self.came.at[chip], self.core[chip], self.wires.peer(CORE)
            )
        )

    def begin(self):
        for chip in (3, 1, 2, 0):
            self.load(chip).start()
            self.start(
                self.wires.copy(
                    self.part(chip, 1), self.came.at[chip], self.core[chip], self.wires.peer(CORE)
                )
            )

    def add_core(self, chip):
        if self.part is not None:
            self.load(chip).wait()
        place = self.came.at[chip]
        self.wires.copy(place, place, self.core[chip], self.wires.peer(CORE)).wait_recv()
        add_rows(self.held.at[chip], [place], 64)

    def part_of_corner(self, which):
        return self.held.at[3, pl.ds(which * self.half, self.half)]

    def send_corner(self):
        self.add_core(3)
        for which, bits in enumerate((XBIT, YBIT)):
            self.start(
                self.wires.copy(
                    self.part_of_corner(which),
                    self.diag.at[which],
                    self.corner[which],
                    self.wires.peer(bits),
                )
            )

    def add_cores(self):
        for chip in (1, 2, 0):
            self.add_core(chip)

    def send_sides(self):
        for which, (bits, chip) in enumerate(((XBIT, 2), (YBIT, 1))):
            place = self.diag.at[which]
            self.wires.copy(place, place, self.corner[which], self.wires.peer(bits)).wait_recv()
            add_rows(self.held.at[chip, pl.ds(which * self.half, self.half)], [place], 64)
            self.start(
                self.wires.copy(
                    self.held.at[chip],
                    self.side.at[1 - which],
                    self.edge[1 - which],
                    self.wires.peer((XBIT | YBIT) ^ bits),
                )
            )

    def end(self):
        for which, bits in enumerate((XBIT, YBIT)):
            place = self.side.at[which]
            self.wires.copy(place, place, self.edge[which], self.wires.peer(bits)).wait_recv()
        add_rows(self.held.at[0], [self.side.at[0], self.side.at[1]], 64)

    def drain(self):
        for copy in self.sent:
            copy.wait_send()


class LineSum:
    def __init__(self, wires, shards, source, landing):
        self.wires, self.shards, self.source, self.landing = wires, shards, source, landing
        self.slots = [wires.slot() for _ in range(shards - 1)]

    def sends(self):
        wires = self.wires
        for step in range(1, self.shards):
            peer = wires.peer(step=step, shards=self.shards)
            yield wires.copy(
                self.source(peer[1]), self.landing(wires.shard), self.slots[step - 1], peer
            )

    def begin(self):
        for copy in self.sends():
            copy.start()

    def arrive(self):
        wires = self.wires
        for step in range(1, self.shards):
            peer = wires.peer(step=self.shards - step, shards=self.shards)
            place = self.landing(peer[1])
            wires.copy(place, place, self.slots[step - 1], peer).wait_recv()

    def drain(self):
        for copy in self.sends():
            copy.wait_send()


class LineFlow:
    def __init__(self, wires, shards, own, flow):
        self.wires, self.shards, self.own, self.flow = wires, shards, own, flow
        self.slots = [[wires.slot() for _ in range(shards)] for _ in range(2)]
        self.order = [
            (way, (shards - 1 - step) if way == 0 else step)
            for step in range(shards - 1)
            for way in range(2)
        ]

    def copy(self, way, block, source):
        wires = self.wires
        peer = (wires.device, wires.shard + (1 if way == 0 else -1))
        return wires.copy(source, self.flow.at[way, block], self.slots[way][block], peer)

    def first(self, way):
        return self.wires.shard == (0 if way == 0 else self.shards - 1)

    def passes(self, way, block):
        shard = self.wires.shard
        inner = jnp.logical_and(shard > 0, shard < block)
        if way == 1:
            inner = jnp.logical_and(shard < self.shards - 1, shard > block)
        return inner

    def begin(self):
        for way, block in self.order:

            @pl.when(self.first(way))
            def _(way=way, block=block):
                self.copy(way, block, self.own(block)).start()

    def forward(self, way, block):
        @pl.when(self.passes(way, block))
        def _():
            place = self.flow.at[way, block]
            self.copy(way, block, place).wait_recv()
            add_rows(place, [self.own(block)], 64)
            self.copy(way, block, place).start()

    def end(self):
        shard = self.wires.shard
        for block in range(self.shards):

            @pl.when(shard == block)
            def _(block=block):
                sources = []
                for way in range(2):
                    if block != (0 if way == 0 else self.shards - 1):
                        place = self.flow.at[way, block]
                        self.copy(way, block, place).wait_recv()
                        sources.append(place)
                add_rows(self.own(block), sources, 64)

    def drain(self):
        for way, block in self.order:
            sends = jnp.logical_or(self.first(way), self.passes(way, block))

            @pl.when(sends)
            def _(way=way, block=block):
                self.copy(way, block, self.own(block)).wait_send()


def line_total(landing, shards):
    total = landing[0].astype(jnp.float32)
    for shard in range(1, shards):
        total = total + landing[shard].astype(jnp.float32)
    return total


def aligned(index, size):
    return pl.ds(pl.multiple_of(index * size, size), size)


def expert_kernel(
    index, experts, shards, x, g, keep, wide_w, router_w, down_w, hot, *refs
):
    if index == 0:
        gate, up, down, _, out, grad, pull, wide_sum, down_sum, next_wide, next_down = refs[:11]
        acc, dacc, wide_out, down_out, send, recv, local, sems = refs[11:]
    else:
        old_out, old_grad, old_pull, wide_sent, down_sent = refs[:5]
        out, grad, wide_sum, down_sum, router_sum, wide_came, down_came = refs[5:12]
        acc, racc, dacc, wide_out, down_out, send, recv, local, sems = refs[12:]
    step, steps = pl.program_id(0), pl.num_programs(0)
    wires = Wires(send, recv)
    if index == 0:
        travel = [Units(wires, shards, 1, gate, up, down, next_wide, next_down, local, 0, (1, 2))]
    else:
        travel = [
            LineSum(wires, shards, lambda t: wide_sent.at[t], lambda s: wide_came.at[s]),
            LineSum(wires, shards, lambda t: down_sent.at[t], lambda s: down_came.at[s]),
        ]
        stay = [
            pltpu.make_async_copy(
                sent.at[wires.shard], came.at[wires.shard], local.at[place]
            )
            for place, (sent, came) in enumerate(((wide_sent, wide_came), (down_sent, down_came)))
        ]

    @pl.when(step == 0)
    def _():
        greet([wires.peer(step=hop, shards=shards) for hop in range(1, shards)])
        for group in travel:
            group.begin()
        acc[...] = jnp.zeros_like(acc)
        dacc[...] = jnp.zeros_like(dacc)
        if index == 1:
            for copy in stay:
                copy.start()
            racc[...] = jnp.zeros_like(racc)

    _, each, part = down_w.shape
    wide = jnp.dot(x[...], wide_w[...], preferred_element_type=jnp.float32)
    back = nt_dot(g[:, :part], down_w[0])
    for shard in range(1, shards):
        back = back + nt_dot(g[:, shard * part : (shard + 1) * part], down_w[shard])
    if index == 0:
        logits = jnp.dot(x[...], router_w[...], preferred_element_type=jnp.float32)
        lane = lax.broadcasted_iota(jnp.int32, logits.shape, 1)
        logits = jnp.where(lane < experts, logits, -1e30)
        shifted = jnp.exp(logits - jnp.max(logits, axis=-1, keepdims=True))
        probs = shifted / jnp.sum(shifted, axis=-1, keepdims=True)
    else:
        lane = lax.broadcasted_iota(jnp.int32, old_pull.shape, 1)
        probs = jnp.where(lane < experts, old_pull[...], 0.0)
    mark = hot[index : index + 1, :]
    kept = keep[:, index : index + 1]
    route = jnp.sum(probs * mark, axis=-1, keepdims=True) * kept
    gated, lifted = wide[:, :each], wide[:, each:]
    sigma = 1.0 / (1.0 + jnp.exp(-gated))
    silu = gated * sigma
    act = silu * lifted
    pulled = jnp.sum(act * back, axis=-1, keepdims=True) * kept
    act_low = (act * route).astype(jnp.bfloat16)
    act_grad = back * route
    wide_low = jnp.concatenate(
        [
            (act_grad * lifted * sigma * (1.0 + gated * (1.0 - sigma))).astype(jnp.bfloat16),
            (act_grad * silu).astype(jnp.bfloat16),
        ],
        axis=1,
    )
    result = nt_dot(wide_low, wide_w[...])
    if index == 0:
        pull[...] = jnp.where(lane < experts, probs, jnp.where(lane == 127, pulled, 0.0))
    else:
        dense = pulled * mark + old_pull[:, 127:] * hot[0:1, :]
        logit_grad = probs * (dense - jnp.sum(probs * dense, axis=-1, keepdims=True))
        logit_low = logit_grad.astype(jnp.bfloat16)
        result = result + nt_dot(logit_low, router_w[...]) + old_grad[...].astype(jnp.float32)
        racc[...] += tn_dot(x[...], logit_low)
    grad[...] = result.astype(jnp.bfloat16)
    for shard in range(shards):
        span = slice(shard * part, (shard + 1) * part)
        value = jnp.dot(act_low, down_w[shard], preferred_element_type=jnp.float32)
        if index == 1:
            value = value + old_out[:, span].astype(jnp.float32)
        out[:, span] = value.astype(jnp.bfloat16)
        dacc[shard] += tn_dot(act_low, g[:, span])
    acc[...] += tn_dot(x[...], wide_low)

    @pl.when(step == steps - 1)
    def _():
        wide_out[...] = acc[...].astype(jnp.bfloat16)
        wide_copy = pltpu.make_async_copy(wide_out, wide_sum, sems.at[0])
        wide_copy.start()
        down_out[...] = dacc[...].astype(jnp.bfloat16)
        down_copy = pltpu.make_async_copy(down_out, down_sum, sems.at[1])
        down_copy.start()
        if index == 1:
            router_copy = pltpu.make_async_copy(racc, router_sum, sems.at[2])
            router_copy.start()
            router_copy.wait()
        wide_copy.wait()
        down_copy.wait()
        if index == 0:
            travel[0].end()
        else:
            for copy in stay:
                copy.wait()
            for group in travel:
                group.arrive()
                group.drain()


def expert_call(index, x_all, g_all, keep, wide_w, router_w, down_w, hot, experts, weights, before):
    planes, _, width = x_all.shape
    rows = keep.shape[1]
    shards = down_w.shape[0]
    tile = 512
    per = rows // tile
    hbm = pl.BlockSpec(memory_space=pltpu.HBM)

    def whole(value):
        zeros = (0,) * value.ndim
        return pl.BlockSpec(value.shape, lambda i: zeros, pipeline_mode=pl.Buffered(1))

    def rowwise(lanes):
        return pl.BlockSpec((None, tile, lanes), lambda i: (i // per, i % per, 0))

    low = jnp.bfloat16
    tall = pltpu.HBM((planes, rows, width), low)
    narrow = pltpu.HBM((planes, rows, 128), jnp.float32)
    wide_shape = pltpu.HBM(wide_w.shape, low)
    down_shape = pltpu.HBM(down_w.shape, low)
    came = pltpu.HBM((shards, width // shards, wide_w.shape[1]), low)
    if index == 0:
        others = [hbm] * 4
        out_specs = [rowwise(width)] * 2 + [rowwise(128)] + [hbm] * 4
        spare = [pltpu.HBM((planes, rows + extra, width), low) for extra in (32, 48)]
        shapes = (*spare, narrow, wide_shape, down_shape, came, down_shape)
        operands = held_in_hbm(*weights)
    else:
        others = [rowwise(width)] * 2 + [rowwise(128)] + [hbm] * 2
        out_specs = [rowwise(width)] * 2 + [hbm] * 5
        router_shape = pltpu.HBM(router_w.shape, jnp.float32)
        shapes = (tall, tall, wide_shape, down_shape, router_shape, came, down_shape)
        operands = held_in_hbm(*before)
    return pl.pallas_call(
        functools.partial(expert_kernel, index, experts, shards),
        grid=(planes * per,),
        in_specs=[
            rowwise(width),
            rowwise(width),
            rowwise(keep.shape[2]),
            whole(wide_w),
            whole(router_w),
            whole(down_w),
            whole(hot),
        ]
        + others,
        out_specs=out_specs,
        scratch_shapes=[pltpu.VMEM(wide_w.shape, jnp.float32)]
        + ([] if index == 0 else [pltpu.VMEM(router_w.shape, jnp.float32)])
        + [
            pltpu.VMEM(down_w.shape, jnp.float32),
            pltpu.VMEM(wide_w.shape, low),
            pltpu.VMEM(down_w.shape, low),
            pltpu.SemaphoreType.DMA((12,)),
            pltpu.SemaphoreType.DMA((12,)),
            pltpu.SemaphoreType.DMA((3,)),
            pltpu.SemaphoreType.DMA((3,)),
        ],
        out_shape=shapes,
        input_output_aliases={10: 6} if index == 0 else {},
        compiler_params=pltpu.CompilerParams(
            collective_id=7 + index, has_side_effects=True, vmem_limit_bytes=52 * MIB
        ),
        cost_estimate=pl.CostEstimate(
            flops=planes * rows * width * 12 * down_w.shape[1],
            bytes_accessed=100 * MIB,
            transcendentals=planes * rows * down_w.shape[1],
        ),
    )(*held_in_hbm(x_all, g_all), keep, wide_w, router_w, down_w, hot, *operands)


def returning_kernel(
    shards, ins, outs, wide, down, in_total, out_total, wide_all, down_all,
    held, came, diag, side, held2, came2, diag2, side2, landing, send, recv, local,
):
    wires = Wires(send, recv)
    device, shard = wires.device, wires.shard
    rows = in_total.shape[0]
    greet(
        [wires.peer(step=step, shards=shards) for step in range(1, shards)]
        + [wires.peer(XBIT), wires.peer(YBIT), wires.peer(CORE)]
    )

    def rel(source):
        return lambda chip, core: source.at[device ^ (2 * chip + core)]

    grads = PlaneSum(wires, rel(ins), held, came, diag, side, local, 0)
    values = PlaneSum(wires, rel(outs), held2, came2, diag2, side2, local, 6)
    weights = [
        LineSum(wires, shards, lambda t: wide.at[t], lambda s: wide_all.at[s]),
        LineSum(wires, shards, lambda t: down.at[t], lambda s: down_all.at[s]),
    ]
    line = LineSum(
        wires, shards, lambda t: held.at[0, aligned(t, rows)], lambda s: landing.at[s]
    )
    grads.begin()
    for group in weights:
        group.begin()
    own = [
        pltpu.make_async_copy(wide.at[shard], wide_all.at[shard], local.at[4]),
        pltpu.make_async_copy(down.at[shard], down_all.at[shard], local.at[5]),
    ]
    for copy in own:
        copy.start()
    grads.send_corner()
    values.begin()
    grads.add_cores()
    grads.send_sides()
    values.send_corner()
    values.add_cores()
    grads.end()
    line.begin()
    values.send_sides()
    landing[shard] = held[0, aligned(shard, rows), :]
    line.arrive()
    in_total[...] = line_total(landing, shards)
    values.end()
    back = pltpu.make_async_copy(held2.at[0], out_total, local.at[10])
    back.start()
    for copy in own:
        copy.wait()
    back.wait()
    for group in weights:
        group.arrive()
    for group in (grads, values, line, *weights):
        group.drain()


def sum_work(rows, lanes):
    low = jnp.bfloat16
    return [
        pltpu.VMEM((4, rows, lanes), low),
        pltpu.VMEM((4, rows, lanes), low),
        pltpu.VMEM((2, rows // 2, lanes), low),
        pltpu.VMEM((2, rows, lanes), low),
    ]


def returning_call(ins, outs, wide, down):
    _, seq, width = ins.shape
    shards = wide.shape[0]
    rows = seq // shards
    hbm = pl.BlockSpec(memory_space=pltpu.HBM)
    vmem = pl.BlockSpec(memory_space=pltpu.VMEM)
    return pl.pallas_call(
        functools.partial(returning_kernel, shards),
        in_specs=[hbm] * 4,
        out_specs=[vmem, hbm, hbm, hbm],
        out_shape=(
            jax.ShapeDtypeStruct((rows, width), jnp.float32),
            jax.ShapeDtypeStruct((seq, width), jnp.bfloat16),
            pltpu.HBM(wide.shape, wide.dtype),
            pltpu.HBM(down.shape, down.dtype),
        ),
        scratch_shapes=sum_work(seq, width)
        + sum_work(seq, width)
        + [
            pltpu.VMEM((shards, rows, width), jnp.bfloat16),
            pltpu.SemaphoreType.DMA((36,)),
            pltpu.SemaphoreType.DMA((36,)),
            pltpu.SemaphoreType.DMA((11,)),
        ],
        compiler_params=pltpu.CompilerParams(
            collective_id=4, has_side_effects=True, vmem_limit_bytes=56 * MIB
        ),
        cost_estimate=pl.CostEstimate(flops=0, bytes_accessed=300 * MIB, transcendentals=0),
    )(*held_in_hbm(ins, outs, wide, down))


def back_through_heads(
    mixed_grad, raw, low, total, query_gain, key_gain, cosine, sine, allowed, qkv_grad
):
    part = raw.shape[1] // 2
    gain_sums = [None, None]
    for head in range(part // HD):
        span = pl.ds(head * HD, HD)
        query, key = low[:, span], low[:, pl.ds(part + head * HD, HD)]
        value = low[:, pl.ds(2 * part + head * HD, HD)]
        out_grad = mixed_grad[:, span]
        scores = jnp.where(allowed, nt_dot(query, key), -1e30)
        probs = jnp.exp(scores - total[:, head : head + 1])
        prob_grad = nt_dot(out_grad, value)
        value_grad = tn_dot(probs.astype(jnp.bfloat16), out_grad)
        qkv_grad[:, pl.ds(2 * part + head * HD, HD)] = value_grad.astype(jnp.bfloat16)
        inner = jnp.sum(probs * prob_grad, axis=-1, keepdims=True)
        score_grad = (probs * (prob_grad - inner)).astype(jnp.bfloat16)
        rotated = (
            jnp.dot(score_grad, key, preferred_element_type=jnp.float32) * HD ** (-0.5),
            tn_dot(score_grad, query),
        )
        for which, (offset, scale_gain) in enumerate(((0, query_gain), (part, key_gain))):
            grad = rotated[which]
            grad = grad * cosine[...] - pltpu.roll(grad, HD // 2, 1) * sine[...]
            source = raw[:, pl.ds(offset + head * HD, HD)]
            factor = norm_factor(source)
            gain_sum = jnp.sum(grad * source * factor, axis=0, keepdims=True)
            gain_sums[which] = gain_sum if head == 0 else gain_sums[which] + gain_sum
            scaled = grad * scale_gain[...]
            inner = jnp.mean(scaled * source, axis=-1, keepdims=True)
            result = factor * scaled - source * (factor * factor * factor) * inner
            qkv_grad[:, pl.ds(offset + head * HD, HD)] = result.astype(jnp.bfloat16)
    return gain_sums


def closing_kernel(
    shards, planes,
    hidden, grad, out_grad, ffn_gain, raw, low, total, query_gain, key_gain, cosine, sine, seg_row,
    tokens, gain, own_mixed, normed, router, out_w, qkv_w, out_total,
    input_grad, mixed_out, query_out, key_out, value_out, weight_out, gain_out, router_out, vectors_out,
    held, came, diag, side, held2, came2, diag2, side2,
    weights, hidden_grad, attn_low, message, message_land, qkv_grad, normed_grad, vectors,
    out_own, norm_land, out_land, qkv_land, weight_land, gain_mine, gain_land, gain_line, router_land, router_sum, router_line,
    vector_land, vector_sum, vector_line, send, recv, local,
):
    wires = Wires(send, recv)
    device, shard = wires.device, wires.shard
    rows, width = tokens.shape
    block = query_out.shape[0]
    part = width // shards
    lines = router_out.shape[0]
    lanes = qkv_w.shape[1]
    line_peers = [wires.peer(step=step, shards=shards) for step in range(1, shards)]
    plane_peers = [wires.peer(bits) for bits in range(1, planes)]
    load_out = pltpu.make_async_copy(out_w, weights, local.at[0])
    load_out.start()
    load_value = pltpu.make_async_copy(out_total, out_own, local.at[2])
    load_value.start()
    greet(line_peers + plane_peers)

    back = LineSum(
        wires, shards, lambda t: message.at[t], lambda s: message_land.at[aligned(s, rows)]
    )
    norms = LineFlow(wires, shards, lambda b: normed_grad.at[aligned(b, rows)], norm_land)
    values = LineFlow(wires, shards, lambda b: out_own.at[aligned(b, rows)], out_land)
    qkv = PlaneSum(wires, None, held, came, diag, side, local, 0)
    weight = PlaneSum(wires, None, held2, came2, diag2, side2, local, 0)
    qkv_line = LineSum(
        wires, shards, lambda t: held.at[0, aligned(t, block)], lambda s: qkv_land.at[s]
    )
    weight_line = LineSum(
        wires, shards, lambda t: held2.at[0, aligned(t, block)], lambda s: weight_land.at[s]
    )
    sent = []

    def spread(slots, source, landing):
        for bits in range(1, planes):
            copy = wires.copy(
                source(device ^ bits), landing.at[device], slots[bits - 1], wires.peer(bits)
            )
            copy.start()
            sent.append(copy)

    def collect(slots, landing):
        for bits in range(1, planes):
            place = landing.at[device ^ bits]
            wires.copy(place, place, slots[bits - 1], wires.peer(bits)).wait_recv()
        total = landing[0]
        for other in range(1, planes):
            total = total + landing[other]
        return total

    router_slots = [wires.slot() for _ in range(1, planes)]
    vector_slots = [wires.slot() for _ in range(1, planes)]
    gain_slots = [wires.slot() for _ in range(1, planes)]
    spread(router_slots, lambda e: router.at[aligned(e, shards * lines)], router_land)
    router_land[device] = router[aligned(device, shards * lines), :]

    factor = norm_factor(hidden[...])
    vectors[:, :width] = jnp.sum(grad[...] * hidden[...] * factor, axis=0, keepdims=True)
    scaled = grad[...] * ffn_gain[...]
    inner = jnp.mean(scaled * hidden[...], axis=-1, keepdims=True)
    change = out_grad[...].astype(jnp.float32) + factor * scaled
    change = change - hidden[...] * (factor * factor * factor) * inner
    hidden_grad[...] = change
    attn_low[...] = change.astype(jnp.bfloat16)
    load_out.wait()
    for target in range(shards):
        message[target] = nt_dot(attn_low[...], weights[pl.ds(target * part, part), :]).astype(
            jnp.bfloat16
        )
    back.begin()
    load_value.wait()
    values.begin()
    load_qkv = pltpu.make_async_copy(qkv_w, weights.at[:, pl.ds(0, lanes)], local.at[1])
    load_qkv.start()
    message_land[aligned(shard, rows), :] = message[shard]

    def addends(group, left, right):
        for core in (1, 0):
            for chip in (3, 1, 2, 0):
                owner = device ^ (2 * chip + core)
                columns = pl.ds(pl.multiple_of(owner * shards * block, shards * block), shards * block)
                if core == 0:
                    group.sent[(3, 1, 2, 0).index(chip)].wait_send()
                group.held[chip] = tn_dot(left[:, columns], right[...]).astype(jnp.bfloat16)
                if core == 1:
                    group.give(chip)
        group.sent = []

    addends(weight, own_mixed, attn_low)
    weight.send_corner()
    weight.add_cores()
    far = shards - 1
    router_sum[...] = collect(router_slots, router_land)
    router_pass = LineSum(
        wires, shards, lambda t: router_sum.at[aligned(t, lines)], lambda s: router_line.at[s]
    )

    back.arrive()
    allowed = same_document(seg_row)
    query_sum, key_sum = back_through_heads(
        message_land, raw, low, total, query_gain, key_gain, cosine, sine, allowed, qkv_grad
    )
    vectors[:, pl.ds(width, HD)] = query_sum
    vectors[:, pl.ds(width + HD, HD)] = key_sum
    load_qkv.wait()
    normed_grad[...] = nt_dot(qkv_grad[...], weights[:, pl.ds(0, lanes)]).astype(jnp.bfloat16)
    norms.begin()
    values.forward(0, far)
    values.forward(1, 0)
    router_pass.begin()
    spread(vector_slots, lambda e: vectors, vector_land)
    vector_land[device] = vectors[...]
    weight.send_sides()
    for step in range(1, shards - 1):
        values.forward(0, far - step)
        values.forward(1, step)
    addends(qkv, normed, qkv_grad)
    norms.forward(0, far)
    norms.forward(1, 0)
    qkv.send_corner()
    qkv.add_cores()
    for step in range(1, shards - 1):
        norms.forward(0, far - step)
        norms.forward(1, step)
    vector_sum[...] = collect(vector_slots, vector_land)
    vector_pass = LineSum(wires, shards, lambda t: vector_sum, lambda s: vector_line.at[s])
    vector_pass.begin()
    vector_line[shard] = vector_sum[...]
    router_line[shard] = router_sum[aligned(shard, lines), :]
    qkv.send_sides()
    weight.end()
    weight_line.begin()
    weight_land[shard] = held2[0, aligned(shard, block), :]
    values.end()
    mine = aligned(shard, rows)
    mixed_out[...] = (hidden[...] + out_own[mine, :].astype(jnp.float32)).astype(jnp.bfloat16)

    norms.end()
    change = normed_grad[mine, :].astype(jnp.float32)
    given = tokens[...].astype(jnp.float32)
    factor = norm_factor(given)
    gain_mine[...] = jnp.sum(change * given * factor, axis=0, keepdims=True)
    spread(gain_slots, lambda e: gain_mine, gain_land)
    scaled = change * gain[...]
    inner = jnp.mean(scaled * given, axis=-1, keepdims=True)
    result = hidden_grad[...] + factor * scaled - given * (factor * factor * factor) * inner
    input_grad[...] = result.astype(jnp.bfloat16)
    qkv.end()
    qkv_line.begin()
    qkv_land[shard] = held[0, aligned(shard, block), :]
    gain_land[device] = gain_mine[...]
    gain_line[shard] = collect(gain_slots, gain_land)
    gain_pass = LineSum(wires, shards, lambda t: gain_line.at[shard], lambda s: gain_line.at[s])
    gain_pass.begin()
    router_pass.arrive()
    router_out[...] = line_total(router_line, shards)
    vector_pass.arrive()
    vectors_out[...] = line_total(vector_line, shards)
    weight_line.arrive()
    weight_out[...] = line_total(weight_land, shards)
    qkv_line.arrive()
    for source in range(shards):
        for which, result_out in enumerate((query_out, key_out, value_out)):
            result_out[:, pl.ds(source * part, part)] = qkv_land[
                source, :, pl.ds(which * part, part)
            ].astype(jnp.float32)
    gain_pass.arrive()
    gain_out[...] = line_total(gain_line, shards)
    for copy in sent:
        copy.wait_send()
    groups = (back, norms, values, qkv, weight, qkv_line, weight_line, router_pass, vector_pass)
    for group in (*groups, gain_pass):
        group.drain()


def closing_call(
    hidden, grad, out_grad, ffn_gain, raw, low, total, query_gain, key_gain, tables, seg_row,
    tokens, gain, own_mixed, normed, router, out_w, qkv_w, out_total, planes, shards,
):
    rows, width = tokens.shape
    seq, lanes = low.shape
    each = width // planes
    block = each // shards
    lines = router.shape[0] // (planes * shards)
    hbm = pl.BlockSpec(memory_space=pltpu.HBM)
    vmem = pl.BlockSpec(memory_space=pltpu.VMEM)
    half, full = jnp.bfloat16, jnp.float32
    weight_shape = jax.ShapeDtypeStruct((block, width), full)
    vector = width + 2 * HD
    return pl.pallas_call(
        functools.partial(closing_kernel, shards, planes),
        in_specs=[vmem] * 17 + [hbm] * 3,
        out_specs=[vmem] * 9,
        out_shape=(
            jax.ShapeDtypeStruct((rows, width), half),
            jax.ShapeDtypeStruct((rows, width), half),
            weight_shape,
            weight_shape,
            weight_shape,
            weight_shape,
            jax.ShapeDtypeStruct((1, width), full),
            jax.ShapeDtypeStruct((lines, 128), full),
            jax.ShapeDtypeStruct((1, vector), full),
        ),
        scratch_shapes=sum_work(each, lanes)
        + sum_work(each, width)
        + [
            pltpu.VMEM((width, width), half),
            pltpu.VMEM((rows, width), full),
            pltpu.VMEM((rows, width), half),
            pltpu.VMEM((shards, rows, width // shards), half),
            pltpu.VMEM((seq, width // shards), half),
            pltpu.VMEM((seq, lanes), half),
            pltpu.VMEM((seq, width), half),
            pltpu.VMEM((1, vector), full),
            pltpu.VMEM((seq, width), half),
            pltpu.VMEM((2, shards, rows, width), half),
            pltpu.VMEM((2, shards, rows, width), half),
            pltpu.VMEM((shards, block, lanes), half),
            pltpu.VMEM((shards, block, width), half),
            pltpu.VMEM((1, width), full),
            pltpu.VMEM((planes, 1, width), full),
            pltpu.VMEM((shards, 1, width), full),
            pltpu.VMEM((planes, shards * lines, 128), full),
            pltpu.VMEM((shards * lines, 128), full),
            pltpu.VMEM((shards, lines, 128), full),
            pltpu.VMEM((planes, 1, vector), full),
            pltpu.VMEM((1, vector), full),
            pltpu.VMEM((shards, 1, vector), full),
            pltpu.SemaphoreType.DMA((80,)),
            pltpu.SemaphoreType.DMA((80,)),
            pltpu.SemaphoreType.DMA((3,)),
        ],
        compiler_params=pltpu.CompilerParams(
            collective_id=6, has_side_effects=True, vmem_limit_bytes=62 * MIB
        ),
        cost_estimate=pl.CostEstimate(flops=0, bytes_accessed=300 * MIB, transcendentals=0),
    )(
        hidden, grad, out_grad, ffn_gain, raw, low, total, query_gain, key_gain, *tables, seg_row,
        tokens, gain, own_mixed, normed, router, *held_in_hbm(out_w, qkv_w, out_total),
    )


LOW = jnp.bfloat16
WIDE = jnp.float32


def fast_local(
    tokens,
    segment_ids,
    routes,
    pair_order,
    attn_gain,
    w_query,
    w_key,
    w_value,
    query_gain,
    key_gain,
    w_out,
    ffn_gain,
    w_router,
    w_gate,
    w_up,
    w_down,
    out_grad,
):
    rows, width = tokens.shape
    top_count = routes.shape[1]
    planes = lax.axis_size(EXPERT)
    shards = lax.axis_size(SHARD)
    own_experts = w_gate.shape[0]
    experts = own_experts * planes
    capacity = 5 * rows * top_count // (4 * own_experts)
    seq = segment_ids.shape[0]
    device = lax.axis_index(EXPERT)
    shard = lax.axis_index(SHARD)
    part = width // shards

    index = device * shards + shard

    def placed(values, size):
        owner = jnp.arange(size) // values.size
        return jnp.where(owner == index, jnp.tile(values, size // values.size), 0)

    gains = [placed(attn_gain, width), placed(ffn_gain, width)]
    gains += [placed(query_gain, HD), placed(key_gain, HD)]
    gains = jnp.concatenate(gains)
    gains = jnp.pad(gains, (0, -gains.size % (16 * 128))).reshape(-1, 128)
    router_pad = jnp.pad(w_router, ((0, 0), (0, 128 - experts)))
    tables = turn_tables(seq)
    seg_row = segment_ids.reshape(1, seq)
    opened = opening_call(
        routes.T,
        pair_order.reshape(rows, top_count).T,
        gains,
        seg_row,
        tables,
        router_pad,
        w_query,
        w_key,
        w_value,
        tokens,
        w_out,
        out_grad,
        experts,
        own_experts,
        capacity,
        planes,
        shards,
    )
    kept, attn_row, ffn_row, query_row, key_row, normed_low, raw, low, total, mixed_all = opened[:10]
    router_w, qkv_w, tokens_seq, out_w, grad_all = opened[10:]
    router_w = router_w.reshape(width, 128)
    hidden, own_mixed, token_all, wide_w, down_w, down_next = meeting_call(
        tokens_seq, ffn_row, mixed_all, out_w, w_gate, w_up, w_down, planes, shards
    )
    grad_all = grad_all.reshape(planes, seq, width)
    own_ids = device * own_experts + jnp.arange(own_experts, dtype=jnp.int32)
    own_hot = (own_ids[:, None] == jnp.arange(128, dtype=jnp.int32)[None, :]).astype(WIDE)
    out_first, in_first, pull, wide_sum, down_sum, wide_next, down_next = expert_call(
        0,
        token_all,
        grad_all,
        kept,
        wide_w.reshape(width, -1),
        router_w,
        down_w,
        own_hot,
        experts,
        (w_gate, w_up, w_down, down_next),
        None,
    )
    before = (out_first, in_first, pull, wide_sum.reshape(shards, part, -1), down_sum)
    out_parts, in_parts, wide_sum, down_sum, router_grad, wide0, down0 = expert_call(
        1,
        token_all,
        grad_all,
        kept,
        wide_next.reshape(width, -1),
        router_w,
        down_next,
        own_hot,
        experts,
        None,
        before,
    )
    normed_two_grad, out_total, wide1, down1 = returning_call(
        in_parts, out_parts, wide_sum.reshape(shards, part, -1), down_sum
    )
    closed = closing_call(
        hidden,
        normed_two_grad,
        out_grad,
        ffn_row,
        raw,
        low,
        total,
        query_row,
        key_row,
        tables,
        seg_row,
        tokens,
        attn_row,
        own_mixed,
        normed_low,
        router_grad[:, :experts].reshape(-1, 128),
        out_w,
        qkv_w,
        out_total,
        planes,
        shards,
    )
    input_grad, mixed_out, query_w_grad, key_w_grad, value_w_grad, out_w_grad = closed[:6]
    attn_scale_grad, router_out, vectors = closed[6:]
    gate_grad, up_grad, down_grad = unpack_units((wide0, wide1), (down0, down1))
    flat = vectors.reshape(-1)

    def own_piece(values, start, size):
        return lax.dynamic_slice_in_dim(values, start + index * size, size)

    return (
        mixed_out,
        input_grad,
        own_piece(attn_scale_grad.reshape(-1), 0, attn_gain.size),
        query_w_grad,
        key_w_grad,
        value_w_grad,
        own_piece(flat, width, query_gain.size),
        own_piece(flat, width + HD, key_gain.size),
        out_w_grad,
        own_piece(flat, 0, ffn_gain.size),
        router_out.reshape(-1, experts),
        gate_grad,
        up_grad,
        down_grad,
    )


def solution(mesh):
    local = fast_local if mesh.shape[EXPERT] == 8 else general_local
    return jax.shard_map(
        local,
        mesh=mesh,
        in_specs=(
            P(BOTH, None),
            P(EXPERT),
            P(BOTH, None),
            P(BOTH),
            P(BOTH),
            P(BOTH, None),
            P(BOTH, None),
            P(BOTH, None),
            P(BOTH),
            P(BOTH),
            P(BOTH, None),
            P(BOTH),
            P(BOTH, None),
            P(EXPERT, SHARD, None),
            P(EXPERT, SHARD, None),
            P(EXPERT, None, SHARD),
            P(BOTH, None),
        ),
        out_specs=(
            P(BOTH, None),
            P(BOTH, None),
            P(BOTH),
            P(BOTH, None),
            P(BOTH, None),
            P(BOTH, None),
            P(BOTH),
            P(BOTH),
            P(BOTH, None),
            P(BOTH),
            P(BOTH, None),
            P(EXPERT, SHARD, None),
            P(EXPERT, SHARD, None),
            P(EXPERT, None, SHARD),
        ),
        check_vma=False,
    )
```

```python
import functools

import jax
import jax.numpy as jnp
import numpy as np
from jax import lax
from jax.experimental import pallas as pl
from jax.experimental.pallas import tpu as pltpu
from jax.sharding import PartitionSpec as P

HEADS = 16
HD = 128


EXPERT = "expert"
SHARD = "wshard"
BOTH = (EXPERT, SHARD)

SUM_QHD_KHD_HQK = "qhd,khd->hqk"
SUM_HQK_KHD_QHD = "hqk,khd->qhd"
SUM_ECD_EDF_ECF = "ecd,edf->ecf"
SUM_ECF_EFD_ECD = "ecf,efd->ecd"
SUM_TK_TKD_TD = "tk,tkd->td"
SUM_TD_TKD_TK = "td,tkd->tk"
SUM_ECD_EFD_ECF = "ecd,efd->ecf"
SUM_ECF_ECD_EFD = "ecf,ecd->efd"
SUM_ECD_ECF_EDF = "ecd,ecf->edf"
SUM_ECF_EDF_ECD = "ecf,edf->ecd"
SUM_HQK_QHD_KHD = "hqk,qhd->khd"
EPSILON = 1e-06
THETA = 10000.0


def matmul(left, right):
    return jnp.dot(left, right, preferred_element_type=jnp.float32)


def matmul_tn(left, right):
    return lax.dot_general(
        left, right, (((0,), (0,)), ((), ())), preferred_element_type=jnp.float32
    )


def matmul_nt(left, right):
    return lax.dot_general(
        left, right, (((1,), (1,)), ((), ())), preferred_element_type=jnp.float32
    )


def rms_scale(values, scale_gain):
    factor = lax.rsqrt(jnp.mean(values * values, axis=-1, keepdims=True) + EPSILON)
    return values * factor * scale_gain


def rope_tables(positions):
    exponent = jnp.arange(HD // 2, dtype=jnp.float32) * (2.0 / HD)
    frequency = jnp.power(jnp.float32(THETA), -exponent)
    angles = positions.astype(jnp.float32)[:, None] * frequency[None, :]
    return (jnp.cos(angles), jnp.sin(angles))


def rotate(values, cosine, sine):
    first_half = values[..., : HD // 2]
    second_half = values[..., HD // 2 :]
    cos_part = cosine[:, None, :]
    sin_part = sine[:, None, :]
    return jnp.concatenate(
        [
            first_half * cos_part - second_half * sin_part,
            second_half * cos_part + first_half * sin_part,
        ],
        axis=-1,
    )


def padded_rows(rows):
    return jnp.concatenate([jnp.zeros((1,) + rows.shape[1:], rows.dtype), rows], axis=0)


def masked_scores(query_rot, key_rot, query_segment, key_segment):
    scores = jnp.einsum(SUM_QHD_KHD_HQK, query_rot, key_rot, preferred_element_type=jnp.float32)
    allowed = query_segment[:, None] == key_segment[None, :]
    return jnp.where(allowed[None], scores, -1e30)


def swiglu_fn(gate_in, up_in):
    return jax.nn.silu(gate_in) * up_in


def general_local(
    tokens,
    segment_ids,
    routes,
    pair_order,
    attn_gain,
    w_query,
    w_key,
    w_value,
    query_gain,
    key_gain,
    w_out,
    ffn_gain,
    w_router,
    w_gate,
    w_up,
    w_down,
    out_grad,
):
    tok_rows, width = tokens.shape
    top_count = routes.shape[1]
    expert_devs = lax.axis_size(EXPERT)
    shard_devs = lax.axis_size(SHARD)
    local_experts = w_gate.shape[0]
    expert_count = local_experts * expert_devs
    most_rows = 2 * tok_rows * top_count // expert_count
    capacity = 5 * tok_rows * top_count // (4 * local_experts)
    seq_length = segment_ids.shape[0]
    device_expert = lax.axis_index(EXPERT)
    device_shard = lax.axis_index(SHARD)
    low_type = jnp.bfloat16
    wide_type = jnp.float32
    gathered = (
        lax.all_gather(attn_gain, BOTH, axis=0, tiled=True),
        lax.all_gather(w_query, BOTH, axis=0, tiled=True),
        lax.all_gather(w_key, BOTH, axis=0, tiled=True),
        lax.all_gather(w_value, BOTH, axis=0, tiled=True),
        lax.all_gather(query_gain, BOTH, axis=0, tiled=True),
        lax.all_gather(key_gain, BOTH, axis=0, tiled=True),
        lax.all_gather(w_out, BOTH, axis=0, tiled=True),
        lax.all_gather(ffn_gain, BOTH, axis=0, tiled=True),
        lax.all_gather(w_router, BOTH, axis=0, tiled=True),
    )
    attn_scale = gathered[0].astype(wide_type)
    query_w, key_w, value_w = (gathered[1], gathered[2], gathered[3])
    query_scale = gathered[4].astype(wide_type)
    key_scale = gathered[5].astype(wide_type)
    out_w = gathered[6]
    ffn_scale = gathered[7].astype(wide_type)
    router_w = gathered[8]
    inputs = tokens.astype(wide_type)
    normed, norm_one_pull = jax.vjp(rms_scale, inputs, attn_scale)
    normed_low = normed.astype(low_type)
    query_raw = matmul(normed_low, query_w)
    key_raw = matmul(normed_low, key_w)
    value_low = matmul(normed_low, value_w).astype(low_type)
    positions = device_shard * tok_rows + jnp.arange(tok_rows, dtype=jnp.int32)
    cosine, sine = rope_tables(positions)

    def prepare(query_in, key_in, query_g, key_g):
        query_heads = rms_scale(query_in.reshape(tok_rows, HEADS, HD), query_g)
        key_heads = rms_scale(key_in.reshape(tok_rows, HEADS, HD), key_g)
        return (rotate(query_heads, cosine, sine) * HD ** (-0.5), rotate(key_heads, cosine, sine))

    rotated, prepare_pull = jax.vjp(prepare, query_raw, key_raw, query_scale, key_scale)
    query_low = rotated[0].astype(low_type)
    key_low = rotated[1].astype(low_type).reshape(tok_rows, width)
    seq_keys, seq_values = (
        lax.all_gather(key_low, SHARD, axis=0, tiled=True),
        lax.all_gather(value_low, SHARD, axis=0, tiled=True),
    )
    query_segment = lax.dynamic_slice_in_dim(segment_ids, device_shard * tok_rows, tok_rows)
    scores = masked_scores(
        query_low, seq_keys.reshape(seq_length, HEADS, HD), query_segment, segment_ids
    )
    row_max = jnp.max(scores, axis=-1, keepdims=True)
    shifted = jnp.exp(scores - row_max)
    totals = jnp.sum(shifted, axis=-1, keepdims=True)
    log_total = row_max + jnp.log(totals)
    probs_low = (shifted / totals).astype(low_type)
    mixed = jnp.einsum(
        SUM_HQK_KHD_QHD,
        probs_low,
        seq_values.reshape(seq_length, HEADS, HD),
        preferred_element_type=wide_type,
    )
    mixed_low = mixed.reshape(tok_rows, width).astype(low_type)
    hidden = inputs + matmul(mixed_low, out_w)
    normed_two, norm_two_pull = jax.vjp(rms_scale, hidden, ffn_scale)
    normed_two_low = normed_two.astype(low_type)
    logits = matmul(normed_two_low, router_w)

    def router_weights(logit_values):
        return jnp.take_along_axis(jax.nn.softmax(logit_values, axis=-1), routes, axis=1)

    route_weight, route_pull = jax.vjp(router_weights, logits)
    group_routes, group_order = (
        lax.all_gather(routes, EXPERT, axis=0, tiled=True),
        lax.all_gather(pair_order, EXPERT, axis=0, tiled=True),
    )
    per_source = tok_rows * top_count
    group_pairs = per_source * expert_devs
    expert_of = group_routes.reshape(-1)
    pair_index = jnp.arange(group_pairs, dtype=jnp.int32)
    source_of = pair_index // per_source
    expert_ids = jnp.arange(expert_count, dtype=jnp.int32)
    onehot = (expert_of.reshape(expert_devs, per_source, 1) == expert_ids).astype(jnp.int32)
    position_of = (jnp.sum(jnp.cumsum(onehot, axis=1) * onehot, axis=-1) - 1).reshape(-1)
    order_span = group_pairs * shard_devs
    sort_keys = expert_of * order_span + group_order
    sorted_pairs = jnp.argsort(sort_keys)
    placement = jnp.zeros((group_pairs,), jnp.int32).at[sorted_pairs].set(pair_index)
    expert_counts = jnp.sum(onehot, axis=(0, 1))
    expert_start = jnp.cumsum(expert_counts) - expert_counts
    start_of = jnp.sum(onehot.reshape(group_pairs, expert_count) * expert_start[None, :], axis=-1)
    slot_rank = placement - start_of
    retained = slot_rank < capacity
    own_expert = routes.reshape(-1)
    own_position = lax.dynamic_slice_in_dim(position_of, device_expert * per_source, per_source)
    send_slot = own_expert * most_rows + own_position
    send_pair = (
        jnp.zeros((expert_count * most_rows,), jnp.int32)
        .at[send_slot]
        .set(jnp.arange(per_source, dtype=jnp.int32) + 1)
    )
    send_token = jnp.where(send_pair > 0, (send_pair - 1) // top_count + 1, 0)
    owner_local = expert_of % local_experts
    is_mine = expert_of // local_experts == device_expert
    recv_row = source_of * (local_experts * most_rows) + owner_local * most_rows + position_of
    slot_target = jnp.where(
        is_mine & retained, owner_local * capacity + slot_rank, local_experts * capacity
    )
    slot_source = (
        jnp.zeros((local_experts * capacity,), jnp.int32)
        .at[slot_target]
        .set(recv_row + 1, mode="drop")
    )
    back_room = expert_devs * local_experts * most_rows
    back_target = jnp.where(is_mine, recv_row, back_room)
    back_source = (
        jnp.zeros((back_room,), jnp.int32)
        .at[back_target]
        .set(jnp.where(retained, owner_local * capacity + slot_rank + 1, 0), mode="drop")
    )
    send_rows = padded_rows(normed_two_low)[send_token].reshape(
        expert_devs, local_experts * most_rows, width
    )
    recv_rows = lax.all_to_all(
        send_rows, EXPERT, split_axis=0, concat_axis=0, tiled=True
    ).reshape(-1, width)
    slot_rows = padded_rows(recv_rows)[slot_source].reshape(local_experts, capacity, width)
    full_gate, full_up, full_down = (
        lax.all_gather(w_gate, SHARD, axis=1, tiled=True),
        lax.all_gather(w_up, SHARD, axis=1, tiled=True),
        lax.all_gather(w_down, SHARD, axis=2, tiled=True),
    )
    gate_act = jnp.einsum(SUM_ECD_EDF_ECF, slot_rows, full_gate, preferred_element_type=wide_type)
    up_act = jnp.einsum(SUM_ECD_EDF_ECF, slot_rows, full_up, preferred_element_type=wide_type)
    swiglu_out, swiglu_pull = jax.vjp(swiglu_fn, gate_act, up_act)
    swiglu_low = swiglu_out.astype(low_type)
    expert_out = jnp.einsum(
        SUM_ECF_EFD_ECD, swiglu_low, full_down, preferred_element_type=wide_type
    ).astype(low_type)
    back_rows = padded_rows(expert_out.reshape(-1, width))[back_source].reshape(
        expert_devs, local_experts * most_rows, width
    )
    returned = lax.all_to_all(back_rows, EXPERT, split_axis=0, concat_axis=0, tiled=True).reshape(
        -1, width
    )
    pair_rows = returned[send_slot].reshape(tok_rows, top_count, width)
    combined = jnp.einsum(SUM_TK_TKD_TD, route_weight, pair_rows, preferred_element_type=wide_type)
    mixed_out = (hidden + combined).astype(low_type)
    result_grad = out_grad.astype(wide_type)
    weight_grad = jnp.einsum(SUM_TD_TKD_TK, result_grad, pair_rows, preferred_element_type=wide_type)
    pair_grad = (
        (route_weight[:, :, None] * result_grad[:, None, :])
        .astype(low_type)
        .reshape(per_source, width)
    )
    send_grad = padded_rows(pair_grad)[send_pair].reshape(
        expert_devs, local_experts * most_rows, width
    )
    recv_grad = lax.all_to_all(
        send_grad, EXPERT, split_axis=0, concat_axis=0, tiled=True
    ).reshape(-1, width)
    slot_grad = padded_rows(recv_grad)[slot_source].reshape(local_experts, capacity, width)
    act_grad = jnp.einsum(SUM_ECD_EFD_ECF, slot_grad, full_down, preferred_element_type=wide_type)
    down_grad = jnp.einsum(SUM_ECF_ECD_EFD, swiglu_low, slot_grad, preferred_element_type=wide_type)
    gate_grad, up_grad = swiglu_pull(act_grad)
    gate_low = gate_grad.astype(low_type)
    up_low = up_grad.astype(low_type)
    gate_w_grad = jnp.einsum(SUM_ECD_ECF_EDF, slot_rows, gate_low, preferred_element_type=wide_type)
    up_w_grad = jnp.einsum(SUM_ECD_ECF_EDF, slot_rows, up_low, preferred_element_type=wide_type)
    slot_in_grad = jnp.einsum(SUM_ECF_EDF_ECD, gate_low, full_gate, preferred_element_type=wide_type)
    slot_in_grad = (
        slot_in_grad + jnp.einsum(SUM_ECF_EDF_ECD, up_low, full_up, preferred_element_type=wide_type)
    ).astype(low_type)
    gate_shard, up_shard, down_shard = (
        lax.psum_scatter(
            gate_w_grad.astype(jnp.bfloat16), SHARD, scatter_dimension=1, tiled=True
        ).astype(jnp.float32),
        lax.psum_scatter(
            up_w_grad.astype(jnp.bfloat16), SHARD, scatter_dimension=1, tiled=True
        ).astype(jnp.float32),
        lax.psum_scatter(
            down_grad.astype(jnp.bfloat16), SHARD, scatter_dimension=2, tiled=True
        ).astype(jnp.float32),
    )
    back_grad = padded_rows(slot_in_grad.reshape(-1, width))[back_source].reshape(
        expert_devs, local_experts * most_rows, width
    )
    returned_grad = lax.all_to_all(
        back_grad, EXPERT, split_axis=0, concat_axis=0, tiled=True
    ).reshape(-1, width)
    expert_in_grad = jnp.sum(
        returned_grad[send_slot].reshape(tok_rows, top_count, width).astype(wide_type), axis=1
    )
    logit_grad = route_pull(weight_grad)[0]
    logit_low = logit_grad.astype(low_type)
    router_grad = matmul_tn(normed_two_low, logit_low)
    normed_two_grad = expert_in_grad + matmul_nt(logit_low, router_w)
    hidden_norm_grad, ffn_scale_grad = norm_two_pull(normed_two_grad)
    hidden_grad = result_grad + hidden_norm_grad
    attn_low = hidden_grad.astype(low_type)
    out_w_grad = matmul_tn(mixed_low, attn_low)
    mixed_grad = matmul_nt(attn_low, out_w).astype(low_type).reshape(tok_rows, HEADS, HD)
    back_keys, back_values = (seq_keys, seq_values)
    key_heads = back_keys.reshape(seq_length, HEADS, HD)
    value_heads = back_values.reshape(seq_length, HEADS, HD)
    scores_again = masked_scores(query_low, key_heads, query_segment, segment_ids)
    probs_again = jnp.exp(scores_again - log_total)
    probs_again_low = probs_again.astype(low_type)
    prob_grad = jnp.einsum(
        SUM_QHD_KHD_HQK, mixed_grad, value_heads, preferred_element_type=wide_type
    )
    value_part = jnp.einsum(
        SUM_HQK_QHD_KHD, probs_again_low, mixed_grad, preferred_element_type=wide_type
    )
    row_inner = jnp.sum(probs_again * prob_grad, axis=-1, keepdims=True)
    score_low = (probs_again * (prob_grad - row_inner)).astype(low_type)
    query_rot_grad = jnp.einsum(
        SUM_HQK_KHD_QHD, score_low, key_heads, preferred_element_type=wide_type
    )
    key_part = jnp.einsum(SUM_HQK_QHD_KHD, score_low, query_low, preferred_element_type=wide_type)
    key_rot_grad, value_grad = (
        lax.psum_scatter(
            key_part.reshape(seq_length, width).astype(jnp.bfloat16),
            SHARD,
            scatter_dimension=0,
            tiled=True,
        ).astype(jnp.float32),
        lax.psum_scatter(
            value_part.reshape(seq_length, width).astype(jnp.bfloat16),
            SHARD,
            scatter_dimension=0,
            tiled=True,
        ).astype(jnp.float32),
    )
    query_raw_grad, key_raw_grad, query_scale_grad, key_scale_grad = prepare_pull(
        (query_rot_grad, key_rot_grad.reshape(tok_rows, HEADS, HD))
    )
    query_grad_low = query_raw_grad.astype(low_type)
    key_grad_low = key_raw_grad.astype(low_type)
    value_grad_low = value_grad.astype(low_type)
    query_w_grad = matmul_tn(normed_low, query_grad_low)
    key_w_grad = matmul_tn(normed_low, key_grad_low)
    value_w_grad = matmul_tn(normed_low, value_grad_low)
    normed_grad = (
        matmul_nt(query_grad_low, query_w)
        + matmul_nt(key_grad_low, key_w)
        + matmul_nt(value_grad_low, value_w)
    )
    input_norm_grad, attn_scale_grad = norm_one_pull(normed_grad)
    input_grad = (hidden_grad + input_norm_grad).astype(low_type)
    summed = (
        lax.psum_scatter(attn_scale_grad, BOTH, scatter_dimension=0, tiled=True),
        lax.psum_scatter(query_w_grad, BOTH, scatter_dimension=0, tiled=True),
        lax.psum_scatter(key_w_grad, BOTH, scatter_dimension=0, tiled=True),
        lax.psum_scatter(value_w_grad, BOTH, scatter_dimension=0, tiled=True),
        lax.psum_scatter(query_scale_grad, BOTH, scatter_dimension=0, tiled=True),
        lax.psum_scatter(key_scale_grad, BOTH, scatter_dimension=0, tiled=True),
        lax.psum_scatter(out_w_grad, BOTH, scatter_dimension=0, tiled=True),
        lax.psum_scatter(ffn_scale_grad, BOTH, scatter_dimension=0, tiled=True),
        lax.psum_scatter(router_grad, BOTH, scatter_dimension=0, tiled=True),
    )
    return (
        mixed_out,
        input_grad,
        summed[0],
        summed[1],
        summed[2],
        summed[3],
        summed[4],
        summed[5],
        summed[6],
        summed[7],
        summed[8],
        gate_shard,
        up_shard,
        down_shard,
    )


MIB = 1 << 20


def nt_dot(left, right):
    return lax.dot_general(
        left, right, (((1,), (1,)), ((), ())), preferred_element_type=jnp.float32
    )


def tn_dot(left, right):
    return lax.dot_general(
        left, right, (((0,), (0,)), ((), ())), preferred_element_type=jnp.float32
    )


def vmem_params(mib):
    return pltpu.CompilerParams(vmem_limit_bytes=mib * MIB)


def turn_tables(length):
    exponent = np.arange(HD // 2, dtype=np.float32) * np.float32(2.0 / HD)
    frequency = np.power(np.float32(THETA), -exponent).astype(np.float32)
    angles = np.arange(length, dtype=np.float32)[:, None] * frequency[None, :]
    cosine, sine = np.cos(angles), np.sin(angles)
    return (
        jnp.asarray(np.concatenate([cosine, cosine], axis=1), jnp.float32),
        jnp.asarray(np.concatenate([-sine, sine], axis=1), jnp.float32),
    )


def norm_factor(values):
    return lax.rsqrt(jnp.mean(values * values, axis=-1, keepdims=True) + EPSILON)


def same_document(seg_row):
    row = seg_row[...].astype(jnp.float32)
    column = jnp.broadcast_to(row, (128, row.shape[1])).T[:, :1]
    return column == row


def attend(
    tokens, gain, weight, query_gain, key_gain, cosine, sine, allowed,
    normed_out, raw_out, low_out, mixed_out, total_out, qkv,
):
    part = mixed_out.shape[1]
    values = tokens[...].astype(jnp.float32)
    normed = (values * norm_factor(values) * gain[...]).astype(jnp.bfloat16)
    normed_out[...] = normed
    qkv[...] = jnp.dot(normed, weight[...], preferred_element_type=jnp.float32)
    raw_out[...] = qkv[:, : 2 * part]
    low_out[:, 2 * part :] = qkv[:, 2 * part :].astype(jnp.bfloat16)
    for head in range(part // HD):
        span = pl.ds(head * HD, HD)
        for offset, scale_gain, scale in ((0, query_gain, HD ** (-0.5)), (part, key_gain, 1.0)):
            raw = qkv[:, pl.ds(offset + head * HD, HD)]
            unit = raw * norm_factor(raw) * scale_gain[...]
            turned = unit * cosine[...] + pltpu.roll(unit, HD // 2, 1) * sine[...]
            low_out[:, pl.ds(offset + head * HD, HD)] = (turned * scale).astype(jnp.bfloat16)
        query, key = low_out[:, span], low_out[:, pl.ds(part + head * HD, HD)]
        scores = jnp.where(allowed, nt_dot(query, key), -1e30)
        top = jnp.max(scores, axis=-1, keepdims=True)
        shifted = jnp.exp(scores - top)
        total = jnp.sum(shifted, axis=-1, keepdims=True)
        probs = (shifted / total).astype(jnp.bfloat16)
        mixed = jnp.dot(
            probs, low_out[:, pl.ds(2 * part + head * HD, HD)], preferred_element_type=jnp.float32
        )
        mixed_out[:, span] = mixed.astype(jnp.bfloat16)
        total_out[:, head : head + 1] = top + jnp.log(total)


def unpack_kernel(gate0, gate1, up0, up1, down0, down1, gate_out, up_out, down_out):
    for index, group in enumerate(((gate0, up0, down0), (gate1, up1, down1))):

        @pl.when(pl.program_id(0) == index)
        def _(group=group):
            for source, result in zip(group, (gate_out, up_out, down_out), strict=True):
                result[...] = source[...].astype(result.dtype)


def unpack_units(wides, downs):
    shards, part, lanes = wides[0].shape
    each = lanes // 2

    def held(index, e, s):
        return jnp.where(e == index, s, (shards - 1) * (1 - index))

    def wide_spec(index, which):
        return pl.BlockSpec((1, part, each), lambda e, s: (held(index, e, s), 0, which))

    def down_spec(index):
        return pl.BlockSpec((1, each, part), lambda e, s: (held(index, e, s), 0, 0))

    wide_out = pl.BlockSpec((1, part, each), lambda e, s: (e, 0, s))
    shape = jax.ShapeDtypeStruct((2, part, shards * each), jnp.float32)
    return pl.pallas_call(
        unpack_kernel,
        grid=(2, shards),
        in_specs=[wide_spec(index, which) for which in range(2) for index in range(2)]
        + [down_spec(index) for index in range(2)],
        out_specs=[wide_out, wide_out, pl.BlockSpec((1, each, part), lambda e, s: (e, s, 0))],
        out_shape=[shape, shape, jax.ShapeDtypeStruct((2, shards * each, part), jnp.float32)],
        compiler_params=vmem_params(24),
    )(wides[0], wides[1], wides[0], wides[1], *downs)


def mark_kept(small_all, first, experts, own, capacity, bits, shards, keep_out):
    devices, _, rows = small_all.shape
    row = lax.broadcasted_iota(jnp.int32, (devices, rows), 0)
    group = lax.rem(row, shards)
    for index in range(own):
        order = jnp.zeros((devices, rows), jnp.float32)
        for expert in range(experts):
            high = small_all[:, expert, :].astype(jnp.float32)
            low = small_all[:, experts + expert, :].astype(jnp.float32)
            order = order + jnp.where(first + index == expert, high * 256.0 + low, 0.0)
        there = order > 0.0
        bound = jnp.zeros_like(order)
        for bit in reversed(range(bits)):
            trial = bound + float(1 << bit)
            within = jnp.where(there & (order <= trial), 1.0, 0.0)
            for shard in range(shards):
                here = group == shard
                count = jnp.sum(jnp.where(here, within, 0.0), keepdims=True)
                bound = jnp.where(here & (count <= float(capacity)), trial, bound)
        kept = jnp.where(there & (order <= bound), 1.0, 0.0).T
        for block in range(devices):
            place = keep_out.at[block // shards, pl.ds(block % shards * rows, rows)]
            place[:, index : index + 1] = kept[:, block : block + 1]


CORE, XBIT, YBIT = 1, 2, 4


MESH = pl.DeviceIdType.MESH


def held_in_hbm(*values):
    return [pltpu.with_memory_space_constraint(value, pltpu.HBM) for value in values]


class Wires:
    def __init__(self, send, recv):
        self.send, self.recv, self.used = send, recv, 0
        self.device, self.shard = lax.axis_index(EXPERT), lax.axis_index(SHARD)

    def slot(self):
        self.used += 1
        return self.used - 1

    def peer(self, bits=0, step=0, shards=1):
        shard = lax.rem(self.shard + step, shards) if step else self.shard
        return (self.device ^ bits, shard)

    def copy(self, source, target, slot, peer):
        return pltpu.make_async_remote_copy(
            src_ref=source,
            dst_ref=target,
            send_sem=self.send.at[slot],
            recv_sem=self.recv.at[slot],
            device_id=peer,
            device_id_type=MESH,
        )


def greet(peers):
    barrier = pltpu.get_barrier_semaphore()
    for peer in peers:
        pl.semaphore_signal(barrier, inc=1, device_id=peer, device_id_type=MESH)
    pl.semaphore_wait(barrier, len(peers))


class Relay:
    def __init__(self, wires, shards, views):
        self.wires, self.shards, self.views = wires, shards, views
        self.slots = [[[wires.slot() for _ in views] for _ in range(shards - 1)] for _ in range(2)]

    def copies(self, way, step, block):
        wires = self.wires
        peer = (wires.device, wires.shard + (1 if way == 0 else -1))
        return [
            wires.copy(view(block), view(block), slot, peer)
            for view, slot in zip(self.views, self.slots[way][step], strict=True)
        ]

    def has(self, way, step):
        shard = self.wires.shard
        return shard - step >= 0 if way == 0 else shard + step < self.shards

    def sends(self, way, step):
        shard = self.wires.shard
        edge = shard < self.shards - 1 if way == 0 else shard > 0
        return jnp.logical_and(edge, self.has(way, step))

    def block(self, way, step):
        return self.wires.shard + (-step if way == 0 else step)

    def run(self, step, first=None):
        wires = self.wires
        for index, view in enumerate(self.views):
            for way in range(2):
                block = self.block(way, step)
                peer = (wires.device, wires.shard + (1 if way == 0 else -1))
                if step > 0:

                    @pl.when(self.has(way, step))
                    def _(way=way, block=block, index=index, view=view, peer=peer):
                        slot = self.slots[way][step - 1][index]
                        wires.copy(view(block), view(block), slot, peer).wait_recv()

                if step < self.shards - 1:

                    @pl.when(self.sends(way, step))
                    def _(way=way, block=block, index=index, view=view, peer=peer):
                        source = view(block) if first is None else first[index]
                        slot = self.slots[way][step][index]
                        wires.copy(source, view(block), slot, peer).start()

    def drain(self):
        for way in range(2):
            for step in range(self.shards - 1):

                @pl.when(self.sends(way, step))
                def _(way=way, step=step):
                    for copy in self.copies(way, step, self.block(way, step)):
                        copy.wait_send()


class Plane:
    def __init__(self, wires, views, whole):
        self.wires, self.views, self.whole = wires, views, whole
        count = len(views)
        self.first = [[wires.slot() for _ in range(count)] for _ in range(2)]
        self.second = [[[wires.slot() for _ in range(count)] for _ in range(2)] for _ in range(2)]
        self.last = [[wires.slot() for _ in range(count)] for _ in range(4)]
        self.sent = []

    def start(self, copies):
        for copy in copies:
            copy.start()
        self.sent += copies

    def one(self, owner, half, bits, slots):
        wires = self.wires
        return [
            wires.copy(view(owner, half), view(owner, half), slot, wires.peer(bits))
            for view, slot in zip(self.views, slots, strict=True)
        ]

    def step_one(self):
        me = self.wires.device
        for half, bits in enumerate((XBIT, YBIT)):
            self.start(self.one(me, half, bits, self.first[half]))

    def step_two(self):
        me = self.wires.device
        for half, bits in enumerate((XBIT, YBIT)):
            for copy in self.one(me ^ bits, half, bits, self.first[half]):
                copy.wait_recv()
        for half, bits in enumerate((XBIT, YBIT)):
            other = (XBIT | YBIT) ^ bits
            self.start(self.one(me, half, other, self.second[half][0]))
            self.start(self.one(me ^ bits, half, other, self.second[half][1]))

    def cores(self, index):
        wires = self.wires
        owner = wires.device ^ (0, XBIT, YBIT, XBIT | YBIT)[index]
        return [
            wires.copy(place(owner), place(owner), slot, wires.peer(CORE))
            for place, slot in zip(self.whole, self.last[index], strict=True)
        ]

    def step_three(self):
        me = self.wires.device
        for half, bits in enumerate((XBIT, YBIT)):
            other = (XBIT | YBIT) ^ bits
            for owner, slots in ((me ^ other, 0), (me ^ other ^ bits, 1)):
                for copy in self.one(owner, half, other, self.second[half][slots]):
                    copy.wait_recv()
        for index in range(1, 4):
            self.start(self.cores(index))

    def finish(self):
        for index, bits in enumerate((0, XBIT, YBIT, XBIT | YBIT)):
            owner = self.wires.device ^ CORE ^ bits
            for place, slot in zip(self.whole, self.last[index], strict=True):
                self.wires.copy(
                    place(owner), place(owner), slot, self.wires.peer(CORE)
                ).wait_recv()
        for copy in self.sent:
            copy.wait_send()


def opening_kernel(
    shards, planes, experts, own_experts, capacity, bits,
    routes, order, gains, seg_row, cosine, sine,
    router, w_query, w_key, w_value, tokens, w_out, out_grad,
    kept_out, attn_row, ffn_row, query_row, key_row, normed_out, raw_out, low_out, total_out, mixed_all,
    router_all, qkv_w_out, tokens_all, out_w_out, grad_out,
    small, small_all, grad_all, qkv_w, out_w, mixed, qkv, send, recv, local, store,
):
    wires = Wires(send, recv)
    device, shard = wires.device, wires.shard
    weights = (w_query, w_key, w_value)
    block, width = w_query.shape
    rows = tokens.shape[0]
    part = width // shards
    mine = device * shards + shard
    greet(
        [wires.peer(step=step, shards=shards) for step in range(1, shards)]
        + [wires.peer(XBIT), wires.peer(YBIT), wires.peer(CORE)]
    )

    def place(source_shard, which):
        start = pl.multiple_of((device * shards + source_shard) * block, block)
        return qkv_w.at[pl.ds(start, block), pl.ds(which * part, part)]

    def cut(which, target):
        return weights[which].at[:, pl.ds(pl.multiple_of(target * part, part), part)]

    def token_rows(b):
        return tokens_all.at[pl.ds(pl.multiple_of(b * rows, rows), rows)]

    def out_rows(owner, source):
        return out_w.at[pl.ds(pl.multiple_of((owner * shards + source) * block, block), block)]

    def grad_block(owner, source):
        return (owner * shards + source) * rows

    def grad_rows(owner, source):
        return grad_all.at[pl.ds(pl.multiple_of(grad_block(owner, source), rows), rows)]

    def grad_half(source):
        def view(owner, half):
            start = grad_block(owner, source) + half * (rows // 2)
            return grad_all.at[pl.ds(pl.multiple_of(start, rows // 2), rows // 2)]

        return view

    exchange = [[wires.slot() for _ in range(5)] for _ in range(1, shards)]
    sent = []
    for step in range(1, shards):
        peer = wires.peer(step=step, shards=shards)
        slots = exchange[step - 1]
        copies = [
            wires.copy(cut(which, peer[1]), place(shard, which), slots[which], peer)
            for which in range(3)
        ]
        copies.append(wires.copy(router, router_all.at[mine], slots[4], peer))
        for copy in copies:
            copy.start()
        sent += copies
    grad_line = Relay(wires, shards, [lambda b: grad_rows(device, b)])
    token_line = Relay(wires, shards, [token_rows])
    out_line = Relay(wires, shards, [lambda b: out_rows(device, b)])
    mixed_line = Relay(wires, shards, [lambda b: mixed_all.at[b]])
    own = [
        pltpu.make_async_copy(out_grad, grad_rows(device, shard), local.at[0]),
        pltpu.make_async_copy(router, router_all.at[mine], local.at[1]),
        pltpu.make_async_copy(tokens, token_rows(shard), local.at[2]),
        pltpu.make_async_copy(w_out, out_rows(device, shard), local.at[3]),
    ]
    own += [
        pltpu.make_async_copy(cut(which, shard), place(shard, which), local.at[4 + which])
        for which in range(3)
    ]
    for copy in own:
        copy.start()
    turns = [shard] + [
        sum(jnp.where(shard == index, source, 0) for index, source in enumerate(row))
        for row in ((1, 0, 1, 2), (2, 2, 3, 1), (3, 3, 0, 0))
    ]
    stages = [
        Plane(wires, [grad_half(source)], [lambda owner, source=source: grad_rows(owner, source)])
        for source in turns
    ]
    stored = []

    def begin(stage):
        stage.step_one()
        stage.start(stage.cores(0))

    def keep(turn):
        stages[turn].finish()
        for owner in range(planes):
            start = pl.multiple_of(grad_block(owner, turns[turn]), rows)
            copy = pltpu.make_async_copy(
                grad_rows(owner, turns[turn]),
                grad_out.at[pl.ds(start, rows)],
                store.at[turn * planes + owner],
            )
            copy.start()
            stored.append(copy)

    own[0].wait()
    begin(stages[0])
    expert = lax.broadcasted_iota(jnp.int32, (experts, rows), 0)
    dense = jnp.zeros((experts, rows), jnp.int32)
    for choice in range(routes.shape[0]):
        named = routes[choice : choice + 1, :] == expert
        dense = dense + jnp.where(named, order[choice : choice + 1, :] + 1, 0)
    high = lax.shift_right_logical(dense, 8)
    for start, digits in ((0, high), (experts, dense - high * 256)):
        small[pl.ds(start, experts), :] = digits.astype(jnp.float32).astype(small.dtype)
    small[pl.ds(2 * experts, gains.shape[0]), :] = gains[...]
    small_all[mine] = small[...]
    for step in range(1, shards):
        peer = wires.peer(step=step, shards=shards)
        copy = wires.copy(small, small_all.at[mine], exchange[step - 1][3], peer)
        copy.start()
        sent.append(copy)
    out_line.run(0, (w_out,))
    token_line.run(0, (tokens,))
    stages[0].step_two()
    for copy in own[1:]:
        copy.wait()
    for step in range(1, shards):
        peer = wires.peer(step=shards - step, shards=shards)
        source = peer[1]
        slots = exchange[step - 1]
        for which in range(3):
            wires.copy(place(source, which), place(source, which), slots[which], peer).wait_recv()
        wires.copy(router, router_all.at[device * shards + source], slots[4], peer).wait_recv()
        wires.copy(small, small_all.at[device * shards + source], slots[3], peer).wait_recv()

    each = shards * block // 2

    def rows_of(owner, half):
        return qkv_w.at[pl.ds(pl.multiple_of((owner * 2 + half) * each, each), each)]

    def small_of(owner, half):
        return small_all.at[pl.ds((owner * 2 + half) * (shards // 2), shards // 2)]

    def router_of(owner, half):
        return router_all.at[pl.ds((owner * 2 + half) * (shards // 2), shards // 2)]

    plane = Plane(
        wires,
        [rows_of, small_of, router_of],
        [
            lambda owner: qkv_w.at[pl.ds(pl.multiple_of(owner * 2 * each, 2 * each), 2 * each)],
            lambda owner: small_all.at[pl.ds(owner * shards, shards)],
            lambda owner: router_all.at[pl.ds(owner * shards, shards)],
        ],
    )
    outs = [
        Plane(
            wires,
            [
                lambda owner, side, index=index: out_w.at[
                    pl.ds(
                        pl.multiple_of(owner * 2 * each + index * each + side * (each // 2), each // 2),
                        each // 2,
                    )
                ]
            ],
            [
                lambda owner, index=index: out_w.at[
                    pl.ds(pl.multiple_of((owner * 2 + index) * each, each), each)
                ]
            ],
        )
        for index in range(2)
    ]
    begin(plane)
    stages[0].step_three()
    out_line.run(1)
    token_line.run(1)
    plane.step_two()
    out_line.run(2)
    token_line.run(2)
    grad_line.run(0, (out_grad,))
    plane.step_three()
    keep(0)
    out_line.run(3)
    for stage in outs:
        begin(stage)
    plane.finish()

    count = width // 128
    start = 2 * experts
    summed = small_all[0, pl.ds(start, gains.shape[0]), :].astype(jnp.float32)
    for other in range(1, planes * shards):
        summed = summed + small_all[other, pl.ds(start, gains.shape[0]), :].astype(jnp.float32)
    attn_row[...] = jnp.concatenate([summed[i : i + 1] for i in range(count)], axis=1)
    ffn_row[...] = jnp.concatenate([summed[count + i : count + i + 1] for i in range(count)], axis=1)
    query_row[...] = summed[2 * count : 2 * count + 1]
    key_row[...] = summed[2 * count + 1 : 2 * count + 2]
    for stage in outs:
        stage.step_two()
    token_line.run(3)
    attend(
        tokens_all, attn_row, qkv_w, query_row, key_row, cosine, sine, same_document(seg_row),
        normed_out, raw_out, low_out, mixed, total_out, qkv,
    )
    mixed_line.run(0, (mixed,))
    mixed_all[shard] = mixed[...]
    save_qkv = pltpu.make_async_copy(qkv_w, qkv_w_out, local.at[7])
    save_qkv.start()
    grad_line.run(1)
    begin(stages[1])
    for stage in outs:
        stage.step_three()
    mixed_line.run(1)
    stages[1].step_two()
    grad_line.run(2)
    begin(stages[2])
    for stage in outs:
        stage.finish()
    save_out = pltpu.make_async_copy(out_w, out_w_out, local.at[8])
    save_out.start()
    mixed_line.run(2)
    stages[1].step_three()
    stages[2].step_two()
    mark_kept(
        small_all, device * own_experts, experts, own_experts, capacity, bits, shards, kept_out
    )
    grad_line.run(3)
    begin(stages[3])
    stages[2].step_three()
    keep(1)
    mixed_line.run(3)
    stages[3].step_two()
    keep(2)
    stages[3].step_three()
    keep(3)
    for copy in sent:
        copy.wait_send()
    for group in (token_line, grad_line, out_line, mixed_line):
        group.drain()
    for copy in stored:
        copy.wait()
    save_qkv.wait()
    save_out.wait()


def opening_call(
    routes, order, gains, seg_row, tables, router, w_query, w_key, w_value, tokens, w_out, out_grad,
    experts, own_experts, capacity, planes, shards,
):
    block, width = w_query.shape
    top_count, rows = routes.shape
    seq, part = shards * rows, width // shards
    hbm = pl.BlockSpec(memory_space=pltpu.HBM)
    vmem = pl.BlockSpec(memory_space=pltpu.VMEM)
    place = pl.BlockSpec(memory_space=pl.ANY)
    slots = 144
    low, full = tokens.dtype, jnp.float32
    small = (2 * experts + gains.shape[0], 128)
    most = planes * shards * rows * top_count
    return pl.pallas_call(
        functools.partial(
            opening_kernel, shards, planes, experts, own_experts, capacity, most.bit_length()
        ),
        in_specs=[vmem] * 6 + [place] * 7,
        out_specs=[vmem] * 10 + [place, hbm, vmem, hbm, hbm],
        out_shape=(
            jax.ShapeDtypeStruct((planes, seq, own_experts), full),
            jax.ShapeDtypeStruct((1, width), full),
            jax.ShapeDtypeStruct((1, width), full),
            jax.ShapeDtypeStruct((1, HD), full),
            jax.ShapeDtypeStruct((1, HD), full),
            jax.ShapeDtypeStruct((seq, width), low),
            jax.ShapeDtypeStruct((seq, 2 * part), full),
            jax.ShapeDtypeStruct((seq, 3 * part), low),
            jax.ShapeDtypeStruct((seq, 128), full),
            jax.ShapeDtypeStruct((shards, seq, part), low),
            jax.ShapeDtypeStruct((planes * shards,) + router.shape, router.dtype),
            pltpu.HBM((width, 3 * part), low),
            jax.ShapeDtypeStruct((seq, width), low),
            pltpu.HBM((width, width), low),
            pltpu.HBM((planes * seq, width), low),
        ),
        scratch_shapes=[
            pltpu.VMEM(small, gains.dtype),
            pltpu.VMEM((planes * shards,) + small, gains.dtype),
            pltpu.VMEM((planes * seq, width), low),
            pltpu.VMEM((width, 3 * part), low),
            pltpu.VMEM((width, width), low),
            pltpu.VMEM((seq, part), low),
            pltpu.VMEM((seq, 3 * part), full),
            pltpu.SemaphoreType.DMA((slots,)),
            pltpu.SemaphoreType.DMA((slots,)),
            pltpu.SemaphoreType.DMA((9,)),
            pltpu.SemaphoreType.DMA((planes * shards,)),
        ],
        compiler_params=pltpu.CompilerParams(
            collective_id=1, has_side_effects=True, vmem_limit_bytes=60 * MIB
        ),
        cost_estimate=pl.CostEstimate(flops=0, bytes_accessed=200 * MIB, transcendentals=0),
    )(
        routes, order, gains, seg_row, *tables, router, w_query, w_key, w_value, tokens, w_out, out_grad
    )


class Units:
    def __init__(self, wires, shards, index, gate, up, down, wide_w, down_w, local, base, piece=(0, 1)):
        self.wires, self.shards, self.index = wires, shards, index
        self.gate, self.up, self.down, self.wide_w, self.down_w = gate, up, down, wide_w, down_w
        self.local, self.base, self.piece = local, base, piece
        count = (0 if wide_w is None else 2) + (0 if down_w is None else 1)
        self.slots = [[wires.slot() for _ in range(count)] for _ in range(1, shards)]

    def pairs(self, source, target):
        each = self.gate.shape[2] // self.shards
        span = pl.ds(pl.multiple_of(target * each, each), each)
        result = []
        if self.wide_w is not None:
            result += [
                (self.gate.at[self.index, :, span], self.wide_w.at[source, :, pl.ds(0, each)]),
                (self.up.at[self.index, :, span], self.wide_w.at[source, :, pl.ds(each, each)]),
            ]
        if self.down_w is not None:
            number, pieces = self.piece
            size = each // pieces
            start = pl.multiple_of(target * each + number * size, size)
            place = self.down_w.at[source, pl.ds(number * size, size), :]
            result.append((self.down.at[self.index, pl.ds(start, size), :], place))
        return result

    def own(self):
        shard = self.wires.shard
        return [
            pltpu.make_async_copy(source, place, self.local.at[self.base + slot])
            for slot, (source, place) in enumerate(self.pairs(shard, shard))
        ]

    def sends(self):
        wires = self.wires
        for step in range(1, self.shards):
            peer = wires.peer(step=step, shards=self.shards)
            pairs = self.pairs(wires.shard, peer[1])
            for slot, (source, place) in zip(self.slots[step - 1], pairs, strict=True):
                yield wires.copy(source, place, slot, peer)

    def begin(self):
        for copy in self.own():
            copy.start()
        for copy in self.sends():
            copy.start()

    def end(self):
        wires = self.wires
        for copy in self.own():
            copy.wait()
        for step in range(1, self.shards):
            back = wires.peer(step=self.shards - step, shards=self.shards)
            pairs = self.pairs(back[1], wires.shard)
            for slot, (_, place) in zip(self.slots[step - 1], pairs, strict=True):
                wires.copy(place, place, slot, back).wait_recv()
        for copy in self.sends():
            copy.wait_send()


def meeting_kernel(
    shards, planes, tokens, gain, mixed_all, out_w, gate, up, down,
    hidden_out, mixed_own, normed_out, wide_w, down_w, down_next, normed_all, send, recv, local, store,
):
    wires = Wires(send, recv)
    device, shard = wires.device, wires.shard
    seq, _ = tokens.shape
    rows, part = hidden_out.shape[0], mixed_all.shape[2]
    half = seq // 2
    greet(
        [wires.peer(step=step, shards=shards) for step in range(1, shards)]
        + [wires.peer(XBIT), wires.peer(YBIT), wires.peer(CORE)]
    )
    units = [
        Units(wires, shards, 0, gate, up, down, wide_w, down_w, local, 0),
        Units(wires, shards, 1, gate, up, down, None, down_next, local, 3, (0, 2)),
    ]
    for group in units:
        group.begin()

    def stage(index):
        def view(owner, start, size):
            return normed_all.at[owner, pl.ds(start, size)]

        return Plane(
            wires,
            [lambda owner, side: view(owner, index * half + side * (half // 2), half // 2)],
            [lambda owner: view(owner, index * half, half)],
        )

    stages = [stage(index) for index in range(2)]
    for side in range(2):
        span = pl.ds(side * half, half)
        total = tokens[span, :].astype(jnp.float32)
        for source in range(shards):
            total = total + jnp.dot(
                mixed_all[source, span, :],
                out_w[pl.ds(source * part, part), :],
                preferred_element_type=jnp.float32,
            )
        normed_all[device, span, :] = (total * norm_factor(total) * gain[...]).astype(
            normed_all.dtype
        )
        stages[side].step_one()
        stages[side].start(stages[side].cores(0))
        for inner in range(half // rows):

            @pl.when(shard == side * (half // rows) + inner)
            def _(total=total, inner=inner):
                hidden_out[...] = total[inner * rows : (inner + 1) * rows, :]

    stored = []

    def keep(owner, side):
        span = pl.ds(side * half, half)
        copy = pltpu.make_async_copy(
            normed_all.at[owner, span], normed_out.at[owner, span], store.at[len(stored)]
        )
        copy.start()
        stored.append(copy)

    for source in range(shards):
        mixed_own[:, pl.ds(source * part, part)] = mixed_all[
            source, pl.ds(pl.multiple_of(shard * rows, rows), rows), :
        ]
    for plane in stages:
        plane.step_two()
    for side, plane in enumerate(stages):
        plane.step_three()
        for chip in range(4):
            keep(device ^ (2 * chip), side)
    for side, plane in enumerate(stages):
        plane.finish()
        for chip in range(4):
            keep(device ^ (2 * chip + 1), side)
    for group in units:
        group.end()
    for copy in stored:
        copy.wait()


def unit_shapes(gate, shards):
    _, part, hidden_units = gate.shape
    each = hidden_units // shards
    return (
        jax.ShapeDtypeStruct((shards, part, 2 * each), gate.dtype),
        jax.ShapeDtypeStruct((shards, each, part), gate.dtype),
    )


def meeting_call(tokens, gain, mixed_all, out_w, gate, up, down, planes, shards):
    hbm = pl.BlockSpec(memory_space=pltpu.HBM)
    vmem = pl.BlockSpec(memory_space=pltpu.VMEM)
    seq, width = tokens.shape
    rows = seq // shards
    slots = 32
    low = tokens.dtype
    return pl.pallas_call(
        functools.partial(meeting_kernel, shards, planes),
        in_specs=[vmem] * 4 + [hbm] * 3,
        out_specs=[vmem] * 2 + [hbm] * 4,
        out_shape=(
            pltpu.HBM((rows, width), jnp.float32),
            pltpu.HBM((rows, width), low),
            pltpu.HBM((planes, seq + 16, width), low),
        )
        + unit_shapes(gate, shards)
        + unit_shapes(gate, shards)[1:],
        scratch_shapes=[
            pltpu.VMEM((planes, seq, width), low),
            pltpu.SemaphoreType.DMA((slots,)),
            pltpu.SemaphoreType.DMA((slots,)),
            pltpu.SemaphoreType.DMA((4,)),
            pltpu.SemaphoreType.DMA((2 * planes,)),
        ],
        compiler_params=pltpu.CompilerParams(
            collective_id=3, has_side_effects=True, vmem_limit_bytes=40 * MIB
        ),
        cost_estimate=pl.CostEstimate(
            flops=2 * seq * width * width, bytes_accessed=300 * MIB, transcendentals=0
        ),
    )(tokens, gain, mixed_all, out_w, *held_in_hbm(gate, up, down))


def add_rows(target, sources, lines):
    rows = target.shape[0]

    def body(index, carry):
        span = pl.ds(pl.multiple_of(index * lines, lines), lines)
        total = target[span, :].astype(jnp.float32)
        for source in sources:
            total = total + source[span, :].astype(jnp.float32)
        target[span, :] = total.astype(target.dtype)
        return carry

    lax.fori_loop(0, rows // lines, body, 0)


class PlaneSum:
    def __init__(self, wires, part, held, came, diag, side, local, base):
        self.wires, self.part, self.local, self.base = wires, part, local, base
        self.held, self.came, self.diag, self.side = held, came, diag, side
        self.half = held.shape[1] // 2
        self.core = [wires.slot() for _ in range(4)]
        self.corner = [wires.slot() for _ in range(2)]
        self.edge = [wires.slot() for _ in range(2)]
        self.sent = []

    def start(self, copy):
        copy.start()
        self.sent.append(copy)

    def load(self, chip):
        return pltpu.make_async_copy(
            self.part(chip, 0), self.held.at[chip], self.local.at[self.base + chip]
        )

    def give(self, chip):
        self.start(
            self.wires.copy(
                self.held.at[chip], self.came.at[chip], self.core[chip], self.wires.peer(CORE)
            )
        )

    def begin(self):
        for chip in (3, 1, 2, 0):
            self.load(chip).start()
            self.start(
                self.wires.copy(
                    self.part(chip, 1), self.came.at[chip], self.core[chip], self.wires.peer(CORE)
                )
            )

    def add_core(self, chip):
        if self.part is not None:
            self.load(chip).wait()
        place = self.came.at[chip]
        self.wires.copy(place, place, self.core[chip], self.wires.peer(CORE)).wait_recv()
        add_rows(self.held.at[chip], [place], 64)

    def part_of_corner(self, which):
        return self.held.at[3, pl.ds(which * self.half, self.half)]

    def send_corner(self):
        self.add_core(3)
        for which, bits in enumerate((XBIT, YBIT)):
            self.start(
                self.wires.copy(
                    self.part_of_corner(which),
                    self.diag.at[which],
                    self.corner[which],
                    self.wires.peer(bits),
                )
            )

    def add_cores(self):
        for chip in (1, 2, 0):
            self.add_core(chip)

    def send_sides(self):
        for which, (bits, chip) in enumerate(((XBIT, 2), (YBIT, 1))):
            place = self.diag.at[which]
            self.wires.copy(place, place, self.corner[which], self.wires.peer(bits)).wait_recv()
            add_rows(self.held.at[chip, pl.ds(which * self.half, self.half)], [place], 64)
            self.start(
                self.wires.copy(
                    self.held.at[chip],
                    self.side.at[1 - which],
                    self.edge[1 - which],
                    self.wires.peer((XBIT | YBIT) ^ bits),
                )
            )

    def end(self):
        for which, bits in enumerate((XBIT, YBIT)):
            place = self.side.at[which]
            self.wires.copy(place, place, self.edge[which], self.wires.peer(bits)).wait_recv()
        add_rows(self.held.at[0], [self.side.at[0], self.side.at[1]], 64)

    def drain(self):
        for copy in self.sent:
            copy.wait_send()


class LineSum:
    def __init__(self, wires, shards, source, landing):
        self.wires, self.shards, self.source, self.landing = wires, shards, source, landing
        self.slots = [wires.slot() for _ in range(shards - 1)]

    def sends(self):
        wires = self.wires
        for step in range(1, self.shards):
            peer = wires.peer(step=step, shards=self.shards)
            yield wires.copy(
                self.source(peer[1]), self.landing(wires.shard), self.slots[step - 1], peer
            )

    def begin(self):
        for copy in self.sends():
            copy.start()

    def arrive(self):
        wires = self.wires
        for step in range(1, self.shards):
            peer = wires.peer(step=self.shards - step, shards=self.shards)
            place = self.landing(peer[1])
            wires.copy(place, place, self.slots[step - 1], peer).wait_recv()

    def drain(self):
        for copy in self.sends():
            copy.wait_send()


class LineFlow:
    def __init__(self, wires, shards, own, flow):
        self.wires, self.shards, self.own, self.flow = wires, shards, own, flow
        self.slots = [[wires.slot() for _ in range(shards)] for _ in range(2)]
        self.order = [
            (way, (shards - 1 - step) if way == 0 else step)
            for step in range(shards - 1)
            for way in range(2)
        ]

    def copy(self, way, block, source):
        wires = self.wires
        peer = (wires.device, wires.shard + (1 if way == 0 else -1))
        return wires.copy(source, self.flow.at[way, block], self.slots[way][block], peer)

    def first(self, way):
        return self.wires.shard == (0 if way == 0 else self.shards - 1)

    def passes(self, way, block):
        shard = self.wires.shard
        inner = jnp.logical_and(shard > 0, shard < block)
        if way == 1:
            inner = jnp.logical_and(shard < self.shards - 1, shard > block)
        return inner

    def begin(self):
        for way, block in self.order:

            @pl.when(self.first(way))
            def _(way=way, block=block):
                self.copy(way, block, self.own(block)).start()

    def forward(self, way, block):
        @pl.when(self.passes(way, block))
        def _():
            place = self.flow.at[way, block]
            self.copy(way, block, place).wait_recv()
            add_rows(place, [self.own(block)], 64)
            self.copy(way, block, place).start()

    def end(self):
        shard = self.wires.shard
        for block in range(self.shards):

            @pl.when(shard == block)
            def _(block=block):
                sources = []
                for way in range(2):
                    if block != (0 if way == 0 else self.shards - 1):
                        place = self.flow.at[way, block]
                        self.copy(way, block, place).wait_recv()
                        sources.append(place)
                add_rows(self.own(block), sources, 64)

    def drain(self):
        for way, block in self.order:
            sends = jnp.logical_or(self.first(way), self.passes(way, block))

            @pl.when(sends)
            def _(way=way, block=block):
                self.copy(way, block, self.own(block)).wait_send()


def line_total(landing, shards):
    total = landing[0].astype(jnp.float32)
    for shard in range(1, shards):
        total = total + landing[shard].astype(jnp.float32)
    return total


def aligned(index, size):
    return pl.ds(pl.multiple_of(index * size, size), size)


def expert_kernel(
    index, experts, shards, x, g, keep, wide_w, router_w, down_w, hot, *refs
):
    if index == 0:
        gate, up, down, _, out, grad, pull, wide_sum, down_sum, next_wide, next_down = refs[:11]
        acc, dacc, wide_out, down_out, send, recv, local, sems = refs[11:]
    else:
        old_out, old_grad, old_pull, wide_sent, down_sent = refs[:5]
        out, grad, wide_sum, down_sum, router_sum, wide_came, down_came = refs[5:12]
        acc, racc, dacc, wide_out, down_out, send, recv, local, sems = refs[12:]
    step, steps = pl.program_id(0), pl.num_programs(0)
    wires = Wires(send, recv)
    if index == 0:
        travel = [Units(wires, shards, 1, gate, up, down, next_wide, next_down, local, 0, (1, 2))]
    else:
        travel = [
            LineSum(wires, shards, lambda t: wide_sent.at[t], lambda s: wide_came.at[s]),
            LineSum(wires, shards, lambda t: down_sent.at[t], lambda s: down_came.at[s]),
        ]
        stay = [
            pltpu.make_async_copy(
                sent.at[wires.shard], came.at[wires.shard], local.at[place]
            )
            for place, (sent, came) in enumerate(((wide_sent, wide_came), (down_sent, down_came)))
        ]

    @pl.when(step == 0)
    def _():
        greet([wires.peer(step=hop, shards=shards) for hop in range(1, shards)])
        for group in travel:
            group.begin()
        acc[...] = jnp.zeros_like(acc)
        dacc[...] = jnp.zeros_like(dacc)
        if index == 1:
            for copy in stay:
                copy.start()
            racc[...] = jnp.zeros_like(racc)

    _, each, part = down_w.shape
    wide = jnp.dot(x[...], wide_w[...], preferred_element_type=jnp.float32)
    back = nt_dot(g[:, :part], down_w[0])
    for shard in range(1, shards):
        back = back + nt_dot(g[:, shard * part : (shard + 1) * part], down_w[shard])
    if index == 0:
        logits = jnp.dot(x[...], router_w[...], preferred_element_type=jnp.float32)
        lane = lax.broadcasted_iota(jnp.int32, logits.shape, 1)
        logits = jnp.where(lane < experts, logits, -1e30)
        shifted = jnp.exp(logits - jnp.max(logits, axis=-1, keepdims=True))
        probs = shifted / jnp.sum(shifted, axis=-1, keepdims=True)
    else:
        lane = lax.broadcasted_iota(jnp.int32, old_pull.shape, 1)
        probs = jnp.where(lane < experts, old_pull[...], 0.0)
    mark = hot[index : index + 1, :]
    kept = keep[:, index : index + 1]
    route = jnp.sum(probs * mark, axis=-1, keepdims=True) * kept
    gated, lifted = wide[:, :each], wide[:, each:]
    sigma = 1.0 / (1.0 + jnp.exp(-gated))
    silu = gated * sigma
    act = silu * lifted
    pulled = jnp.sum(act * back, axis=-1, keepdims=True) * kept
    act_low = (act * route).astype(jnp.bfloat16)
    act_grad = back * route
    wide_low = jnp.concatenate(
        [
            (act_grad * lifted * sigma * (1.0 + gated * (1.0 - sigma))).astype(jnp.bfloat16),
            (act_grad * silu).astype(jnp.bfloat16),
        ],
        axis=1,
    )
    result = nt_dot(wide_low, wide_w[...])
    if index == 0:
        pull[...] = jnp.where(lane < experts, probs, jnp.where(lane == 127, pulled, 0.0))
    else:
        dense = pulled * mark + old_pull[:, 127:] * hot[0:1, :]
        logit_grad = probs * (dense - jnp.sum(probs * dense, axis=-1, keepdims=True))
        logit_low = logit_grad.astype(jnp.bfloat16)
        result = result + nt_dot(logit_low, router_w[...]) + old_grad[...].astype(jnp.float32)
        racc[...] += tn_dot(x[...], logit_low)
    grad[...] = result.astype(jnp.bfloat16)
    for shard in range(shards):
        span = slice(shard * part, (shard + 1) * part)
        value = jnp.dot(act_low, down_w[shard], preferred_element_type=jnp.float32)
        if index == 1:
            value = value + old_out[:, span].astype(jnp.float32)
        out[:, span] = value.astype(jnp.bfloat16)
        dacc[shard] += tn_dot(act_low, g[:, span])
    acc[...] += tn_dot(x[...], wide_low)

    @pl.when(step == steps - 1)
    def _():
        wide_out[...] = acc[...].astype(jnp.bfloat16)
        wide_copy = pltpu.make_async_copy(wide_out, wide_sum, sems.at[0])
        wide_copy.start()
        down_out[...] = dacc[...].astype(jnp.bfloat16)
        down_copy = pltpu.make_async_copy(down_out, down_sum, sems.at[1])
        down_copy.start()
        if index == 1:
            router_copy = pltpu.make_async_copy(racc, router_sum, sems.at[2])
            router_copy.start()
            router_copy.wait()
        wide_copy.wait()
        down_copy.wait()
        if index == 0:
            travel[0].end()
        else:
            for copy in stay:
                copy.wait()
            for group in travel:
                group.arrive()
                group.drain()


def expert_call(index, x_all, g_all, keep, wide_w, router_w, down_w, hot, experts, weights, before):
    planes, _, width = x_all.shape
    rows = keep.shape[1]
    shards = down_w.shape[0]
    tile = 512 if index == 0 else 256
    per = rows // tile
    hbm = pl.BlockSpec(memory_space=pltpu.HBM)

    def whole(value):
        zeros = (0,) * value.ndim
        return pl.BlockSpec(value.shape, lambda i: zeros, pipeline_mode=pl.Buffered(1))

    def rowwise(lanes):
        return pl.BlockSpec((None, tile, lanes), lambda i: (i // per, i % per, 0))

    low = jnp.bfloat16
    tall = pltpu.HBM((planes, rows, width), low)
    narrow = pltpu.HBM((planes, rows, 128), jnp.float32)
    wide_shape = pltpu.HBM(wide_w.shape, low)
    down_shape = pltpu.HBM(down_w.shape, low)
    came = pltpu.HBM((shards, width // shards, wide_w.shape[1]), low)
    if index == 0:
        others = [hbm] * 4
        out_specs = [rowwise(width)] * 2 + [rowwise(128)] + [hbm] * 4
        spare = [pltpu.HBM((planes, rows + extra, width), low) for extra in (32, 48)]
        shapes = (*spare, narrow, wide_shape, down_shape, came, down_shape)
        operands = held_in_hbm(*weights)
    else:
        others = [rowwise(width)] * 2 + [rowwise(128)] + [hbm] * 2
        out_specs = [rowwise(width)] * 2 + [hbm] * 5
        router_shape = pltpu.HBM(router_w.shape, jnp.float32)
        shapes = (tall, tall, wide_shape, down_shape, router_shape, came, down_shape)
        operands = held_in_hbm(*before)
    return pl.pallas_call(
        functools.partial(expert_kernel, index, experts, shards),
        grid=(planes * per,),
        in_specs=[
            rowwise(width),
            rowwise(width),
            rowwise(keep.shape[2]),
            whole(wide_w),
            whole(router_w),
            whole(down_w),
            whole(hot),
        ]
        + others,
        out_specs=out_specs,
        scratch_shapes=[pltpu.VMEM(wide_w.shape, jnp.float32)]
        + ([] if index == 0 else [pltpu.VMEM(router_w.shape, jnp.float32)])
        + [
            pltpu.VMEM(down_w.shape, jnp.float32),
            pltpu.VMEM(wide_w.shape, low),
            pltpu.VMEM(down_w.shape, low),
            pltpu.SemaphoreType.DMA((12,)),
            pltpu.SemaphoreType.DMA((12,)),
            pltpu.SemaphoreType.DMA((3,)),
            pltpu.SemaphoreType.DMA((3,)),
        ],
        out_shape=shapes,
        input_output_aliases={10: 6} if index == 0 else {},
        compiler_params=pltpu.CompilerParams(
            collective_id=7 + index, has_side_effects=True, vmem_limit_bytes=52 * MIB
        ),
        cost_estimate=pl.CostEstimate(
            flops=planes * rows * width * 12 * down_w.shape[1],
            bytes_accessed=100 * MIB,
            transcendentals=planes * rows * down_w.shape[1],
        ),
    )(*held_in_hbm(x_all, g_all), keep, wide_w, router_w, down_w, hot, *operands)


def returning_kernel(
    shards, ins, outs, wide, down, in_total, out_total, wide_all, down_all,
    held, came, diag, side, held2, came2, diag2, side2, landing, send, recv, local,
):
    wires = Wires(send, recv)
    device, shard = wires.device, wires.shard
    rows = in_total.shape[0]
    greet(
        [wires.peer(step=step, shards=shards) for step in range(1, shards)]
        + [wires.peer(XBIT), wires.peer(YBIT), wires.peer(CORE)]
    )

    def rel(source):
        return lambda chip, core: source.at[device ^ (2 * chip + core)]

    grads = PlaneSum(wires, rel(ins), held, came, diag, side, local, 0)
    values = PlaneSum(wires, rel(outs), held2, came2, diag2, side2, local, 6)
    weights = [
        LineSum(wires, shards, lambda t: wide.at[t], lambda s: wide_all.at[s]),
        LineSum(wires, shards, lambda t: down.at[t], lambda s: down_all.at[s]),
    ]
    line = LineSum(
        wires, shards, lambda t: held.at[0, aligned(t, rows)], lambda s: landing.at[s]
    )
    grads.begin()
    for group in weights:
        group.begin()
    own = [
        pltpu.make_async_copy(wide.at[shard], wide_all.at[shard], local.at[4]),
        pltpu.make_async_copy(down.at[shard], down_all.at[shard], local.at[5]),
    ]
    for copy in own:
        copy.start()
    grads.send_corner()
    values.begin()
    grads.add_cores()
    grads.send_sides()
    values.send_corner()
    values.add_cores()
    grads.end()
    line.begin()
    values.send_sides()
    landing[shard] = held[0, aligned(shard, rows), :]
    line.arrive()
    in_total[...] = line_total(landing, shards)
    values.end()
    back = pltpu.make_async_copy(held2.at[0], out_total, local.at[10])
    back.start()
    for copy in own:
        copy.wait()
    back.wait()
    for group in weights:
        group.arrive()
    for group in (grads, values, line, *weights):
        group.drain()


def sum_work(rows, lanes):
    low = jnp.bfloat16
    return [
        pltpu.VMEM((4, rows, lanes), low),
        pltpu.VMEM((4, rows, lanes), low),
        pltpu.VMEM((2, rows // 2, lanes), low),
        pltpu.VMEM((2, rows, lanes), low),
    ]


def returning_call(ins, outs, wide, down):
    _, seq, width = ins.shape
    shards = wide.shape[0]
    rows = seq // shards
    hbm = pl.BlockSpec(memory_space=pltpu.HBM)
    vmem = pl.BlockSpec(memory_space=pltpu.VMEM)
    return pl.pallas_call(
        functools.partial(returning_kernel, shards),
        in_specs=[hbm] * 4,
        out_specs=[vmem, hbm, hbm, hbm],
        out_shape=(
            jax.ShapeDtypeStruct((rows, width), jnp.float32),
            jax.ShapeDtypeStruct((seq, width), jnp.bfloat16),
            pltpu.HBM(wide.shape, wide.dtype),
            pltpu.HBM(down.shape, down.dtype),
        ),
        scratch_shapes=sum_work(seq, width)
        + sum_work(seq, width)
        + [
            pltpu.VMEM((shards, rows, width), jnp.bfloat16),
            pltpu.SemaphoreType.DMA((36,)),
            pltpu.SemaphoreType.DMA((36,)),
            pltpu.SemaphoreType.DMA((11,)),
        ],
        compiler_params=pltpu.CompilerParams(
            collective_id=4, has_side_effects=True, vmem_limit_bytes=56 * MIB
        ),
        cost_estimate=pl.CostEstimate(flops=0, bytes_accessed=300 * MIB, transcendentals=0),
    )(*held_in_hbm(ins, outs, wide, down))


def back_through_heads(
    mixed_grad, raw, low, total, query_gain, key_gain, cosine, sine, allowed, qkv_grad
):
    part = raw.shape[1] // 2
    gain_sums = [None, None]
    for head in range(part // HD):
        span = pl.ds(head * HD, HD)
        query, key = low[:, span], low[:, pl.ds(part + head * HD, HD)]
        value = low[:, pl.ds(2 * part + head * HD, HD)]
        out_grad = mixed_grad[:, span]
        scores = jnp.where(allowed, nt_dot(query, key), -1e30)
        probs = jnp.exp(scores - total[:, head : head + 1])
        prob_grad = nt_dot(out_grad, value)
        value_grad = tn_dot(probs.astype(jnp.bfloat16), out_grad)
        qkv_grad[:, pl.ds(2 * part + head * HD, HD)] = value_grad.astype(jnp.bfloat16)
        inner = jnp.sum(probs * prob_grad, axis=-1, keepdims=True)
        score_grad = (probs * (prob_grad - inner)).astype(jnp.bfloat16)
        rotated = (
            jnp.dot(score_grad, key, preferred_element_type=jnp.float32) * HD ** (-0.5),
            tn_dot(score_grad, query),
        )
        for which, (offset, scale_gain) in enumerate(((0, query_gain), (part, key_gain))):
            grad = rotated[which]
            grad = grad * cosine[...] - pltpu.roll(grad, HD // 2, 1) * sine[...]
            source = raw[:, pl.ds(offset + head * HD, HD)]
            factor = norm_factor(source)
            gain_sum = jnp.sum(grad * source * factor, axis=0, keepdims=True)
            gain_sums[which] = gain_sum if head == 0 else gain_sums[which] + gain_sum
            scaled = grad * scale_gain[...]
            inner = jnp.mean(scaled * source, axis=-1, keepdims=True)
            result = factor * scaled - source * (factor * factor * factor) * inner
            qkv_grad[:, pl.ds(offset + head * HD, HD)] = result.astype(jnp.bfloat16)
    return gain_sums


def closing_kernel(
    shards, planes,
    hidden, grad, out_grad, ffn_gain, raw, low, total, query_gain, key_gain, cosine, sine, seg_row,
    tokens, gain, own_mixed, normed, router, out_w, qkv_w, out_total,
    input_grad, mixed_out, query_out, key_out, value_out, weight_out, gain_out, router_out, vectors_out,
    held, came, diag, side, held2, came2, diag2, side2,
    weights, hidden_grad, attn_low, message, message_land, qkv_grad, normed_grad, vectors,
    out_own, norm_land, out_land, qkv_land, weight_land, gain_mine, gain_land, gain_line, router_land, router_sum, router_line,
    vector_land, vector_sum, vector_line, send, recv, local,
):
    wires = Wires(send, recv)
    device, shard = wires.device, wires.shard
    rows, width = tokens.shape
    block = query_out.shape[0]
    part = width // shards
    lines = router_out.shape[0]
    lanes = qkv_w.shape[1]
    line_peers = [wires.peer(step=step, shards=shards) for step in range(1, shards)]
    plane_peers = [wires.peer(bits) for bits in range(1, planes)]
    load_out = pltpu.make_async_copy(out_w, weights, local.at[0])
    load_out.start()
    load_value = pltpu.make_async_copy(out_total, out_own, local.at[2])
    load_value.start()
    greet(line_peers + plane_peers)

    back = LineSum(
        wires, shards, lambda t: message.at[t], lambda s: message_land.at[aligned(s, rows)]
    )
    norms = LineFlow(wires, shards, lambda b: normed_grad.at[aligned(b, rows)], norm_land)
    values = LineFlow(wires, shards, lambda b: out_own.at[aligned(b, rows)], out_land)
    qkv = PlaneSum(wires, None, held, came, diag, side, local, 0)
    weight = PlaneSum(wires, None, held2, came2, diag2, side2, local, 0)
    qkv_line = LineSum(
        wires, shards, lambda t: held.at[0, aligned(t, block)], lambda s: qkv_land.at[s]
    )
    weight_line = LineSum(
        wires, shards, lambda t: held2.at[0, aligned(t, block)], lambda s: weight_land.at[s]
    )
    sent = []

    def spread(slots, source, landing):
        for bits in range(1, planes):
            copy = wires.copy(
                source(device ^ bits), landing.at[device], slots[bits - 1], wires.peer(bits)
            )
            copy.start()
            sent.append(copy)

    def collect(slots, landing):
        for bits in range(1, planes):
            place = landing.at[device ^ bits]
            wires.copy(place, place, slots[bits - 1], wires.peer(bits)).wait_recv()
        total = landing[0]
        for other in range(1, planes):
            total = total + landing[other]
        return total

    router_slots = [wires.slot() for _ in range(1, planes)]
    vector_slots = [wires.slot() for _ in range(1, planes)]
    gain_slots = [wires.slot() for _ in range(1, planes)]
    spread(router_slots, lambda e: router.at[aligned(e, shards * lines)], router_land)
    router_land[device] = router[aligned(device, shards * lines), :]

    factor = norm_factor(hidden[...])
    vectors[:, :width] = jnp.sum(grad[...] * hidden[...] * factor, axis=0, keepdims=True)
    scaled = grad[...] * ffn_gain[...]
    inner = jnp.mean(scaled * hidden[...], axis=-1, keepdims=True)
    change = out_grad[...].astype(jnp.float32) + factor * scaled
    change = change - hidden[...] * (factor * factor * factor) * inner
    hidden_grad[...] = change
    attn_low[...] = change.astype(jnp.bfloat16)
    load_out.wait()
    for target in range(shards):
        message[target] = nt_dot(attn_low[...], weights[pl.ds(target * part, part), :]).astype(
            jnp.bfloat16
        )
    back.begin()
    load_value.wait()
    values.begin()
    load_qkv = pltpu.make_async_copy(qkv_w, weights.at[:, pl.ds(0, lanes)], local.at[1])
    load_qkv.start()
    message_land[aligned(shard, rows), :] = message[shard]

    def addends(group, left, right):
        for core in (1, 0):
            for chip in (3, 1, 2, 0):
                owner = device ^ (2 * chip + core)
                columns = pl.ds(pl.multiple_of(owner * shards * block, shards * block), shards * block)
                if core == 0:
                    group.sent[(3, 1, 2, 0).index(chip)].wait_send()
                group.held[chip] = tn_dot(left[:, columns], right[...]).astype(jnp.bfloat16)
                if core == 1:
                    group.give(chip)
        group.sent = []

    addends(weight, own_mixed, attn_low)
    weight.send_corner()
    weight.add_cores()
    far = shards - 1
    router_sum[...] = collect(router_slots, router_land)
    router_pass = LineSum(
        wires, shards, lambda t: router_sum.at[aligned(t, lines)], lambda s: router_line.at[s]
    )

    back.arrive()
    allowed = same_document(seg_row)
    query_sum, key_sum = back_through_heads(
        message_land, raw, low, total, query_gain, key_gain, cosine, sine, allowed, qkv_grad
    )
    vectors[:, pl.ds(width, HD)] = query_sum
    vectors[:, pl.ds(width + HD, HD)] = key_sum
    load_qkv.wait()
    normed_grad[...] = nt_dot(qkv_grad[...], weights[:, pl.ds(0, lanes)]).astype(jnp.bfloat16)
    norms.begin()
    values.forward(0, far)
    values.forward(1, 0)
    router_pass.begin()
    spread(vector_slots, lambda e: vectors, vector_land)
    vector_land[device] = vectors[...]
    weight.send_sides()
    for step in range(1, shards - 1):
        values.forward(0, far - step)
        values.forward(1, step)
    addends(qkv, normed, qkv_grad)
    norms.forward(0, far)
    norms.forward(1, 0)
    qkv.send_corner()
    qkv.add_cores()
    for step in range(1, shards - 1):
        norms.forward(0, far - step)
        norms.forward(1, step)
    vector_sum[...] = collect(vector_slots, vector_land)
    vector_pass = LineSum(wires, shards, lambda t: vector_sum, lambda s: vector_line.at[s])
    vector_pass.begin()
    vector_line[shard] = vector_sum[...]
    router_line[shard] = router_sum[aligned(shard, lines), :]
    qkv.send_sides()
    weight.end()
    weight_line.begin()
    weight_land[shard] = held2[0, aligned(shard, block), :]
    values.end()
    mine = aligned(shard, rows)
    mixed_out[...] = (hidden[...] + out_own[mine, :].astype(jnp.float32)).astype(jnp.bfloat16)

    norms.end()
    change = normed_grad[mine, :].astype(jnp.float32)
    given = tokens[...].astype(jnp.float32)
    factor = norm_factor(given)
    gain_mine[...] = jnp.sum(change * given * factor, axis=0, keepdims=True)
    spread(gain_slots, lambda e: gain_mine, gain_land)
    scaled = change * gain[...]
    inner = jnp.mean(scaled * given, axis=-1, keepdims=True)
    result = hidden_grad[...] + factor * scaled - given * (factor * factor * factor) * inner
    input_grad[...] = result.astype(jnp.bfloat16)
    qkv.end()
    qkv_line.begin()
    qkv_land[shard] = held[0, aligned(shard, block), :]
    gain_land[device] = gain_mine[...]
    gain_line[shard] = collect(gain_slots, gain_land)
    gain_pass = LineSum(wires, shards, lambda t: gain_line.at[shard], lambda s: gain_line.at[s])
    gain_pass.begin()
    router_pass.arrive()
    router_out[...] = line_total(router_line, shards)
    vector_pass.arrive()
    vectors_out[...] = line_total(vector_line, shards)
    weight_line.arrive()
    weight_out[...] = line_total(weight_land, shards)
    qkv_line.arrive()
    for source in range(shards):
        for which, result_out in enumerate((query_out, key_out, value_out)):
            result_out[:, pl.ds(source * part, part)] = qkv_land[
                source, :, pl.ds(which * part, part)
            ].astype(jnp.float32)
    gain_pass.arrive()
    gain_out[...] = line_total(gain_line, shards)
    for copy in sent:
        copy.wait_send()
    groups = (back, norms, values, qkv, weight, qkv_line, weight_line, router_pass, vector_pass)
    for group in (*groups, gain_pass):
        group.drain()


def closing_call(
    hidden, grad, out_grad, ffn_gain, raw, low, total, query_gain, key_gain, tables, seg_row,
    tokens, gain, own_mixed, normed, router, out_w, qkv_w, out_total, planes, shards,
):
    rows, width = tokens.shape
    seq, lanes = low.shape
    each = width // planes
    block = each // shards
    lines = router.shape[0] // (planes * shards)
    hbm = pl.BlockSpec(memory_space=pltpu.HBM)
    vmem = pl.BlockSpec(memory_space=pltpu.VMEM)
    half, full = jnp.bfloat16, jnp.float32
    weight_shape = jax.ShapeDtypeStruct((block, width), full)
    vector = width + 2 * HD
    return pl.pallas_call(
        functools.partial(closing_kernel, shards, planes),
        in_specs=[vmem] * 17 + [hbm] * 3,
        out_specs=[vmem] * 9,
        out_shape=(
            jax.ShapeDtypeStruct((rows, width), half),
            jax.ShapeDtypeStruct((rows, width), half),
            weight_shape,
            weight_shape,
            weight_shape,
            weight_shape,
            jax.ShapeDtypeStruct((1, width), full),
            jax.ShapeDtypeStruct((lines, 128), full),
            jax.ShapeDtypeStruct((1, vector), full),
        ),
        scratch_shapes=sum_work(each, lanes)
        + sum_work(each, width)
        + [
            pltpu.VMEM((width, width), half),
            pltpu.VMEM((rows, width), full),
            pltpu.VMEM((rows, width), half),
            pltpu.VMEM((shards, rows, width // shards), half),
            pltpu.VMEM((seq, width // shards), half),
            pltpu.VMEM((seq, lanes), half),
            pltpu.VMEM((seq, width), half),
            pltpu.VMEM((1, vector), full),
            pltpu.VMEM((seq, width), half),
            pltpu.VMEM((2, shards, rows, width), half),
            pltpu.VMEM((2, shards, rows, width), half),
            pltpu.VMEM((shards, block, lanes), half),
            pltpu.VMEM((shards, block, width), half),
            pltpu.VMEM((1, width), full),
            pltpu.VMEM((planes, 1, width), full),
            pltpu.VMEM((shards, 1, width), full),
            pltpu.VMEM((planes, shards * lines, 128), full),
            pltpu.VMEM((shards * lines, 128), full),
            pltpu.VMEM((shards, lines, 128), full),
            pltpu.VMEM((planes, 1, vector), full),
            pltpu.VMEM((1, vector), full),
            pltpu.VMEM((shards, 1, vector), full),
            pltpu.SemaphoreType.DMA((80,)),
            pltpu.SemaphoreType.DMA((80,)),
            pltpu.SemaphoreType.DMA((3,)),
        ],
        compiler_params=pltpu.CompilerParams(
            collective_id=6, has_side_effects=True, vmem_limit_bytes=62 * MIB
        ),
        cost_estimate=pl.CostEstimate(flops=0, bytes_accessed=300 * MIB, transcendentals=0),
    )(
        hidden, grad, out_grad, ffn_gain, raw, low, total, query_gain, key_gain, *tables, seg_row,
        tokens, gain, own_mixed, normed, router, *held_in_hbm(out_w, qkv_w, out_total),
    )


LOW = jnp.bfloat16
WIDE = jnp.float32


def fast_local(
    tokens,
    segment_ids,
    routes,
    pair_order,
    attn_gain,
    w_query,
    w_key,
    w_value,
    query_gain,
    key_gain,
    w_out,
    ffn_gain,
    w_router,
    w_gate,
    w_up,
    w_down,
    out_grad,
):
    rows, width = tokens.shape
    top_count = routes.shape[1]
    planes = lax.axis_size(EXPERT)
    shards = lax.axis_size(SHARD)
    own_experts = w_gate.shape[0]
    experts = own_experts * planes
    capacity = 5 * rows * top_count // (4 * own_experts)
    seq = segment_ids.shape[0]
    device = lax.axis_index(EXPERT)
    shard = lax.axis_index(SHARD)
    part = width // shards

    index = device * shards + shard

    def placed(values, size):
        owner = jnp.arange(size) // values.size
        return jnp.where(owner == index, jnp.tile(values, size // values.size), 0)

    gains = [placed(attn_gain, width), placed(ffn_gain, width)]
    gains += [placed(query_gain, HD), placed(key_gain, HD)]
    gains = jnp.concatenate(gains)
    gains = jnp.pad(gains, (0, -gains.size % (16 * 128))).reshape(-1, 128)
    router_pad = jnp.pad(w_router, ((0, 0), (0, 128 - experts)))
    tables = turn_tables(seq)
    seg_row = segment_ids.reshape(1, seq)
    opened = opening_call(
        routes.T,
        pair_order.reshape(rows, top_count).T,
        gains,
        seg_row,
        tables,
        router_pad,
        w_query,
        w_key,
        w_value,
        tokens,
        w_out,
        out_grad,
        experts,
        own_experts,
        capacity,
        planes,
        shards,
    )
    kept, attn_row, ffn_row, query_row, key_row, normed_low, raw, low, total, mixed_all = opened[:10]
    router_w, qkv_w, tokens_seq, out_w, grad_all = opened[10:]
    router_w = router_w.reshape(width, 128)
    hidden, own_mixed, token_all, wide_w, down_w, down_next = meeting_call(
        tokens_seq, ffn_row, mixed_all, out_w, w_gate, w_up, w_down, planes, shards
    )
    grad_all = grad_all.reshape(planes, seq, width)
    own_ids = device * own_experts + jnp.arange(own_experts, dtype=jnp.int32)
    own_hot = (own_ids[:, None] == jnp.arange(128, dtype=jnp.int32)[None, :]).astype(WIDE)
    out_first, in_first, pull, wide_sum, down_sum, wide_next, down_next = expert_call(
        0,
        token_all,
        grad_all,
        kept,
        wide_w.reshape(width, -1),
        router_w,
        down_w,
        own_hot,
        experts,
        (w_gate, w_up, w_down, down_next),
        None,
    )
    before = (out_first, in_first, pull, wide_sum.reshape(shards, part, -1), down_sum)
    out_parts, in_parts, wide_sum, down_sum, router_grad, wide0, down0 = expert_call(
        1,
        token_all,
        grad_all,
        kept,
        wide_next.reshape(width, -1),
        router_w,
        down_next,
        own_hot,
        experts,
        None,
        before,
    )
    normed_two_grad, out_total, wide1, down1 = returning_call(
        in_parts, out_parts, wide_sum.reshape(shards, part, -1), down_sum
    )
    closed = closing_call(
        hidden,
        normed_two_grad,
        out_grad,
        ffn_row,
        raw,
        low,
        total,
        query_row,
        key_row,
        tables,
        seg_row,
        tokens,
        attn_row,
        own_mixed,
        normed_low,
        router_grad[:, :experts].reshape(-1, 128),
        out_w,
        qkv_w,
        out_total,
        planes,
        shards,
    )
    input_grad, mixed_out, query_w_grad, key_w_grad, value_w_grad, out_w_grad = closed[:6]
    attn_scale_grad, router_out, vectors = closed[6:]
    gate_grad, up_grad, down_grad = unpack_units((wide0, wide1), (down0, down1))
    flat = vectors.reshape(-1)

    def own_piece(values, start, size):
        return lax.dynamic_slice_in_dim(values, start + index * size, size)

    return (
        mixed_out,
        input_grad,
        own_piece(attn_scale_grad.reshape(-1), 0, attn_gain.size),
        query_w_grad,
        key_w_grad,
        value_w_grad,
        own_piece(flat, width, query_gain.size),
        own_piece(flat, width + HD, key_gain.size),
        out_w_grad,
        own_piece(flat, 0, ffn_gain.size),
        router_out.reshape(-1, experts),
        gate_grad,
        up_grad,
        down_grad,
    )


def solution(mesh):
    local = fast_local if mesh.shape[EXPERT] == 8 else general_local
    return jax.shard_map(
        local,
        mesh=mesh,
        in_specs=(
            P(BOTH, None),
            P(EXPERT),
            P(BOTH, None),
            P(BOTH),
            P(BOTH),
            P(BOTH, None),
            P(BOTH, None),
            P(BOTH, None),
            P(BOTH),
            P(BOTH),
            P(BOTH, None),
            P(BOTH),
            P(BOTH, None),
            P(EXPERT, SHARD, None),
            P(EXPERT, SHARD, None),
            P(EXPERT, None, SHARD),
            P(BOTH, None),
        ),
        out_specs=(
            P(BOTH, None),
            P(BOTH, None),
            P(BOTH),
            P(BOTH, None),
            P(BOTH, None),
            P(BOTH, None),
            P(BOTH),
            P(BOTH),
            P(BOTH, None),
            P(BOTH),
            P(BOTH, None),
            P(EXPERT, SHARD, None),
            P(EXPERT, SHARD, None),
            P(EXPERT, None, SHARD),
        ),
        check_vma=False,
    )
```
